32 devices in a mesh: grp: 4 (over z), shard: 8 (over y, x, core).
Axes of the slice: x: 2, y: 2, z: 4, core: 2. Of those that a mesh axis runs over, the one named last changes fastest.
Arguments:
- frames: bfloat16 [8192, 1024], P(('grp', 'shard')), may hold values from -6 to 6
- cotangent: bfloat16 [8192, 1024], P(('grp', 'shard')), may hold values from -6 to 6
- seg_start: int32 [32, 3], P(('grp', 'shard')), may hold values from 0 to 2047, as said below
- seg_length: int32 [32, 3], P(('grp', 'shard')), may hold values from 0 to 2044, as said below
- seg_step: int32 [32, 3], P(('grp', 'shard')), may hold values from 0 to 31, as said below
- time_table: float32 [32, 1024], replicated, may hold values from -6 to 6
- w_ada: bfloat16 [1024, 6144], P('shard', 'grp'), may hold values from -0.1875 to 0.1875
- b_ada: bfloat16 [6144], P('shard'), may hold values from -3 to 3
- w_qkv: bfloat16 [1024, 3072], P('shard', 'grp'), may hold values from -0.125 to 0.125
- b_qkv: bfloat16 [3072], P('shard'), may hold values from -0.29882812 to 0.29882812
- w_out: bfloat16 [1024, 1024], P('shard', 'grp'), may hold values from -1.5 to 1.5
- b_out: bfloat16 [1024], P('shard'), may hold values from -3 to 3
- w_up: bfloat16 [1024, 2048], P('shard', 'grp'), may hold values from -0.1875 to 0.1875
- b_up: bfloat16 [2048], P('shard'), may hold values from -3 to 3
- w_down: bfloat16 [2048, 1024], P('shard', 'grp'), may hold values from -0.125 to 0.125
- b_down: bfloat16 [1024], P('shard'), may hold values from -3 to 3
Outputs:
- output: bfloat16 [8192, 1024], P(('grp', 'shard'))
- grad_frames: float32 [8192, 1024], P(('grp', 'shard'))
- grad_time_table: float32 [32, 1024], P(None, 'shard')
- grad_w_ada: float32 [1024, 6144], P('shard', 'grp')
- grad_b_ada: float32 [6144], P('shard')
- grad_w_qkv: float32 [1024, 3072], P('shard', 'grp')
- grad_b_qkv: float32 [3072], P('shard')
- grad_w_out: float32 [1024, 1024], P('shard', 'grp')
- grad_b_out: float32 [1024], P('shard')
- grad_w_up: float32 [1024, 2048], P('shard', 'grp')
- grad_b_up: float32 [2048], P('shard')
- grad_w_down: float32 [2048, 1024], P('shard', 'grp')
- grad_b_down: float32 [1024], P('shard')
The draws below stay inside these ranges and needn't reach their ends.
Inputs may be any that keep to these rules, and one draw needn't show every extreme that they name: `seg_start`: frame f lies at position f % 2048 of packed row f // 2048; row block b holds frames b * 256 to (b + 1) * 256 - 1. The 3 slots of block b list every segment that intersects it, by start position in its packed row; every frame lies in exactly one listed segment; slots of length 0 are empty and hold start 0. Segments stay inside their packed row, and in every packed row one segment starts in its first block and ends in its last, and the other segments lie inside the first or the last block. `seg_length`: A segment has the same start and length in every block that lists it. `seg_step`: A segment has the same timestep row in every block that lists it; empty slots hold 0.
All inputs are finite; a program needn't handle non-finite values.
Results may differ from the reference program's by a relative error of at most 0.014.
Values may be sent and summed in bfloat16 or wider, within the bound.
No kernel may reach another device: no remote copies, remote signals or barrier semaphores. Data moves between devices by JAX's collectives and lax.ppermute only.
A program may use at most 256 MiB of HBM per device.

```python
import jax
import jax.numpy as jnp
from jax import lax

D = 1024
H = 16
HD = 64
FF = 2048
TOK_DEV = 256
STEPS = 32
SLOTS = 3
ROW = 2048
FRAMES = 8192
BLOCKS = 32
N_GRP = 4
N_SHARD = 8


def segment_tables(key):
    group_keys = jax.random.split(jax.random.fold_in(key, 17), N_GRP)
    group_ids = jnp.arange(N_GRP, dtype=jnp.int32)

    def one_group(group_key, group_id):
        key_head, key_tail, key_cut_head, key_cut_tail, key_labels = jax.random.split(group_key, 5)
        opening_group = group_id == 0
        head_frames = jnp.where(opening_group, 2, jax.random.randint(key_head, (), 2, TOK_DEV))
        tail_frames = jnp.where(opening_group, 2, jax.random.randint(key_tail, (), 2, TOK_DEV))
        head_cut = jax.random.randint(key_cut_head, (), 1, head_frames)
        tail_cut = jnp.where(opening_group, tail_frames - 1, jax.random.randint(key_cut_tail, (), 1, tail_frames))
        labels = jax.random.randint(key_labels, (5,), 0, STEPS)
        labels = labels.at[0].set(jnp.where(opening_group, STEPS - 1, labels[0]))
        tail_start = ROW - tail_frames
        long_length = ROW - head_frames - tail_frames
        block_ids = jnp.arange(N_SHARD, dtype=jnp.int32)
        opening = block_ids == 0
        closing = block_ids == N_SHARD - 1
        zero_int = jnp.zeros((N_SHARD,), jnp.int32)
        start_first = jnp.where(opening, 0, head_frames) + zero_int
        start_second = jnp.where(opening, head_cut, jnp.where(closing, tail_start, 0)) + zero_int
        start_third = jnp.where(opening, head_frames, jnp.where(closing, tail_start + tail_cut, 0)) + zero_int
        length_first = jnp.where(opening, head_cut, long_length) + zero_int
        length_second = jnp.where(opening, head_frames - head_cut, jnp.where(closing, tail_cut, 0)) + zero_int
        length_third = jnp.where(opening, long_length, jnp.where(closing, tail_frames - tail_cut, 0)) + zero_int
        label_first = jnp.where(opening, labels[0], labels[2]) + zero_int
        label_second = jnp.where(opening, labels[1], jnp.where(closing, labels[3], 0)) + zero_int
        label_third = jnp.where(opening, labels[2], jnp.where(closing, labels[4], 0)) + zero_int
        starts = jnp.stack((start_first, start_second, start_third), axis=1)
        lengths = jnp.stack((length_first, length_second, length_third), axis=1)
        steps_table = jnp.stack((label_first, label_second, label_third), axis=1)
        return (starts, lengths, steps_table)
    starts, lengths, steps_table = jax.vmap(one_group)(group_keys, group_ids)
    return (starts.reshape(BLOCKS, SLOTS).astype(jnp.int32), lengths.reshape(BLOCKS, SLOTS).astype(jnp.int32), steps_table.reshape(BLOCKS, SLOTS).astype(jnp.int32))


def draw_seg_start(key, part):
    tables = segment_tables(key)
    return tables[0]


def draw_seg_length(key, part):
    tables = segment_tables(key)
    return tables[1]


def draw_seg_step(key, part):
    tables = segment_tables(key)
    return tables[2]


def levels(own_key, shape, cuts, low, high):
    gain, own = 1.0, jax.random.fold_in(own_key, 6)
    for axis_at, shards_of in cuts:
        steps = jnp.exp(jax.random.uniform(jax.random.fold_in(own, axis_at), (shards_of,), jnp.float32, low / len(cuts), high / len(cuts)))
        gain = gain * jnp.repeat(steps, shape[axis_at] // shards_of).reshape([-1 if axis == axis_at else 1 for axis in range(len(shape))])
    return gain


def gaussian(stream_key, shape, deviation, limit, cuts=(), kind=jnp.bfloat16):
    gain = levels(stream_key, shape, cuts, -0.22, 0.18) if cuts else 1.0
    result = jax.random.normal(stream_key, shape, jnp.float32) * deviation * gain
    return jnp.minimum(jnp.maximum(result, -limit), limit).astype(kind)


def setup_inputs(seed: int = 0) -> dict:
    arg_keys = jax.random.split(jax.random.key(seed), 17)
    frames = gaussian(arg_keys[0], (FRAMES, D), 1.0, 6.0, ((0, 32),))
    cotangent = gaussian(arg_keys[1], (FRAMES, D), 1.0, 6.0, ((0, 32),))
    seg_start = draw_seg_start(jax.random.fold_in(arg_keys[16], 71), 0)
    seg_length = draw_seg_length(jax.random.fold_in(arg_keys[16], 71), 0)
    seg_step = draw_seg_step(jax.random.fold_in(arg_keys[16], 71), 0)
    time_table = gaussian(arg_keys[5], (STEPS, D), 1.0, 6.0, (), jnp.float32)
    w_ada = gaussian(arg_keys[6], (D, 6 * D), D ** -0.5, 0.1875, ((0, 8), (1, 4)))
    b_ada = gaussian(arg_keys[7], (6 * D,), 0.5, 3.0, ((0, 8),))
    w_qkv = gaussian(arg_keys[8], (D, 3 * D), (2 * D) ** -0.5, 0.125, ((0, 8), (1, 4)))
    b_qkv = gaussian(arg_keys[9], (3 * D,), 0.05, 0.29882812, ((0, 8),))
    w_out = gaussian(arg_keys[10], (D, D), (max(D // 64, 4)) ** -0.5, 1.5, ((0, 8), (1, 4)))
    b_out = gaussian(arg_keys[11], (D,), 0.5, 3.0, ((0, 8),))
    w_up = gaussian(arg_keys[12], (D, FF), D ** -0.5, 0.1875, ((0, 8), (1, 4)))
    b_up = gaussian(arg_keys[13], (FF,), 0.5, 3.0, ((0, 8),))
    w_down = gaussian(arg_keys[14], (FF, D), FF ** -0.5, 0.125, ((0, 8), (1, 4)))
    b_down = gaussian(arg_keys[15], (D,), 0.5, 3.0, ((0, 8),))
    return dict(frames=frames, cotangent=cotangent, seg_start=seg_start, seg_length=seg_length, seg_step=seg_step, time_table=time_table, w_ada=w_ada, b_ada=b_ada, w_qkv=w_qkv, b_qkv=b_qkv, w_out=w_out, b_out=b_out, w_up=w_up, b_up=b_up, w_down=w_down, b_down=b_down)


@jax.custom_vjp
def low(v):
    return lax.optimization_barrier(v.astype(jnp.bfloat16)).astype(jnp.float32)

@jax.custom_vjp
def low_back(v):
    return v

def low_keep(v):
    return (low(v), None)

def low_pass(kept, grad):
    return (grad,)

def back_keep(v):
    return (v, None)

def back_low(kept, grad):
    return (low(grad),)
low.defvjp(low_keep, low_pass)
low_back.defvjp(back_keep, back_low)
eps_norm = 1e-06
top_precision = lax.Precision.HIGHEST

def normalize(tensor):
    centred = tensor - lax.optimization_barrier(jnp.mean(tensor, axis=-1, keepdims=True))
    return centred * lax.rsqrt(lax.optimization_barrier(jnp.mean(centred * centred, axis=-1, keepdims=True)) + eps_norm)

def modulate(tensor, scale_vec, shift_vec):
    return normalize(tensor) * (1.0 + scale_vec) + shift_vec

def angles(positions):
    half_width = HD // 2
    inverse = 10000.0 ** (-jnp.arange(half_width, dtype=jnp.float32) / half_width)
    phase_grid = positions[:, None] * inverse[None, :]
    return (jnp.cos(phase_grid), jnp.sin(phase_grid))

def rotate(tensor, cosine_vals, sine_vals):
    row_total = tensor.shape[0]
    halves = tensor.reshape(row_total, H, 2, HD // 2)
    former = halves[:, :, 0]
    latter = halves[:, :, 1]
    cosine_part = cosine_vals[:, None, :]
    sine_part = sine_vals[:, None, :]
    turned = jnp.stack((former * cosine_part - latter * sine_part, latter * cosine_part + former * sine_part), axis=2)
    return turned.reshape(row_total, D)

def attend(queries, key_rows, values, seg_low):
    tile_rows = 512 if ROW % 512 == 0 else ROW
    tiles = ROW // tile_rows
    key_heads = key_rows.reshape(ROW, H, HD)
    value_heads = values.reshape(ROW, H, HD)

    @jax.checkpoint
    def one_tile(tile_item):
        query_tile, low_tile = tile_item
        scores = low_back(0.125 * jnp.einsum('qhd,khd->hqk', query_tile.reshape(tile_rows, H, HD), key_heads, precision=top_precision))
        inside = low_tile[:, None] == seg_low[None, :]
        expo = jnp.where(inside[None], jnp.exp(scores), 0.0)
        numerator = jnp.einsum('hqk,khd->qhd', low(expo), value_heads, precision=top_precision)
        return (numerator, lax.optimization_barrier(jnp.sum(expo, axis=2)))
    numerator, denominator = lax.map(one_tile, (queries.reshape(tiles, tile_rows, D), seg_low.reshape(tiles, tile_rows)))
    return (numerator.reshape(ROW, H, HD), jnp.transpose(denominator, (0, 2, 1)).reshape(ROW, H))

def forward(frames, time_table, w_ada, b_ada, w_qkv, b_qkv, w_out, b_out, w_up, b_up, w_down, b_down, member, seg_low, cosine_vals, sine_vals, seg_step):
    activated = low(jax.nn.silu(time_table[seg_step]))
    modulation = jnp.einsum('bjd,dc->bjc', activated, w_ada, precision=top_precision) + b_ada
    frame_mod = jnp.einsum('btj,bjc->btc', member, modulation, precision=top_precision).reshape(FRAMES, 6 * D)
    shift_attn, scale_attn, gate_attn, shift_ff, scale_ff, gate_ff = jnp.split(frame_mod, 6, axis=1)
    hidden_attn = low(modulate(frames, scale_attn, shift_attn))
    projected = low_back(jnp.dot(hidden_attn, w_qkv, precision=top_precision) + b_qkv)
    queries = low(rotate(projected[:, :D], cosine_vals, sine_vals))
    key_rows = low(rotate(projected[:, D:2 * D], cosine_vals, sine_vals))
    values = low(projected[:, 2 * D:])
    numerator, denominator = lax.map(lambda group_item: attend(*group_item), (queries.reshape(N_GRP, ROW, D), key_rows.reshape(N_GRP, ROW, D), values.reshape(N_GRP, ROW, D), seg_low.reshape(N_GRP, ROW)))
    numerator = low_back(numerator.reshape(FRAMES, H, HD))
    mixed = low(low_back((numerator / denominator.reshape(FRAMES, H)[:, :, None]).reshape(FRAMES, D)))
    attn_branch = low_back(jnp.dot(mixed, w_out, precision=top_precision) + b_out)
    after_attn = frames + gate_attn * attn_branch
    hidden_ff = low(modulate(after_attn, scale_ff, shift_ff))
    upward = low_back(jnp.dot(hidden_ff, w_up, precision=top_precision) + b_up)
    activation = low(jax.nn.gelu(upward, approximate=True))
    ff_branch = low_back(jnp.dot(activation, w_down, precision=top_precision) + b_down)
    return after_attn + gate_ff * ff_branch

def reference(frames, cotangent, seg_start, seg_length, seg_step, time_table, w_ada, b_ada, w_qkv, b_qkv, w_out, b_out, w_up, b_up, w_down, b_down):
    block_ids = jnp.arange(BLOCKS, dtype=jnp.int32)
    local_pos = (block_ids % N_SHARD)[:, None] * TOK_DEV + jnp.arange(TOK_DEV, dtype=jnp.int32)[None, :]
    slot_end = seg_start + seg_length
    member_mask = (local_pos[:, :, None] >= seg_start[:, None, :]) & (local_pos[:, :, None] < slot_end[:, None, :])
    member = member_mask.astype(jnp.float32)
    seg_low = lax.optimization_barrier(jnp.sum(jnp.where(member_mask, seg_start[:, None, :], 0), axis=2)).reshape(FRAMES).astype(jnp.int32)
    cosine_vals, sine_vals = angles((local_pos.reshape(FRAMES) - seg_low).astype(jnp.float32))
    params = tuple((tensor.astype(jnp.float32) for tensor in (frames, time_table, w_ada, b_ada, w_qkv, b_qkv, w_out, b_out, w_up, b_up, w_down, b_down)))

    def closed(*arrays):
        return forward(*arrays, member, seg_low, cosine_vals, sine_vals, seg_step)
    output, pullback = jax.vjp(closed, *params)
    gradients = pullback(cotangent.astype(jnp.float32))
    return (output.astype(jnp.bfloat16), gradients[0], gradients[1], gradients[2], gradients[3], gradients[4], gradients[5], gradients[6], gradients[7], gradients[8], gradients[9], gradients[10], gradients[11])
```

```python
from functools import partial

import jax
import jax.numpy as jnp
from jax import lax
from jax.experimental import pallas as pl
from jax.experimental.pallas import tpu as pltpu
from jax.sharding import PartitionSpec as P

D = 1024
H = 16
HD = 64


eps_norm = 1e-06
top_precision = lax.Precision.HIGHEST


def normalize(tensor):
    centred = tensor - jnp.mean(tensor, axis=-1, keepdims=True)
    return centred * lax.rsqrt(jnp.mean(centred * centred, axis=-1, keepdims=True) + eps_norm)


def modulate(tensor, scale_vec, shift_vec):
    return normalize(tensor) * (1.0 + scale_vec) + shift_vec


def angles(positions):
    half_width = HD // 2
    inverse = 10000.0 ** (-jnp.arange(half_width, dtype=jnp.float32) / half_width)
    phase_grid = positions[:, None] * inverse[None, :]
    return (jnp.cos(phase_grid), jnp.sin(phase_grid))


def rotate(tensor, cosine_vals, sine_vals):
    row_total = tensor.shape[0]
    halves = tensor.reshape(row_total, H, 2, HD // 2)
    former = halves[:, :, 0]
    latter = halves[:, :, 1]
    cosine_part = cosine_vals[:, None, :]
    sine_part = sine_vals[:, None, :]
    turned = jnp.stack(
        (former * cosine_part - latter * sine_part, latter * cosine_part + former * sine_part),
        axis=2,
    )
    return turned.reshape(row_total, D)


def tile_width(row_total):
    for candidate in (512, 256, 128):
        return candidate
    return row_total


def head_view(tensor):
    return tensor.reshape(tensor.shape[0], H, HD)


def local_any(
    frames,
    cotangent,
    seg_start,
    seg_length,
    seg_step,
    time_table,
    w_ada,
    b_ada,
    w_qkv,
    b_qkv,
    w_out,
    b_out,
    w_up,
    b_up,
    w_down,
    b_down,
):
    frame_rows = frames.shape[0]
    positions = lax.axis_index("shard") * frame_rows + jnp.arange(frame_rows, dtype=jnp.int32)
    slot_start = seg_start[0]
    slot_end = slot_start + seg_length[0]
    member_mask = (positions[:, None] >= slot_start[None, :]) & (
        positions[:, None] < slot_end[None, :]
    )
    member = member_mask.astype(jnp.float32)
    seg_low = jnp.sum(jnp.where(member_mask, slot_start[None, :], 0), axis=1)
    seg_high = jnp.sum(jnp.where(member_mask, slot_end[None, :], 0), axis=1)
    cosine_vals, sine_vals = angles((positions - seg_low).astype(jnp.float32))
    columns = (
        lax.all_gather(w_ada, "grp", axis=1, tiled=True),
        lax.all_gather(w_qkv, "grp", axis=1, tiled=True),
        lax.all_gather(w_out, "grp", axis=1, tiled=True),
        lax.all_gather(w_up, "grp", axis=1, tiled=True),
        lax.all_gather(w_down, "grp", axis=1, tiled=True),
    )
    gathered = (
        lax.all_gather(columns[0], "shard", axis=0, tiled=True),
        lax.all_gather(columns[1], "shard", axis=0, tiled=True),
        lax.all_gather(columns[2], "shard", axis=0, tiled=True),
        lax.all_gather(columns[3], "shard", axis=0, tiled=True),
        lax.all_gather(columns[4], "shard", axis=0, tiled=True),
        lax.all_gather(b_ada, "shard", axis=0, tiled=True),
        lax.all_gather(b_qkv, "shard", axis=0, tiled=True),
        lax.all_gather(b_out, "shard", axis=0, tiled=True),
        lax.all_gather(b_up, "shard", axis=0, tiled=True),
        lax.all_gather(b_down, "shard", axis=0, tiled=True),
    )
    ada_full, qkv_full, out_full, up_full, down_full = (
        gathered[0],
        gathered[1],
        gathered[2],
        gathered[3],
        gathered[4],
    )
    ada_bias, qkv_bias, out_bias, up_bias, down_bias = [
        bias_row.astype(jnp.float32) for bias_row in gathered[5:]
    ]
    step_onehot = (
        seg_step[0][:, None] == jnp.arange(time_table.shape[0], dtype=jnp.int32)[None, :]
    ).astype(jnp.float32)
    time_rows = jnp.dot(step_onehot, time_table, precision=top_precision)
    activated = jax.nn.silu(time_rows).astype(jnp.bfloat16)
    modulation = jnp.dot(activated, ada_full, preferred_element_type=jnp.float32) + ada_bias
    frame_mod = jnp.dot(member, modulation, precision=top_precision)
    shift_attn, scale_attn, gate_attn, shift_ff, scale_ff, gate_ff = jnp.split(frame_mod, 6, axis=1)
    inputs = frames.astype(jnp.float32)
    hidden_attn = modulate(inputs, scale_attn, shift_attn).astype(jnp.bfloat16)
    projected = jnp.dot(hidden_attn, qkv_full, preferred_element_type=jnp.float32) + qkv_bias
    queries = rotate(projected[:, :D], cosine_vals, sine_vals).astype(jnp.bfloat16)
    keys_rot = rotate(projected[:, D : 2 * D], cosine_vals, sine_vals).astype(jnp.bfloat16)
    values = projected[:, 2 * D :].astype(jnp.bfloat16)
    query_heads = head_view(queries)
    key_heads = head_view(keys_rot)
    value_heads = head_view(values)
    zero_heads = jnp.zeros((frame_rows, H, HD), jnp.float32)
    key_piece = lax.all_gather(keys_rot, "shard", axis=0, tiled=True)
    value_piece = lax.all_gather(values, "shard", axis=0, tiled=True)
    piece_rows = key_piece.shape[0]
    tile_rows = tile_width(piece_rows)
    tiles = piece_rows // tile_rows

    def tile_step(partial_sums, tile_item):
        key_tile, value_tile, offset = tile_item
        key_pos = offset + jnp.arange(tile_rows, dtype=jnp.int32)
        inside = (key_pos[None, :] >= seg_low[:, None]) & (key_pos[None, :] < seg_high[:, None])
        scores = 0.125 * jnp.einsum(
            "rhd,khd->hrk", query_heads, head_view(key_tile), preferred_element_type=jnp.float32
        )
        expo = jnp.where(inside[None], jnp.exp(scores), 0.0)
        numerator, denominator = partial_sums
        numerator = numerator + jnp.einsum(
            "hrk,khd->rhd",
            expo.astype(jnp.bfloat16),
            head_view(value_tile),
            preferred_element_type=jnp.float32,
        )
        denominator = denominator + jnp.sum(expo, axis=2).T
        return ((numerator, denominator), None)

    tile_items = (
        key_piece.reshape(tiles, tile_rows, D),
        value_piece.reshape(tiles, tile_rows, D),
        jnp.arange(tiles, dtype=jnp.int32) * tile_rows,
    )
    numerator, denominator = lax.scan(
        tile_step, (zero_heads, jnp.zeros((frame_rows, H), jnp.float32)), tile_items
    )[0]
    mixed = numerator / denominator[:, :, None]
    mixed_low = mixed.reshape(frame_rows, D).astype(jnp.bfloat16)
    attn_branch = jnp.dot(mixed_low, out_full, preferred_element_type=jnp.float32) + out_bias
    after_attn = inputs + gate_attn * attn_branch
    hidden_ff = modulate(after_attn, scale_ff, shift_ff).astype(jnp.bfloat16)
    upward = jnp.dot(hidden_ff, up_full, preferred_element_type=jnp.float32) + up_bias
    activation = jax.nn.gelu(upward, approximate=True).astype(jnp.bfloat16)
    ff_branch = jnp.dot(activation, down_full, preferred_element_type=jnp.float32) + down_bias
    output = (after_attn + gate_ff * ff_branch).astype(jnp.bfloat16)
    columns_back = (
        lax.all_gather(w_ada, "grp", axis=1, tiled=True),
        lax.all_gather(w_qkv, "grp", axis=1, tiled=True),
        lax.all_gather(w_out, "grp", axis=1, tiled=True),
        lax.all_gather(w_up, "grp", axis=1, tiled=True),
        lax.all_gather(w_down, "grp", axis=1, tiled=True),
    )
    gathered_back = (
        lax.all_gather(columns_back[0], "shard", axis=0, tiled=True),
        lax.all_gather(columns_back[1], "shard", axis=0, tiled=True),
        lax.all_gather(columns_back[2], "shard", axis=0, tiled=True),
        lax.all_gather(columns_back[3], "shard", axis=0, tiled=True),
        lax.all_gather(columns_back[4], "shard", axis=0, tiled=True),
    )
    ada_back, qkv_back, out_back, up_back, down_back = (
        gathered_back[0],
        gathered_back[1],
        gathered_back[2],
        gathered_back[3],
        gathered_back[4],
    )
    grad_out = cotangent.astype(jnp.float32)
    d_branch = (gate_ff * grad_out).astype(jnp.bfloat16)
    d_gate_ff = grad_out * ff_branch
    g_down = jnp.dot(activation.T, d_branch, preferred_element_type=jnp.float32)
    gb_down = jnp.sum(d_branch.astype(jnp.float32), axis=0)
    d_activation = jnp.dot(d_branch, down_back.T, preferred_element_type=jnp.float32)
    gelu_pull = jax.vjp(partial(jax.nn.gelu, approximate=True), upward)[1]
    d_upward = gelu_pull(d_activation)[0].astype(jnp.bfloat16)
    g_up = jnp.dot(hidden_ff.T, d_upward, preferred_element_type=jnp.float32)
    gb_up = jnp.sum(d_upward.astype(jnp.float32), axis=0)
    d_hidden_ff = jnp.dot(d_upward, up_back.T, preferred_element_type=jnp.float32)
    ff_pull = jax.vjp(modulate, after_attn, scale_ff, shift_ff)[1]
    dx_ff, d_scale_ff, d_shift_ff = ff_pull(d_hidden_ff)
    d_after = grad_out + dx_ff
    d_attn = (gate_attn * d_after).astype(jnp.bfloat16)
    d_gate_attn = d_after * attn_branch
    g_out = jnp.dot(mixed_low.T, d_attn, preferred_element_type=jnp.float32)
    gb_out = jnp.sum(d_attn.astype(jnp.float32), axis=0)
    d_mixed = jnp.dot(d_attn, out_back.T, preferred_element_type=jnp.float32).astype(jnp.bfloat16)
    d_mixed_heads = head_view(d_mixed).astype(jnp.float32)
    delta = jnp.sum(d_mixed_heads * mixed, axis=2) / denominator
    d_numer = (d_mixed_heads / denominator[:, :, None]).astype(jnp.bfloat16).reshape(frame_rows, D)
    dnum_heads = head_view(d_numer)
    delta_heads = delta.T
    key_piece = lax.all_gather(keys_rot, "shard", axis=0, tiled=True)
    value_piece = lax.all_gather(values, "shard", axis=0, tiled=True)
    piece_rows = key_piece.shape[0]
    fold_tile_rows = tile_width(piece_rows)
    tiles = piece_rows // fold_tile_rows

    def tile_step(grad_sum, tile_item):
        key_tile, value_tile, offset = tile_item
        key_pos = offset + jnp.arange(fold_tile_rows, dtype=jnp.int32)
        inside = (key_pos[None, :] >= seg_low[:, None]) & (key_pos[None, :] < seg_high[:, None])
        scores = 0.125 * jnp.einsum(
            "rhd,khd->hrk", query_heads, head_view(key_tile), preferred_element_type=jnp.float32
        )
        expo = jnp.where(inside[None], jnp.exp(scores), 0.0)
        slope = jnp.einsum(
            "rhd,khd->hrk", dnum_heads, head_view(value_tile), preferred_element_type=jnp.float32
        )
        d_scores = (expo * (slope - delta_heads[:, :, None])).astype(jnp.bfloat16)
        grad_sum = grad_sum + 0.125 * jnp.einsum(
            "hrk,khd->rhd", d_scores, head_view(key_tile), preferred_element_type=jnp.float32
        )
        return (grad_sum, None)

    tile_items = (
        key_piece.reshape(tiles, fold_tile_rows, D),
        value_piece.reshape(tiles, fold_tile_rows, D),
        jnp.arange(tiles, dtype=jnp.int32) * fold_tile_rows,
    )
    d_query = lax.scan(tile_step, zero_heads, tile_items)[0]
    delta_all = lax.all_gather(delta, "shard", axis=0, tiled=True)

    def fold_key_grad(running, piece):
        query_piece, dnum_piece = piece
        piece_rows = query_piece.shape[0]
        tile_rows = tile_width(piece_rows)
        tiles = piece_rows // tile_rows

        def tile_step(grad_pair, tile_item):
            query_tile, dnum_tile, delta_tile, offset = tile_item
            query_pos = offset + jnp.arange(tile_rows, dtype=jnp.int32)
            inside = (query_pos[:, None] >= seg_low[None, :]) & (
                query_pos[:, None] < seg_high[None, :]
            )
            query_tile_heads = head_view(query_tile)
            dnum_tile_heads = head_view(dnum_tile)
            scores = 0.125 * jnp.einsum(
                "qhd,rhd->hqr", query_tile_heads, key_heads, preferred_element_type=jnp.float32
            )
            expo = jnp.where(inside[None], jnp.exp(scores), 0.0)
            slope = jnp.einsum(
                "qhd,rhd->hqr", dnum_tile_heads, value_heads, preferred_element_type=jnp.float32
            )
            d_scores = (expo * (slope - delta_tile.T[:, :, None])).astype(jnp.bfloat16)
            d_keys, d_values = grad_pair
            d_keys = d_keys + 0.125 * jnp.einsum(
                "hqr,qhd->rhd", d_scores, query_tile_heads, preferred_element_type=jnp.float32
            )
            d_values = d_values + jnp.einsum(
                "hqr,qhd->rhd",
                expo.astype(jnp.bfloat16),
                dnum_tile_heads,
                preferred_element_type=jnp.float32,
            )
            return ((d_keys, d_values), None)

        tile_items = (
            query_piece.reshape(tiles, tile_rows, D),
            dnum_piece.reshape(tiles, tile_rows, D),
            delta_all.reshape(tiles, tile_rows, H),
            jnp.arange(tiles, dtype=jnp.int32) * tile_rows,
        )
        return lax.scan(tile_step, running, tile_items)[0]

    d_keys, d_values = fold_key_grad(
        (zero_heads, zero_heads),
        (
            lax.all_gather(queries, "shard", axis=0, tiled=True),
            lax.all_gather(d_numer, "shard", axis=0, tiled=True),
        ),
    )
    grad_query = rotate(d_query.reshape(frame_rows, D), cosine_vals, -sine_vals)
    grad_key = rotate(d_keys.reshape(frame_rows, D), cosine_vals, -sine_vals)
    d_projected = jnp.concatenate(
        (grad_query, grad_key, d_values.reshape(frame_rows, D)), axis=1
    ).astype(jnp.bfloat16)
    g_qkv = jnp.dot(hidden_attn.T, d_projected, preferred_element_type=jnp.float32)
    gb_qkv = jnp.sum(d_projected.astype(jnp.float32), axis=0)
    d_hidden_attn = jnp.dot(d_projected, qkv_back.T, preferred_element_type=jnp.float32)
    attn_pull = jax.vjp(modulate, inputs, scale_attn, shift_attn)[1]
    dx_attn, d_scale_attn, d_shift_attn = attn_pull(d_hidden_attn)
    grad_frames = d_after + dx_attn
    d_frame_mod = jnp.concatenate(
        (d_shift_attn, d_scale_attn, d_gate_attn, d_shift_ff, d_scale_ff, d_gate_ff), axis=1
    )
    d_slot = jnp.dot(member.T, d_frame_mod, precision=top_precision)
    g_ada = jnp.dot(activated.astype(jnp.float32).T, d_slot, precision=top_precision)
    gb_ada = jnp.sum(d_slot, axis=0)
    d_activated = jnp.dot(
        d_slot, ada_back.T, precision=top_precision, preferred_element_type=jnp.float32
    )
    silu_pull = jax.vjp(jax.nn.silu, time_rows)[1]
    d_time_rows = silu_pull(d_activated)[0]
    g_table = jnp.dot(step_onehot.T, d_time_rows, precision=top_precision)
    group_sums = (
        lax.psum_scatter(g_ada, "shard", scatter_dimension=0, tiled=True),
        lax.psum_scatter(g_qkv, "shard", scatter_dimension=0, tiled=True),
        lax.psum_scatter(g_out, "shard", scatter_dimension=0, tiled=True),
        lax.psum_scatter(g_up, "shard", scatter_dimension=0, tiled=True),
        lax.psum_scatter(g_down, "shard", scatter_dimension=0, tiled=True),
        lax.psum_scatter(gb_ada, "shard", scatter_dimension=0, tiled=True),
        lax.psum_scatter(gb_qkv, "shard", scatter_dimension=0, tiled=True),
        lax.psum_scatter(gb_out, "shard", scatter_dimension=0, tiled=True),
        lax.psum_scatter(gb_up, "shard", scatter_dimension=0, tiled=True),
        lax.psum_scatter(gb_down, "shard", scatter_dimension=0, tiled=True),
        lax.psum_scatter(g_table, "shard", scatter_dimension=1, tiled=True),
    )
    wide_sums = (
        lax.psum_scatter(group_sums[0], "grp", scatter_dimension=1, tiled=True),
        lax.psum_scatter(group_sums[1], "grp", scatter_dimension=1, tiled=True),
        lax.psum_scatter(group_sums[2], "grp", scatter_dimension=1, tiled=True),
        lax.psum_scatter(group_sums[3], "grp", scatter_dimension=1, tiled=True),
        lax.psum_scatter(group_sums[4], "grp", scatter_dimension=1, tiled=True),
    )
    small_sums = lax.psum(
        (group_sums[5], group_sums[6], group_sums[7], group_sums[8], group_sums[9], group_sums[10]),
        "grp",
    )
    finals = tuple(wide_sums) + tuple(small_sums)
    return (
        output,
        grad_frames,
        finals[10],
        finals[0],
        finals[5],
        finals[1],
        finals[6],
        finals[2],
        finals[7],
        finals[3],
        finals[8],
        finals[4],
        finals[9],
    )


LANES = 128
SEPARATE = -(2.0**100)
GELU_C = 0.7978845608028654
GELU_A = 0.044715
NT = (((1,), (1,)), ((), ()))
TN = (((0,), (0,)), ((), ()))
f32 = jnp.float32
bf16 = jnp.bfloat16


def dot(left, right, dims=(((1,), (0,)), ((), ()))):
    return lax.dot_general(left, right, dims, preferred_element_type=f32)


def params(limit_mib, steps=1):
    return pltpu.CompilerParams(
        dimension_semantics=("arbitrary",) * steps, vmem_limit_bytes=limit_mib * 2**20
    )


def moments(value):
    centred = value - jnp.mean(value, axis=1, keepdims=True)
    inv = lax.rsqrt(jnp.mean(centred * centred, axis=1, keepdims=True) + eps_norm)
    return centred * inv, inv


def norm_back(weighted, normal, inv):
    return (
        weighted
        - jnp.mean(weighted, axis=1, keepdims=True)
        - normal * jnp.mean(weighted * normal, axis=1, keepdims=True)
    ) * inv


def swap_halves(value):
    lane = lax.broadcasted_iota(jnp.int32, value.shape, 1)
    return jnp.where(lane % HD < HD // 2, pltpu.roll(value, 96, 1), pltpu.roll(value, 32, 1))


def members(seg_ref, block, rows):
    place = block * rows + lax.broadcasted_iota(jnp.int32, (rows, 1), 0)
    out = []
    for slot in range(3):
        begin = seg_ref[block, slot]
        inside = (place >= begin) & (place < begin + seg_ref[block, 3 + slot])
        out.append(inside.astype(f32))
    return out


def mod_rows(table_ref, seg_ref, block, member, part):
    total = None
    for slot in range(3):
        row = table_ref[pl.ds(seg_ref[block, 6 + slot], 1), pl.ds(part * D, D)]
        term = member[slot] * row
        total = term if total is None else total + term
    return total


def slot_sums(member, value):
    return [jnp.sum(column * value, axis=0, keepdims=True) for column in member]


def qkv_kernel(seg_ref, x_ref, table_ref, w_ref, b_ref, cos_ref, sin_ref, q_ref, k_ref, v_ref, h_ref):
    block = pl.program_id(0)
    last = pl.num_programs(0) - 1
    rows = x_ref.shape[0]
    member = members(seg_ref, block, rows)
    normal, _ = moments(x_ref[...].astype(f32))
    shift = mod_rows(table_ref, seg_ref, block, member, 0)
    scale = mod_rows(table_ref, seg_ref, block, member, 1)
    hidden = (normal * (1.0 + scale) + shift).astype(bf16)
    h_ref[...] = hidden
    projected = dot(hidden, w_ref[...]) + b_ref[...]
    cosine, sine = cos_ref[...], sin_ref[...]
    turned = []
    for part in range(2):
        piece = projected[:, part * LANES : (part + 1) * LANES]
        turned.append(piece * cosine + swap_halves(piece) * sine)
    queries = turned[0].astype(bf16).astype(f32) * 0.125
    keys = turned[1]
    values = projected[:, 2 * LANES :]
    lane = lax.broadcasted_iota(jnp.int32, (rows, LANES), 1)
    place = block * rows + lax.broadcasted_iota(jnp.int32, (rows, 1), 0)
    query_extra = jnp.zeros((rows, LANES), f32)
    key_extra = jnp.zeros((rows, LANES), f32)
    for index in range(6):
        where, slot = (0, index) if index < 3 else (last, index - 3)
        begin = seg_ref[where, slot]
        inside = (place >= begin) & (place < begin + seg_ref[where, 3 + slot])
        here = lane == HD + index
        query_extra = jnp.where(here, jnp.where(inside, 0.0, SEPARATE), query_extra)
        key_extra = jnp.where(here, jnp.where(inside, 1.0, 0.0), key_extra)
    value_extra = jnp.where((lane >= HD) & (lane < HD + 3), 1.0, 0.0)
    low = lane < HD
    for head in range(2):
        for ref, value, extra in (
            (q_ref, queries, query_extra),
            (k_ref, keys, key_extra),
            (v_ref, values, value_extra),
        ):
            own = value if head == 0 else pltpu.roll(value, HD, 1)
            ref[head] = jnp.where(low, own, extra).astype(bf16)


def attend_kernel(q_ref, k_ref, v_ref, o_ref, mixed_ref, l_ref):
    keys_in_all = k_ref.shape[1]
    tile = 512
    ratios, sums = [], []
    for head in range(2):
        query = q_ref[head]
        total = None
        for at in range(0, keys_in_all, tile):
            expo = jnp.exp(dot(query, k_ref[head, at : at + tile], NT))
            term = dot(expo.astype(bf16), v_ref[head, at : at + tile])
            total = term if total is None else total + term
        norm = total[:, HD : HD + 1]
        ratios.append(total / norm)
        sums.append(norm)
    lane = lax.broadcasted_iota(jnp.int32, ratios[0].shape, 1)
    mixed = jnp.where(lane < HD, ratios[0], pltpu.roll(ratios[1], HD, 1))
    mixed_ref[...] = mixed
    o_ref[...] = mixed.astype(bf16)
    l_ref[...] = jnp.where(lane < HD, sums[0], sums[1])


def block_kernel(
    base_ref, seg_ref, x_ref, cot_ref, o_ref, table_ref, w_ref, b_out_ref, b_up_ref, b_down_ref,
    out_ref, dx1_ref, do_ref, h2_ref, du_ref, act_ref, dff_ref, da_ref, slots_ref, gb_out_ref, gb_up_ref, gb_down_ref,
):
    rows = x_ref.shape[0]
    shards, groups = w_ref.shape[:2]
    block = base_ref[0]
    member = members(seg_ref, block, rows)
    modulation = partial(mod_rows, table_ref, seg_ref, block, member)
    wide = D // groups

    def weight(group, start):
        return w_ref[:, group, start : start + LANES, :].reshape(D, wide)

    def weight_down(group):
        return w_ref[:, group, 0 : 2 * LANES, :].reshape(2 * D, wide)

    mixed = jnp.concatenate([o_ref[shard] for shard in range(shards)], axis=1)
    attn = jnp.concatenate([dot(mixed, weight(group, 256)) for group in range(groups)], axis=1)
    attn = attn + b_out_ref[...]
    gate1 = modulation(2)
    after = x_ref[...].astype(f32) + gate1 * attn
    normal, inv = moments(after)
    scale2 = 1.0 + modulation(4)
    hidden = (normal * scale2 + modulation(3)).astype(bf16)
    h2_ref[...] = hidden
    up = [dot(hidden, weight(group, start)) for group in range(groups) for start in (384, 512)]
    up = jnp.concatenate(up, axis=1) + b_up_ref[...]
    inner = jnp.tanh(GELU_C * (up + GELU_A * (up * up * up)))
    act = (0.5 * up * (1.0 + inner)).astype(bf16)
    act_ref[...] = act
    slope = 0.5 * (1.0 + inner) + (0.5 * GELU_C) * up * (1.0 - inner * inner) * (
        1.0 + (3.0 * GELU_A) * up * up
    )
    branch = jnp.concatenate([dot(act, weight_down(group)) for group in range(groups)], axis=1)
    branch = branch + b_down_ref[...]
    gate2 = modulation(5)
    out_ref[...] = (after + gate2 * branch).astype(bf16)

    cot = cot_ref[...].astype(f32)
    dff = (gate2 * cot).astype(bf16)
    dff_ref[...] = dff
    gb_down_ref[...] = jnp.sum(dff.astype(f32), axis=0, keepdims=True)
    d_gate2 = slot_sums(member, cot * branch)
    d_act = sum(dot(dff[:, g * wide : (g + 1) * wide], weight_down(g), NT) for g in range(groups))
    du = (d_act * slope).astype(bf16)
    du_ref[...] = du
    gb_up_ref[...] = jnp.sum(du.astype(f32), axis=0, keepdims=True)
    d_hidden = None
    for index in range(2 * groups):
        piece = du[:, index * wide : (index + 1) * wide]
        term = dot(piece, weight(index // 2, 384 + 128 * (index % 2)), NT)
        d_hidden = term if d_hidden is None else d_hidden + term
    d_shift2 = slot_sums(member, d_hidden)
    d_scale2 = slot_sums(member, d_hidden * normal)
    d_after = cot + norm_back(d_hidden * scale2, normal, inv)
    dx1_ref[...] = d_after
    d_gate1 = slot_sums(member, d_after * attn)
    da = (gate1 * d_after).astype(bf16)
    da_ref[...] = da
    gb_out_ref[...] = jnp.sum(da.astype(f32), axis=0, keepdims=True)
    d_mixed = sum(dot(da[:, g * wide : (g + 1) * wide], weight(g, 256), NT) for g in range(groups))
    d_mixed = d_mixed.astype(bf16)
    for shard in range(shards):
        do_ref[shard] = d_mixed[:, shard * LANES : (shard + 1) * LANES]
    slots_ref[...] = jnp.concatenate(d_gate1 + d_shift2 + d_scale2 + d_gate2, axis=0)


def weight_grad_kernel(o_ref, da_ref, h2_ref, du_ref, act_ref, dff_ref, g_ref):
    shards = o_ref.shape[0]
    wide = g_ref.shape[3]
    g_ref[:, 0, 0:256, :] = dot(act_ref[...], dff_ref[...], TN).astype(bf16).reshape(shards, 256, wide)
    mixed = jnp.concatenate([o_ref[shard] for shard in range(shards)], axis=1)
    g_ref[:, 0, 256:384, :] = dot(mixed, da_ref[...], TN).astype(bf16).reshape(shards, LANES, wide)
    for half in range(2):
        piece = dot(h2_ref[...], du_ref[:, half * wide : (half + 1) * wide], TN).astype(bf16)
        start = 384 + 128 * half
        g_ref[:, 0, start : start + 128, :] = piece.reshape(shards, LANES, wide)


def attend_back_kernel(
    q_ref, k_ref, v_ref, do_ref, mixed_ref, l_ref, cos_ref, sin_ref, dq_ref, dk_ref, dv_ref, gb_ref, dn, dq_t
):
    step = pl.program_id(0)
    rows = k_ref.shape[1]
    frames = q_ref.shape[1]
    tile = 512
    lane = lax.broadcasted_iota(jnp.int32, (rows, LANES), 1)
    low = lane < HD

    @pl.when(step == 0)
    def _():
        gb_ref[...] = jnp.zeros_like(gb_ref)
        dq_t[...] = jnp.zeros_like(dq_t)
        for at in range(0, frames, rows):
            here = slice(at, at + rows)
            d_out = do_ref[here].astype(f32)
            norm = l_ref[here]
            d_num = (d_out / norm).astype(bf16).astype(f32)
            both = d_out * mixed_ref[here]
            for head in range(2):
                mine = low if head == 0 else ~low
                total = jnp.sum(jnp.where(mine, both, 0.0), axis=1, keepdims=True)
                delta = -total / norm[:, head * HD : head * HD + 1]
                first = delta.astype(bf16).astype(f32)
                second = (delta - first).astype(bf16).astype(f32)
                third = delta - first - second
                extra = jnp.where(lane == HD, first, jnp.where(lane == HD + 1, second, third))
                extra = jnp.where(lane < HD + 3, extra, 0.0)
                own = d_num if head == 0 else pltpu.roll(d_num, HD, 1)
                dn[head, here] = jnp.where(low, own, extra).astype(bf16)

    d_keys, d_values = [], []
    for head in range(2):
        key, value = k_ref[head], v_ref[head]
        key_t = key.T
        dk_total, dv_total = None, None
        for at in range(0, frames, tile):
            here = slice(at, at + tile)
            query, d_num = q_ref[head, here], dn[head, here]
            expo = jnp.exp(dot(key, query, NT))
            d_score = (expo * dot(value, d_num, NT)).astype(bf16)
            dk_term = dot(d_score, query)
            dv_term = dot(expo.astype(bf16), d_num)
            dk_total = dk_term if dk_total is None else dk_total + dk_term
            dv_total = dv_term if dv_total is None else dv_total + dv_term
            dq_t[head, :, here] += dot(key_t, d_score)
        d_keys.append(dk_total)
        d_values.append(dv_total)

    def both_heads(pair):
        return jnp.where(low, pair[0], pltpu.roll(pair[1], HD, 1))

    def turn_back(value, here):
        return (value * cos_ref[here] - swap_halves(value) * sin_ref[here]).astype(bf16)

    here = pl.ds(pl.multiple_of(step * rows, rows), rows)
    d_key = turn_back(both_heads(d_keys), here)
    d_value = both_heads(d_values).astype(bf16)
    dk_ref[...] = d_key
    dv_ref[...] = d_value
    gb_ref[1:2] += jnp.sum(d_key.astype(f32), axis=0, keepdims=True)
    gb_ref[2:3] += jnp.sum(d_value.astype(f32), axis=0, keepdims=True)

    @pl.when(step == pl.num_programs(0) - 1)
    def _():
        for at in range(0, frames, rows):
            part = slice(at, at + rows)
            d_query = both_heads([0.125 * dq_t[head, :, part].T for head in range(2)])
            d_query = turn_back(d_query, part)
            dq_ref[part] = d_query
            gb_ref[0:1] += jnp.sum(d_query.astype(f32), axis=0, keepdims=True)


def input_grad_kernel(base_ref, seg_ref, d_ref, w_ref, x_ref, dx1_ref, table_ref, grad_ref, slots_ref):
    block = base_ref[0]
    rows = x_ref.shape[0]
    member = members(seg_ref, block, rows)
    scale = 1.0 + mod_rows(table_ref, seg_ref, block, member, 1)
    d_hidden = sum(dot(d_ref[shard], w_ref[shard], NT) for shard in range(d_ref.shape[0]))
    normal, inv = moments(x_ref[...].astype(f32))
    grad_ref[...] = dx1_ref[...] + norm_back(d_hidden * scale, normal, inv)
    sums = slot_sums(member, d_hidden) + slot_sums(member, d_hidden * normal)
    slots_ref[...] = jnp.concatenate(sums + [jnp.zeros((2, D), f32)], axis=0)


def exchange(pieces, axis, size):
    own = lax.axis_index(axis)
    out = [lax.dynamic_index_in_dim(pieces, own, 0, keepdims=False)]
    for step in range(1, size):
        block = lax.dynamic_index_in_dim(pieces, (own - step) % size, 0, keepdims=False)
        out.append(lax.ppermute(block, axis, [(i, (i - step) % size) for i in range(size)]))
    return out


def shape(*dims, kind=bf16):
    return jax.ShapeDtypeStruct(dims, kind)


def whole(*dims):
    return pl.BlockSpec(dims, lambda *_: (0,) * len(dims))


smem = pl.BlockSpec(memory_space=pltpu.SMEM)


def local_heads(
    groups, shards, frames, cotangent, seg_start, seg_length, seg_step, time_table,
    w_ada, b_ada, w_qkv, b_qkv, w_out, b_out, w_up, b_up, w_down, b_down,
):
    rows = frames.shape[0]
    packed = rows * shards
    steps = time_table.shape[0]
    shard = lax.axis_index("shard")
    depth = D // shards
    wide = D // groups

    frames_all = lax.all_gather(frames, "shard", axis=0, tiled=True)
    w_cols = lax.all_gather(w_qkv, "grp", axis=1, tiled=True)
    w_cols = w_cols.reshape(depth, 3, shards, LANES).transpose(2, 0, 1, 3).reshape(shards, depth, 3 * LANES)
    w_heads = lax.all_to_all(w_cols, "shard", split_axis=0, concat_axis=0, tiled=True).reshape(D, 3 * LANES)

    activated = jax.nn.silu(time_table).astype(bf16)
    act_own = lax.dynamic_slice_in_dim(activated, shard * depth, depth, 1)
    partial_mod = dot(act_own, w_ada)
    mod_wide = partial_mod.shape[1]
    segs = jnp.concatenate((seg_start, seg_length, seg_step), axis=1).astype(f32)
    biases = [b.astype(f32) for b in (b_ada, b_qkv, b_out, b_up, b_down)]
    sizes = [b.shape[0] for b in biases]
    extra = jnp.concatenate(biases + [segs[0]])
    extra_rows = -(-extra.shape[0] // mod_wide)
    extra = jnp.pad(extra, (0, extra_rows * mod_wide - extra.shape[0])).reshape(extra_rows, mod_wide)
    small = lax.all_gather(jnp.concatenate((partial_mod, extra), axis=0), "shard", axis=0)
    mod_own = jnp.sum(small[:, :steps], axis=0)
    extra = small[:, steps:].reshape(shards, extra_rows * mod_wide)
    full, at = [], 0
    for size in sizes:
        full.append(extra[:, at : at + size].reshape(1, shards * size))
        at += size
    ada_bias, qkv_bias, out_bias, up_bias, down_bias = full
    seg_all = extra[:, at : at + 9].astype(jnp.int32)
    table = lax.all_gather(mod_own, "grp", axis=1, tiled=True) + ada_bias
    qkv_bias = lax.dynamic_index_in_dim(qkv_bias.reshape(3, shards, LANES), shard, 1, keepdims=False)
    qkv_bias = qkv_bias.reshape(1, 3 * LANES)

    place = jnp.arange(packed, dtype=jnp.int32).reshape(shards, rows)
    begin = seg_all[:, None, 0:3]
    inside = (place[:, :, None] >= begin) & (place[:, :, None] < begin + seg_all[:, None, 3:6])
    seg_low = jnp.sum(jnp.where(inside, begin, 0), axis=2)
    cosine, sine = angles((place - seg_low).astype(f32).reshape(packed))
    cosine = jnp.tile(cosine, (1, 4))
    sine = jnp.concatenate((-sine, sine, -sine, sine), axis=1)

    by_block = lambda width: pl.BlockSpec((rows, width), lambda i: (i, 0))
    two_heads = pl.BlockSpec((2, rows, LANES), lambda i: (0, i, 0))
    q, k, v, h1_all = pl.pallas_call(
        qkv_kernel,
        grid=(shards,),
        in_specs=[
            smem, by_block(D), whole(steps, 2 * D), whole(D, 3 * LANES), whole(1, 3 * LANES),
            by_block(LANES), by_block(LANES),
        ],
        out_specs=[two_heads, two_heads, two_heads, by_block(D)],
        out_shape=[shape(2, packed, LANES)] * 3 + [shape(packed, D)],
        compiler_params=params(40),
        cost_estimate=pl.CostEstimate(flops=2 * packed * D * 384, bytes_accessed=2 * packed * D * 4, transcendentals=0),
        name="qkv",
    )(seg_all, frames_all, table[:, : 2 * D], w_heads, qkv_bias, cosine, sine)

    attn_flops = 2 * 2 * packed * packed * 256
    o_heads, mixed, norm = pl.pallas_call(
        attend_kernel,
        grid=(shards,),
        in_specs=[two_heads, whole(2, packed, LANES), whole(2, packed, LANES)],
        out_specs=[by_block(LANES)] * 3,
        out_shape=[shape(packed, LANES), shape(packed, LANES, kind=f32), shape(packed, LANES, kind=f32)],
        compiler_params=params(40),
        cost_estimate=pl.CostEstimate(flops=2 * attn_flops, bytes_accessed=2**22, transcendentals=2 * packed * packed),
        name="attend",
    )(q, k, v)

    pack = jnp.concatenate((w_down, w_out, w_up[:, :wide], w_up[:, wide:]), axis=0)
    pack_rows = pack.shape[0]
    weights = lax.all_gather(lax.all_gather(pack, "grp", axis=0), "shard", axis=0)

    o = lax.all_to_all(o_heads.reshape(shards, rows, LANES), "shard", split_axis=0, concat_axis=0, tiled=True)
    base = shard.astype(jnp.int32).reshape(1)
    block_flops = 2 * rows * D * D * 10
    out, dx1, d_mixed, h2, du, act, dff, da, slots_ff, gb_out, gb_up, gb_down = pl.pallas_call(
        block_kernel,
        in_specs=[smem, smem] + [pl.BlockSpec(memory_space=pltpu.VMEM)] * 8,
        out_specs=[pl.BlockSpec(memory_space=pltpu.VMEM)] * 12,
        out_shape=[
            shape(rows, D), shape(rows, D, kind=f32), shape(shards, rows, LANES), shape(rows, D), shape(rows, 2 * D),
            shape(rows, 2 * D), shape(rows, D), shape(rows, D), shape(12, D, kind=f32),
            shape(1, D, kind=f32), shape(1, 2 * D, kind=f32), shape(1, D, kind=f32),
        ],
        compiler_params=pltpu.CompilerParams(vmem_limit_bytes=56 * 2**20),
        cost_estimate=pl.CostEstimate(flops=block_flops, bytes_accessed=2**24, transcendentals=rows * 2 * D),
        name="block",
    )(base, seg_all, frames, cotangent, o, table, weights, out_bias, up_bias, down_bias)

    d_heads = lax.all_to_all(d_mixed, "shard", split_axis=0, concat_axis=0, tiled=True).reshape(packed, LANES)

    by_group = lambda width: pl.BlockSpec((rows, width), lambda i: (0, i))
    grad_pack = pl.pallas_call(
        weight_grad_kernel,
        grid=(groups,),
        in_specs=[
            whole(shards, rows, LANES), by_group(wide), whole(rows, D), by_group(2 * wide), whole(rows, 2 * D), by_group(wide),
        ],
        out_specs=pl.BlockSpec((shards, 1, pack_rows, wide), lambda i: (0, i, 0, 0)),
        out_shape=shape(shards, groups, pack_rows, wide),
        compiler_params=params(40),
        cost_estimate=pl.CostEstimate(flops=block_flops // 2, bytes_accessed=2**24, transcendentals=0),
        name="weight_grads",
    )(o, da, h2, du, act, dff)
    grad_pack = lax.psum_scatter(grad_pack, "shard", scatter_dimension=0, tiled=False)
    grad_pack = lax.psum_scatter(grad_pack, "grp", scatter_dimension=0, tiled=False).astype(f32)
    g_down = grad_pack[: 2 * LANES]
    g_out = grad_pack[2 * LANES : 3 * LANES]
    g_up = jnp.concatenate((grad_pack[3 * LANES : 4 * LANES], grad_pack[4 * LANES :]), axis=1)

    dq, dk, dv, gb_qkv = pl.pallas_call(
        attend_back_kernel,
        grid=(shards,),
        in_specs=[
            whole(2, packed, LANES), two_heads, two_heads, whole(packed, LANES), whole(packed, LANES),
            whole(packed, LANES), whole(packed, LANES), whole(packed, LANES),
        ],
        out_specs=[whole(packed, LANES), by_block(LANES), by_block(LANES), whole(3, LANES)],
        out_shape=[shape(packed, LANES)] * 3 + [shape(3, LANES, kind=f32)],
        scratch_shapes=[pltpu.VMEM((2, packed, LANES), bf16), pltpu.VMEM((2, LANES, packed), f32)],
        compiler_params=params(48),
        cost_estimate=pl.CostEstimate(flops=5 * attn_flops, bytes_accessed=2**23, transcendentals=2 * packed * packed),
        name="attend_back",
    )(q, k, v, d_heads, mixed, norm, cosine, sine)

    d_own = jnp.concatenate((dq, dk, dv), axis=1)
    d_rows = lax.all_to_all(d_own.reshape(shards, rows, 3 * LANES), "shard", split_axis=0, concat_axis=0, tiled=True)
    w_all = lax.all_gather(w_heads, "shard", axis=0)
    grad_frames, slots_qkv = pl.pallas_call(
        input_grad_kernel,
        in_specs=[smem, smem] + [pl.BlockSpec(memory_space=pltpu.VMEM)] * 5,
        out_specs=[pl.BlockSpec(memory_space=pltpu.VMEM)] * 2,
        out_shape=[shape(rows, D, kind=f32), shape(8, D, kind=f32)],
        compiler_params=pltpu.CompilerParams(vmem_limit_bytes=40 * 2**20),
        cost_estimate=pl.CostEstimate(flops=2 * rows * D * 3 * D, bytes_accessed=2**23, transcendentals=0),
        name="input_grad",
    )(base, seg_all, d_rows, w_all, frames, dx1, table[:, : 2 * D])

    g_heads = dot(h1_all, d_own, TN).astype(bf16).reshape(shards, depth, 3 * LANES)
    g_rows = lax.all_to_all(g_heads, "shard", split_axis=0, concat_axis=0, tiled=True)
    g_rows = g_rows.reshape(shards, depth, 3, LANES).transpose(1, 2, 0, 3).reshape(depth, groups, 3 * D // groups)
    g_qkv = sum(piece.astype(f32) for piece in exchange(g_rows.transpose(1, 0, 2), "grp", groups))

    d_slot = jnp.concatenate((slots_qkv[:6], slots_ff), axis=0).reshape(6, 3, D).transpose(1, 0, 2).reshape(3, 6 * D)
    row_sums = jnp.concatenate((gb_qkv.reshape(-1), gb_out[0], gb_up[0], gb_down[0]))
    sum_rows = -(-row_sums.shape[0] // (6 * D))
    row_sums = jnp.pad(row_sums, (0, sum_rows * 6 * D - row_sums.shape[0])).reshape(sum_rows, 6 * D)
    tail = lax.all_gather(jnp.concatenate((d_slot, row_sums), axis=0), "shard", axis=0)
    d_slots = tail[:, :3]
    d_segs = jnp.concatenate(
        (d_slots[0], d_slots[shards - 1], jnp.sum(d_slots[1 : shards - 1], axis=(0, 1))[None]), axis=0
    )
    step_ids = jnp.concatenate((seg_all[0, 6:], seg_all[shards - 1, 6:], jnp.sum(seg_all[1, 6:])[None])).astype(f32)
    rest = tail[:, 3:].reshape(shards, sum_rows * 6 * D)
    gb_heads = rest[:, : 3 * LANES].reshape(shards, 3, LANES).transpose(1, 0, 2).reshape(3 * D)
    others = jnp.sum(rest[:, 3 * LANES : 3 * LANES + 4 * D], axis=0)
    sums = (
        jnp.sum(d_segs, axis=0), gb_heads, others[:D], others[D : 3 * D], others[3 * D : 4 * D],
    )
    own_sums = [lax.dynamic_slice_in_dim(total, shard * size, size) for total, size in zip(sums, sizes)]
    send = jnp.concatenate(own_sums + [step_ids])
    send_rows = -(-send.shape[0] // mod_wide)
    send = jnp.pad(send, (0, send_rows * mod_wide - send.shape[0])).reshape(1, send_rows, mod_wide)
    parts = jnp.concatenate(
        (d_segs.reshape(7, groups, mod_wide).transpose(1, 0, 2), jnp.broadcast_to(send, (groups, send_rows, mod_wide))), axis=1
    )
    parts = exchange(parts, "grp", groups)
    d_rows_all = jnp.concatenate([piece[:7] for piece in parts], axis=0)
    rest = [piece[7:].reshape(-1) for piece in parts]
    at = sum(sizes)
    ids = jnp.concatenate([piece[at : at + 7] for piece in rest])
    onehot = (ids[None, :] == jnp.arange(steps, dtype=f32)[:, None]).astype(f32)
    d_table = jnp.dot(onehot, d_rows_all, precision=top_precision)
    g_ada = jnp.dot(act_own.astype(f32).T, d_table, precision=top_precision)
    bias_sums = sum(piece[:at] for piece in rest)
    bias_grads, start = [], 0
    for size in sizes:
        bias_grads.append(bias_sums[start : start + size])
        start += size
    gb_ada, gb_qkv, gb_out, gb_up, gb_down = bias_grads

    d_act = lax.dot_general(d_table, w_ada.astype(f32), NT, precision=top_precision, preferred_element_type=f32)
    table_own = lax.dynamic_slice_in_dim(time_table, shard * depth, depth, 1)
    g_table = jax.vjp(jax.nn.silu, table_own)[1](d_act)[0]
    for_all = jnp.broadcast_to(g_table[None], (groups,) + g_table.shape)
    g_table = sum(exchange(for_all, "grp", groups))
    return (
        out, grad_frames, g_table, g_ada, gb_ada, g_qkv, gb_qkv, g_out, gb_out, g_up, gb_up, g_down, gb_down,
    )


def solution(mesh):
    in_specs = (
        P(("grp", "shard"), None),
        P(("grp", "shard"), None),
        P(("grp", "shard"), None),
        P(("grp", "shard"), None),
        P(("grp", "shard"), None),
        P(),
        P("shard", "grp"),
        P("shard"),
        P("shard", "grp"),
        P("shard"),
        P("shard", "grp"),
        P("shard"),
        P("shard", "grp"),
        P("shard"),
        P("shard", "grp"),
        P("shard"),
    )
    out_specs = (
        P(("grp", "shard"), None),
        P(("grp", "shard"), None),
        P(None, "shard"),
        P("shard", "grp"),
        P("shard"),
        P("shard", "grp"),
        P("shard"),
        P("shard", "grp"),
        P("shard"),
        P("shard", "grp"),
        P("shard"),
        P("shard", "grp"),
        P("shard"),
    )
    by_heads = mesh.shape["shard"] * 2 * HD == D
    local = partial(local_heads, mesh.shape["grp"], mesh.shape["shard"]) if by_heads else local_any
    return jax.shard_map(local, mesh=mesh, in_specs=in_specs, out_specs=out_specs, check_vma=False)
```

```python
from functools import partial

import jax
import jax.numpy as jnp
from jax import lax
from jax.experimental import pallas as pl
from jax.experimental.pallas import tpu as pltpu
from jax.sharding import PartitionSpec as P

D = 1024
H = 16
HD = 64


eps_norm = 1e-06
top_precision = lax.Precision.HIGHEST


def normalize(tensor):
    centred = tensor - jnp.mean(tensor, axis=-1, keepdims=True)
    return centred * lax.rsqrt(jnp.mean(centred * centred, axis=-1, keepdims=True) + eps_norm)


def modulate(tensor, scale_vec, shift_vec):
    return normalize(tensor) * (1.0 + scale_vec) + shift_vec


def angles(positions):
    half_width = HD // 2
    inverse = 10000.0 ** (-jnp.arange(half_width, dtype=jnp.float32) / half_width)
    phase_grid = positions[:, None] * inverse[None, :]
    return (jnp.cos(phase_grid), jnp.sin(phase_grid))


def rotate(tensor, cosine_vals, sine_vals):
    row_total = tensor.shape[0]
    halves = tensor.reshape(row_total, H, 2, HD // 2)
    former = halves[:, :, 0]
    latter = halves[:, :, 1]
    cosine_part = cosine_vals[:, None, :]
    sine_part = sine_vals[:, None, :]
    turned = jnp.stack(
        (former * cosine_part - latter * sine_part, latter * cosine_part + former * sine_part),
        axis=2,
    )
    return turned.reshape(row_total, D)


def tile_width(row_total):
    for candidate in (512, 256, 128):
        return candidate
    return row_total


def head_view(tensor):
    return tensor.reshape(tensor.shape[0], H, HD)


def local_any(
    frames,
    cotangent,
    seg_start,
    seg_length,
    seg_step,
    time_table,
    w_ada,
    b_ada,
    w_qkv,
    b_qkv,
    w_out,
    b_out,
    w_up,
    b_up,
    w_down,
    b_down,
):
    frame_rows = frames.shape[0]
    positions = lax.axis_index("shard") * frame_rows + jnp.arange(frame_rows, dtype=jnp.int32)
    slot_start = seg_start[0]
    slot_end = slot_start + seg_length[0]
    member_mask = (positions[:, None] >= slot_start[None, :]) & (
        positions[:, None] < slot_end[None, :]
    )
    member = member_mask.astype(jnp.float32)
    seg_low = jnp.sum(jnp.where(member_mask, slot_start[None, :], 0), axis=1)
    seg_high = jnp.sum(jnp.where(member_mask, slot_end[None, :], 0), axis=1)
    cosine_vals, sine_vals = angles((positions - seg_low).astype(jnp.float32))
    columns = (
        lax.all_gather(w_ada, "grp", axis=1, tiled=True),
        lax.all_gather(w_qkv, "grp", axis=1, tiled=True),
        lax.all_gather(w_out, "grp", axis=1, tiled=True),
        lax.all_gather(w_up, "grp", axis=1, tiled=True),
        lax.all_gather(w_down, "grp", axis=1, tiled=True),
    )
    gathered = (
        lax.all_gather(columns[0], "shard", axis=0, tiled=True),
        lax.all_gather(columns[1], "shard", axis=0, tiled=True),
        lax.all_gather(columns[2], "shard", axis=0, tiled=True),
        lax.all_gather(columns[3], "shard", axis=0, tiled=True),
        lax.all_gather(columns[4], "shard", axis=0, tiled=True),
        lax.all_gather(b_ada, "shard", axis=0, tiled=True),
        lax.all_gather(b_qkv, "shard", axis=0, tiled=True),
        lax.all_gather(b_out, "shard", axis=0, tiled=True),
        lax.all_gather(b_up, "shard", axis=0, tiled=True),
        lax.all_gather(b_down, "shard", axis=0, tiled=True),
    )
    ada_full, qkv_full, out_full, up_full, down_full = (
        gathered[0],
        gathered[1],
        gathered[2],
        gathered[3],
        gathered[4],
    )
    ada_bias, qkv_bias, out_bias, up_bias, down_bias = [
        bias_row.astype(jnp.float32) for bias_row in gathered[5:]
    ]
    step_onehot = (
        seg_step[0][:, None] == jnp.arange(time_table.shape[0], dtype=jnp.int32)[None, :]
    ).astype(jnp.float32)
    time_rows = jnp.dot(step_onehot, time_table, precision=top_precision)
    activated = jax.nn.silu(time_rows).astype(jnp.bfloat16)
    modulation = jnp.dot(activated, ada_full, preferred_element_type=jnp.float32) + ada_bias
    frame_mod = jnp.dot(member, modulation, precision=top_precision)
    shift_attn, scale_attn, gate_attn, shift_ff, scale_ff, gate_ff = jnp.split(frame_mod, 6, axis=1)
    inputs = frames.astype(jnp.float32)
    hidden_attn = modulate(inputs, scale_attn, shift_attn).astype(jnp.bfloat16)
    projected = jnp.dot(hidden_attn, qkv_full, preferred_element_type=jnp.float32) + qkv_bias
    queries = rotate(projected[:, :D], cosine_vals, sine_vals).astype(jnp.bfloat16)
    keys_rot = rotate(projected[:, D : 2 * D], cosine_vals, sine_vals).astype(jnp.bfloat16)
    values = projected[:, 2 * D :].astype(jnp.bfloat16)
    query_heads = head_view(queries)
    key_heads = head_view(keys_rot)
    value_heads = head_view(values)
    zero_heads = jnp.zeros((frame_rows, H, HD), jnp.float32)
    key_piece = lax.all_gather(keys_rot, "shard", axis=0, tiled=True)
    value_piece = lax.all_gather(values, "shard", axis=0, tiled=True)
    piece_rows = key_piece.shape[0]
    tile_rows = tile_width(piece_rows)
    tiles = piece_rows // tile_rows

    def tile_step(partial_sums, tile_item):
        key_tile, value_tile, offset = tile_item
        key_pos = offset + jnp.arange(tile_rows, dtype=jnp.int32)
        inside = (key_pos[None, :] >= seg_low[:, None]) & (key_pos[None, :] < seg_high[:, None])
        scores = 0.125 * jnp.einsum(
            "rhd,khd->hrk", query_heads, head_view(key_tile), preferred_element_type=jnp.float32
        )
        expo = jnp.where(inside[None], jnp.exp(scores), 0.0)
        numerator, denominator = partial_sums
        numerator = numerator + jnp.einsum(
            "hrk,khd->rhd",
            expo.astype(jnp.bfloat16),
            head_view(value_tile),
            preferred_element_type=jnp.float32,
        )
        denominator = denominator + jnp.sum(expo, axis=2).T
        return ((numerator, denominator), None)

    tile_items = (
        key_piece.reshape(tiles, tile_rows, D),
        value_piece.reshape(tiles, tile_rows, D),
        jnp.arange(tiles, dtype=jnp.int32) * tile_rows,
    )
    numerator, denominator = lax.scan(
        tile_step, (zero_heads, jnp.zeros((frame_rows, H), jnp.float32)), tile_items
    )[0]
    mixed = numerator / denominator[:, :, None]
    mixed_low = mixed.reshape(frame_rows, D).astype(jnp.bfloat16)
    attn_branch = jnp.dot(mixed_low, out_full, preferred_element_type=jnp.float32) + out_bias
    after_attn = inputs + gate_attn * attn_branch
    hidden_ff = modulate(after_attn, scale_ff, shift_ff).astype(jnp.bfloat16)
    upward = jnp.dot(hidden_ff, up_full, preferred_element_type=jnp.float32) + up_bias
    activation = jax.nn.gelu(upward, approximate=True).astype(jnp.bfloat16)
    ff_branch = jnp.dot(activation, down_full, preferred_element_type=jnp.float32) + down_bias
    output = (after_attn + gate_ff * ff_branch).astype(jnp.bfloat16)
    columns_back = (
        lax.all_gather(w_ada, "grp", axis=1, tiled=True),
        lax.all_gather(w_qkv, "grp", axis=1, tiled=True),
        lax.all_gather(w_out, "grp", axis=1, tiled=True),
        lax.all_gather(w_up, "grp", axis=1, tiled=True),
        lax.all_gather(w_down, "grp", axis=1, tiled=True),
    )
    gathered_back = (
        lax.all_gather(columns_back[0], "shard", axis=0, tiled=True),
        lax.all_gather(columns_back[1], "shard", axis=0, tiled=True),
        lax.all_gather(columns_back[2], "shard", axis=0, tiled=True),
        lax.all_gather(columns_back[3], "shard", axis=0, tiled=True),
        lax.all_gather(columns_back[4], "shard", axis=0, tiled=True),
    )
    ada_back, qkv_back, out_back, up_back, down_back = (
        gathered_back[0],
        gathered_back[1],
        gathered_back[2],
        gathered_back[3],
        gathered_back[4],
    )
    grad_out = cotangent.astype(jnp.float32)
    d_branch = (gate_ff * grad_out).astype(jnp.bfloat16)
    d_gate_ff = grad_out * ff_branch
    g_down = jnp.dot(activation.T, d_branch, preferred_element_type=jnp.float32)
    gb_down = jnp.sum(d_branch.astype(jnp.float32), axis=0)
    d_activation = jnp.dot(d_branch, down_back.T, preferred_element_type=jnp.float32)
    gelu_pull = jax.vjp(partial(jax.nn.gelu, approximate=True), upward)[1]
    d_upward = gelu_pull(d_activation)[0].astype(jnp.bfloat16)
    g_up = jnp.dot(hidden_ff.T, d_upward, preferred_element_type=jnp.float32)
    gb_up = jnp.sum(d_upward.astype(jnp.float32), axis=0)
    d_hidden_ff = jnp.dot(d_upward, up_back.T, preferred_element_type=jnp.float32)
    ff_pull = jax.vjp(modulate, after_attn, scale_ff, shift_ff)[1]
    dx_ff, d_scale_ff, d_shift_ff = ff_pull(d_hidden_ff)
    d_after = grad_out + dx_ff
    d_attn = (gate_attn * d_after).astype(jnp.bfloat16)
    d_gate_attn = d_after * attn_branch
    g_out = jnp.dot(mixed_low.T, d_attn, preferred_element_type=jnp.float32)
    gb_out = jnp.sum(d_attn.astype(jnp.float32), axis=0)
    d_mixed = jnp.dot(d_attn, out_back.T, preferred_element_type=jnp.float32).astype(jnp.bfloat16)
    d_mixed_heads = head_view(d_mixed).astype(jnp.float32)
    delta = jnp.sum(d_mixed_heads * mixed, axis=2) / denominator
    d_numer = (d_mixed_heads / denominator[:, :, None]).astype(jnp.bfloat16).reshape(frame_rows, D)
    dnum_heads = head_view(d_numer)
    delta_heads = delta.T
    key_piece = lax.all_gather(keys_rot, "shard", axis=0, tiled=True)
    value_piece = lax.all_gather(values, "shard", axis=0, tiled=True)
    piece_rows = key_piece.shape[0]
    fold_tile_rows = tile_width(piece_rows)
    tiles = piece_rows // fold_tile_rows

    def tile_step(grad_sum, tile_item):
        key_tile, value_tile, offset = tile_item
        key_pos = offset + jnp.arange(fold_tile_rows, dtype=jnp.int32)
        inside = (key_pos[None, :] >= seg_low[:, None]) & (key_pos[None, :] < seg_high[:, None])
        scores = 0.125 * jnp.einsum(
            "rhd,khd->hrk", query_heads, head_view(key_tile), preferred_element_type=jnp.float32
        )
        expo = jnp.where(inside[None], jnp.exp(scores), 0.0)
        slope = jnp.einsum(
            "rhd,khd->hrk", dnum_heads, head_view(value_tile), preferred_element_type=jnp.float32
        )
        d_scores = (expo * (slope - delta_heads[:, :, None])).astype(jnp.bfloat16)
        grad_sum = grad_sum + 0.125 * jnp.einsum(
            "hrk,khd->rhd", d_scores, head_view(key_tile), preferred_element_type=jnp.float32
        )
        return (grad_sum, None)

    tile_items = (
        key_piece.reshape(tiles, fold_tile_rows, D),
        value_piece.reshape(tiles, fold_tile_rows, D),
        jnp.arange(tiles, dtype=jnp.int32) * fold_tile_rows,
    )
    d_query = lax.scan(tile_step, zero_heads, tile_items)[0]
    delta_all = lax.all_gather(delta, "shard", axis=0, tiled=True)

    def fold_key_grad(running, piece):
        query_piece, dnum_piece = piece
        piece_rows = query_piece.shape[0]
        tile_rows = tile_width(piece_rows)
        tiles = piece_rows // tile_rows

        def tile_step(grad_pair, tile_item):
            query_tile, dnum_tile, delta_tile, offset = tile_item
            query_pos = offset + jnp.arange(tile_rows, dtype=jnp.int32)
            inside = (query_pos[:, None] >= seg_low[None, :]) & (
                query_pos[:, None] < seg_high[None, :]
            )
            query_tile_heads = head_view(query_tile)
            dnum_tile_heads = head_view(dnum_tile)
            scores = 0.125 * jnp.einsum(
                "qhd,rhd->hqr", query_tile_heads, key_heads, preferred_element_type=jnp.float32
            )
            expo = jnp.where(inside[None], jnp.exp(scores), 0.0)
            slope = jnp.einsum(
                "qhd,rhd->hqr", dnum_tile_heads, value_heads, preferred_element_type=jnp.float32
            )
            d_scores = (expo * (slope - delta_tile.T[:, :, None])).astype(jnp.bfloat16)
            d_keys, d_values = grad_pair
            d_keys = d_keys + 0.125 * jnp.einsum(
                "hqr,qhd->rhd", d_scores, query_tile_heads, preferred_element_type=jnp.float32
            )
            d_values = d_values + jnp.einsum(
                "hqr,qhd->rhd",
                expo.astype(jnp.bfloat16),
                dnum_tile_heads,
                preferred_element_type=jnp.float32,
            )
            return ((d_keys, d_values), None)

        tile_items = (
            query_piece.reshape(tiles, tile_rows, D),
            dnum_piece.reshape(tiles, tile_rows, D),
            delta_all.reshape(tiles, tile_rows, H),
            jnp.arange(tiles, dtype=jnp.int32) * tile_rows,
        )
        return lax.scan(tile_step, running, tile_items)[0]

    d_keys, d_values = fold_key_grad(
        (zero_heads, zero_heads),
        (
            lax.all_gather(queries, "shard", axis=0, tiled=True),
            lax.all_gather(d_numer, "shard", axis=0, tiled=True),
        ),
    )
    grad_query = rotate(d_query.reshape(frame_rows, D), cosine_vals, -sine_vals)
    grad_key = rotate(d_keys.reshape(frame_rows, D), cosine_vals, -sine_vals)
    d_projected = jnp.concatenate(
        (grad_query, grad_key, d_values.reshape(frame_rows, D)), axis=1
    ).astype(jnp.bfloat16)
    g_qkv = jnp.dot(hidden_attn.T, d_projected, preferred_element_type=jnp.float32)
    gb_qkv = jnp.sum(d_projected.astype(jnp.float32), axis=0)
    d_hidden_attn = jnp.dot(d_projected, qkv_back.T, preferred_element_type=jnp.float32)
    attn_pull = jax.vjp(modulate, inputs, scale_attn, shift_attn)[1]
    dx_attn, d_scale_attn, d_shift_attn = attn_pull(d_hidden_attn)
    grad_frames = d_after + dx_attn
    d_frame_mod = jnp.concatenate(
        (d_shift_attn, d_scale_attn, d_gate_attn, d_shift_ff, d_scale_ff, d_gate_ff), axis=1
    )
    d_slot = jnp.dot(member.T, d_frame_mod, precision=top_precision)
    g_ada = jnp.dot(activated.astype(jnp.float32).T, d_slot, precision=top_precision)
    gb_ada = jnp.sum(d_slot, axis=0)
    d_activated = jnp.dot(
        d_slot, ada_back.T, precision=top_precision, preferred_element_type=jnp.float32
    )
    silu_pull = jax.vjp(jax.nn.silu, time_rows)[1]
    d_time_rows = silu_pull(d_activated)[0]
    g_table = jnp.dot(step_onehot.T, d_time_rows, precision=top_precision)
    group_sums = (
        lax.psum_scatter(g_ada, "shard", scatter_dimension=0, tiled=True),
        lax.psum_scatter(g_qkv, "shard", scatter_dimension=0, tiled=True),
        lax.psum_scatter(g_out, "shard", scatter_dimension=0, tiled=True),
        lax.psum_scatter(g_up, "shard", scatter_dimension=0, tiled=True),
        lax.psum_scatter(g_down, "shard", scatter_dimension=0, tiled=True),
        lax.psum_scatter(gb_ada, "shard", scatter_dimension=0, tiled=True),
        lax.psum_scatter(gb_qkv, "shard", scatter_dimension=0, tiled=True),
        lax.psum_scatter(gb_out, "shard", scatter_dimension=0, tiled=True),
        lax.psum_scatter(gb_up, "shard", scatter_dimension=0, tiled=True),
        lax.psum_scatter(gb_down, "shard", scatter_dimension=0, tiled=True),
        lax.psum_scatter(g_table, "shard", scatter_dimension=1, tiled=True),
    )
    wide_sums = (
        lax.psum_scatter(group_sums[0], "grp", scatter_dimension=1, tiled=True),
        lax.psum_scatter(group_sums[1], "grp", scatter_dimension=1, tiled=True),
        lax.psum_scatter(group_sums[2], "grp", scatter_dimension=1, tiled=True),
        lax.psum_scatter(group_sums[3], "grp", scatter_dimension=1, tiled=True),
        lax.psum_scatter(group_sums[4], "grp", scatter_dimension=1, tiled=True),
    )
    small_sums = lax.psum(
        (group_sums[5], group_sums[6], group_sums[7], group_sums[8], group_sums[9], group_sums[10]),
        "grp",
    )
    finals = tuple(wide_sums) + tuple(small_sums)
    return (
        output,
        grad_frames,
        finals[10],
        finals[0],
        finals[5],
        finals[1],
        finals[6],
        finals[2],
        finals[7],
        finals[3],
        finals[8],
        finals[4],
        finals[9],
    )


LANES = 128
FREE = pl.CostEstimate(flops=2**20, bytes_accessed=2**16, transcendentals=0)
CHIPS = (2, 4, 6)
ORDER = (0, 2, 4, 6, 1, 3, 5, 7)
SEPARATE = -(2.0**100)
GELU_C = 0.7978845608028654
GELU_A = 0.044715
NT = (((1,), (1,)), ((), ()))
TN = (((0,), (0,)), ((), ()))
f32 = jnp.float32
bf16 = jnp.bfloat16


def dot(left, right, dims=(((1,), (0,)), ((), ()))):
    return lax.dot_general(left, right, dims, preferred_element_type=f32)


def params(limit_mib, steps=1):
    return pltpu.CompilerParams(
        dimension_semantics=("arbitrary",) * steps, vmem_limit_bytes=limit_mib * 2**20
    )


def moments(value):
    centred = value - jnp.mean(value, axis=1, keepdims=True)
    inv = lax.rsqrt(jnp.mean(centred * centred, axis=1, keepdims=True) + eps_norm)
    return centred * inv, inv


def norm_back(weighted, normal, inv):
    return (
        weighted
        - jnp.mean(weighted, axis=1, keepdims=True)
        - normal * jnp.mean(weighted * normal, axis=1, keepdims=True)
    ) * inv


def swap_halves(value):
    lane = lax.broadcasted_iota(jnp.int32, value.shape, 1)
    return jnp.where(lane % HD < HD // 2, pltpu.roll(value, 96, 1), pltpu.roll(value, 32, 1))


def rotary(cos_ref, sin_ref, here):
    cosine, sine = cos_ref[:, here].T, sin_ref[:, here].T
    return jnp.concatenate([cosine] * 4, axis=1), jnp.concatenate([-sine, sine] * 2, axis=1)


def members(seg_ref, block, rows):
    place = block * rows + lax.broadcasted_iota(jnp.int32, (rows, 1), 0)
    out = []
    for slot in range(3):
        begin = seg_ref[block, slot]
        inside = (place >= begin) & (place < begin + seg_ref[block, 3 + slot])
        out.append(inside.astype(f32))
    return out


def mod_rows(table_ref, seg_ref, block, member, part):
    total = None
    for slot in range(3):
        row = table_ref[pl.ds(seg_ref[block, 6 + slot], 1), pl.ds(part * D, D)]
        term = member[slot] * row
        total = term if total is None else total + term
    return total


def slot_sums(member, value):
    return [jnp.sum(column * value, axis=0, keepdims=True) for column in member]


def qkv_kernel(order_ref, seg_ref, *refs):
    step = pl.program_id(0)
    last = pl.num_programs(0) - 1
    *pieces, table_ref, w_ref, b_ref, cos_ref, sin_ref, q_ref, k_ref, v_ref, h_ref, x_all, arrived = refs
    block = order_ref[step]
    rows = x_all.shape[1]
    copies, at = [], 0
    for piece in pieces:
        here = x_all.at[at : at + piece.shape[0]]
        copies.append((at, pltpu.make_async_copy(piece, here, arrived.at[len(copies)])))
        at += piece.shape[0]

    @pl.when(step == 0)
    def _():
        for _, copy in copies:
            copy.start()

    for at, copy in copies:

        @pl.when(step == at)
        def _(copy=copy):
            copy.wait()

    member = members(seg_ref, block, rows)
    normal, _ = moments(x_all[step].astype(f32))
    shift = mod_rows(table_ref, seg_ref, block, member, 0)
    scale = mod_rows(table_ref, seg_ref, block, member, 1)
    hidden = (normal * (1.0 + scale) + shift).astype(bf16)
    h_ref[...] = hidden
    projected = dot(hidden, w_ref[...]) + b_ref[...]
    cosine, sine = rotary(cos_ref, sin_ref, slice(None))
    turned = []
    for part in range(2):
        piece = projected[:, part * LANES : (part + 1) * LANES]
        turned.append(piece * cosine + swap_halves(piece) * sine)
    queries = turned[0].astype(bf16).astype(f32) * 0.125
    keys = turned[1]
    values = projected[:, 2 * LANES :]
    lane = lax.broadcasted_iota(jnp.int32, (rows, LANES), 1)
    place = block * rows + lax.broadcasted_iota(jnp.int32, (rows, 1), 0)
    query_extra = jnp.zeros((rows, LANES), f32)
    key_extra = jnp.zeros((rows, LANES), f32)
    for index in range(6):
        where, slot = (0, index) if index < 3 else (last, index - 3)
        begin = seg_ref[where, slot]
        inside = (place >= begin) & (place < begin + seg_ref[where, 3 + slot])
        here = lane == HD + index
        query_extra = jnp.where(here, jnp.where(inside, 0.0, SEPARATE), query_extra)
        key_extra = jnp.where(here, jnp.where(inside, 1.0, 0.0), key_extra)
    value_extra = jnp.where((lane >= HD) & (lane < HD + 3), 1.0, 0.0)
    low = lane < HD
    for head in range(2):
        for ref, value, extra in (
            (q_ref, queries, query_extra),
            (k_ref, keys, key_extra),
            (v_ref, values, value_extra),
        ):
            own = value if head == 0 else pltpu.roll(value, HD, 1)
            ref[head] = jnp.where(low, own, extra).astype(bf16)


def attend_kernel(q_ref, k_ref, v_ref, o_ref, mixed_ref, l_ref):
    keys_in_all = k_ref.shape[1]
    tile = 512
    ratios, sums = [], []
    for head in range(2):
        query = q_ref[head]
        total = None
        for at in range(0, keys_in_all, tile):
            expo = jnp.exp(dot(query, k_ref[head, at : at + tile], NT))
            term = dot(expo.astype(bf16), v_ref[head, at : at + tile])
            total = term if total is None else total + term
        norm = total[:, HD : HD + 1]
        ratios.append(total / norm)
        sums.append(norm)
    lane = lax.broadcasted_iota(jnp.int32, ratios[0].shape, 1)
    mixed = jnp.where(lane < HD, ratios[0], pltpu.roll(ratios[1], HD, 1))
    mixed_ref[...] = mixed
    o_ref[...] = mixed.astype(bf16)
    l_ref[...] = jnp.where(lane < HD, sums[0], sums[1])


def block_kernel(
    order_ref, seg_ref, x_ref, cot_ref, o_ref, table_ref, w_ref, b_out_ref, b_up_ref, b_down_ref,
    out_ref, dx1_ref, do_ref, pair_ref, keep_ref, send_ref, slots_ref, gb_out_ref, gb_up_ref, gb_down_ref,
):
    rows = x_ref.shape[0]
    groups, shards = w_ref.shape[:2]
    block = order_ref[0]
    member = members(seg_ref, block, rows)
    modulation = partial(mod_rows, table_ref, seg_ref, block, member)
    wide = D // groups

    def weight(group, start):
        return w_ref[group, :, start : start + LANES, :].reshape(D, wide)

    def weight_down(group):
        return w_ref[group, :, 0 : 2 * LANES, :].reshape(2 * D, wide)

    def by_core(value, width, other):
        parts = [value[:, at : at + width] for at in range(0, value.shape[1], width)]
        even, odd = jnp.concatenate(parts[0::2], axis=1), jnp.concatenate(parts[1::2], axis=1)
        return jnp.where((block % 2 == 0) != other, even, odd)

    def share(start, value, width):
        half = value.shape[1] // 2
        keep_ref[:, start : start + half] = by_core(value, width, False)
        send_ref[:, start : start + half] = by_core(value, width, True)

    mixed = jnp.concatenate([o_ref[shard] for shard in range(shards)], axis=1)
    share(D, mixed, LANES)
    attn = jnp.concatenate([dot(mixed, weight(group, 256)) for group in range(groups)], axis=1)
    attn = attn + b_out_ref[...]
    gate1 = modulation(2)
    after = x_ref[...].astype(f32) + gate1 * attn
    normal, inv = moments(after)
    scale2 = 1.0 + modulation(4)
    hidden = (normal * scale2 + modulation(3)).astype(bf16)
    share(D + D // 2, hidden, LANES)
    up = [dot(hidden, weight(group, start)) for group in range(groups) for start in (384, 512)]
    up = jnp.concatenate(up, axis=1) + b_up_ref[...]
    inner = jnp.tanh(GELU_C * (up + GELU_A * (up * up * up)))
    act = (0.5 * up * (1.0 + inner)).astype(bf16)
    share(0, act, 2 * LANES)
    slope = 0.5 * (1.0 + inner) + (0.5 * GELU_C) * up * (1.0 - inner * inner) * (
        1.0 + (3.0 * GELU_A) * up * up
    )
    branch = jnp.concatenate([dot(act, weight_down(group)) for group in range(groups)], axis=1)
    branch = branch + b_down_ref[...]
    gate2 = modulation(5)
    out_ref[...] = (after + gate2 * branch).astype(bf16)

    cot = cot_ref[...].astype(f32)
    dff = (gate2 * cot).astype(bf16)
    pair_ref[:, 0:D] = dff
    gb_down_ref[...] = jnp.sum(dff.astype(f32), axis=0, keepdims=True)
    d_gate2 = slot_sums(member, cot * branch)
    d_act = sum(dot(dff[:, g * wide : (g + 1) * wide], weight_down(g), NT) for g in range(groups))
    du = (d_act * slope).astype(bf16)
    pair_ref[:, 2 * D :] = du
    gb_up_ref[...] = jnp.sum(du.astype(f32), axis=0, keepdims=True)
    d_hidden = None
    for index in range(2 * groups):
        piece = du[:, index * wide : (index + 1) * wide]
        term = dot(piece, weight(index // 2, 384 + LANES * (index % 2)), NT)
        d_hidden = term if d_hidden is None else d_hidden + term
    d_shift2 = slot_sums(member, d_hidden)
    d_scale2 = slot_sums(member, d_hidden * normal)
    d_after = cot + norm_back(d_hidden * scale2, normal, inv)
    dx1_ref[...] = d_after
    d_gate1 = slot_sums(member, d_after * attn)
    da = (gate1 * d_after).astype(bf16)
    pair_ref[:, D : 2 * D] = da
    gb_out_ref[...] = jnp.sum(da.astype(f32), axis=0, keepdims=True)
    d_mixed = sum(dot(da[:, g * wide : (g + 1) * wide], weight(g, 256), NT) for g in range(groups))
    d_mixed = d_mixed.astype(bf16)
    for shard in range(shards):
        do_ref[shard] = d_mixed[:, shard * LANES : (shard + 1) * LANES]
    slots_ref[...] = jnp.concatenate(d_gate1 + d_shift2 + d_scale2 + d_gate2, axis=0)


def weight_grad_kernel(
    order_ref, group_ref, keep_ref, send_ref, pair_ref, pair2_ref, first_x, first_y, own_x, own_y
):
    groups, wide = 4, first_x.shape[3]

    def product(at, width, start, stop):
        here = pl.ds(pl.multiple_of(at, LANES), width)
        return (
            dot(keep_ref[:, here], pair_ref[:, start:stop], TN) + dot(send_ref[:, here], pair2_ref[:, start:stop], TN)
        ).astype(bf16)

    places = (((own_x, 0), (own_y, 0)), ((first_x, 0), (own_y, 1)), ((own_x, 1), (first_y, 0)), ((first_x, 1), (first_y, 1)))
    for index in range(4):
        chip = order_ref[index] // 2
        down = product(chip * 2 * LANES, 2 * LANES, 0, D)
        out = product(D + chip * LANES, LANES, D, 2 * D)
        up = product(D + D // 2 + chip * LANES, LANES, 2 * D, 4 * D)
        for group in range(groups):
            to = (group + groups - group_ref[0]) % groups

            def store(ref, entry, to):
                ref[entry, to, 0:256, :] = down[:, group * wide : (group + 1) * wide]
                ref[entry, to, 256:384, :] = out[:, group * wide : (group + 1) * wide]
                for half in range(2):
                    at = (2 * group + half) * wide
                    ref[entry, to, 384 + 128 * half : 512 + 128 * half, :] = up[:, at : at + wide]

            @pl.when(to < 2)
            def _():
                store(*places[index][0], to)

            @pl.when(to >= 2)
            def _():
                store(*places[index][1], to - 2)


def attend_back_kernel(head, q_ref, k_ref, v_ref, do_ref, mixed_ref, l_ref, cos_ref, sin_ref, *refs):
    *refs, dn, dq_t, dk_all = refs
    if head == 0:
        qk_ref, dv_ref = refs
    else:
        qk_first, dv_first, qk_ref, own_ref, gb_ref = refs
    step = pl.program_id(0)
    rows = k_ref.shape[1]
    frames = q_ref.shape[1]
    tile = 512
    lane = lax.broadcasted_iota(jnp.int32, (rows, LANES), 1)
    low = lane < HD

    @pl.when(step == 0)
    def _():
        dq_t[...] = jnp.zeros_like(dq_t)
        for at in range(0, frames, rows):
            here = slice(at, at + rows)
            d_out = do_ref[here].astype(f32)
            norm = l_ref[here]
            d_num = (d_out / norm).astype(bf16).astype(f32)
            mine = low if head == 0 else ~low
            total = jnp.sum(jnp.where(mine, d_out * mixed_ref[here], 0.0), axis=1, keepdims=True)
            delta = -total / norm[:, head * HD : head * HD + 1]
            first = delta.astype(bf16).astype(f32)
            second = (delta - first).astype(bf16).astype(f32)
            third = delta - first - second
            extra = jnp.where(lane == HD, first, jnp.where(lane == HD + 1, second, third))
            extra = jnp.where(lane < HD + 3, extra, 0.0)
            own = d_num if head == 0 else pltpu.roll(d_num, HD, 1)
            dn[here] = jnp.where(low, own, extra).astype(bf16)

    key, value = k_ref[0], v_ref[0]
    key_t = key.T
    dk_total, dv_total = None, None
    for at in range(0, frames, tile):
        here = slice(at, at + tile)
        query, d_num = q_ref[0, here], dn[here]
        expo = jnp.exp(dot(key, query, NT))
        d_score = (expo * dot(value, d_num, NT)).astype(bf16)
        dk_term = dot(d_score, query)
        dv_term = dot(expo.astype(bf16), d_num)
        dk_total = dk_term if dk_total is None else dk_total + dk_term
        dv_total = dv_term if dv_total is None else dv_total + dv_term
        dq_t[:, here] += dot(key_t, d_score)

    here = pl.ds(pl.multiple_of(step * rows, rows), rows)
    dk_all[here] = dk_total
    if head == 0:
        dv_ref[here] = dv_total.astype(bf16)
    else:
        own_ref[here, 2 * LANES :] = jnp.where(low, dv_first[here].astype(f32), pltpu.roll(dv_total, HD, 1)).astype(bf16)

    @pl.when(step == pl.num_programs(0) - 1)
    def _():
        for at in range(0, frames, rows):
            part = slice(at, at + rows)
            cosine, sine = rotary(cos_ref, sin_ref, part)
            both = jnp.where(low, 0.125 * dq_t[:, part].T, pltpu.roll(dk_all[part], HD, 1))
            both = (both * cosine - swap_halves(both) * sine).astype(bf16)
            qk_ref[part] = both
            if head == 1:
                first, second = qk_first[part].astype(f32), both.astype(f32)
                own_ref[part, 0:LANES] = jnp.where(low, first, pltpu.roll(second, HD, 1)).astype(bf16)
                own_ref[part, LANES : 2 * LANES] = jnp.where(low, pltpu.roll(first, HD, 1), second).astype(bf16)
        if head == 1:
            ones = jnp.ones((8, frames), bf16)
            sums = dot(ones, own_ref[...])[0:1]
            for index in range(3):
                gb_ref[index : index + 1] = sums[:, index * LANES : (index + 1) * LANES]


def input_grad_kernel(
    base_ref, seg_ref, first_ref, second_ref, w_ref, x_ref, dx1_ref, table_ref, grad_ref, slots_ref
):
    block = base_ref[0]
    rows = x_ref.shape[0]
    member = members(seg_ref, block, rows)
    scale = 1.0 + mod_rows(table_ref, seg_ref, block, member, 1)
    low = lax.broadcasted_iota(jnp.int32, (rows, LANES), 1) < HD
    d_hidden = None
    for shard in range(first_ref.shape[0]):
        first, second = first_ref[shard].astype(f32), second_ref[shard, :, :LANES].astype(f32)
        queries = jnp.where(low, first, pltpu.roll(second, HD, 1)).astype(bf16)
        keys = jnp.where(low, pltpu.roll(first, HD, 1), second).astype(bf16)
        whole_row = jnp.concatenate([queries, keys, second_ref[shard, :, LANES:]], axis=1)
        term = dot(whole_row, w_ref[shard], NT)
        d_hidden = term if d_hidden is None else d_hidden + term
    normal, inv = moments(x_ref[...].astype(f32))
    grad_ref[...] = dx1_ref[...] + norm_back(d_hidden * scale, normal, inv)
    sums = slot_sums(member, d_hidden) + slot_sums(member, d_hidden * normal)
    slots_ref[...] = jnp.concatenate(sums + [jnp.zeros((2, D), f32)], axis=0)


def spread(value, axis, size):
    return [value] + [
        lax.ppermute(value, axis, [(i, (i - step) % size) for i in range(size)]) for step in range(1, size)
    ]


def trade(pieces, axis, size):
    return [pieces[0]] + [
        lax.ppermute(pieces[size - step], axis, [(i, (i - step) % size) for i in range(size)])
        for step in range(1, size)
    ]


def in_order(pieces, axis, size):
    own = lax.axis_index(axis)
    out = []
    for place in range(size):
        pick = (place - own) % size
        value = pieces[0]
        for index in range(1, size):
            value = jnp.where(pick == index, pieces[index], value)
        out.append(value)
    return out


def hop(value, step):
    return lax.ppermute(value, "shard", [(i, i ^ step) for i in range(8)])


def after(value, *others):
    anywhere = pl.BlockSpec(memory_space=pl.ANY)
    return pl.pallas_call(
        lambda *refs: None,
        in_specs=[anywhere] * (1 + len(others)),
        out_specs=anywhere,
        out_shape=jax.ShapeDtypeStruct(value.shape, value.dtype),
        input_output_aliases={0: 0},
        cost_estimate=FREE,
        name="after",
    )(value, *others)


def shape(*dims, kind=bf16):
    return jax.ShapeDtypeStruct(dims, kind)


def whole(*dims):
    return pl.BlockSpec(dims, lambda *_: (0,) * len(dims))


smem = pl.BlockSpec(memory_space=pltpu.SMEM)


def local_heads(
    groups, shards, frames, cotangent, seg_start, seg_length, seg_step, time_table,
    w_ada, b_ada, w_qkv, b_qkv, w_out, b_out, w_up, b_up, w_down, b_down,
):
    rows = frames.shape[0]
    packed = rows * shards
    steps = time_table.shape[0]
    shard = lax.axis_index("shard")
    depth = D // shards
    wide = D // groups

    group = lax.axis_index("grp")
    order = shard ^ jnp.array(ORDER, jnp.int32)

    inverse = 10000.0 ** (-jnp.arange(HD // 2, dtype=f32) / (HD // 2))
    phase = inverse[:, None] * jnp.arange(packed, dtype=f32)[None, :]
    cosine, sine = jnp.cos(phase), jnp.sin(phase)

    activated = jax.nn.silu(time_table).astype(bf16)
    act_own = lax.dynamic_slice_in_dim(activated, shard * depth, depth, 1)
    partial_mod = dot(act_own, w_ada)
    mod_wide = partial_mod.shape[1]
    biases = [b.astype(f32) for b in (b_ada, b_qkv, b_out, b_up, b_down)]
    sizes = [b.shape[0] for b in biases]
    segs = jnp.concatenate((seg_start, seg_length, seg_step), axis=1).astype(f32)
    extra = jnp.concatenate(biases + [jnp.floor(segs[0] / 128.0), segs[0] % 128.0])
    extra_rows = -(-extra.shape[0] // mod_wide)
    extra = jnp.pad(extra, (0, extra_rows * mod_wide - extra.shape[0])).reshape(extra_rows, mod_wide)
    units = 3 * shards // groups
    first = group * units
    by_unit = w_qkv.reshape(depth, units, LANES).transpose(1, 0, 2)
    which = jnp.minimum((jnp.arange(shards) - first) % shards, units - 1)
    by_shard = jnp.take(by_unit, which, axis=0, mode="clip")
    w_cols = jnp.broadcast_to(by_shard[None], (groups, shards, depth, LANES)).reshape(groups * shards, depth, LANES)
    w_cols = lax.all_to_all(w_cols, ("grp", "shard"), split_axis=0, concat_axis=0, tiled=True).reshape(groups, D, LANES)
    small = jnp.concatenate((partial_mod, extra), axis=0).astype(bf16)
    small = lax.all_gather(small, "shard", axis=0).astype(f32)
    held = after(frames, small)
    chips = [held] + [hop(held, step) for step in CHIPS]

    mod_own = jnp.sum(small[:, :steps], axis=0).astype(bf16)
    high = lax.all_gather(after(mod_own, w_cols), "grp", axis=1, tiled=True)

    w_heads = jnp.concatenate(
        [lax.dynamic_index_in_dim(w_cols, (part * shards + shard) // units, 0, keepdims=False) for part in range(3)], axis=1
    )

    chips = [chips[0]] + [after(piece, high) for piece in chips[1:]]
    others = hop(jnp.stack(chips), 1)

    pack = jnp.concatenate((w_down, w_out, w_up[:, :wide], w_up[:, wide:]), axis=0)
    weights = lax.all_gather(pack, ("grp", "shard"), axis=0).reshape(groups, shards, 5 * LANES, wide)

    extra = small[:, steps:].reshape(shards, extra_rows * mod_wide)
    full, at = [], 0
    for size in sizes:
        full.append(extra[:, at : at + size].reshape(1, shards * size))
        at += size
    ada_bias, qkv_bias, out_bias, up_bias, down_bias = full
    seg_all = (extra[:, at : at + 9] * 128.0 + extra[:, at + 9 : at + 18]).astype(jnp.int32)
    qkv_bias = lax.dynamic_index_in_dim(qkv_bias.reshape(3, shards, LANES), shard, 1, keepdims=False)
    qkv_bias = qkv_bias.reshape(1, 3 * LANES)
    table = high.astype(f32) + ada_bias

    ordered = lambda width: pl.BlockSpec((rows, width), lambda i, order: (order[i], 0))
    ordered_heads = pl.BlockSpec((2, rows, LANES), lambda i, order: (0, order[i], 0))
    by_block = lambda width: pl.BlockSpec((rows, width), lambda i: (i, 0))
    two_heads = pl.BlockSpec((2, rows, LANES), lambda i: (0, i, 0))
    frame_pieces = [piece[None] for piece in chips] + [others]
    q, k, v, h1_all = pl.pallas_call(
        qkv_kernel,
        grid_spec=pltpu.PrefetchScalarGridSpec(
            num_scalar_prefetch=1,
            grid=(shards,),
            in_specs=[smem]
            + [pl.BlockSpec(memory_space=pl.ANY)] * len(frame_pieces)
            + [whole(steps, 2 * D), whole(D, 3 * LANES), whole(1, 3 * LANES)] + [pl.BlockSpec((HD // 2, rows), lambda i, order: (0, order[i]))] * 2,
            out_specs=[ordered_heads] * 3 + [ordered(D)],
            scratch_shapes=[pltpu.VMEM((shards, rows, D), bf16), pltpu.SemaphoreType.DMA((len(frame_pieces),))],
        ),
        out_shape=[shape(2, packed, LANES)] * 3 + [shape(packed, D)],
        compiler_params=params(60),
        cost_estimate=FREE,
        name="qkv",
    )(order, seg_all, *frame_pieces, table[:, : 2 * D], w_heads, qkv_bias, cosine, sine)

    attn_flops = 2 * 2 * packed * packed * 256
    o_heads, mixed, norm = pl.pallas_call(
        attend_kernel,
        grid=(shards,),
        in_specs=[two_heads, whole(2, packed, LANES), whole(2, packed, LANES)],
        out_specs=[by_block(LANES)] * 3,
        out_shape=[shape(packed, LANES), shape(packed, LANES, kind=f32), shape(packed, LANES, kind=f32)],
        compiler_params=params(60),
        cost_estimate=FREE,
        name="attend",
    )(q, k, v)

    o = lax.all_to_all(o_heads.reshape(shards, rows, LANES), "shard", split_axis=0, concat_axis=0, tiled=True)
    base = shard.astype(jnp.int32).reshape(1)
    block_flops = 2 * rows * D * D * 10
    out, dx1, d_mixed, pair, keep, send, slots_ff, gb_out, gb_up, gb_down = pl.pallas_call(
        block_kernel,
        grid=(1,),
        in_specs=[
            smem, smem, whole(rows, D), whole(rows, D), whole(shards, rows, LANES), whole(steps, 6 * D),
            whole(groups, shards, 5 * LANES, wide), whole(1, D), whole(1, 2 * D), whole(1, D),
        ],
        out_specs=[
            whole(rows, D), whole(rows, D), whole(shards, rows, LANES), whole(rows, 4 * D), whole(rows, 2 * D),
            whole(rows, 2 * D), whole(12, D), whole(1, D), whole(1, 2 * D), whole(1, D),
        ],
        out_shape=[
            shape(rows, D), shape(rows, D, kind=f32), shape(shards, rows, LANES), shape(rows, 4 * D), shape(rows, 2 * D),
            shape(rows, 2 * D), shape(12, D, kind=f32),
            shape(1, D, kind=f32), shape(1, 2 * D, kind=f32), shape(1, D, kind=f32),
        ],
        compiler_params=params(60),
        cost_estimate=FREE,
        name="block",
    )(order, seg_all, frames, cotangent, o, table, weights, out_bias, up_bias, down_bias)

    d_heads = lax.all_to_all(d_mixed, "shard", split_axis=0, concat_axis=0, tiled=True).reshape(packed, LANES)

    send, pair_send = hop(send, 1), hop(pair, 1)
    half = (2, groups // 2, 5 * LANES, wide)
    first_x, first_y, own_x, own_y = pl.pallas_call(
        weight_grad_kernel,
        grid=(1,),
        in_specs=[smem, smem, whole(rows, 2 * D), whole(rows, 2 * D), whole(rows, 4 * D), whole(rows, 4 * D)],
        out_specs=[whole(*half)] * 4,
        out_shape=[shape(*half)] * 4,
        compiler_params=params(60),
        cost_estimate=FREE,
        name="weight_grads",
    )(order, group.astype(jnp.int32).reshape(1), keep, send, pair, pair_send)
    first_x, first_y = after(first_x, d_heads), after(first_y, d_heads)
    d_heads = after(d_heads, first_x, first_y)
    add = lambda *pieces: sum(piece.astype(f32) for piece in pieces).astype(bf16)

    back_specs = lambda head: [
        pl.BlockSpec((1, packed, LANES), lambda i: (head, 0, 0)),
        pl.BlockSpec((1, rows, LANES), lambda i: (head, i, 0)),
        pl.BlockSpec((1, rows, LANES), lambda i: (head, i, 0)),
    ] + [whole(packed, LANES)] * 3 + [whole(HD // 2, packed)] * 2
    back_scratch = [pltpu.VMEM((packed, LANES), bf16), pltpu.VMEM((LANES, packed), f32), pltpu.VMEM((packed, LANES), f32)]
    arguments = (q, k, v, d_heads, mixed, norm, cosine, sine)
    came_x, came_y = hop(first_x, 2), hop(first_y, 4)
    qk_first, dv_first = pl.pallas_call(
        partial(attend_back_kernel, 0),
        grid=(shards,),
        in_specs=back_specs(0),
        out_specs=[whole(packed, LANES), whole(packed, LANES)],
        out_shape=[shape(packed, LANES)] * 2,
        scratch_shapes=back_scratch,
        compiler_params=params(60),
        cost_estimate=FREE,
        name="attend_back_first",
    )(*arguments)
    came_x, came_y = after(came_x, qk_first), after(came_y, qk_first)
    next_y, next_x = add(own_x[1], came_x[1]), add(own_y[1], came_y[1])
    dv_first = after(dv_first, next_y, next_x)
    next_y, next_x = hop(next_y, 4), hop(next_x, 2)
    d_first = lax.all_to_all(qk_first.reshape(shards, rows, LANES), "shard", split_axis=0, concat_axis=0, tiled=True)
    qk_second, d_own, gb_qkv = pl.pallas_call(
        partial(attend_back_kernel, 1),
        grid=(shards,),
        in_specs=back_specs(1) + [whole(packed, LANES)] * 2,
        out_specs=[whole(packed, LANES), whole(packed, 3 * LANES), whole(3, LANES)],
        out_shape=[shape(packed, LANES), shape(packed, 3 * LANES), shape(3, LANES, kind=f32)],
        scratch_shapes=back_scratch,
        compiler_params=params(60),
        cost_estimate=FREE,
        name="attend_back_second",
    )(*arguments, qk_first, dv_first)
    next_y, next_x = after(next_y, qk_second), after(next_x, qk_second)
    totals = (add(own_x[0], came_x[0], next_y), add(own_y[0], came_y[0], next_x))
    d_own_late = after(d_own, *totals)
    grads = trade([totals[i // 2][i % 2] for i in range(groups)], "grp", groups)
    grads = sum(piece.astype(f32) for piece in grads)
    g_down, g_out = grads[: 2 * LANES], grads[2 * LANES : 3 * LANES]
    g_up = jnp.concatenate((grads[3 * LANES : 4 * LANES], grads[4 * LANES :]), axis=1)

    second = jnp.concatenate((qk_second.reshape(shards, rows, LANES), d_own[:, 2 * LANES :].reshape(shards, rows, LANES)), axis=2)
    d_second = lax.all_to_all(second, "shard", split_axis=0, concat_axis=0, tiled=True)
    w_all = lax.all_gather(after(w_heads, o), "shard", axis=0)
    grad_frames, slots_qkv = pl.pallas_call(
        input_grad_kernel,
        in_specs=[smem, smem] + [pl.BlockSpec(memory_space=pltpu.VMEM)] * 6,
        out_specs=[pl.BlockSpec(memory_space=pltpu.VMEM)] * 2,
        out_shape=[shape(rows, D, kind=f32), shape(8, D, kind=f32)],
        compiler_params=pltpu.CompilerParams(vmem_limit_bytes=40 * 2**20),
        cost_estimate=FREE,
        name="input_grad",
    )(base, seg_all, d_first, d_second, w_all, frames, dx1, table[:, : 2 * D])

    g_heads = dot(h1_all, d_own_late, TN).astype(bf16).reshape(shards, depth, 3 * LANES)
    part = jnp.stack([jnp.clip((units * to + units - 1 - shard) // shards, 0, 2) for to in range(groups)])
    g_send = jnp.stack(
        [lax.dynamic_slice_in_dim(g_heads, part[to] * LANES, LANES, 2) for to in range(groups)]
    ).reshape(groups * shards, depth, LANES)
    g_came = lax.all_to_all(g_send, ("grp", "shard"), split_axis=0, concat_axis=0, tiled=True)
    g_came = jnp.sum(g_came.reshape(groups, shards, depth, LANES).astype(f32), axis=0)
    g_qkv = jnp.concatenate(
        [lax.dynamic_index_in_dim(g_came, (first + unit) % shards, 0, keepdims=False) for unit in range(units)], axis=1
    )

    d_slot = jnp.concatenate((slots_qkv[:6], slots_ff), axis=0).reshape(6, 3, D).transpose(1, 0, 2).reshape(3, 6 * D)
    row_sums = jnp.concatenate((gb_qkv.reshape(-1), gb_out[0], gb_up[0], gb_down[0]))
    sum_rows = -(-row_sums.shape[0] // (6 * D))
    row_sums = jnp.pad(row_sums, (0, sum_rows * 6 * D - row_sums.shape[0])).reshape(sum_rows, 6 * D)
    tail = lax.all_gather(after(jnp.concatenate((d_slot, row_sums), axis=0), grads), "shard", axis=0)
    d_slots = tail[:, :3]
    d_segs = jnp.concatenate(
        (d_slots[0], d_slots[shards - 1], jnp.sum(d_slots[1 : shards - 1], axis=(0, 1))[None]), axis=0
    )
    step_ids = jnp.concatenate((seg_all[0, 6:], seg_all[shards - 1, 6:], jnp.sum(seg_all[1, 6:])[None])).astype(f32)
    rest = tail[:, 3:].reshape(shards, sum_rows * 6 * D)
    gb_heads = rest[:, : 3 * LANES].reshape(shards, 3, LANES).transpose(1, 0, 2).reshape(3 * D)
    others = jnp.sum(rest[:, 3 * LANES : 3 * LANES + 4 * D], axis=0)
    sums = (
        jnp.sum(d_segs, axis=0), gb_heads, others[:D], others[D : 3 * D], others[3 * D : 4 * D],
    )
    own_sums = [lax.dynamic_slice_in_dim(total, shard * size, size) for total, size in zip(sums, sizes)]
    send = jnp.concatenate(own_sums + [step_ids])
    send_rows = -(-send.shape[0] // mod_wide)
    send = jnp.pad(send, (0, send_rows * mod_wide - send.shape[0])).reshape(send_rows, mod_wide)
    d_segs = d_segs.reshape(7, groups, mod_wide).transpose(1, 0, 2)
    at_group = lambda pieces: [lax.dynamic_index_in_dim(pieces, (group + i) % groups, 0, keepdims=False) for i in range(groups)]
    parts = trade([jnp.concatenate((piece, send), axis=0) for piece in at_group(d_segs)], "grp", groups)
    d_rows_all = jnp.concatenate([piece[:7] for piece in parts], axis=0)
    rest = [piece[7:].reshape(-1) for piece in parts]
    at = sum(sizes)
    ids = jnp.concatenate([piece[at : at + 7] for piece in rest])
    onehot = (ids[None, :] == jnp.arange(steps, dtype=f32)[:, None]).astype(f32)
    d_table = jnp.dot(onehot, d_rows_all, precision=top_precision)
    g_ada = jnp.dot(act_own.astype(f32).T, d_table, precision=top_precision)
    bias_sums = sum(piece[:at] for piece in rest)
    bias_grads, start = [], 0
    for size in sizes:
        bias_grads.append(bias_sums[start : start + size])
        start += size
    gb_ada, gb_qkv, gb_out, gb_up, gb_down = bias_grads

    d_act = lax.dot_general(d_table, w_ada.astype(f32), NT, precision=top_precision, preferred_element_type=f32)
    table_own = lax.dynamic_slice_in_dim(time_table, shard * depth, depth, 1)
    g_table = jax.vjp(jax.nn.silu, table_own)[1](d_act)[0]
    g_table = sum(spread(g_table, "grp", groups))
    return (
        out, grad_frames, g_table, g_ada, gb_ada, g_qkv, gb_qkv, g_out, gb_out, g_up, gb_up, g_down, gb_down,
    )


def solution(mesh):
    in_specs = (
        P(("grp", "shard"), None),
        P(("grp", "shard"), None),
        P(("grp", "shard"), None),
        P(("grp", "shard"), None),
        P(("grp", "shard"), None),
        P(),
        P("shard", "grp"),
        P("shard"),
        P("shard", "grp"),
        P("shard"),
        P("shard", "grp"),
        P("shard"),
        P("shard", "grp"),
        P("shard"),
        P("shard", "grp"),
        P("shard"),
    )
    out_specs = (
        P(("grp", "shard"), None),
        P(("grp", "shard"), None),
        P(None, "shard"),
        P("shard", "grp"),
        P("shard"),
        P("shard", "grp"),
        P("shard"),
        P("shard", "grp"),
        P("shard"),
        P("shard", "grp"),
        P("shard"),
        P("shard", "grp"),
        P("shard"),
    )
    by_heads = mesh.shape["shard"] * 2 * HD == D
    local = partial(local_heads, mesh.shape["grp"], mesh.shape["shard"]) if by_heads else local_any
    return jax.shard_map(local, mesh=mesh, in_specs=in_specs, out_specs=out_specs, check_vma=False)
```

```python
from functools import partial

import jax
import jax.numpy as jnp
from jax import lax
from jax.experimental import pallas as pl
from jax.experimental.pallas import tpu as pltpu
from jax.sharding import PartitionSpec as P

D = 1024
H = 16
HD = 64


eps_norm = 1e-06
top_precision = lax.Precision.HIGHEST


def normalize(tensor):
    centred = tensor - jnp.mean(tensor, axis=-1, keepdims=True)
    return centred * lax.rsqrt(jnp.mean(centred * centred, axis=-1, keepdims=True) + eps_norm)


def modulate(tensor, scale_vec, shift_vec):
    return normalize(tensor) * (1.0 + scale_vec) + shift_vec


def angles(positions):
    half_width = HD // 2
    inverse = 10000.0 ** (-jnp.arange(half_width, dtype=jnp.float32) / half_width)
    phase_grid = positions[:, None] * inverse[None, :]
    return (jnp.cos(phase_grid), jnp.sin(phase_grid))


def rotate(tensor, cosine_vals, sine_vals):
    row_total = tensor.shape[0]
    halves = tensor.reshape(row_total, H, 2, HD // 2)
    former = halves[:, :, 0]
    latter = halves[:, :, 1]
    cosine_part = cosine_vals[:, None, :]
    sine_part = sine_vals[:, None, :]
    turned = jnp.stack(
        (former * cosine_part - latter * sine_part, latter * cosine_part + former * sine_part),
        axis=2,
    )
    return turned.reshape(row_total, D)


def tile_width(row_total):
    for candidate in (512, 256, 128):
        return candidate
    return row_total


def head_view(tensor):
    return tensor.reshape(tensor.shape[0], H, HD)


def local_any(
    frames,
    cotangent,
    seg_start,
    seg_length,
    seg_step,
    time_table,
    w_ada,
    b_ada,
    w_qkv,
    b_qkv,
    w_out,
    b_out,
    w_up,
    b_up,
    w_down,
    b_down,
):
    frame_rows = frames.shape[0]
    positions = lax.axis_index("shard") * frame_rows + jnp.arange(frame_rows, dtype=jnp.int32)
    slot_start = seg_start[0]
    slot_end = slot_start + seg_length[0]
    member_mask = (positions[:, None] >= slot_start[None, :]) & (
        positions[:, None] < slot_end[None, :]
    )
    member = member_mask.astype(jnp.float32)
    seg_low = jnp.sum(jnp.where(member_mask, slot_start[None, :], 0), axis=1)
    seg_high = jnp.sum(jnp.where(member_mask, slot_end[None, :], 0), axis=1)
    cosine_vals, sine_vals = angles((positions - seg_low).astype(jnp.float32))
    columns = (
        lax.all_gather(w_ada, "grp", axis=1, tiled=True),
        lax.all_gather(w_qkv, "grp", axis=1, tiled=True),
        lax.all_gather(w_out, "grp", axis=1, tiled=True),
        lax.all_gather(w_up, "grp", axis=1, tiled=True),
        lax.all_gather(w_down, "grp", axis=1, tiled=True),
    )
    gathered = (
        lax.all_gather(columns[0], "shard", axis=0, tiled=True),
        lax.all_gather(columns[1], "shard", axis=0, tiled=True),
        lax.all_gather(columns[2], "shard", axis=0, tiled=True),
        lax.all_gather(columns[3], "shard", axis=0, tiled=True),
        lax.all_gather(columns[4], "shard", axis=0, tiled=True),
        lax.all_gather(b_ada, "shard", axis=0, tiled=True),
        lax.all_gather(b_qkv, "shard", axis=0, tiled=True),
        lax.all_gather(b_out, "shard", axis=0, tiled=True),
        lax.all_gather(b_up, "shard", axis=0, tiled=True),
        lax.all_gather(b_down, "shard", axis=0, tiled=True),
    )
    ada_full, qkv_full, out_full, up_full, down_full = (
        gathered[0],
        gathered[1],
        gathered[2],
        gathered[3],
        gathered[4],
    )
    ada_bias, qkv_bias, out_bias, up_bias, down_bias = [
        bias_row.astype(jnp.float32) for bias_row in gathered[5:]
    ]
    step_onehot = (
        seg_step[0][:, None] == jnp.arange(time_table.shape[0], dtype=jnp.int32)[None, :]
    ).astype(jnp.float32)
    time_rows = jnp.dot(step_onehot, time_table, precision=top_precision)
    activated = jax.nn.silu(time_rows).astype(jnp.bfloat16)
    modulation = jnp.dot(activated, ada_full, preferred_element_type=jnp.float32) + ada_bias
    frame_mod = jnp.dot(member, modulation, precision=top_precision)
    shift_attn, scale_attn, gate_attn, shift_ff, scale_ff, gate_ff = jnp.split(frame_mod, 6, axis=1)
    inputs = frames.astype(jnp.float32)
    hidden_attn = modulate(inputs, scale_attn, shift_attn).astype(jnp.bfloat16)
    projected = jnp.dot(hidden_attn, qkv_full, preferred_element_type=jnp.float32) + qkv_bias
    queries = rotate(projected[:, :D], cosine_vals, sine_vals).astype(jnp.bfloat16)
    keys_rot = rotate(projected[:, D : 2 * D], cosine_vals, sine_vals).astype(jnp.bfloat16)
    values = projected[:, 2 * D :].astype(jnp.bfloat16)
    query_heads = head_view(queries)
    key_heads = head_view(keys_rot)
    value_heads = head_view(values)
    zero_heads = jnp.zeros((frame_rows, H, HD), jnp.float32)
    key_piece = lax.all_gather(keys_rot, "shard", axis=0, tiled=True)
    value_piece = lax.all_gather(values, "shard", axis=0, tiled=True)
    piece_rows = key_piece.shape[0]
    tile_rows = tile_width(piece_rows)
    tiles = piece_rows // tile_rows

    def tile_step(partial_sums, tile_item):
        key_tile, value_tile, offset = tile_item
        key_pos = offset + jnp.arange(tile_rows, dtype=jnp.int32)
        inside = (key_pos[None, :] >= seg_low[:, None]) & (key_pos[None, :] < seg_high[:, None])
        scores = 0.125 * jnp.einsum(
            "rhd,khd->hrk", query_heads, head_view(key_tile), preferred_element_type=jnp.float32
        )
        expo = jnp.where(inside[None], jnp.exp(scores), 0.0)
        numerator, denominator = partial_sums
        numerator = numerator + jnp.einsum(
            "hrk,khd->rhd",
            expo.astype(jnp.bfloat16),
            head_view(value_tile),
            preferred_element_type=jnp.float32,
        )
        denominator = denominator + jnp.sum(expo, axis=2).T
        return ((numerator, denominator), None)

    tile_items = (
        key_piece.reshape(tiles, tile_rows, D),
        value_piece.reshape(tiles, tile_rows, D),
        jnp.arange(tiles, dtype=jnp.int32) * tile_rows,
    )
    numerator, denominator = lax.scan(
        tile_step, (zero_heads, jnp.zeros((frame_rows, H), jnp.float32)), tile_items
    )[0]
    mixed = numerator / denominator[:, :, None]
    mixed_low = mixed.reshape(frame_rows, D).astype(jnp.bfloat16)
    attn_branch = jnp.dot(mixed_low, out_full, preferred_element_type=jnp.float32) + out_bias
    after_attn = inputs + gate_attn * attn_branch
    hidden_ff = modulate(after_attn, scale_ff, shift_ff).astype(jnp.bfloat16)
    upward = jnp.dot(hidden_ff, up_full, preferred_element_type=jnp.float32) + up_bias
    activation = jax.nn.gelu(upward, approximate=True).astype(jnp.bfloat16)
    ff_branch = jnp.dot(activation, down_full, preferred_element_type=jnp.float32) + down_bias
    output = (after_attn + gate_ff * ff_branch).astype(jnp.bfloat16)
    columns_back = (
        lax.all_gather(w_ada, "grp", axis=1, tiled=True),
        lax.all_gather(w_qkv, "grp", axis=1, tiled=True),
        lax.all_gather(w_out, "grp", axis=1, tiled=True),
        lax.all_gather(w_up, "grp", axis=1, tiled=True),
        lax.all_gather(w_down, "grp", axis=1, tiled=True),
    )
    gathered_back = (
        lax.all_gather(columns_back[0], "shard", axis=0, tiled=True),
        lax.all_gather(columns_back[1], "shard", axis=0, tiled=True),
        lax.all_gather(columns_back[2], "shard", axis=0, tiled=True),
        lax.all_gather(columns_back[3], "shard", axis=0, tiled=True),
        lax.all_gather(columns_back[4], "shard", axis=0, tiled=True),
    )
    ada_back, qkv_back, out_back, up_back, down_back = (
        gathered_back[0],
        gathered_back[1],
        gathered_back[2],
        gathered_back[3],
        gathered_back[4],
    )
    grad_out = cotangent.astype(jnp.float32)
    d_branch = (gate_ff * grad_out).astype(jnp.bfloat16)
    d_gate_ff = grad_out * ff_branch
    g_down = jnp.dot(activation.T, d_branch, preferred_element_type=jnp.float32)
    gb_down = jnp.sum(d_branch.astype(jnp.float32), axis=0)
    d_activation = jnp.dot(d_branch, down_back.T, preferred_element_type=jnp.float32)
    gelu_pull = jax.vjp(partial(jax.nn.gelu, approximate=True), upward)[1]
    d_upward = gelu_pull(d_activation)[0].astype(jnp.bfloat16)
    g_up = jnp.dot(hidden_ff.T, d_upward, preferred_element_type=jnp.float32)
    gb_up = jnp.sum(d_upward.astype(jnp.float32), axis=0)
    d_hidden_ff = jnp.dot(d_upward, up_back.T, preferred_element_type=jnp.float32)
    ff_pull = jax.vjp(modulate, after_attn, scale_ff, shift_ff)[1]
    dx_ff, d_scale_ff, d_shift_ff = ff_pull(d_hidden_ff)
    d_after = grad_out + dx_ff
    d_attn = (gate_attn * d_after).astype(jnp.bfloat16)
    d_gate_attn = d_after * attn_branch
    g_out = jnp.dot(mixed_low.T, d_attn, preferred_element_type=jnp.float32)
    gb_out = jnp.sum(d_attn.astype(jnp.float32), axis=0)
    d_mixed = jnp.dot(d_attn, out_back.T, preferred_element_type=jnp.float32).astype(jnp.bfloat16)
    d_mixed_heads = head_view(d_mixed).astype(jnp.float32)
    delta = jnp.sum(d_mixed_heads * mixed, axis=2) / denominator
    d_numer = (d_mixed_heads / denominator[:, :, None]).astype(jnp.bfloat16).reshape(frame_rows, D)
    dnum_heads = head_view(d_numer)
    delta_heads = delta.T
    key_piece = lax.all_gather(keys_rot, "shard", axis=0, tiled=True)
    value_piece = lax.all_gather(values, "shard", axis=0, tiled=True)
    piece_rows = key_piece.shape[0]
    fold_tile_rows = tile_width(piece_rows)
    tiles = piece_rows // fold_tile_rows

    def tile_step(grad_sum, tile_item):
        key_tile, value_tile, offset = tile_item
        key_pos = offset + jnp.arange(fold_tile_rows, dtype=jnp.int32)
        inside = (key_pos[None, :] >= seg_low[:, None]) & (key_pos[None, :] < seg_high[:, None])
        scores = 0.125 * jnp.einsum(
            "rhd,khd->hrk", query_heads, head_view(key_tile), preferred_element_type=jnp.float32
        )
        expo = jnp.where(inside[None], jnp.exp(scores), 0.0)
        slope = jnp.einsum(
            "rhd,khd->hrk", dnum_heads, head_view(value_tile), preferred_element_type=jnp.float32
        )
        d_scores = (expo * (slope - delta_heads[:, :, None])).astype(jnp.bfloat16)
        grad_sum = grad_sum + 0.125 * jnp.einsum(
            "hrk,khd->rhd", d_scores, head_view(key_tile), preferred_element_type=jnp.float32
        )
        return (grad_sum, None)

    tile_items = (
        key_piece.reshape(tiles, fold_tile_rows, D),
        value_piece.reshape(tiles, fold_tile_rows, D),
        jnp.arange(tiles, dtype=jnp.int32) * fold_tile_rows,
    )
    d_query = lax.scan(tile_step, zero_heads, tile_items)[0]
    delta_all = lax.all_gather(delta, "shard", axis=0, tiled=True)

    def fold_key_grad(running, piece):
        query_piece, dnum_piece = piece
        piece_rows = query_piece.shape[0]
        tile_rows = tile_width(piece_rows)
        tiles = piece_rows // tile_rows

        def tile_step(grad_pair, tile_item):
            query_tile, dnum_tile, delta_tile, offset = tile_item
            query_pos = offset + jnp.arange(tile_rows, dtype=jnp.int32)
            inside = (query_pos[:, None] >= seg_low[None, :]) & (
                query_pos[:, None] < seg_high[None, :]
            )
            query_tile_heads = head_view(query_tile)
            dnum_tile_heads = head_view(dnum_tile)
            scores = 0.125 * jnp.einsum(
                "qhd,rhd->hqr", query_tile_heads, key_heads, preferred_element_type=jnp.float32
            )
            expo = jnp.where(inside[None], jnp.exp(scores), 0.0)
            slope = jnp.einsum(
                "qhd,rhd->hqr", dnum_tile_heads, value_heads, preferred_element_type=jnp.float32
            )
            d_scores = (expo * (slope - delta_tile.T[:, :, None])).astype(jnp.bfloat16)
            d_keys, d_values = grad_pair
            d_keys = d_keys + 0.125 * jnp.einsum(
                "hqr,qhd->rhd", d_scores, query_tile_heads, preferred_element_type=jnp.float32
            )
            d_values = d_values + jnp.einsum(
                "hqr,qhd->rhd",
                expo.astype(jnp.bfloat16),
                dnum_tile_heads,
                preferred_element_type=jnp.float32,
            )
            return ((d_keys, d_values), None)

        tile_items = (
            query_piece.reshape(tiles, tile_rows, D),
            dnum_piece.reshape(tiles, tile_rows, D),
            delta_all.reshape(tiles, tile_rows, H),
            jnp.arange(tiles, dtype=jnp.int32) * tile_rows,
        )
        return lax.scan(tile_step, running, tile_items)[0]

    d_keys, d_values = fold_key_grad(
        (zero_heads, zero_heads),
        (
            lax.all_gather(queries, "shard", axis=0, tiled=True),
            lax.all_gather(d_numer, "shard", axis=0, tiled=True),
        ),
    )
    grad_query = rotate(d_query.reshape(frame_rows, D), cosine_vals, -sine_vals)
    grad_key = rotate(d_keys.reshape(frame_rows, D), cosine_vals, -sine_vals)
    d_projected = jnp.concatenate(
        (grad_query, grad_key, d_values.reshape(frame_rows, D)), axis=1
    ).astype(jnp.bfloat16)
    g_qkv = jnp.dot(hidden_attn.T, d_projected, preferred_element_type=jnp.float32)
    gb_qkv = jnp.sum(d_projected.astype(jnp.float32), axis=0)
    d_hidden_attn = jnp.dot(d_projected, qkv_back.T, preferred_element_type=jnp.float32)
    attn_pull = jax.vjp(modulate, inputs, scale_attn, shift_attn)[1]
    dx_attn, d_scale_attn, d_shift_attn = attn_pull(d_hidden_attn)
    grad_frames = d_after + dx_attn
    d_frame_mod = jnp.concatenate(
        (d_shift_attn, d_scale_attn, d_gate_attn, d_shift_ff, d_scale_ff, d_gate_ff), axis=1
    )
    d_slot = jnp.dot(member.T, d_frame_mod, precision=top_precision)
    g_ada = jnp.dot(activated.astype(jnp.float32).T, d_slot, precision=top_precision)
    gb_ada = jnp.sum(d_slot, axis=0)
    d_activated = jnp.dot(
        d_slot, ada_back.T, precision=top_precision, preferred_element_type=jnp.float32
    )
    silu_pull = jax.vjp(jax.nn.silu, time_rows)[1]
    d_time_rows = silu_pull(d_activated)[0]
    g_table = jnp.dot(step_onehot.T, d_time_rows, precision=top_precision)
    group_sums = (
        lax.psum_scatter(g_ada, "shard", scatter_dimension=0, tiled=True),
        lax.psum_scatter(g_qkv, "shard", scatter_dimension=0, tiled=True),
        lax.psum_scatter(g_out, "shard", scatter_dimension=0, tiled=True),
        lax.psum_scatter(g_up, "shard", scatter_dimension=0, tiled=True),
        lax.psum_scatter(g_down, "shard", scatter_dimension=0, tiled=True),
        lax.psum_scatter(gb_ada, "shard", scatter_dimension=0, tiled=True),
        lax.psum_scatter(gb_qkv, "shard", scatter_dimension=0, tiled=True),
        lax.psum_scatter(gb_out, "shard", scatter_dimension=0, tiled=True),
        lax.psum_scatter(gb_up, "shard", scatter_dimension=0, tiled=True),
        lax.psum_scatter(gb_down, "shard", scatter_dimension=0, tiled=True),
        lax.psum_scatter(g_table, "shard", scatter_dimension=1, tiled=True),
    )
    wide_sums = (
        lax.psum_scatter(group_sums[0], "grp", scatter_dimension=1, tiled=True),
        lax.psum_scatter(group_sums[1], "grp", scatter_dimension=1, tiled=True),
        lax.psum_scatter(group_sums[2], "grp", scatter_dimension=1, tiled=True),
        lax.psum_scatter(group_sums[3], "grp", scatter_dimension=1, tiled=True),
        lax.psum_scatter(group_sums[4], "grp", scatter_dimension=1, tiled=True),
    )
    small_sums = lax.psum(
        (group_sums[5], group_sums[6], group_sums[7], group_sums[8], group_sums[9], group_sums[10]),
        "grp",
    )
    finals = tuple(wide_sums) + tuple(small_sums)
    return (
        output,
        grad_frames,
        finals[10],
        finals[0],
        finals[5],
        finals[1],
        finals[6],
        finals[2],
        finals[7],
        finals[3],
        finals[8],
        finals[4],
        finals[9],
    )


LANES = 128
FREE = pl.CostEstimate(flops=2**20, bytes_accessed=2**16, transcendentals=0)
CHIPS = (2, 4, 6)
ORDER = (0, 2, 4, 6, 1, 3, 5, 7)
SEPARATE = -(2.0**100)
GELU_C = 0.7978845608028654
GELU_A = 0.044715
NT = (((1,), (1,)), ((), ()))
TN = (((0,), (0,)), ((), ()))
f32 = jnp.float32
bf16 = jnp.bfloat16


def dot(left, right, dims=(((1,), (0,)), ((), ()))):
    return lax.dot_general(left, right, dims, preferred_element_type=f32)


def params(limit_mib, steps=1):
    return pltpu.CompilerParams(
        dimension_semantics=("arbitrary",) * steps, vmem_limit_bytes=limit_mib * 2**20
    )


def moments(value):
    centred = value - jnp.mean(value, axis=1, keepdims=True)
    inv = lax.rsqrt(jnp.mean(centred * centred, axis=1, keepdims=True) + eps_norm)
    return centred * inv, inv


def norm_back(weighted, normal, inv):
    return (
        weighted
        - jnp.mean(weighted, axis=1, keepdims=True)
        - normal * jnp.mean(weighted * normal, axis=1, keepdims=True)
    ) * inv


def swap_halves(value):
    lane = lax.broadcasted_iota(jnp.int32, value.shape, 1)
    return jnp.where(lane % HD < HD // 2, pltpu.roll(value, 96, 1), pltpu.roll(value, 32, 1))


def rotary(cos_ref, sin_ref, here):
    cosine, sine = cos_ref[:, here].T, sin_ref[:, here].T
    return jnp.concatenate([cosine] * 4, axis=1), jnp.concatenate([-sine, sine] * 2, axis=1)


def members(seg_ref, block, rows):
    place = block * rows + lax.broadcasted_iota(jnp.int32, (rows, LANES), 0)
    out = []
    for slot in range(3):
        begin = seg_ref[block, slot]
        out.append((place >= begin) & (place < begin + seg_ref[block, 3 + slot]))
    return out


def mod_rows(table_ref, seg_ref, block, member, part):
    first, second, third = [table_ref[pl.ds(seg_ref[block, 6 + slot], 1), pl.ds(part * D, D)] for slot in range(3)]
    out = []
    for at in range(0, D, LANES):
        here = slice(at, at + LANES)
        out.append(jnp.where(member[0], first[:, here], jnp.where(member[1], second[:, here], third[:, here])))
    return jnp.concatenate(out, axis=1)


def slot_sums(member, value):
    out = []
    for column in member:
        sums = [
            jnp.sum(jnp.where(column, value[:, at : at + LANES], 0.0), axis=0, keepdims=True) for at in range(0, D, LANES)
        ]
        out.append(jnp.concatenate(sums, axis=1))
    return out


def qkv_kernel(order_ref, seg_ref, *refs):
    step = pl.program_id(0)
    last = pl.num_programs(0) - 1
    *pieces, table_ref, w_ref, b_ref, cos_ref, sin_ref, q_ref, k_ref, v_ref, h_ref, x_all, arrived = refs
    block = order_ref[step]
    rows = x_all.shape[1]
    copies, at = [], 0
    for piece in pieces:
        here = x_all.at[at : at + piece.shape[0]]
        copies.append((at, pltpu.make_async_copy(piece, here, arrived.at[len(copies)])))
        at += piece.shape[0]

    @pl.when(step == 0)
    def _():
        for _, copy in copies:
            copy.start()

    for at, copy in copies:

        @pl.when(step == at)
        def _(copy=copy):
            copy.wait()

    member = members(seg_ref, block, rows)
    normal, _ = moments(x_all[step].astype(f32))
    shift = mod_rows(table_ref, seg_ref, block, member, 0)
    scale = mod_rows(table_ref, seg_ref, block, member, 1)
    hidden = (normal * (1.0 + scale) + shift).astype(bf16)
    h_ref[...] = hidden
    projected = dot(hidden, w_ref[...]) + b_ref[...]
    cosine, sine = rotary(cos_ref, sin_ref, slice(None))
    turned = []
    for part in range(2):
        piece = projected[:, part * LANES : (part + 1) * LANES]
        turned.append(piece * cosine + swap_halves(piece) * sine)
    queries = turned[0].astype(bf16).astype(f32) * 0.125
    keys = turned[1]
    values = projected[:, 2 * LANES :]
    lane = lax.broadcasted_iota(jnp.int32, (rows, LANES), 1)
    lane_row = lane[:1]
    begins, ends = jnp.full((1, LANES), 2**30, jnp.int32), jnp.zeros((1, LANES), jnp.int32)
    for index in range(6):
        where, slot = (0, index) if index < 3 else (last, index - 3)
        begin = seg_ref[where, slot]
        begins = jnp.where(lane_row == HD + index, begin, begins)
        ends = jnp.where(lane_row == HD + index, begin + seg_ref[where, 3 + slot], ends)
    place = block * rows + lax.broadcasted_iota(jnp.int32, (rows, LANES), 0)
    inside = (place >= begins) & (place < ends)
    query_extra = jnp.where(inside | (lane >= HD + 6), 0.0, SEPARATE)
    key_extra = jnp.where(inside, 1.0, 0.0)
    value_extra = jnp.where((lane >= HD) & (lane < HD + 3), 1.0, 0.0)
    low = lane < HD
    for head in range(2):
        for ref, value, extra in (
            (q_ref, queries, query_extra),
            (k_ref, keys, key_extra),
            (v_ref, values, value_extra),
        ):
            own = value if head == 0 else pltpu.roll(value, HD, 1)
            ref[head] = jnp.where(low, own, extra).astype(bf16)


def attend_kernel(q_ref, k_ref, v_ref, o_ref, mixed_ref, l_ref):
    keys_in_all = k_ref.shape[1]
    tile = 256
    ratios, sums = [], []
    for head in range(2):
        query = q_ref[head]
        total = None
        for at in range(0, keys_in_all, tile):
            expo = jnp.exp(dot(query, k_ref[head, at : at + tile], NT))
            term = dot(expo.astype(bf16), v_ref[head, at : at + tile])
            total = term if total is None else total + term
        norm = total[:, HD : HD + 1]
        ratios.append(total / norm)
        sums.append(norm)
    lane = lax.broadcasted_iota(jnp.int32, ratios[0].shape, 1)
    mixed = jnp.where(lane < HD, ratios[0], pltpu.roll(ratios[1], HD, 1))
    mixed_ref[...] = mixed
    o_ref[...] = mixed.astype(bf16)
    l_ref[...] = jnp.where(lane < HD, sums[0], sums[1])


def block_kernel(
    order_ref, seg_ref, x_ref, cot_ref, o_ref, table_ref, w_ref, b_out_ref, b_up_ref, b_down_ref,
    out_ref, dx1_ref, do_ref, pair_ref, keep_ref, send_ref, slots_ref, gb_out_ref, gb_up_ref, gb_down_ref,
):
    rows = x_ref.shape[0]
    groups, shards = w_ref.shape[:2]
    block = order_ref[0]
    member = members(seg_ref, block, rows)
    modulation = partial(mod_rows, table_ref, seg_ref, block, member)
    wide = D // groups

    def weight(group, start):
        return w_ref[group, :, start : start + LANES, :].reshape(D, wide)

    def weight_down(group):
        return w_ref[group, :, 0 : 2 * LANES, :].reshape(2 * D, wide)

    def by_core(value, width, other):
        parts = [value[:, at : at + width] for at in range(0, value.shape[1], width)]
        even, odd = jnp.concatenate(parts[0::2], axis=1), jnp.concatenate(parts[1::2], axis=1)
        return jnp.where((block % 2 == 0) != other, even, odd)

    def share(start, value, width):
        half = value.shape[1] // 2
        keep_ref[:, start : start + half] = by_core(value, width, False)
        send_ref[:, start : start + half] = by_core(value, width, True)

    mixed = jnp.concatenate([o_ref[shard] for shard in range(shards)], axis=1)
    share(D, mixed, LANES)
    attn = jnp.concatenate([dot(mixed, weight(group, 256)) for group in range(groups)], axis=1)
    attn = attn + b_out_ref[...]
    gate1 = modulation(2)
    after = x_ref[...].astype(f32) + gate1 * attn
    normal, inv = moments(after)
    scale2 = 1.0 + modulation(4)
    hidden = (normal * scale2 + modulation(3)).astype(bf16)
    share(D + D // 2, hidden, LANES)
    up = [dot(hidden, weight(group, start)) for group in range(groups) for start in (384, 512)]
    up = jnp.concatenate(up, axis=1) + b_up_ref[...]
    inner = jnp.tanh(GELU_C * (up + GELU_A * (up * up * up)))
    act = (0.5 * up * (1.0 + inner)).astype(bf16)
    share(0, act, 2 * LANES)
    slope = 0.5 * (1.0 + inner) + (0.5 * GELU_C) * up * (1.0 - inner * inner) * (
        1.0 + (3.0 * GELU_A) * up * up
    )
    branch = jnp.concatenate([dot(act, weight_down(group)) for group in range(groups)], axis=1)
    branch = branch + b_down_ref[...]
    gate2 = modulation(5)
    out_ref[...] = (after + gate2 * branch).astype(bf16)

    cot = cot_ref[...].astype(f32)
    dff = (gate2 * cot).astype(bf16)
    pair_ref[:, 0:D] = dff
    gb_down_ref[...] = jnp.sum(dff.astype(f32), axis=0, keepdims=True)
    d_gate2 = slot_sums(member, cot * branch)
    d_act = sum(dot(dff[:, g * wide : (g + 1) * wide], weight_down(g), NT) for g in range(groups))
    du = (d_act * slope).astype(bf16)
    pair_ref[:, 2 * D :] = du
    gb_up_ref[...] = jnp.sum(du.astype(f32), axis=0, keepdims=True)
    d_hidden = None
    for index in range(2 * groups):
        piece = du[:, index * wide : (index + 1) * wide]
        term = dot(piece, weight(index // 2, 384 + LANES * (index % 2)), NT)
        d_hidden = term if d_hidden is None else d_hidden + term
    d_shift2 = slot_sums(member, d_hidden)
    d_scale2 = slot_sums(member, d_hidden * normal)
    d_after = cot + norm_back(d_hidden * scale2, normal, inv)
    dx1_ref[...] = d_after
    d_gate1 = slot_sums(member, d_after * attn)
    da = (gate1 * d_after).astype(bf16)
    pair_ref[:, D : 2 * D] = da
    gb_out_ref[...] = jnp.sum(da.astype(f32), axis=0, keepdims=True)
    d_mixed = sum(dot(da[:, g * wide : (g + 1) * wide], weight(g, 256), NT) for g in range(groups))
    d_mixed = d_mixed.astype(bf16)
    for shard in range(shards):
        do_ref[shard] = d_mixed[:, shard * LANES : (shard + 1) * LANES]
    slots_ref[...] = jnp.concatenate(d_gate1 + d_shift2 + d_scale2 + d_gate2, axis=0)


def weight_grad_kernel(
    order_ref, group_ref, keep_ref, send_ref, pair_ref, pair2_ref, first_x, first_y, own_x, own_y
):
    groups, half, wide = first_x.shape[1:]

    def product(at, width, start, stop):
        here = pl.ds(pl.multiple_of(at, LANES), width)
        return (
            dot(keep_ref[:, here], pair_ref[:, start:stop], TN) + dot(send_ref[:, here], pair2_ref[:, start:stop], TN)
        ).astype(bf16)

    places = (((own_x, 0), (own_y, 0)), ((first_x, 0), (own_y, 1)), ((own_x, 1), (first_y, 0)), ((first_x, 1), (first_y, 1)))
    for index in range(4):
        chip = order_ref[index] // 2
        down = product(chip * 2 * LANES, 2 * LANES, 0, D)
        out = product(D + chip * LANES, LANES, D, 2 * D)
        up = product(D + D // 2 + chip * LANES, LANES, 2 * D, 4 * D)
        (by_x, at_x), (by_y, at_y) = places[index]
        for group in range(groups):
            to = (group + groups - group_ref[0]) % groups
            columns = slice(group * wide, (group + 1) * wide)
            by_x[at_x, to, 0:256, :] = down[:, columns]
            by_x[at_x, to, 256:half, :] = out[: half - 256, columns]
            by_y[at_y, to, 0 : 384 - half, :] = out[half - 256 :, columns]
            for part in range(2):
                start = 384 - half + 128 * part
                at = (2 * group + part) * wide
                by_y[at_y, to, start : start + 128, :] = up[:, at : at + wide]


def attend_back_kernel(head, q_ref, k_ref, v_ref, do_ref, mixed_ref, l_ref, cos_ref, sin_ref, *refs):
    *refs, dn, dq_t, dk_all = refs
    if head == 0:
        qk_ref, dv_ref = refs
    else:
        qk_first, dv_first, second_ref, own_ref, gb_ref = refs
        qk_ref = second_ref.at[:, :LANES]
    step = pl.program_id(0)
    rows = k_ref.shape[1]
    frames = q_ref.shape[1]
    tile = 256
    lane = lax.broadcasted_iota(jnp.int32, (rows, LANES), 1)
    low = lane < HD

    @pl.when(step == 0)
    def _():
        dq_t[...] = jnp.zeros_like(dq_t)
        for at in range(0, frames, rows):
            here = slice(at, at + rows)
            d_out = do_ref[here].astype(f32)
            norm = l_ref[here]
            d_num = (d_out / norm).astype(bf16).astype(f32)
            mine = low if head == 0 else ~low
            total = jnp.sum(jnp.where(mine, d_out * mixed_ref[here], 0.0), axis=1, keepdims=True)
            delta = -total / norm[:, head * HD : head * HD + 1]
            first = delta.astype(bf16).astype(f32)
            second = (delta - first).astype(bf16).astype(f32)
            third = delta - first - second
            extra = jnp.where(lane == HD, first, jnp.where(lane == HD + 1, second, third))
            extra = jnp.where(lane < HD + 3, extra, 0.0)
            own = d_num if head == 0 else pltpu.roll(d_num, HD, 1)
            dn[here] = jnp.where(low, own, extra).astype(bf16)

    key, value = k_ref[0], v_ref[0]
    key_t = key.T
    dk_total, dv_total = None, None
    for at in range(0, frames, tile):
        here = slice(at, at + tile)
        query, d_num = q_ref[0, here], dn[here]
        expo = jnp.exp(dot(key, query, NT))
        d_score = (expo * dot(value, d_num, NT)).astype(bf16)
        dk_term = dot(d_score, query)
        dv_term = dot(expo.astype(bf16), d_num)
        dk_total = dk_term if dk_total is None else dk_total + dk_term
        dv_total = dv_term if dv_total is None else dv_total + dv_term
        dq_t[:, here] += dot(key_t, d_score)

    here = pl.ds(pl.multiple_of(step * rows, rows), rows)
    dk_all[here] = dk_total
    if head == 0:
        dv_ref[here] = dv_total.astype(bf16)
    else:
        both = jnp.where(low, dv_first[here].astype(f32), pltpu.roll(dv_total, HD, 1)).astype(bf16)
        own_ref[here, 2 * LANES :] = both
        second_ref[here, LANES:] = both

    @pl.when(step == pl.num_programs(0) - 1)
    def _():
        for at in range(0, frames, rows):
            part = slice(at, at + rows)
            cosine, sine = rotary(cos_ref, sin_ref, part)
            both = jnp.where(low, 0.125 * dq_t[:, part].T, pltpu.roll(dk_all[part], HD, 1))
            both = (both * cosine - swap_halves(both) * sine).astype(bf16)
            qk_ref[part] = both
            if head == 1:
                first, second = qk_first[part].astype(f32), both.astype(f32)
                own_ref[part, 0:LANES] = jnp.where(low, first, pltpu.roll(second, HD, 1)).astype(bf16)
                own_ref[part, LANES : 2 * LANES] = jnp.where(low, pltpu.roll(first, HD, 1), second).astype(bf16)
        if head == 1:
            ones = jnp.ones((8, frames), bf16)
            sums = dot(ones, own_ref[...])[0:1]
            for index in range(3):
                gb_ref[index : index + 1] = sums[:, index * LANES : (index + 1) * LANES]


def input_grad_kernel(
    base_ref, seg_ref, first_ref, second_ref, w_ref, x_ref, dx1_ref, table_ref, grad_ref, slots_ref, w_all, arrived
):
    shards, rows = first_ref.shape[:2]
    copies = [pltpu.make_async_copy(w_ref.at[shard], w_all.at[shard], arrived.at[shard]) for shard in range(shards)]
    for copy in copies:
        copy.start()
    block = base_ref[0]
    member = members(seg_ref, block, rows)
    scale = 1.0 + mod_rows(table_ref, seg_ref, block, member, 1)
    normal, inv = moments(x_ref[...].astype(f32))
    low = lax.broadcasted_iota(jnp.int32, (rows, LANES), 1) < HD
    d_hidden = None
    for shard in range(shards):
        first, second = first_ref[shard].astype(f32), second_ref[shard, :, :LANES].astype(f32)
        queries = jnp.where(low, first, pltpu.roll(second, HD, 1)).astype(bf16)
        keys = jnp.where(low, pltpu.roll(first, HD, 1), second).astype(bf16)
        whole_row = jnp.concatenate([queries, keys, second_ref[shard, :, LANES:]], axis=1)
        copies[shard].wait()
        term = dot(whole_row, w_all[shard], NT)
        d_hidden = term if d_hidden is None else d_hidden + term
    grad_ref[...] = dx1_ref[...] + norm_back(d_hidden * scale, normal, inv)
    sums = slot_sums(member, d_hidden) + slot_sums(member, d_hidden * normal)
    slots_ref[...] = jnp.concatenate(sums + [jnp.zeros((2, D), f32)], axis=0)


def add_kernel(own_x, came_x, own_y, came_y, by_y, by_x):
    by_y[...] = (own_x[0].astype(f32) + came_x[0].astype(f32)).astype(bf16)
    by_x[...] = (own_y[0].astype(f32) + came_y[0].astype(f32)).astype(bf16)


def total_kernel(own_x, came_x, by_y, own_y, came_y, by_x, *out_refs):
    half = by_y.shape[1]
    for group, ref in enumerate(out_refs):
        first = own_x[0, group].astype(f32) + came_x[0, group].astype(f32) + by_y[group].astype(f32)
        second = own_y[0, group].astype(f32) + came_y[0, group].astype(f32) + by_x[group].astype(f32)
        ref[:half] = first.astype(bf16)
        ref[half:] = second.astype(bf16)


def last_sum_kernel(*refs):
    *pieces, down_ref, out_ref, up_ref = refs
    total = sum(piece[...].astype(f32) for piece in pieces)
    wide = total.shape[1]
    down_ref[...] = total[: 2 * LANES]
    out_ref[...] = total[2 * LANES : 3 * LANES]
    up_ref[:, :wide] = total[3 * LANES : 4 * LANES]
    up_ref[:, wide:] = total[4 * LANES :]


def qkv_grad_kernel(part_ref, h_ref, d_ref, out_ref):
    groups, shards, depth = out_ref.shape[:3]
    for shard in range(shards):
        product = dot(h_ref[:, shard * depth : (shard + 1) * depth], d_ref[...], TN).astype(bf16)
        units = [product[:, at : at + LANES] for at in range(0, 3 * LANES, LANES)]
        for group in range(groups):
            part = part_ref[group]
            out_ref[group, shard] = jnp.where(part == 0, units[0], jnp.where(part == 1, units[1], units[2]))


def qkv_sum_kernel(first_ref, came_ref, out_ref):
    groups, shards = came_ref.shape[:2]
    for unit in range(out_ref.shape[1] // LANES):
        at = lax.rem(first_ref[0] + unit, shards)
        out_ref[:, unit * LANES : (unit + 1) * LANES] = sum(came_ref[group, at].astype(f32) for group in range(groups))


def collect_kernel(shard_ref, seg_ref, tail_ref, out_ref, rows_ref, others_ref):
    shards = tail_ref.shape[0]
    groups = out_ref.shape[0]
    wide = out_ref.shape[2] - 2 * LANES
    shard = shard_ref[0]
    rows_ref[0:3] = tail_ref[0, 0:3]
    rows_ref[3:6] = tail_ref[shards - 1, 0:3]
    middle = sum(tail_ref[index, 0:3] for index in range(1, shards - 1))
    rows_ref[6:7] = jnp.sum(middle, axis=0, keepdims=True)
    rows_ref[7:8] = jnp.zeros((1, rows_ref.shape[1]), f32)
    others_ref[...] = sum(tail_ref[index, 3:4, 3 * LANES : 3 * LANES + 4 * D] for index in range(shards))

    def own(start, size):
        return pl.ds(pl.multiple_of(start + shard * size, LANES), size)

    sums = [jnp.sum(rows_ref[:, own(0, 6 * D // shards)], axis=0, keepdims=True)]
    for index in range(3 * D // shards // LANES):
        chunk = shard * (3 * D // shards // LANES) + index
        part = pl.ds(pl.multiple_of(chunk // shards * LANES, LANES), LANES)
        sums.append(tail_ref[lax.rem(chunk, shards), 3:4, part])
    sums += [others_ref[:, own(0, D // shards)], others_ref[:, own(D, 2 * D // shards)]]
    lane = lax.broadcasted_iota(jnp.int32, (1, LANES), 1)
    ids = jnp.zeros((1, LANES), jnp.int32)
    for index in range(6):
        where, slot = (0, index) if index < 3 else (shards - 1, index - 3)
        ids = jnp.where(lane == index, seg_ref[where, 6 + slot], ids)
    ids = jnp.where(lane == 6, seg_ref[1, 6] + seg_ref[1, 7] + seg_ref[1, 8], ids)
    rows_ref[7:8, 0:wide] = jnp.concatenate(sums, axis=1)
    for group in range(groups):
        out_ref[group, 0:7, 0:wide] = rows_ref[0:7, group * wide : (group + 1) * wide]
        out_ref[group, 7:8, 0:wide] = rows_ref[7:8, 0:wide]
        out_ref[group, :, wide:] = jnp.zeros((8, 2 * LANES), f32)
        out_ref[group, 0:1, wide : wide + LANES] = others_ref[:, own(3 * D, D // shards)]
        out_ref[group, 0:1, wide + LANES :] = ids.astype(f32)


def three(value):
    first = value.astype(bf16)
    second = (value - first.astype(f32)).astype(bf16)
    return [first, second, (value - first.astype(f32) - second.astype(f32)).astype(bf16)]


def table_kernel(*refs):
    all_parts, act_ref, w_ref, time_ref, ada_ref, time_grad_ref, b_ada, b_qkv, b_out, b_up, b_down = refs
    steps, wide = time_ref.shape[0], w_ref.shape[1]
    parts = [all_parts.at[index] for index in range(all_parts.shape[0])]
    step = lax.broadcasted_iota(jnp.int32, (steps, 1), 0)
    total = jnp.zeros((steps, wide), f32)
    for part in parts:
        for row in range(7):
            at = wide + LANES + row
            picked = part[0:1, at : at + 1].astype(jnp.int32) == step
            total = total + jnp.where(picked, part[row : row + 1, :wide], 0.0)
    pieces = three(total)
    act = act_ref[...]
    ada_ref[...] = dot(jnp.concatenate([act] * 3, axis=0), jnp.concatenate(pieces, axis=0), TN)
    d_act = dot(jnp.concatenate(pieces, axis=0), w_ref[...], NT)
    d_act = d_act[:steps] + d_act[steps : 2 * steps] + d_act[2 * steps :]
    value = time_ref[...]
    gate = 1.0 / (1.0 + jnp.exp(-value))
    time_grad_ref[...] = d_act * gate * (1.0 + value * (1.0 - gate))
    first_row = sum(part[7:8, :wide] for part in parts)
    at = 0
    for ref in (b_ada, b_qkv, b_out, b_up):
        ref[...] = first_row[:, at : at + ref.shape[1]]
        at += ref.shape[1]
    b_down[...] = sum(part[0:1, wide : wide + b_down.shape[1]] for part in parts)


def spread(value, axis, size):
    return [value] + [
        lax.ppermute(value, axis, [(i, (i - step) % size) for i in range(size)]) for step in range(1, size)
    ]


def trade(pieces, axis, size):
    return [pieces[0]] + [
        lax.ppermute(pieces[size - step], axis, [(i, (i - step) % size) for i in range(size)])
        for step in range(1, size)
    ]


def in_order(pieces, axis, size):
    own = lax.axis_index(axis)
    out = []
    for place in range(size):
        pick = (place - own) % size
        value = pieces[0]
        for index in range(1, size):
            value = jnp.where(pick == index, pieces[index], value)
        out.append(value)
    return out


def hop(value, step):
    return lax.ppermute(value, "shard", [(i, i ^ step) for i in range(8)])


def after(value, *others):
    anywhere = pl.BlockSpec(memory_space=pl.ANY)
    return pl.pallas_call(
        lambda *refs: None,
        in_specs=[anywhere] * (1 + len(others)),
        out_specs=anywhere,
        out_shape=jax.ShapeDtypeStruct(value.shape, value.dtype),
        input_output_aliases={0: 0},
        cost_estimate=FREE,
        name="after",
    )(value, *others)


def shape(*dims, kind=bf16):
    return jax.ShapeDtypeStruct(dims, kind)


def whole(*dims):
    return pl.BlockSpec(dims, lambda *_: (0,) * len(dims))


smem = pl.BlockSpec(memory_space=pltpu.SMEM)


def local_heads(
    groups, shards, frames, cotangent, seg_start, seg_length, seg_step, time_table,
    w_ada, b_ada, w_qkv, b_qkv, w_out, b_out, w_up, b_up, w_down, b_down,
):
    rows = frames.shape[0]
    packed = rows * shards
    steps = time_table.shape[0]
    shard = lax.axis_index("shard")
    depth = D // shards
    wide = D // groups

    group = lax.axis_index("grp")
    order = shard ^ jnp.array(ORDER, jnp.int32)

    inverse = 10000.0 ** (-jnp.arange(HD // 2, dtype=f32) / (HD // 2))
    phase = inverse[:, None] * jnp.arange(packed, dtype=f32)[None, :]
    cosine, sine = jnp.cos(phase), jnp.sin(phase)

    activated = jax.nn.silu(time_table).astype(bf16)
    act_own = lax.dynamic_slice_in_dim(activated, shard * depth, depth, 1)
    partial_mod = dot(act_own, w_ada)
    mod_wide = partial_mod.shape[1]
    biases = [b.astype(f32) for b in (b_ada, b_qkv, b_out, b_up, b_down)]
    sizes = [b.shape[0] for b in biases]
    segs = jnp.concatenate((seg_start, seg_length, seg_step), axis=1).astype(f32)
    extra = jnp.concatenate(biases + [jnp.floor(segs[0] / 128.0), segs[0] % 128.0])
    extra_rows = -(-extra.shape[0] // mod_wide)
    extra = jnp.pad(extra, (0, extra_rows * mod_wide - extra.shape[0])).reshape(extra_rows, mod_wide)
    units = 3 * shards // groups
    first = group * units
    by_unit = w_qkv.reshape(depth, units, LANES).transpose(1, 0, 2)
    which = jnp.minimum((jnp.arange(shards) - first) % shards, units - 1)
    by_shard = jnp.take(by_unit, which, axis=0, mode="clip")
    w_cols = jnp.broadcast_to(by_shard[None], (groups, shards, depth, LANES)).reshape(groups * shards, depth, LANES)
    w_cols = lax.all_to_all(w_cols, ("grp", "shard"), split_axis=0, concat_axis=0, tiled=True).reshape(groups, D, LANES)
    small = jnp.concatenate((partial_mod, extra), axis=0).astype(bf16)
    small = lax.all_gather(small, "shard", axis=0).astype(f32)
    held = after(frames, small)
    chips = [held] + [hop(held, step) for step in CHIPS]

    mod_own = jnp.sum(small[:, :steps], axis=0).astype(bf16)
    high = lax.all_gather(after(mod_own, w_cols), "grp", axis=1, tiled=True)

    w_heads = jnp.concatenate(
        [lax.dynamic_index_in_dim(w_cols, (part * shards + shard) // units, 0, keepdims=False) for part in range(3)], axis=1
    )

    chips = [chips[0]] + [after(piece, high) for piece in chips[1:]]
    others = hop(jnp.stack(chips), 1)

    pack = jnp.concatenate((w_down, w_out, w_up[:, :wide], w_up[:, wide:]), axis=0)
    weights = lax.all_gather(pack, ("grp", "shard"), axis=0).reshape(groups, shards, 5 * LANES, wide)

    extra = small[:, steps:].reshape(shards, extra_rows * mod_wide)
    full, at = [], 0
    for size in sizes:
        full.append(extra[:, at : at + size].reshape(1, shards * size))
        at += size
    ada_bias, qkv_bias, out_bias, up_bias, down_bias = full
    seg_all = (extra[:, at : at + 9] * 128.0 + extra[:, at + 9 : at + 18]).astype(jnp.int32)
    qkv_bias = lax.dynamic_index_in_dim(qkv_bias.reshape(3, shards, LANES), shard, 1, keepdims=False)
    qkv_bias = qkv_bias.reshape(1, 3 * LANES)
    table = high.astype(f32) + ada_bias

    ordered = lambda width: pl.BlockSpec((rows, width), lambda i, order: (order[i], 0))
    ordered_heads = pl.BlockSpec((2, rows, LANES), lambda i, order: (0, order[i], 0))
    by_block = lambda width: pl.BlockSpec((rows, width), lambda i: (i, 0))
    two_heads = pl.BlockSpec((2, rows, LANES), lambda i: (0, i, 0))
    frame_pieces = [piece[None] for piece in chips] + [others]
    q, k, v, h1_all = pl.pallas_call(
        qkv_kernel,
        grid_spec=pltpu.PrefetchScalarGridSpec(
            num_scalar_prefetch=1,
            grid=(shards,),
            in_specs=[smem]
            + [pl.BlockSpec(memory_space=pl.ANY)] * len(frame_pieces)
            + [whole(steps, 2 * D), whole(D, 3 * LANES), whole(1, 3 * LANES)] + [pl.BlockSpec((HD // 2, rows), lambda i, order: (0, order[i]))] * 2,
            out_specs=[ordered_heads] * 3 + [ordered(D)],
            scratch_shapes=[pltpu.VMEM((shards, rows, D), bf16), pltpu.SemaphoreType.DMA((len(frame_pieces),))],
        ),
        out_shape=[shape(2, packed, LANES)] * 3 + [shape(packed, D)],
        compiler_params=params(60),
        cost_estimate=FREE,
        name="qkv",
    )(order, seg_all, *frame_pieces, table[:, : 2 * D], w_heads, qkv_bias, cosine, sine)

    attn_flops = 2 * 2 * packed * packed * 256
    some_rows = packed // 2
    some = pl.BlockSpec((some_rows, LANES), lambda i: (i, 0))
    o_heads, mixed, norm = pl.pallas_call(
        attend_kernel,
        grid=(packed // some_rows,),
        in_specs=[pl.BlockSpec((2, some_rows, LANES), lambda i: (0, i, 0))] + [whole(2, packed, LANES)] * 2,
        out_specs=[some] * 3,
        out_shape=[shape(packed, LANES), shape(packed, LANES, kind=f32), shape(packed, LANES, kind=f32)],
        compiler_params=params(60),
        cost_estimate=FREE,
        name="attend",
    )(q, k, v)

    o = lax.all_to_all(o_heads.reshape(shards, rows, LANES), "shard", split_axis=0, concat_axis=0, tiled=True)
    base = shard.astype(jnp.int32).reshape(1)
    block_flops = 2 * rows * D * D * 10
    out, dx1, d_mixed, pair, keep, send, slots_ff, gb_out, gb_up, gb_down = pl.pallas_call(
        block_kernel,
        grid=(1,),
        in_specs=[
            smem, smem, whole(rows, D), whole(rows, D), whole(shards, rows, LANES), whole(steps, 6 * D),
            whole(groups, shards, 5 * LANES, wide), whole(1, D), whole(1, 2 * D), whole(1, D),
        ],
        out_specs=[
            whole(rows, D), whole(rows, D), whole(shards, rows, LANES), whole(rows, 4 * D), whole(rows, 2 * D),
            whole(rows, 2 * D), whole(12, D), whole(1, D), whole(1, 2 * D), whole(1, D),
        ],
        out_shape=[
            shape(rows, D), shape(rows, D, kind=f32), shape(shards, rows, LANES), shape(rows, 4 * D), shape(rows, 2 * D),
            shape(rows, 2 * D), shape(12, D, kind=f32),
            shape(1, D, kind=f32), shape(1, 2 * D, kind=f32), shape(1, D, kind=f32),
        ],
        compiler_params=params(60),
        cost_estimate=FREE,
        name="block",
    )(order, seg_all, frames, cotangent, o, table, weights, out_bias, up_bias, down_bias)

    d_heads = lax.all_to_all(d_mixed, "shard", split_axis=0, concat_axis=0, tiled=True).reshape(packed, LANES)

    send, pair_send = hop(send, 1), hop(pair, 1)
    half = (2, groups, 5 * LANES // 2, wide)
    first_x, first_y, own_x, own_y = pl.pallas_call(
        weight_grad_kernel,
        grid=(1,),
        in_specs=[smem, smem, whole(rows, 2 * D), whole(rows, 2 * D), whole(rows, 4 * D), whole(rows, 4 * D)],
        out_specs=[whole(*half)] * 4,
        out_shape=[shape(*half)] * 4,
        compiler_params=params(60),
        cost_estimate=FREE,
        name="weight_grads",
    )(order, group.astype(jnp.int32).reshape(1), keep, send, pair, pair_send)
    first_x, first_y = after(first_x, d_heads), after(first_y, d_heads)
    d_heads = after(d_heads, first_x, first_y)

    back_specs = lambda head: [
        pl.BlockSpec((1, packed, LANES), lambda i: (head, 0, 0)),
        pl.BlockSpec((1, packed, LANES), lambda i: (head, i, 0)),
        pl.BlockSpec((1, packed, LANES), lambda i: (head, i, 0)),
    ] + [whole(packed, LANES)] * 3 + [whole(HD // 2, packed)] * 2
    back_scratch = [pltpu.VMEM((packed, LANES), bf16), pltpu.VMEM((LANES, packed), f32), pltpu.VMEM((packed, LANES), f32)]
    arguments = (q, k, v, d_heads, mixed, norm, cosine, sine)
    came_x, came_y = hop(first_x, 2), hop(first_y, 4)
    qk_first, dv_first = pl.pallas_call(
        partial(attend_back_kernel, 0),
        grid=(1,),
        in_specs=back_specs(0),
        out_specs=[whole(packed, LANES), whole(packed, LANES)],
        out_shape=[shape(packed, LANES)] * 2,
        scratch_shapes=back_scratch,
        compiler_params=params(60),
        cost_estimate=FREE,
        name="attend_back_first",
    )(*arguments)
    d_first = lax.all_to_all(qk_first.reshape(shards, rows, LANES), "shard", split_axis=0, concat_axis=0, tiled=True)
    second, d_own, gb_qkv = pl.pallas_call(
        partial(attend_back_kernel, 1),
        grid=(1,),
        in_specs=back_specs(1) + [whole(packed, LANES)] * 2,
        out_specs=[whole(packed, 2 * LANES), whole(packed, 3 * LANES), whole(3, LANES)],
        out_shape=[shape(packed, 2 * LANES), shape(packed, 3 * LANES), shape(3, LANES, kind=f32)],
        scratch_shapes=back_scratch,
        compiler_params=params(60),
        cost_estimate=FREE,
        name="attend_back_second",
    )(*arguments, qk_first, dv_first)
    second = after(second, came_x, came_y)
    piece = (1, *half[2:])
    farther = pl.BlockSpec((1, *piece), lambda i: (1, i, 0, 0))
    next_y, next_x = pl.pallas_call(
        add_kernel,
        grid=(groups,),
        in_specs=[farther] * 4,
        out_specs=[pl.BlockSpec(piece, lambda i: (i, 0, 0))] * 2,
        out_shape=[shape(*half[1:])] * 2,
        compiler_params=params(60),
        cost_estimate=FREE,
        name="add",
    )(own_x, came_x, own_y, came_y)
    part = jnp.stack([jnp.clip((units * to + units - 1 - shard) // shards, 0, 2) for to in range(groups)])
    g_send = pl.pallas_call(
        qkv_grad_kernel,
        grid=(1,),
        in_specs=[smem, whole(packed, D), whole(packed, 3 * LANES)],
        out_specs=whole(groups, shards, depth, LANES),
        out_shape=shape(groups, shards, depth, LANES),
        compiler_params=params(60),
        cost_estimate=pl.CostEstimate(flops=2 * packed * D * 3 * LANES, bytes_accessed=2**24, transcendentals=0),
        name="qkv_grad",
    )(part.astype(jnp.int32), h1_all, after(d_own, next_y, next_x, d_first)).reshape(groups * shards, depth, LANES)

    d_second = lax.all_to_all(second.reshape(shards, rows, 2 * LANES), "shard", split_axis=0, concat_axis=0, tiled=True)
    next_y, next_x = hop(next_y, 4), hop(next_x, 2)
    nearer = whole(1, *half[1:])
    totals = pl.pallas_call(
        total_kernel,
        grid=(1,),
        in_specs=[nearer, nearer, whole(*half[1:])] * 2,
        out_specs=[whole(5 * LANES, wide)] * groups,
        out_shape=[shape(5 * LANES, wide)] * groups,
        compiler_params=params(60),
        cost_estimate=FREE,
        name="total",
    )(own_x, came_x, next_y, own_y, came_y, next_x)
    d_second = after(d_second, g_send, totals[0])
    w_all = lax.all_gather(after(w_heads, q), "shard", axis=0)
    by_shard = lambda *dims: pl.BlockSpec((1, *dims), lambda i: (i, 0, 0))
    grad_frames, slots_qkv = pl.pallas_call(
        input_grad_kernel,
        grid=(1,),
        in_specs=[
            smem, smem, whole(shards, rows, LANES), whole(shards, rows, 2 * LANES), pl.BlockSpec(memory_space=pl.ANY),
            whole(rows, D), whole(rows, D), whole(steps, 2 * D),
        ],
        out_specs=[whole(rows, D), whole(8, D)],
        out_shape=[shape(rows, D, kind=f32), shape(8, D, kind=f32)],
        scratch_shapes=[pltpu.VMEM((shards, D, 3 * LANES), bf16), pltpu.SemaphoreType.DMA((shards,))],
        compiler_params=params(60),
        cost_estimate=FREE,
        name="input_grad",
    )(base, seg_all, d_first, d_second, w_all, frames, dx1, table[:, : 2 * D])

    g_came = lax.all_to_all(after(g_send, slots_qkv), ("grp", "shard"), split_axis=0, concat_axis=0, tiled=True)
    g_qkv = pl.pallas_call(
        qkv_sum_kernel,
        grid=(1,),
        in_specs=[smem, whole(groups, shards, depth, LANES)],
        out_specs=whole(depth, units * LANES),
        out_shape=shape(depth, units * LANES, kind=f32),
        compiler_params=params(60),
        cost_estimate=FREE,
        name="qkv_sum",
    )(first.astype(jnp.int32).reshape(1), g_came.reshape(groups, shards, depth, LANES))

    d_slot = jnp.concatenate((slots_qkv[:6], slots_ff), axis=0).reshape(6, 3, D).transpose(1, 0, 2).reshape(3, 6 * D)
    row_sums = jnp.concatenate((gb_qkv.reshape(-1), gb_out[0], gb_up[0], gb_down[0]))
    sum_rows = -(-row_sums.shape[0] // (6 * D))
    row_sums = jnp.pad(row_sums, (0, sum_rows * 6 * D - row_sums.shape[0])).reshape(sum_rows, 6 * D)
    tail = lax.all_gather(jnp.concatenate((d_slot, row_sums), axis=0), "shard", axis=0)
    totals = trade(totals, "grp", groups)
    tail = after(tail, *totals)
    parts = pl.pallas_call(
        collect_kernel,
        grid=(1,),
        in_specs=[smem, smem, whole(shards, 4, 6 * D)],
        out_specs=whole(groups, 8, mod_wide + 2 * LANES),
        out_shape=shape(groups, 8, mod_wide + 2 * LANES, kind=f32),
        scratch_shapes=[pltpu.VMEM((8, 6 * D), f32), pltpu.VMEM((1, 4 * D), f32)],
        compiler_params=params(60),
        cost_estimate=FREE,
        name="collect",
    )(base, seg_all, tail)
    g_down, g_out, g_up = pl.pallas_call(
        last_sum_kernel,
        grid=(1,),
        in_specs=[whole(5 * LANES, wide)] * groups,
        out_specs=[whole(2 * LANES, wide), whole(LANES, wide), whole(LANES, 2 * wide)],
        out_shape=[shape(2 * LANES, wide, kind=f32), shape(LANES, wide, kind=f32), shape(LANES, 2 * wide, kind=f32)],
        compiler_params=params(60),
        cost_estimate=FREE,
        name="last_sum",
    )(*totals)
    parts = lax.all_to_all(parts, "grp", split_axis=0, concat_axis=0, tiled=True)
    table_own = lax.dynamic_slice_in_dim(time_table, shard * depth, depth, 1)
    g_ada, g_table, *sums = pl.pallas_call(
        table_kernel,
        grid=(1,),
        in_specs=[whole(groups, 8, mod_wide + 2 * LANES), whole(steps, depth), whole(depth, mod_wide), whole(steps, depth)],
        out_specs=[whole(depth, mod_wide), whole(steps, depth)] + [whole(1, size) for size in sizes],
        out_shape=[shape(depth, mod_wide, kind=f32), shape(steps, depth, kind=f32)]
        + [shape(1, size, kind=f32) for size in sizes],
        compiler_params=params(60),
        cost_estimate=FREE,
        name="table",
    )(parts, act_own, w_ada, table_own)
    gb_ada, gb_qkv, gb_out, gb_up, gb_down = [total.reshape(-1) for total in sums]
    g_table = sum(spread(g_table, "grp", groups))
    return (
        out, grad_frames, g_table, g_ada, gb_ada, g_qkv, gb_qkv, g_out, gb_out, g_up, gb_up, g_down, gb_down,
    )


def solution(mesh):
    in_specs = (
        P(("grp", "shard"), None),
        P(("grp", "shard"), None),
        P(("grp", "shard"), None),
        P(("grp", "shard"), None),
        P(("grp", "shard"), None),
        P(),
        P("shard", "grp"),
        P("shard"),
        P("shard", "grp"),
        P("shard"),
        P("shard", "grp"),
        P("shard"),
        P("shard", "grp"),
        P("shard"),
        P("shard", "grp"),
        P("shard"),
    )
    out_specs = (
        P(("grp", "shard"), None),
        P(("grp", "shard"), None),
        P(None, "shard"),
        P("shard", "grp"),
        P("shard"),
        P("shard", "grp"),
        P("shard"),
        P("shard", "grp"),
        P("shard"),
        P("shard", "grp"),
        P("shard"),
        P("shard", "grp"),
        P("shard"),
    )
    by_heads = mesh.shape["shard"] * 2 * HD == D and mesh.shape["grp"] == 4
    local = partial(local_heads, mesh.shape["grp"], mesh.shape["shard"]) if by_heads else local_any
    return jax.shard_map(local, mesh=mesh, in_specs=in_specs, out_specs=out_specs, check_vma=False)
```

```python
from functools import partial

import jax
import jax.numpy as jnp
from jax import lax
from jax.experimental import pallas as pl
from jax.experimental.pallas import tpu as pltpu
from jax.sharding import PartitionSpec as P

D = 1024
H = 16
HD = 64


eps_norm = 1e-06
top_precision = lax.Precision.HIGHEST


def normalize(tensor):
    centred = tensor - jnp.mean(tensor, axis=-1, keepdims=True)
    return centred * lax.rsqrt(jnp.mean(centred * centred, axis=-1, keepdims=True) + eps_norm)


def modulate(tensor, scale_vec, shift_vec):
    return normalize(tensor) * (1.0 + scale_vec) + shift_vec


def angles(positions):
    half_width = HD // 2
    inverse = 10000.0 ** (-jnp.arange(half_width, dtype=jnp.float32) / half_width)
    phase_grid = positions[:, None] * inverse[None, :]
    return (jnp.cos(phase_grid), jnp.sin(phase_grid))


def rotate(tensor, cosine_vals, sine_vals):
    row_total = tensor.shape[0]
    halves = tensor.reshape(row_total, H, 2, HD // 2)
    former = halves[:, :, 0]
    latter = halves[:, :, 1]
    cosine_part = cosine_vals[:, None, :]
    sine_part = sine_vals[:, None, :]
    turned = jnp.stack(
        (former * cosine_part - latter * sine_part, latter * cosine_part + former * sine_part),
        axis=2,
    )
    return turned.reshape(row_total, D)


def tile_width(row_total):
    for candidate in (512, 256, 128):
        return candidate
    return row_total


def head_view(tensor):
    return tensor.reshape(tensor.shape[0], H, HD)


def local_any(
    frames,
    cotangent,
    seg_start,
    seg_length,
    seg_step,
    time_table,
    w_ada,
    b_ada,
    w_qkv,
    b_qkv,
    w_out,
    b_out,
    w_up,
    b_up,
    w_down,
    b_down,
):
    frame_rows = frames.shape[0]
    positions = lax.axis_index("shard") * frame_rows + jnp.arange(frame_rows, dtype=jnp.int32)
    slot_start = seg_start[0]
    slot_end = slot_start + seg_length[0]
    member_mask = (positions[:, None] >= slot_start[None, :]) & (
        positions[:, None] < slot_end[None, :]
    )
    member = member_mask.astype(jnp.float32)
    seg_low = jnp.sum(jnp.where(member_mask, slot_start[None, :], 0), axis=1)
    seg_high = jnp.sum(jnp.where(member_mask, slot_end[None, :], 0), axis=1)
    cosine_vals, sine_vals = angles((positions - seg_low).astype(jnp.float32))
    columns = (
        lax.all_gather(w_ada, "grp", axis=1, tiled=True),
        lax.all_gather(w_qkv, "grp", axis=1, tiled=True),
        lax.all_gather(w_out, "grp", axis=1, tiled=True),
        lax.all_gather(w_up, "grp", axis=1, tiled=True),
        lax.all_gather(w_down, "grp", axis=1, tiled=True),
    )
    gathered = (
        lax.all_gather(columns[0], "shard", axis=0, tiled=True),
        lax.all_gather(columns[1], "shard", axis=0, tiled=True),
        lax.all_gather(columns[2], "shard", axis=0, tiled=True),
        lax.all_gather(columns[3], "shard", axis=0, tiled=True),
        lax.all_gather(columns[4], "shard", axis=0, tiled=True),
        lax.all_gather(b_ada, "shard", axis=0, tiled=True),
        lax.all_gather(b_qkv, "shard", axis=0, tiled=True),
        lax.all_gather(b_out, "shard", axis=0, tiled=True),
        lax.all_gather(b_up, "shard", axis=0, tiled=True),
        lax.all_gather(b_down, "shard", axis=0, tiled=True),
    )
    ada_full, qkv_full, out_full, up_full, down_full = (
        gathered[0],
        gathered[1],
        gathered[2],
        gathered[3],
        gathered[4],
    )
    ada_bias, qkv_bias, out_bias, up_bias, down_bias = [
        bias_row.astype(jnp.float32) for bias_row in gathered[5:]
    ]
    step_onehot = (
        seg_step[0][:, None] == jnp.arange(time_table.shape[0], dtype=jnp.int32)[None, :]
    ).astype(jnp.float32)
    time_rows = jnp.dot(step_onehot, time_table, precision=top_precision)
    activated = jax.nn.silu(time_rows).astype(jnp.bfloat16)
    modulation = jnp.dot(activated, ada_full, preferred_element_type=jnp.float32) + ada_bias
    frame_mod = jnp.dot(member, modulation, precision=top_precision)
    shift_attn, scale_attn, gate_attn, shift_ff, scale_ff, gate_ff = jnp.split(frame_mod, 6, axis=1)
    inputs = frames.astype(jnp.float32)
    hidden_attn = modulate(inputs, scale_attn, shift_attn).astype(jnp.bfloat16)
    projected = jnp.dot(hidden_attn, qkv_full, preferred_element_type=jnp.float32) + qkv_bias
    queries = rotate(projected[:, :D], cosine_vals, sine_vals).astype(jnp.bfloat16)
    keys_rot = rotate(projected[:, D : 2 * D], cosine_vals, sine_vals).astype(jnp.bfloat16)
    values = projected[:, 2 * D :].astype(jnp.bfloat16)
    query_heads = head_view(queries)
    key_heads = head_view(keys_rot)
    value_heads = head_view(values)
    zero_heads = jnp.zeros((frame_rows, H, HD), jnp.float32)
    key_piece = lax.all_gather(keys_rot, "shard", axis=0, tiled=True)
    value_piece = lax.all_gather(values, "shard", axis=0, tiled=True)
    piece_rows = key_piece.shape[0]
    tile_rows = tile_width(piece_rows)
    tiles = piece_rows // tile_rows

    def tile_step(partial_sums, tile_item):
        key_tile, value_tile, offset = tile_item
        key_pos = offset + jnp.arange(tile_rows, dtype=jnp.int32)
        inside = (key_pos[None, :] >= seg_low[:, None]) & (key_pos[None, :] < seg_high[:, None])
        scores = 0.125 * jnp.einsum(
            "rhd,khd->hrk", query_heads, head_view(key_tile), preferred_element_type=jnp.float32
        )
        expo = jnp.where(inside[None], jnp.exp(scores), 0.0)
        numerator, denominator = partial_sums
        numerator = numerator + jnp.einsum(
            "hrk,khd->rhd",
            expo.astype(jnp.bfloat16),
            head_view(value_tile),
            preferred_element_type=jnp.float32,
        )
        denominator = denominator + jnp.sum(expo, axis=2).T
        return ((numerator, denominator), None)

    tile_items = (
        key_piece.reshape(tiles, tile_rows, D),
        value_piece.reshape(tiles, tile_rows, D),
        jnp.arange(tiles, dtype=jnp.int32) * tile_rows,
    )
    numerator, denominator = lax.scan(
        tile_step, (zero_heads, jnp.zeros((frame_rows, H), jnp.float32)), tile_items
    )[0]
    mixed = numerator / denominator[:, :, None]
    mixed_low = mixed.reshape(frame_rows, D).astype(jnp.bfloat16)
    attn_branch = jnp.dot(mixed_low, out_full, preferred_element_type=jnp.float32) + out_bias
    after_attn = inputs + gate_attn * attn_branch
    hidden_ff = modulate(after_attn, scale_ff, shift_ff).astype(jnp.bfloat16)
    upward = jnp.dot(hidden_ff, up_full, preferred_element_type=jnp.float32) + up_bias
    activation = jax.nn.gelu(upward, approximate=True).astype(jnp.bfloat16)
    ff_branch = jnp.dot(activation, down_full, preferred_element_type=jnp.float32) + down_bias
    output = (after_attn + gate_ff * ff_branch).astype(jnp.bfloat16)
    columns_back = (
        lax.all_gather(w_ada, "grp", axis=1, tiled=True),
        lax.all_gather(w_qkv, "grp", axis=1, tiled=True),
        lax.all_gather(w_out, "grp", axis=1, tiled=True),
        lax.all_gather(w_up, "grp", axis=1, tiled=True),
        lax.all_gather(w_down, "grp", axis=1, tiled=True),
    )
    gathered_back = (
        lax.all_gather(columns_back[0], "shard", axis=0, tiled=True),
        lax.all_gather(columns_back[1], "shard", axis=0, tiled=True),
        lax.all_gather(columns_back[2], "shard", axis=0, tiled=True),
        lax.all_gather(columns_back[3], "shard", axis=0, tiled=True),
        lax.all_gather(columns_back[4], "shard", axis=0, tiled=True),
    )
    ada_back, qkv_back, out_back, up_back, down_back = (
        gathered_back[0],
        gathered_back[1],
        gathered_back[2],
        gathered_back[3],
        gathered_back[4],
    )
    grad_out = cotangent.astype(jnp.float32)
    d_branch = (gate_ff * grad_out).astype(jnp.bfloat16)
    d_gate_ff = grad_out * ff_branch
    g_down = jnp.dot(activation.T, d_branch, preferred_element_type=jnp.float32)
    gb_down = jnp.sum(d_branch.astype(jnp.float32), axis=0)
    d_activation = jnp.dot(d_branch, down_back.T, preferred_element_type=jnp.float32)
    gelu_pull = jax.vjp(partial(jax.nn.gelu, approximate=True), upward)[1]
    d_upward = gelu_pull(d_activation)[0].astype(jnp.bfloat16)
    g_up = jnp.dot(hidden_ff.T, d_upward, preferred_element_type=jnp.float32)
    gb_up = jnp.sum(d_upward.astype(jnp.float32), axis=0)
    d_hidden_ff = jnp.dot(d_upward, up_back.T, preferred_element_type=jnp.float32)
    ff_pull = jax.vjp(modulate, after_attn, scale_ff, shift_ff)[1]
    dx_ff, d_scale_ff, d_shift_ff = ff_pull(d_hidden_ff)
    d_after = grad_out + dx_ff
    d_attn = (gate_attn * d_after).astype(jnp.bfloat16)
    d_gate_attn = d_after * attn_branch
    g_out = jnp.dot(mixed_low.T, d_attn, preferred_element_type=jnp.float32)
    gb_out = jnp.sum(d_attn.astype(jnp.float32), axis=0)
    d_mixed = jnp.dot(d_attn, out_back.T, preferred_element_type=jnp.float32).astype(jnp.bfloat16)
    d_mixed_heads = head_view(d_mixed).astype(jnp.float32)
    delta = jnp.sum(d_mixed_heads * mixed, axis=2) / denominator
    d_numer = (d_mixed_heads / denominator[:, :, None]).astype(jnp.bfloat16).reshape(frame_rows, D)
    dnum_heads = head_view(d_numer)
    delta_heads = delta.T
    key_piece = lax.all_gather(keys_rot, "shard", axis=0, tiled=True)
    value_piece = lax.all_gather(values, "shard", axis=0, tiled=True)
    piece_rows = key_piece.shape[0]
    fold_tile_rows = tile_width(piece_rows)
    tiles = piece_rows // fold_tile_rows

    def tile_step(grad_sum, tile_item):
        key_tile, value_tile, offset = tile_item
        key_pos = offset + jnp.arange(fold_tile_rows, dtype=jnp.int32)
        inside = (key_pos[None, :] >= seg_low[:, None]) & (key_pos[None, :] < seg_high[:, None])
        scores = 0.125 * jnp.einsum(
            "rhd,khd->hrk", query_heads, head_view(key_tile), preferred_element_type=jnp.float32
        )
        expo = jnp.where(inside[None], jnp.exp(scores), 0.0)
        slope = jnp.einsum(
            "rhd,khd->hrk", dnum_heads, head_view(value_tile), preferred_element_type=jnp.float32
        )
        d_scores = (expo * (slope - delta_heads[:, :, None])).astype(jnp.bfloat16)
        grad_sum = grad_sum + 0.125 * jnp.einsum(
            "hrk,khd->rhd", d_scores, head_view(key_tile), preferred_element_type=jnp.float32
        )
        return (grad_sum, None)

    tile_items = (
        key_piece.reshape(tiles, fold_tile_rows, D),
        value_piece.reshape(tiles, fold_tile_rows, D),
        jnp.arange(tiles, dtype=jnp.int32) * fold_tile_rows,
    )
    d_query = lax.scan(tile_step, zero_heads, tile_items)[0]
    delta_all = lax.all_gather(delta, "shard", axis=0, tiled=True)

    def fold_key_grad(running, piece):
        query_piece, dnum_piece = piece
        piece_rows = query_piece.shape[0]
        tile_rows = tile_width(piece_rows)
        tiles = piece_rows // tile_rows

        def tile_step(grad_pair, tile_item):
            query_tile, dnum_tile, delta_tile, offset = tile_item
            query_pos = offset + jnp.arange(tile_rows, dtype=jnp.int32)
            inside = (query_pos[:, None] >= seg_low[None, :]) & (
                query_pos[:, None] < seg_high[None, :]
            )
            query_tile_heads = head_view(query_tile)
            dnum_tile_heads = head_view(dnum_tile)
            scores = 0.125 * jnp.einsum(
                "qhd,rhd->hqr", query_tile_heads, key_heads, preferred_element_type=jnp.float32
            )
            expo = jnp.where(inside[None], jnp.exp(scores), 0.0)
            slope = jnp.einsum(
                "qhd,rhd->hqr", dnum_tile_heads, value_heads, preferred_element_type=jnp.float32
            )
            d_scores = (expo * (slope - delta_tile.T[:, :, None])).astype(jnp.bfloat16)
            d_keys, d_values = grad_pair
            d_keys = d_keys + 0.125 * jnp.einsum(
                "hqr,qhd->rhd", d_scores, query_tile_heads, preferred_element_type=jnp.float32
            )
            d_values = d_values + jnp.einsum(
                "hqr,qhd->rhd",
                expo.astype(jnp.bfloat16),
                dnum_tile_heads,
                preferred_element_type=jnp.float32,
            )
            return ((d_keys, d_values), None)

        tile_items = (
            query_piece.reshape(tiles, tile_rows, D),
            dnum_piece.reshape(tiles, tile_rows, D),
            delta_all.reshape(tiles, tile_rows, H),
            jnp.arange(tiles, dtype=jnp.int32) * tile_rows,
        )
        return lax.scan(tile_step, running, tile_items)[0]

    d_keys, d_values = fold_key_grad(
        (zero_heads, zero_heads),
        (
            lax.all_gather(queries, "shard", axis=0, tiled=True),
            lax.all_gather(d_numer, "shard", axis=0, tiled=True),
        ),
    )
    grad_query = rotate(d_query.reshape(frame_rows, D), cosine_vals, -sine_vals)
    grad_key = rotate(d_keys.reshape(frame_rows, D), cosine_vals, -sine_vals)
    d_projected = jnp.concatenate(
        (grad_query, grad_key, d_values.reshape(frame_rows, D)), axis=1
    ).astype(jnp.bfloat16)
    g_qkv = jnp.dot(hidden_attn.T, d_projected, preferred_element_type=jnp.float32)
    gb_qkv = jnp.sum(d_projected.astype(jnp.float32), axis=0)
    d_hidden_attn = jnp.dot(d_projected, qkv_back.T, preferred_element_type=jnp.float32)
    attn_pull = jax.vjp(modulate, inputs, scale_attn, shift_attn)[1]
    dx_attn, d_scale_attn, d_shift_attn = attn_pull(d_hidden_attn)
    grad_frames = d_after + dx_attn
    d_frame_mod = jnp.concatenate(
        (d_shift_attn, d_scale_attn, d_gate_attn, d_shift_ff, d_scale_ff, d_gate_ff), axis=1
    )
    d_slot = jnp.dot(member.T, d_frame_mod, precision=top_precision)
    g_ada = jnp.dot(activated.astype(jnp.float32).T, d_slot, precision=top_precision)
    gb_ada = jnp.sum(d_slot, axis=0)
    d_activated = jnp.dot(
        d_slot, ada_back.T, precision=top_precision, preferred_element_type=jnp.float32
    )
    silu_pull = jax.vjp(jax.nn.silu, time_rows)[1]
    d_time_rows = silu_pull(d_activated)[0]
    g_table = jnp.dot(step_onehot.T, d_time_rows, precision=top_precision)
    group_sums = (
        lax.psum_scatter(g_ada, "shard", scatter_dimension=0, tiled=True),
        lax.psum_scatter(g_qkv, "shard", scatter_dimension=0, tiled=True),
        lax.psum_scatter(g_out, "shard", scatter_dimension=0, tiled=True),
        lax.psum_scatter(g_up, "shard", scatter_dimension=0, tiled=True),
        lax.psum_scatter(g_down, "shard", scatter_dimension=0, tiled=True),
        lax.psum_scatter(gb_ada, "shard", scatter_dimension=0, tiled=True),
        lax.psum_scatter(gb_qkv, "shard", scatter_dimension=0, tiled=True),
        lax.psum_scatter(gb_out, "shard", scatter_dimension=0, tiled=True),
        lax.psum_scatter(gb_up, "shard", scatter_dimension=0, tiled=True),
        lax.psum_scatter(gb_down, "shard", scatter_dimension=0, tiled=True),
        lax.psum_scatter(g_table, "shard", scatter_dimension=1, tiled=True),
    )
    wide_sums = (
        lax.psum_scatter(group_sums[0], "grp", scatter_dimension=1, tiled=True),
        lax.psum_scatter(group_sums[1], "grp", scatter_dimension=1, tiled=True),
        lax.psum_scatter(group_sums[2], "grp", scatter_dimension=1, tiled=True),
        lax.psum_scatter(group_sums[3], "grp", scatter_dimension=1, tiled=True),
        lax.psum_scatter(group_sums[4], "grp", scatter_dimension=1, tiled=True),
    )
    small_sums = lax.psum(
        (group_sums[5], group_sums[6], group_sums[7], group_sums[8], group_sums[9], group_sums[10]),
        "grp",
    )
    finals = tuple(wide_sums) + tuple(small_sums)
    return (
        output,
        grad_frames,
        finals[10],
        finals[0],
        finals[5],
        finals[1],
        finals[6],
        finals[2],
        finals[7],
        finals[3],
        finals[8],
        finals[4],
        finals[9],
    )


LANES = 128
FREE = pl.CostEstimate(flops=2**20, bytes_accessed=2**16, transcendentals=0)
CHIPS = (2, 4, 6)
ORDER = (0, 2, 4, 6, 1, 3, 5, 7)
SEPARATE = -(2.0**100)
GELU_C = 0.7978845608028654
GELU_A = 0.044715
NT = (((1,), (1,)), ((), ()))
TN = (((0,), (0,)), ((), ()))
f32 = jnp.float32
bf16 = jnp.bfloat16


def dot(left, right, dims=(((1,), (0,)), ((), ()))):
    return lax.dot_general(left, right, dims, preferred_element_type=f32)


def params(limit_mib, steps=1):
    return pltpu.CompilerParams(
        dimension_semantics=("arbitrary",) * steps, vmem_limit_bytes=limit_mib * 2**20
    )


def moments(value):
    centred = value - jnp.mean(value, axis=1, keepdims=True)
    inv = lax.rsqrt(jnp.mean(centred * centred, axis=1, keepdims=True) + eps_norm)
    return centred * inv, inv


def norm_back(weighted, normal, inv):
    return (
        weighted
        - jnp.mean(weighted, axis=1, keepdims=True)
        - normal * jnp.mean(weighted * normal, axis=1, keepdims=True)
    ) * inv


def swap_halves(value):
    lane = lax.broadcasted_iota(jnp.int32, value.shape, 1)
    return jnp.where(lane % HD < HD // 2, pltpu.roll(value, 96, 1), pltpu.roll(value, 32, 1))


def rotary(cos_ref, sin_ref, here):
    cosine, sine = cos_ref[:, here].T, sin_ref[:, here].T
    return jnp.concatenate([cosine] * 4, axis=1), jnp.concatenate([-sine, sine] * 2, axis=1)


def members(seg_ref, block, rows):
    place = block * rows + lax.broadcasted_iota(jnp.int32, (rows, LANES), 0)
    out = []
    for slot in range(3):
        begin = seg_ref[block, slot]
        out.append((place >= begin) & (place < begin + seg_ref[block, 3 + slot]))
    return out


def mod_rows(table_ref, seg_ref, block, member, part):
    first, second, third = [table_ref[pl.ds(seg_ref[block, 6 + slot], 1), pl.ds(part * D, D)] for slot in range(3)]
    out = []
    for at in range(0, D, LANES):
        here = slice(at, at + LANES)
        out.append(jnp.where(member[0], first[:, here], jnp.where(member[1], second[:, here], third[:, here])))
    return jnp.concatenate(out, axis=1)


def slot_sums(member, value):
    out = []
    for column in member:
        sums = [
            jnp.sum(jnp.where(column, value[:, at : at + LANES], 0.0), axis=0, keepdims=True) for at in range(0, D, LANES)
        ]
        out.append(jnp.concatenate(sums, axis=1))
    return out


def qkv_kernel(order_ref, seg_ref, *refs):
    step = pl.program_id(0)
    last = pl.num_programs(0) - 1
    *pieces, table_ref, w_ref, b_ref, cos_ref, sin_ref, q_ref, k_ref, v_ref, h_ref, x_all, arrived = refs
    block = order_ref[step]
    rows = x_all.shape[1]
    copies, at = [], 0
    for piece in pieces:
        here = x_all.at[at : at + piece.shape[0]]
        copies.append((at, pltpu.make_async_copy(piece, here, arrived.at[len(copies)])))
        at += piece.shape[0]

    @pl.when(step == 0)
    def _():
        for _, copy in copies:
            copy.start()

    for at, copy in copies:

        @pl.when(step == at)
        def _(copy=copy):
            copy.wait()

    member = members(seg_ref, block, rows)
    normal, _ = moments(x_all[step].astype(f32))
    shift = mod_rows(table_ref, seg_ref, block, member, 0)
    scale = mod_rows(table_ref, seg_ref, block, member, 1)
    hidden = (normal * (1.0 + scale) + shift).astype(bf16)
    h_ref[...] = hidden
    projected = dot(hidden, w_ref[...]) + b_ref[...]
    cosine, sine = rotary(cos_ref, sin_ref, slice(None))
    turned = []
    for part in range(2):
        piece = projected[:, part * LANES : (part + 1) * LANES]
        turned.append(piece * cosine + swap_halves(piece) * sine)
    queries = turned[0].astype(bf16).astype(f32) * 0.125
    keys = turned[1]
    values = projected[:, 2 * LANES :]
    lane = lax.broadcasted_iota(jnp.int32, (rows, LANES), 1)
    lane_row = lane[:1]
    begins, ends = jnp.full((1, LANES), 2**30, jnp.int32), jnp.zeros((1, LANES), jnp.int32)
    for index in range(6):
        where, slot = (0, index) if index < 3 else (last, index - 3)
        begin = seg_ref[where, slot]
        begins = jnp.where(lane_row == HD + index, begin, begins)
        ends = jnp.where(lane_row == HD + index, begin + seg_ref[where, 3 + slot], ends)
    place = block * rows + lax.broadcasted_iota(jnp.int32, (rows, LANES), 0)
    inside = (place >= begins) & (place < ends)
    query_extra = jnp.where(inside | (lane >= HD + 6), 0.0, SEPARATE)
    key_extra = jnp.where(inside, 1.0, 0.0)
    value_extra = jnp.where((lane >= HD) & (lane < HD + 3), 1.0, 0.0)
    low = lane < HD
    for head in range(2):
        for ref, value, extra in (
            (q_ref, queries, query_extra),
            (k_ref, keys, key_extra),
            (v_ref, values, value_extra),
        ):
            own = value if head == 0 else pltpu.roll(value, HD, 1)
            ref[head] = jnp.where(low, own, extra).astype(bf16)


def attend_kernel(q_ref, k_ref, v_ref, o_ref, mixed_ref, l_ref):
    keys_in_all = k_ref.shape[1]
    tile = 256
    ratios, sums = [], []
    for head in range(2):
        query = q_ref[head]
        total = None
        for at in range(0, keys_in_all, tile):
            expo = jnp.exp(dot(query, k_ref[head, at : at + tile], NT))
            term = dot(expo.astype(bf16), v_ref[head, at : at + tile])
            total = term if total is None else total + term
        norm = total[:, HD : HD + 1]
        ratios.append(total / norm)
        sums.append(norm)
    lane = lax.broadcasted_iota(jnp.int32, ratios[0].shape, 1)
    mixed = jnp.where(lane < HD, ratios[0], pltpu.roll(ratios[1], HD, 1))
    mixed_ref[...] = mixed
    o_ref[...] = mixed.astype(bf16)
    l_ref[...] = jnp.where(lane < HD, sums[0], sums[1])


def block_kernel(
    order_ref, seg_ref, x_ref, cot_ref, o_ref, table_ref, w_ref, b_out_ref, b_up_ref, b_down_ref,
    out_ref, dx1_ref, do_ref, pair_ref, keep_ref, send_ref, slots_ref, gb_out_ref, gb_up_ref, gb_down_ref,
):
    rows = x_ref.shape[0]
    groups, shards = w_ref.shape[:2]
    block = order_ref[0]
    member = members(seg_ref, block, rows)
    modulation = partial(mod_rows, table_ref, seg_ref, block, member)
    wide = D // groups

    def weight(group, start):
        return w_ref[group, :, start : start + LANES, :].reshape(D, wide)

    def weight_down(group):
        return w_ref[group, :, 0 : 2 * LANES, :].reshape(2 * D, wide)

    def by_core(value, width, other):
        parts = [value[:, at : at + width] for at in range(0, value.shape[1], width)]
        even, odd = jnp.concatenate(parts[0::2], axis=1), jnp.concatenate(parts[1::2], axis=1)
        return jnp.where((block % 2 == 0) != other, even, odd)

    def share(start, value, width):
        half = value.shape[1] // 2
        keep_ref[:, start : start + half] = by_core(value, width, False)
        send_ref[:, start : start + half] = by_core(value, width, True)

    mixed = jnp.concatenate([o_ref[shard] for shard in range(shards)], axis=1)
    share(D, mixed, LANES)
    attn = jnp.concatenate([dot(mixed, weight(group, 256)) for group in range(groups)], axis=1)
    attn = attn + b_out_ref[...]
    gate1 = modulation(2)
    after = x_ref[...].astype(f32) + gate1 * attn
    normal, inv = moments(after)
    scale2 = 1.0 + modulation(4)
    hidden = (normal * scale2 + modulation(3)).astype(bf16)
    share(D + D // 2, hidden, LANES)
    up = [dot(hidden, weight(group, start)) for group in range(groups) for start in (384, 512)]
    up = jnp.concatenate(up, axis=1) + b_up_ref[...]
    inner = jnp.tanh(GELU_C * (up + GELU_A * (up * up * up)))
    act = (0.5 * up * (1.0 + inner)).astype(bf16)
    share(0, act, 2 * LANES)
    slope = 0.5 * (1.0 + inner) + (0.5 * GELU_C) * up * (1.0 - inner * inner) * (
        1.0 + (3.0 * GELU_A) * up * up
    )
    branch = jnp.concatenate([dot(act, weight_down(group)) for group in range(groups)], axis=1)
    branch = branch + b_down_ref[...]
    gate2 = modulation(5)
    out_ref[...] = (after + gate2 * branch).astype(bf16)

    cot = cot_ref[...].astype(f32)
    dff = (gate2 * cot).astype(bf16)
    pair_ref[:, 0:D] = dff
    gb_down_ref[...] = jnp.sum(dff.astype(f32), axis=0, keepdims=True)
    d_gate2 = slot_sums(member, cot * branch)
    d_act = sum(dot(dff[:, g * wide : (g + 1) * wide], weight_down(g), NT) for g in range(groups))
    du = (d_act * slope).astype(bf16)
    pair_ref[:, 2 * D :] = du
    gb_up_ref[...] = jnp.sum(du.astype(f32), axis=0, keepdims=True)
    d_hidden = None
    for index in range(2 * groups):
        piece = du[:, index * wide : (index + 1) * wide]
        term = dot(piece, weight(index // 2, 384 + LANES * (index % 2)), NT)
        d_hidden = term if d_hidden is None else d_hidden + term
    d_shift2 = slot_sums(member, d_hidden)
    d_scale2 = slot_sums(member, d_hidden * normal)
    d_after = cot + norm_back(d_hidden * scale2, normal, inv)
    dx1_ref[...] = d_after
    d_gate1 = slot_sums(member, d_after * attn)
    da = (gate1 * d_after).astype(bf16)
    pair_ref[:, D : 2 * D] = da
    gb_out_ref[...] = jnp.sum(da.astype(f32), axis=0, keepdims=True)
    d_mixed = sum(dot(da[:, g * wide : (g + 1) * wide], weight(g, 256), NT) for g in range(groups))
    d_mixed = d_mixed.astype(bf16)
    for shard in range(shards):
        do_ref[shard] = d_mixed[:, shard * LANES : (shard + 1) * LANES]
    slots_ref[...] = jnp.concatenate(d_gate1 + d_shift2 + d_scale2 + d_gate2, axis=0)


def weight_grad_kernel(
    order_ref, group_ref, keep_ref, send_ref, pair_ref, pair2_ref, first_x, first_y, own_x, own_y
):
    groups, half, wide = first_x.shape[1:]

    def product(at, width, start, stop):
        here = pl.ds(pl.multiple_of(at, LANES), width)
        return (
            dot(keep_ref[:, here], pair_ref[:, start:stop], TN) + dot(send_ref[:, here], pair2_ref[:, start:stop], TN)
        ).astype(bf16)

    places = (((own_x, 0), (own_y, 0)), ((first_x, 0), (own_y, 1)), ((own_x, 1), (first_y, 0)), ((first_x, 1), (first_y, 1)))
    for index in range(4):
        chip = order_ref[index] // 2
        down = product(chip * 2 * LANES, 2 * LANES, 0, D)
        out = product(D + chip * LANES, LANES, D, 2 * D)
        up = product(D + D // 2 + chip * LANES, LANES, 2 * D, 4 * D)
        (by_x, at_x), (by_y, at_y) = places[index]
        for group in range(groups):
            to = (group + groups - group_ref[0]) % groups
            columns = slice(group * wide, (group + 1) * wide)
            by_x[at_x, to, 0:256, :] = down[:, columns]
            by_x[at_x, to, 256:half, :] = out[: half - 256, columns]
            by_y[at_y, to, 0 : 384 - half, :] = out[half - 256 :, columns]
            for part in range(2):
                start = 384 - half + 128 * part
                at = (2 * group + part) * wide
                by_y[at_y, to, start : start + 128, :] = up[:, at : at + wide]


def attend_back_kernel(head, q_ref, k_ref, v_ref, do_ref, mixed_ref, l_ref, cos_ref, sin_ref, *refs):
    *refs, dn, dq_t, dk_all = refs
    if head == 0:
        qk_ref, dv_ref = refs
    else:
        qk_first, dv_first, second_ref, own_ref, gb_ref = refs
        qk_ref = second_ref.at[:, :LANES]
    step = pl.program_id(0)
    rows = k_ref.shape[1]
    frames = q_ref.shape[1]
    tile = 256
    lane = lax.broadcasted_iota(jnp.int32, (rows, LANES), 1)
    low = lane < HD

    @pl.when(step == 0)
    def _():
        dq_t[...] = jnp.zeros_like(dq_t)
        for at in range(0, frames, rows):
            here = slice(at, at + rows)
            d_out = do_ref[here].astype(f32)
            norm = l_ref[here]
            d_num = (d_out / norm).astype(bf16).astype(f32)
            mine = low if head == 0 else ~low
            total = jnp.sum(jnp.where(mine, d_out * mixed_ref[here], 0.0), axis=1, keepdims=True)
            delta = -total / norm[:, head * HD : head * HD + 1]
            first = delta.astype(bf16).astype(f32)
            second = (delta - first).astype(bf16).astype(f32)
            third = delta - first - second
            extra = jnp.where(lane == HD, first, jnp.where(lane == HD + 1, second, third))
            extra = jnp.where(lane < HD + 3, extra, 0.0)
            own = d_num if head == 0 else pltpu.roll(d_num, HD, 1)
            dn[here] = jnp.where(low, own, extra).astype(bf16)

    key, value = k_ref[0], v_ref[0]
    key_t = key.T
    dk_total, dv_total = None, None
    for at in range(0, frames, tile):
        here = slice(at, at + tile)
        query, d_num = q_ref[0, here], dn[here]
        expo = jnp.exp(dot(key, query, NT))
        d_score = (expo * dot(value, d_num, NT)).astype(bf16)
        dk_term = dot(d_score, query)
        dv_term = dot(expo.astype(bf16), d_num)
        dk_total = dk_term if dk_total is None else dk_total + dk_term
        dv_total = dv_term if dv_total is None else dv_total + dv_term
        dq_t[:, here] += dot(key_t, d_score)

    here = pl.ds(pl.multiple_of(step * rows, rows), rows)
    dk_all[here] = dk_total
    if head == 0:
        dv_ref[here] = dv_total.astype(bf16)
    else:
        both = jnp.where(low, dv_first[here].astype(f32), pltpu.roll(dv_total, HD, 1)).astype(bf16)
        own_ref[here, 2 * LANES :] = both
        second_ref[here, LANES:] = both

    @pl.when(step == pl.num_programs(0) - 1)
    def _():
        for at in range(0, frames, rows):
            part = slice(at, at + rows)
            cosine, sine = rotary(cos_ref, sin_ref, part)
            both = jnp.where(low, 0.125 * dq_t[:, part].T, pltpu.roll(dk_all[part], HD, 1))
            both = (both * cosine - swap_halves(both) * sine).astype(bf16)
            qk_ref[part] = both
            if head == 1:
                first, second = qk_first[part].astype(f32), both.astype(f32)
                own_ref[part, 0:LANES] = jnp.where(low, first, pltpu.roll(second, HD, 1)).astype(bf16)
                own_ref[part, LANES : 2 * LANES] = jnp.where(low, pltpu.roll(first, HD, 1), second).astype(bf16)
        if head == 1:
            ones = jnp.ones((8, frames), bf16)
            sums = dot(ones, own_ref[...])[0:1]
            for index in range(3):
                gb_ref[index : index + 1] = sums[:, index * LANES : (index + 1) * LANES]


def input_grad_kernel(
    base_ref, seg_ref, first_ref, second_ref, w_ref, x_ref, dx1_ref, table_ref, grad_ref, slots_ref, w_all, arrived
):
    shards, rows = first_ref.shape[:2]
    copies = [pltpu.make_async_copy(w_ref.at[shard], w_all.at[shard], arrived.at[shard]) for shard in range(shards)]
    for copy in copies:
        copy.start()
    block = base_ref[0]
    member = members(seg_ref, block, rows)
    scale = 1.0 + mod_rows(table_ref, seg_ref, block, member, 1)
    normal, inv = moments(x_ref[...].astype(f32))
    low = lax.broadcasted_iota(jnp.int32, (rows, LANES), 1) < HD
    d_hidden = None
    for shard in range(shards):
        first, second = first_ref[shard].astype(f32), second_ref[shard, :, :LANES].astype(f32)
        queries = jnp.where(low, first, pltpu.roll(second, HD, 1)).astype(bf16)
        keys = jnp.where(low, pltpu.roll(first, HD, 1), second).astype(bf16)
        whole_row = jnp.concatenate([queries, keys, second_ref[shard, :, LANES:]], axis=1)
        copies[shard].wait()
        term = dot(whole_row, w_all[shard], NT)
        d_hidden = term if d_hidden is None else d_hidden + term
    grad_ref[...] = dx1_ref[...] + norm_back(d_hidden * scale, normal, inv)
    sums = slot_sums(member, d_hidden) + slot_sums(member, d_hidden * normal)
    slots_ref[...] = jnp.concatenate(sums + [jnp.zeros((2, D), f32)], axis=0)


def add_kernel(own_x, came_x, own_y, came_y, by_y, by_x):
    by_y[...] = (own_x[0].astype(f32) + came_x[0].astype(f32)).astype(bf16)
    by_x[...] = (own_y[0].astype(f32) + came_y[0].astype(f32)).astype(bf16)


def total_kernel(own_x, came_x, by_y, own_y, came_y, by_x, *out_refs):
    half = by_y.shape[1]
    for group, ref in enumerate(out_refs):
        first = own_x[0, group].astype(f32) + came_x[0, group].astype(f32) + by_y[group].astype(f32)
        second = own_y[0, group].astype(f32) + came_y[0, group].astype(f32) + by_x[group].astype(f32)
        ref[:half] = first.astype(bf16)
        ref[half:] = second.astype(bf16)


def last_sum_kernel(*refs):
    *pieces, down_ref, out_ref, up_ref = refs
    total = sum(piece[...].astype(f32) for piece in pieces)
    wide = total.shape[1]
    down_ref[...] = total[: 2 * LANES]
    out_ref[...] = total[2 * LANES : 3 * LANES]
    up_ref[:, :wide] = total[3 * LANES : 4 * LANES]
    up_ref[:, wide:] = total[4 * LANES :]


def qkv_grad_kernel(h_ref, d_ref, out_ref):
    shards, depth = out_ref.shape[:2]
    for shard in range(shards):
        out_ref[shard] = dot(h_ref[:, shard * depth : (shard + 1) * depth], d_ref[...], TN).astype(bf16)


def qkv_piece_kernel(group_ref, came_ref, *out_refs):
    shards = came_ref.shape[0]
    units = 3 * shards // len(out_refs)
    for group, ref in enumerate(out_refs):
        start = lax.rem(group_ref[0] + group, len(out_refs)) * units
        for unit in range(units):
            part = pl.ds(pl.multiple_of((start + unit) // shards * LANES, LANES), LANES)
            ref[:, unit * LANES : (unit + 1) * LANES] = came_ref[lax.rem(start + unit, shards), :, part]


def qkv_sum_kernel(*refs):
    refs[-1][...] = sum(piece[...].astype(f32) for piece in refs[:-1])


def collect_kernel(shard_ref, seg_ref, tail_ref, out_ref, rows_ref, others_ref):
    shards = tail_ref.shape[0]
    groups = out_ref.shape[0]
    wide = out_ref.shape[2] - 2 * LANES
    shard = shard_ref[0]
    rows_ref[0:3] = tail_ref[0, 0:3]
    rows_ref[3:6] = tail_ref[shards - 1, 0:3]
    middle = sum(tail_ref[index, 0:3] for index in range(1, shards - 1))
    rows_ref[6:7] = jnp.sum(middle, axis=0, keepdims=True)
    rows_ref[7:8] = jnp.zeros((1, rows_ref.shape[1]), f32)
    others_ref[...] = sum(tail_ref[index, 3:4, 3 * LANES : 3 * LANES + 4 * D] for index in range(shards))

    def own(start, size):
        return pl.ds(pl.multiple_of(start + shard * size, LANES), size)

    sums = [jnp.sum(rows_ref[:, own(0, 6 * D // shards)], axis=0, keepdims=True)]
    for index in range(3 * D // shards // LANES):
        chunk = shard * (3 * D // shards // LANES) + index
        part = pl.ds(pl.multiple_of(chunk // shards * LANES, LANES), LANES)
        sums.append(tail_ref[lax.rem(chunk, shards), 3:4, part])
    sums += [others_ref[:, own(0, D // shards)], others_ref[:, own(D, 2 * D // shards)]]
    lane = lax.broadcasted_iota(jnp.int32, (1, LANES), 1)
    ids = jnp.zeros((1, LANES), jnp.int32)
    for index in range(6):
        where, slot = (0, index) if index < 3 else (shards - 1, index - 3)
        ids = jnp.where(lane == index, seg_ref[where, 6 + slot], ids)
    ids = jnp.where(lane == 6, seg_ref[1, 6] + seg_ref[1, 7] + seg_ref[1, 8], ids)
    rows_ref[7:8, 0:wide] = jnp.concatenate(sums, axis=1)
    for group in range(groups):
        out_ref[group, 0:7, 0:wide] = rows_ref[0:7, group * wide : (group + 1) * wide]
        out_ref[group, 7:8, 0:wide] = rows_ref[7:8, 0:wide]
        out_ref[group, :, wide:] = jnp.zeros((8, 2 * LANES), f32)
        out_ref[group, 0:1, wide : wide + LANES] = others_ref[:, own(3 * D, D // shards)]
        out_ref[group, 0:1, wide + LANES :] = ids.astype(f32)


def three(value):
    first = value.astype(bf16)
    second = (value - first.astype(f32)).astype(bf16)
    return [first, second, (value - first.astype(f32) - second.astype(f32)).astype(bf16)]


def table_kernel(*refs):
    all_parts, act_ref, w_ref, time_ref, ada_ref, time_grad_ref, b_ada, b_qkv, b_out, b_up, b_down = refs
    steps, wide = time_ref.shape[0], w_ref.shape[1]
    parts = [all_parts.at[index] for index in range(all_parts.shape[0])]
    step = lax.broadcasted_iota(jnp.int32, (steps, 1), 0)
    total = jnp.zeros((steps, wide), f32)
    for part in parts:
        for row in range(7):
            at = wide + LANES + row
            picked = part[0:1, at : at + 1].astype(jnp.int32) == step
            total = total + jnp.where(picked, part[row : row + 1, :wide], 0.0)
    pieces = three(total)
    act = act_ref[...]
    ada_ref[...] = dot(jnp.concatenate([act] * 3, axis=0), jnp.concatenate(pieces, axis=0), TN)
    d_act = dot(jnp.concatenate(pieces, axis=0), w_ref[...], NT)
    d_act = d_act[:steps] + d_act[steps : 2 * steps] + d_act[2 * steps :]
    value = time_ref[...]
    gate = 1.0 / (1.0 + jnp.exp(-value))
    time_grad_ref[...] = d_act * gate * (1.0 + value * (1.0 - gate))
    first_row = sum(part[7:8, :wide] for part in parts)
    at = 0
    for ref in (b_ada, b_qkv, b_out, b_up):
        ref[...] = first_row[:, at : at + ref.shape[1]]
        at += ref.shape[1]
    b_down[...] = sum(part[0:1, wide : wide + b_down.shape[1]] for part in parts)


def spread(value, axis, size):
    return [value] + [
        lax.ppermute(value, axis, [(i, (i - step) % size) for i in range(size)]) for step in range(1, size)
    ]


def trade(pieces, axis, size):
    return [pieces[0]] + [
        lax.ppermute(pieces[size - step], axis, [(i, (i - step) % size) for i in range(size)])
        for step in range(1, size)
    ]


def in_order(pieces, axis, size):
    own = lax.axis_index(axis)
    out = []
    for place in range(size):
        pick = (place - own) % size
        value = pieces[0]
        for index in range(1, size):
            value = jnp.where(pick == index, pieces[index], value)
        out.append(value)
    return out


def hop(value, step):
    return lax.ppermute(value, "shard", [(i, i ^ step) for i in range(8)])


def after(value, *others):
    anywhere = pl.BlockSpec(memory_space=pl.ANY)
    return pl.pallas_call(
        lambda *refs: None,
        in_specs=[anywhere] * (1 + len(others)),
        out_specs=anywhere,
        out_shape=jax.ShapeDtypeStruct(value.shape, value.dtype),
        input_output_aliases={0: 0},
        cost_estimate=FREE,
        name="after",
    )(value, *others)


def shape(*dims, kind=bf16):
    return jax.ShapeDtypeStruct(dims, kind)


def whole(*dims):
    return pl.BlockSpec(dims, lambda *_: (0,) * len(dims))


smem = pl.BlockSpec(memory_space=pltpu.SMEM)


def local_heads(
    groups, shards, frames, cotangent, seg_start, seg_length, seg_step, time_table,
    w_ada, b_ada, w_qkv, b_qkv, w_out, b_out, w_up, b_up, w_down, b_down,
):
    rows = frames.shape[0]
    packed = rows * shards
    steps = time_table.shape[0]
    shard = lax.axis_index("shard")
    depth = D // shards
    wide = D // groups

    group = lax.axis_index("grp")
    order = shard ^ jnp.array(ORDER, jnp.int32)

    inverse = 10000.0 ** (-jnp.arange(HD // 2, dtype=f32) / (HD // 2))
    phase = inverse[:, None] * jnp.arange(packed, dtype=f32)[None, :]
    cosine, sine = jnp.cos(phase), jnp.sin(phase)

    activated = jax.nn.silu(time_table).astype(bf16)
    act_own = lax.dynamic_slice_in_dim(activated, shard * depth, depth, 1)
    partial_mod = dot(act_own, w_ada)
    mod_wide = partial_mod.shape[1]
    biases = [b.astype(f32) for b in (b_ada, b_qkv, b_out, b_up, b_down)]
    sizes = [b.shape[0] for b in biases]
    segs = jnp.concatenate((seg_start, seg_length, seg_step), axis=1).astype(f32)
    extra = jnp.concatenate(biases + [jnp.floor(segs[0] / 128.0), segs[0] % 128.0])
    extra_rows = -(-extra.shape[0] // mod_wide)
    extra = jnp.pad(extra, (0, extra_rows * mod_wide - extra.shape[0])).reshape(extra_rows, mod_wide)
    units = 3 * shards // groups
    first = group * units
    by_unit = w_qkv.reshape(depth, units, LANES).transpose(1, 0, 2)
    which = jnp.minimum((jnp.arange(shards) - first) % shards, units - 1)
    by_shard = jnp.take(by_unit, which, axis=0, mode="clip")
    w_cols = jnp.broadcast_to(by_shard[None], (groups, shards, depth, LANES)).reshape(groups * shards, depth, LANES)
    w_cols = lax.all_to_all(w_cols, ("grp", "shard"), split_axis=0, concat_axis=0, tiled=True).reshape(groups, D, LANES)
    small = jnp.concatenate((partial_mod, extra), axis=0).astype(bf16)
    small = lax.all_gather(small, "shard", axis=0).astype(f32)
    held = after(frames, small)
    chips = [held] + [hop(held, step) for step in CHIPS]

    mod_own = jnp.sum(small[:, :steps], axis=0).astype(bf16)
    high = lax.all_gather(after(mod_own, w_cols), "grp", axis=1, tiled=True)

    w_heads = jnp.concatenate(
        [lax.dynamic_index_in_dim(w_cols, (part * shards + shard) // units, 0, keepdims=False) for part in range(3)], axis=1
    )

    chips = [chips[0]] + [after(piece, high) for piece in chips[1:]]
    others = hop(jnp.stack(chips), 1)

    pack = jnp.concatenate((w_down, w_out, w_up[:, :wide], w_up[:, wide:]), axis=0)
    weights = lax.all_gather(pack, ("grp", "shard"), axis=0).reshape(groups, shards, 5 * LANES, wide)

    extra = small[:, steps:].reshape(shards, extra_rows * mod_wide)
    full, at = [], 0
    for size in sizes:
        full.append(extra[:, at : at + size].reshape(1, shards * size))
        at += size
    ada_bias, qkv_bias, out_bias, up_bias, down_bias = full
    seg_all = (extra[:, at : at + 9] * 128.0 + extra[:, at + 9 : at + 18]).astype(jnp.int32)
    qkv_bias = lax.dynamic_index_in_dim(qkv_bias.reshape(3, shards, LANES), shard, 1, keepdims=False)
    qkv_bias = qkv_bias.reshape(1, 3 * LANES)
    table = high.astype(f32) + ada_bias

    ordered = lambda width: pl.BlockSpec((rows, width), lambda i, order: (order[i], 0))
    ordered_heads = pl.BlockSpec((2, rows, LANES), lambda i, order: (0, order[i], 0))
    by_block = lambda width: pl.BlockSpec((rows, width), lambda i: (i, 0))
    two_heads = pl.BlockSpec((2, rows, LANES), lambda i: (0, i, 0))
    frame_pieces = [piece[None] for piece in chips] + [others]
    q, k, v, h1_all = pl.pallas_call(
        qkv_kernel,
        grid_spec=pltpu.PrefetchScalarGridSpec(
            num_scalar_prefetch=1,
            grid=(shards,),
            in_specs=[smem]
            + [pl.BlockSpec(memory_space=pl.ANY)] * len(frame_pieces)
            + [whole(steps, 2 * D), whole(D, 3 * LANES), whole(1, 3 * LANES)] + [pl.BlockSpec((HD // 2, rows), lambda i, order: (0, order[i]))] * 2,
            out_specs=[ordered_heads] * 3 + [ordered(D)],
            scratch_shapes=[pltpu.VMEM((shards, rows, D), bf16), pltpu.SemaphoreType.DMA((len(frame_pieces),))],
        ),
        out_shape=[shape(2, packed, LANES)] * 3 + [shape(packed, D)],
        compiler_params=params(60),
        cost_estimate=FREE,
        name="qkv",
    )(order, seg_all, *frame_pieces, table[:, : 2 * D], w_heads, qkv_bias, cosine, sine)

    attn_flops = 2 * 2 * packed * packed * 256
    some_rows = packed // 2
    some = pl.BlockSpec((some_rows, LANES), lambda i: (i, 0))
    o_heads, mixed, norm = pl.pallas_call(
        attend_kernel,
        grid=(packed // some_rows,),
        in_specs=[pl.BlockSpec((2, some_rows, LANES), lambda i: (0, i, 0))] + [whole(2, packed, LANES)] * 2,
        out_specs=[some] * 3,
        out_shape=[shape(packed, LANES), shape(packed, LANES, kind=f32), shape(packed, LANES, kind=f32)],
        compiler_params=params(60),
        cost_estimate=FREE,
        name="attend",
    )(q, k, v)

    o = lax.all_to_all(o_heads.reshape(shards, rows, LANES), "shard", split_axis=0, concat_axis=0, tiled=True)
    base = shard.astype(jnp.int32).reshape(1)
    block_flops = 2 * rows * D * D * 10
    out, dx1, d_mixed, pair, keep, send, slots_ff, gb_out, gb_up, gb_down = pl.pallas_call(
        block_kernel,
        grid=(1,),
        in_specs=[
            smem, smem, whole(rows, D), whole(rows, D), whole(shards, rows, LANES), whole(steps, 6 * D),
            whole(groups, shards, 5 * LANES, wide), whole(1, D), whole(1, 2 * D), whole(1, D),
        ],
        out_specs=[
            whole(rows, D), whole(rows, D), whole(shards, rows, LANES), whole(rows, 4 * D), whole(rows, 2 * D),
            whole(rows, 2 * D), whole(12, D), whole(1, D), whole(1, 2 * D), whole(1, D),
        ],
        out_shape=[
            shape(rows, D), shape(rows, D, kind=f32), shape(shards, rows, LANES), shape(rows, 4 * D), shape(rows, 2 * D),
            shape(rows, 2 * D), shape(12, D, kind=f32),
            shape(1, D, kind=f32), shape(1, 2 * D, kind=f32), shape(1, D, kind=f32),
        ],
        compiler_params=params(60),
        cost_estimate=FREE,
        name="block",
    )(order, seg_all, frames, cotangent, o, table, weights, out_bias, up_bias, down_bias)

    d_heads = lax.all_to_all(d_mixed, "shard", split_axis=0, concat_axis=0, tiled=True).reshape(packed, LANES)

    send, pair_send = hop(send, 1), hop(pair, 1)
    half = (2, groups, 5 * LANES // 2, wide)
    first_x, first_y, own_x, own_y = pl.pallas_call(
        weight_grad_kernel,
        grid=(1,),
        in_specs=[smem, smem, whole(rows, 2 * D), whole(rows, 2 * D), whole(rows, 4 * D), whole(rows, 4 * D)],
        out_specs=[whole(*half)] * 4,
        out_shape=[shape(*half)] * 4,
        compiler_params=params(60),
        cost_estimate=FREE,
        name="weight_grads",
    )(order, group.astype(jnp.int32).reshape(1), keep, send, pair, pair_send)
    first_x, first_y = after(first_x, d_heads), after(first_y, d_heads)
    d_heads = after(d_heads, first_x, first_y)

    back_specs = lambda head: [
        pl.BlockSpec((1, packed, LANES), lambda i: (head, 0, 0)),
        pl.BlockSpec((1, packed, LANES), lambda i: (head, i, 0)),
        pl.BlockSpec((1, packed, LANES), lambda i: (head, i, 0)),
    ] + [whole(packed, LANES)] * 3 + [whole(HD // 2, packed)] * 2
    back_scratch = [pltpu.VMEM((packed, LANES), bf16), pltpu.VMEM((LANES, packed), f32), pltpu.VMEM((packed, LANES), f32)]
    arguments = (q, k, v, d_heads, mixed, norm, cosine, sine)
    came_x, came_y = hop(first_x, 2), hop(first_y, 4)
    qk_first, dv_first = pl.pallas_call(
        partial(attend_back_kernel, 0),
        grid=(1,),
        in_specs=back_specs(0),
        out_specs=[whole(packed, LANES), whole(packed, LANES)],
        out_shape=[shape(packed, LANES)] * 2,
        scratch_shapes=back_scratch,
        compiler_params=params(60),
        cost_estimate=FREE,
        name="attend_back_first",
    )(*arguments)
    d_first = lax.all_to_all(qk_first.reshape(shards, rows, LANES), "shard", split_axis=0, concat_axis=0, tiled=True)
    second, d_own, gb_qkv = pl.pallas_call(
        partial(attend_back_kernel, 1),
        grid=(1,),
        in_specs=back_specs(1) + [whole(packed, LANES)] * 2,
        out_specs=[whole(packed, 2 * LANES), whole(packed, 3 * LANES), whole(3, LANES)],
        out_shape=[shape(packed, 2 * LANES), shape(packed, 3 * LANES), shape(3, LANES, kind=f32)],
        scratch_shapes=back_scratch,
        compiler_params=params(60),
        cost_estimate=FREE,
        name="attend_back_second",
    )(*arguments, qk_first, dv_first)
    second = after(second, came_x, came_y)
    piece = (1, *half[2:])
    farther = pl.BlockSpec((1, *piece), lambda i: (1, i, 0, 0))
    next_y, next_x = pl.pallas_call(
        add_kernel,
        grid=(groups,),
        in_specs=[farther] * 4,
        out_specs=[pl.BlockSpec(piece, lambda i: (i, 0, 0))] * 2,
        out_shape=[shape(*half[1:])] * 2,
        compiler_params=params(60),
        cost_estimate=FREE,
        name="add",
    )(own_x, came_x, own_y, came_y)
    g_send = pl.pallas_call(
        qkv_grad_kernel,
        grid=(1,),
        in_specs=[whole(packed, D), whole(packed, 3 * LANES)],
        out_specs=whole(shards, depth, 3 * LANES),
        out_shape=shape(shards, depth, 3 * LANES),
        compiler_params=params(60),
        cost_estimate=FREE,
        name="qkv_grad",
    )(h1_all, after(d_own, next_y, next_x, d_first))
    d_second = lax.all_to_all(second.reshape(shards, rows, 2 * LANES), "shard", split_axis=0, concat_axis=0, tiled=True)
    next_y, next_x = hop(next_y, 4), hop(next_x, 2)
    d_second = after(d_second, g_send)
    w_all = lax.all_gather(after(w_heads, q), "shard", axis=0)
    by_shard = lambda *dims: pl.BlockSpec((1, *dims), lambda i: (i, 0, 0))
    grad_frames, slots_qkv = pl.pallas_call(
        input_grad_kernel,
        grid=(1,),
        in_specs=[
            smem, smem, whole(shards, rows, LANES), whole(shards, rows, 2 * LANES), pl.BlockSpec(memory_space=pl.ANY),
            whole(rows, D), whole(rows, D), whole(steps, 2 * D),
        ],
        out_specs=[whole(rows, D), whole(8, D)],
        out_shape=[shape(rows, D, kind=f32), shape(8, D, kind=f32)],
        scratch_shapes=[pltpu.VMEM((shards, D, 3 * LANES), bf16), pltpu.SemaphoreType.DMA((shards,))],
        compiler_params=params(60),
        cost_estimate=FREE,
        name="input_grad",
    )(base, seg_all, d_first, d_second, w_all, frames, dx1, table[:, : 2 * D])

    g_came = lax.all_to_all(after(g_send, slots_qkv), "shard", split_axis=0, concat_axis=0, tiled=True)

    d_slot = jnp.concatenate((slots_qkv[:6], slots_ff), axis=0).reshape(6, 3, D).transpose(1, 0, 2).reshape(3, 6 * D)
    row_sums = jnp.concatenate((gb_qkv.reshape(-1), gb_out[0], gb_up[0], gb_down[0]))
    sum_rows = -(-row_sums.shape[0] // (6 * D))
    row_sums = jnp.pad(row_sums, (0, sum_rows * 6 * D - row_sums.shape[0])).reshape(sum_rows, 6 * D)
    next_y, next_x = after(next_y, slots_qkv), after(next_x, slots_qkv)
    nearer = whole(1, *half[1:])
    totals = pl.pallas_call(
        total_kernel,
        grid=(1,),
        in_specs=[nearer, nearer, whole(*half[1:])] * 2,
        out_specs=[whole(5 * LANES, wide)] * groups,
        out_shape=[shape(5 * LANES, wide)] * groups,
        compiler_params=params(60),
        cost_estimate=FREE,
        name="total",
    )(own_x, came_x, next_y, own_y, came_y, next_x)
    tail = after(jnp.concatenate((d_slot, row_sums), axis=0), totals[0])
    tail = lax.all_gather(tail, "shard", axis=0)
    totals = trade(totals, "grp", groups)
    tail = after(tail, g_came, *totals)
    parts = pl.pallas_call(
        collect_kernel,
        grid=(1,),
        in_specs=[smem, smem, whole(shards, 4, 6 * D)],
        out_specs=whole(groups, 8, mod_wide + 2 * LANES),
        out_shape=shape(groups, 8, mod_wide + 2 * LANES, kind=f32),
        scratch_shapes=[pltpu.VMEM((8, 6 * D), f32), pltpu.VMEM((1, 4 * D), f32)],
        compiler_params=params(60),
        cost_estimate=FREE,
        name="collect",
    )(base, seg_all, tail)
    g_down, g_out, g_up = pl.pallas_call(
        last_sum_kernel,
        grid=(1,),
        in_specs=[whole(5 * LANES, wide)] * groups,
        out_specs=[whole(2 * LANES, wide), whole(LANES, wide), whole(LANES, 2 * wide)],
        out_shape=[shape(2 * LANES, wide, kind=f32), shape(LANES, wide, kind=f32), shape(LANES, 2 * wide, kind=f32)],
        compiler_params=params(60),
        cost_estimate=FREE,
        name="last_sum",
    )(*totals)
    parts = lax.all_to_all(parts, "grp", split_axis=0, concat_axis=0, tiled=True)
    pieces = pl.pallas_call(
        qkv_piece_kernel,
        grid=(1,),
        in_specs=[smem, whole(shards, depth, 3 * LANES)],
        out_specs=[whole(depth, units * LANES)] * groups,
        out_shape=[shape(depth, units * LANES)] * groups,
        compiler_params=params(60),
        cost_estimate=FREE,
        name="qkv_pieces",
    )(group.astype(jnp.int32).reshape(1), after(g_came, tail))
    g_qkv = pl.pallas_call(
        qkv_sum_kernel,
        grid=(1,),
        in_specs=[whole(depth, units * LANES)] * groups,
        out_specs=whole(depth, units * LANES),
        out_shape=shape(depth, units * LANES, kind=f32),
        compiler_params=params(60),
        cost_estimate=FREE,
        name="qkv_sum",
    )(*trade(pieces, "grp", groups))
    table_own = lax.dynamic_slice_in_dim(time_table, shard * depth, depth, 1)
    g_ada, g_table, *sums = pl.pallas_call(
        table_kernel,
        grid=(1,),
        in_specs=[whole(groups, 8, mod_wide + 2 * LANES), whole(steps, depth), whole(depth, mod_wide), whole(steps, depth)],
        out_specs=[whole(depth, mod_wide), whole(steps, depth)] + [whole(1, size) for size in sizes],
        out_shape=[shape(depth, mod_wide, kind=f32), shape(steps, depth, kind=f32)]
        + [shape(1, size, kind=f32) for size in sizes],
        compiler_params=params(60),
        cost_estimate=FREE,
        name="table",
    )(parts, act_own, w_ada, table_own)
    gb_ada, gb_qkv, gb_out, gb_up, gb_down = [total.reshape(-1) for total in sums]
    g_table = jnp.broadcast_to(g_table[None], (groups,) + g_table.shape)
    g_table = jnp.sum(lax.all_to_all(g_table, "grp", split_axis=0, concat_axis=0, tiled=True), axis=0)
    return (
        out, grad_frames, g_table, g_ada, gb_ada, g_qkv, gb_qkv, g_out, gb_out, g_up, gb_up, g_down, gb_down,
    )


def solution(mesh):
    in_specs = (
        P(("grp", "shard"), None),
        P(("grp", "shard"), None),
        P(("grp", "shard"), None),
        P(("grp", "shard"), None),
        P(("grp", "shard"), None),
        P(),
        P("shard", "grp"),
        P("shard"),
        P("shard", "grp"),
        P("shard"),
        P("shard", "grp"),
        P("shard"),
        P("shard", "grp"),
        P("shard"),
        P("shard", "grp"),
        P("shard"),
    )
    out_specs = (
        P(("grp", "shard"), None),
        P(("grp", "shard"), None),
        P(None, "shard"),
        P("shard", "grp"),
        P("shard"),
        P("shard", "grp"),
        P("shard"),
        P("shard", "grp"),
        P("shard"),
        P("shard", "grp"),
        P("shard"),
        P("shard", "grp"),
        P("shard"),
    )
    by_heads = mesh.shape["shard"] * 2 * HD == D and mesh.shape["grp"] == 4
    local = partial(local_heads, mesh.shape["grp"], mesh.shape["shard"]) if by_heads else local_any
    return jax.shard_map(local, mesh=mesh, in_specs=in_specs, out_specs=out_specs, check_vma=False)
```

```python
from functools import partial

import jax
import jax.numpy as jnp
from jax import lax
from jax.experimental import pallas as pl
from jax.experimental.pallas import tpu as pltpu
from jax.sharding import PartitionSpec as P

D = 1024
H = 16
HD = 64


eps_norm = 1e-06
top_precision = lax.Precision.HIGHEST


def normalize(tensor):
    centred = tensor - jnp.mean(tensor, axis=-1, keepdims=True)
    return centred * lax.rsqrt(jnp.mean(centred * centred, axis=-1, keepdims=True) + eps_norm)


def modulate(tensor, scale_vec, shift_vec):
    return normalize(tensor) * (1.0 + scale_vec) + shift_vec


def angles(positions):
    half_width = HD // 2
    inverse = 10000.0 ** (-jnp.arange(half_width, dtype=jnp.float32) / half_width)
    phase_grid = positions[:, None] * inverse[None, :]
    return (jnp.cos(phase_grid), jnp.sin(phase_grid))


def rotate(tensor, cosine_vals, sine_vals):
    row_total = tensor.shape[0]
    halves = tensor.reshape(row_total, H, 2, HD // 2)
    former = halves[:, :, 0]
    latter = halves[:, :, 1]
    cosine_part = cosine_vals[:, None, :]
    sine_part = sine_vals[:, None, :]
    turned = jnp.stack(
        (former * cosine_part - latter * sine_part, latter * cosine_part + former * sine_part),
        axis=2,
    )
    return turned.reshape(row_total, D)


def tile_width(row_total):
    for candidate in (512, 256, 128):
        return candidate
    return row_total


def head_view(tensor):
    return tensor.reshape(tensor.shape[0], H, HD)


def local_any(
    frames,
    cotangent,
    seg_start,
    seg_length,
    seg_step,
    time_table,
    w_ada,
    b_ada,
    w_qkv,
    b_qkv,
    w_out,
    b_out,
    w_up,
    b_up,
    w_down,
    b_down,
):
    frame_rows = frames.shape[0]
    positions = lax.axis_index("shard") * frame_rows + jnp.arange(frame_rows, dtype=jnp.int32)
    slot_start = seg_start[0]
    slot_end = slot_start + seg_length[0]
    member_mask = (positions[:, None] >= slot_start[None, :]) & (
        positions[:, None] < slot_end[None, :]
    )
    member = member_mask.astype(jnp.float32)
    seg_low = jnp.sum(jnp.where(member_mask, slot_start[None, :], 0), axis=1)
    seg_high = jnp.sum(jnp.where(member_mask, slot_end[None, :], 0), axis=1)
    cosine_vals, sine_vals = angles((positions - seg_low).astype(jnp.float32))
    columns = (
        lax.all_gather(w_ada, "grp", axis=1, tiled=True),
        lax.all_gather(w_qkv, "grp", axis=1, tiled=True),
        lax.all_gather(w_out, "grp", axis=1, tiled=True),
        lax.all_gather(w_up, "grp", axis=1, tiled=True),
        lax.all_gather(w_down, "grp", axis=1, tiled=True),
    )
    gathered = (
        lax.all_gather(columns[0], "shard", axis=0, tiled=True),
        lax.all_gather(columns[1], "shard", axis=0, tiled=True),
        lax.all_gather(columns[2], "shard", axis=0, tiled=True),
        lax.all_gather(columns[3], "shard", axis=0, tiled=True),
        lax.all_gather(columns[4], "shard", axis=0, tiled=True),
        lax.all_gather(b_ada, "shard", axis=0, tiled=True),
        lax.all_gather(b_qkv, "shard", axis=0, tiled=True),
        lax.all_gather(b_out, "shard", axis=0, tiled=True),
        lax.all_gather(b_up, "shard", axis=0, tiled=True),
        lax.all_gather(b_down, "shard", axis=0, tiled=True),
    )
    ada_full, qkv_full, out_full, up_full, down_full = (
        gathered[0],
        gathered[1],
        gathered[2],
        gathered[3],
        gathered[4],
    )
    ada_bias, qkv_bias, out_bias, up_bias, down_bias = [
        bias_row.astype(jnp.float32) for bias_row in gathered[5:]
    ]
    step_onehot = (
        seg_step[0][:, None] == jnp.arange(time_table.shape[0], dtype=jnp.int32)[None, :]
    ).astype(jnp.float32)
    time_rows = jnp.dot(step_onehot, time_table, precision=top_precision)
    activated = jax.nn.silu(time_rows).astype(jnp.bfloat16)
    modulation = jnp.dot(activated, ada_full, preferred_element_type=jnp.float32) + ada_bias
    frame_mod = jnp.dot(member, modulation, precision=top_precision)
    shift_attn, scale_attn, gate_attn, shift_ff, scale_ff, gate_ff = jnp.split(frame_mod, 6, axis=1)
    inputs = frames.astype(jnp.float32)
    hidden_attn = modulate(inputs, scale_attn, shift_attn).astype(jnp.bfloat16)
    projected = jnp.dot(hidden_attn, qkv_full, preferred_element_type=jnp.float32) + qkv_bias
    queries = rotate(projected[:, :D], cosine_vals, sine_vals).astype(jnp.bfloat16)
    keys_rot = rotate(projected[:, D : 2 * D], cosine_vals, sine_vals).astype(jnp.bfloat16)
    values = projected[:, 2 * D :].astype(jnp.bfloat16)
    query_heads = head_view(queries)
    key_heads = head_view(keys_rot)
    value_heads = head_view(values)
    zero_heads = jnp.zeros((frame_rows, H, HD), jnp.float32)
    key_piece = lax.all_gather(keys_rot, "shard", axis=0, tiled=True)
    value_piece = lax.all_gather(values, "shard", axis=0, tiled=True)
    piece_rows = key_piece.shape[0]
    tile_rows = tile_width(piece_rows)
    tiles = piece_rows // tile_rows

    def tile_step(partial_sums, tile_item):
        key_tile, value_tile, offset = tile_item
        key_pos = offset + jnp.arange(tile_rows, dtype=jnp.int32)
        inside = (key_pos[None, :] >= seg_low[:, None]) & (key_pos[None, :] < seg_high[:, None])
        scores = 0.125 * jnp.einsum(
            "rhd,khd->hrk", query_heads, head_view(key_tile), preferred_element_type=jnp.float32
        )
        expo = jnp.where(inside[None], jnp.exp(scores), 0.0)
        numerator, denominator = partial_sums
        numerator = numerator + jnp.einsum(
            "hrk,khd->rhd",
            expo.astype(jnp.bfloat16),
            head_view(value_tile),
            preferred_element_type=jnp.float32,
        )
        denominator = denominator + jnp.sum(expo, axis=2).T
        return ((numerator, denominator), None)

    tile_items = (
        key_piece.reshape(tiles, tile_rows, D),
        value_piece.reshape(tiles, tile_rows, D),
        jnp.arange(tiles, dtype=jnp.int32) * tile_rows,
    )
    numerator, denominator = lax.scan(
        tile_step, (zero_heads, jnp.zeros((frame_rows, H), jnp.float32)), tile_items
    )[0]
    mixed = numerator / denominator[:, :, None]
    mixed_low = mixed.reshape(frame_rows, D).astype(jnp.bfloat16)
    attn_branch = jnp.dot(mixed_low, out_full, preferred_element_type=jnp.float32) + out_bias
    after_attn = inputs + gate_attn * attn_branch
    hidden_ff = modulate(after_attn, scale_ff, shift_ff).astype(jnp.bfloat16)
    upward = jnp.dot(hidden_ff, up_full, preferred_element_type=jnp.float32) + up_bias
    activation = jax.nn.gelu(upward, approximate=True).astype(jnp.bfloat16)
    ff_branch = jnp.dot(activation, down_full, preferred_element_type=jnp.float32) + down_bias
    output = (after_attn + gate_ff * ff_branch).astype(jnp.bfloat16)
    columns_back = (
        lax.all_gather(w_ada, "grp", axis=1, tiled=True),
        lax.all_gather(w_qkv, "grp", axis=1, tiled=True),
        lax.all_gather(w_out, "grp", axis=1, tiled=True),
        lax.all_gather(w_up, "grp", axis=1, tiled=True),
        lax.all_gather(w_down, "grp", axis=1, tiled=True),
    )
    gathered_back = (
        lax.all_gather(columns_back[0], "shard", axis=0, tiled=True),
        lax.all_gather(columns_back[1], "shard", axis=0, tiled=True),
        lax.all_gather(columns_back[2], "shard", axis=0, tiled=True),
        lax.all_gather(columns_back[3], "shard", axis=0, tiled=True),
        lax.all_gather(columns_back[4], "shard", axis=0, tiled=True),
    )
    ada_back, qkv_back, out_back, up_back, down_back = (
        gathered_back[0],
        gathered_back[1],
        gathered_back[2],
        gathered_back[3],
        gathered_back[4],
    )
    grad_out = cotangent.astype(jnp.float32)
    d_branch = (gate_ff * grad_out).astype(jnp.bfloat16)
    d_gate_ff = grad_out * ff_branch
    g_down = jnp.dot(activation.T, d_branch, preferred_element_type=jnp.float32)
    gb_down = jnp.sum(d_branch.astype(jnp.float32), axis=0)
    d_activation = jnp.dot(d_branch, down_back.T, preferred_element_type=jnp.float32)
    gelu_pull = jax.vjp(partial(jax.nn.gelu, approximate=True), upward)[1]
    d_upward = gelu_pull(d_activation)[0].astype(jnp.bfloat16)
    g_up = jnp.dot(hidden_ff.T, d_upward, preferred_element_type=jnp.float32)
    gb_up = jnp.sum(d_upward.astype(jnp.float32), axis=0)
    d_hidden_ff = jnp.dot(d_upward, up_back.T, preferred_element_type=jnp.float32)
    ff_pull = jax.vjp(modulate, after_attn, scale_ff, shift_ff)[1]
    dx_ff, d_scale_ff, d_shift_ff = ff_pull(d_hidden_ff)
    d_after = grad_out + dx_ff
    d_attn = (gate_attn * d_after).astype(jnp.bfloat16)
    d_gate_attn = d_after * attn_branch
    g_out = jnp.dot(mixed_low.T, d_attn, preferred_element_type=jnp.float32)
    gb_out = jnp.sum(d_attn.astype(jnp.float32), axis=0)
    d_mixed = jnp.dot(d_attn, out_back.T, preferred_element_type=jnp.float32).astype(jnp.bfloat16)
    d_mixed_heads = head_view(d_mixed).astype(jnp.float32)
    delta = jnp.sum(d_mixed_heads * mixed, axis=2) / denominator
    d_numer = (d_mixed_heads / denominator[:, :, None]).astype(jnp.bfloat16).reshape(frame_rows, D)
    dnum_heads = head_view(d_numer)
    delta_heads = delta.T
    key_piece = lax.all_gather(keys_rot, "shard", axis=0, tiled=True)
    value_piece = lax.all_gather(values, "shard", axis=0, tiled=True)
    piece_rows = key_piece.shape[0]
    fold_tile_rows = tile_width(piece_rows)
    tiles = piece_rows // fold_tile_rows

    def tile_step(grad_sum, tile_item):
        key_tile, value_tile, offset = tile_item
        key_pos = offset + jnp.arange(fold_tile_rows, dtype=jnp.int32)
        inside = (key_pos[None, :] >= seg_low[:, None]) & (key_pos[None, :] < seg_high[:, None])
        scores = 0.125 * jnp.einsum(
            "rhd,khd->hrk", query_heads, head_view(key_tile), preferred_element_type=jnp.float32
        )
        expo = jnp.where(inside[None], jnp.exp(scores), 0.0)
        slope = jnp.einsum(
            "rhd,khd->hrk", dnum_heads, head_view(value_tile), preferred_element_type=jnp.float32
        )
        d_scores = (expo * (slope - delta_heads[:, :, None])).astype(jnp.bfloat16)
        grad_sum = grad_sum + 0.125 * jnp.einsum(
            "hrk,khd->rhd", d_scores, head_view(key_tile), preferred_element_type=jnp.float32
        )
        return (grad_sum, None)

    tile_items = (
        key_piece.reshape(tiles, fold_tile_rows, D),
        value_piece.reshape(tiles, fold_tile_rows, D),
        jnp.arange(tiles, dtype=jnp.int32) * fold_tile_rows,
    )
    d_query = lax.scan(tile_step, zero_heads, tile_items)[0]
    delta_all = lax.all_gather(delta, "shard", axis=0, tiled=True)

    def fold_key_grad(running, piece):
        query_piece, dnum_piece = piece
        piece_rows = query_piece.shape[0]
        tile_rows = tile_width(piece_rows)
        tiles = piece_rows // tile_rows

        def tile_step(grad_pair, tile_item):
            query_tile, dnum_tile, delta_tile, offset = tile_item
            query_pos = offset + jnp.arange(tile_rows, dtype=jnp.int32)
            inside = (query_pos[:, None] >= seg_low[None, :]) & (
                query_pos[:, None] < seg_high[None, :]
            )
            query_tile_heads = head_view(query_tile)
            dnum_tile_heads = head_view(dnum_tile)
            scores = 0.125 * jnp.einsum(
                "qhd,rhd->hqr", query_tile_heads, key_heads, preferred_element_type=jnp.float32
            )
            expo = jnp.where(inside[None], jnp.exp(scores), 0.0)
            slope = jnp.einsum(
                "qhd,rhd->hqr", dnum_tile_heads, value_heads, preferred_element_type=jnp.float32
            )
            d_scores = (expo * (slope - delta_tile.T[:, :, None])).astype(jnp.bfloat16)
            d_keys, d_values = grad_pair
            d_keys = d_keys + 0.125 * jnp.einsum(
                "hqr,qhd->rhd", d_scores, query_tile_heads, preferred_element_type=jnp.float32
            )
            d_values = d_values + jnp.einsum(
                "hqr,qhd->rhd",
                expo.astype(jnp.bfloat16),
                dnum_tile_heads,
                preferred_element_type=jnp.float32,
            )
            return ((d_keys, d_values), None)

        tile_items = (
            query_piece.reshape(tiles, tile_rows, D),
            dnum_piece.reshape(tiles, tile_rows, D),
            delta_all.reshape(tiles, tile_rows, H),
            jnp.arange(tiles, dtype=jnp.int32) * tile_rows,
        )
        return lax.scan(tile_step, running, tile_items)[0]

    d_keys, d_values = fold_key_grad(
        (zero_heads, zero_heads),
        (
            lax.all_gather(queries, "shard", axis=0, tiled=True),
            lax.all_gather(d_numer, "shard", axis=0, tiled=True),
        ),
    )
    grad_query = rotate(d_query.reshape(frame_rows, D), cosine_vals, -sine_vals)
    grad_key = rotate(d_keys.reshape(frame_rows, D), cosine_vals, -sine_vals)
    d_projected = jnp.concatenate(
        (grad_query, grad_key, d_values.reshape(frame_rows, D)), axis=1
    ).astype(jnp.bfloat16)
    g_qkv = jnp.dot(hidden_attn.T, d_projected, preferred_element_type=jnp.float32)
    gb_qkv = jnp.sum(d_projected.astype(jnp.float32), axis=0)
    d_hidden_attn = jnp.dot(d_projected, qkv_back.T, preferred_element_type=jnp.float32)
    attn_pull = jax.vjp(modulate, inputs, scale_attn, shift_attn)[1]
    dx_attn, d_scale_attn, d_shift_attn = attn_pull(d_hidden_attn)
    grad_frames = d_after + dx_attn
    d_frame_mod = jnp.concatenate(
        (d_shift_attn, d_scale_attn, d_gate_attn, d_shift_ff, d_scale_ff, d_gate_ff), axis=1
    )
    d_slot = jnp.dot(member.T, d_frame_mod, precision=top_precision)
    g_ada = jnp.dot(activated.astype(jnp.float32).T, d_slot, precision=top_precision)
    gb_ada = jnp.sum(d_slot, axis=0)
    d_activated = jnp.dot(
        d_slot, ada_back.T, precision=top_precision, preferred_element_type=jnp.float32
    )
    silu_pull = jax.vjp(jax.nn.silu, time_rows)[1]
    d_time_rows = silu_pull(d_activated)[0]
    g_table = jnp.dot(step_onehot.T, d_time_rows, precision=top_precision)
    group_sums = (
        lax.psum_scatter(g_ada, "shard", scatter_dimension=0, tiled=True),
        lax.psum_scatter(g_qkv, "shard", scatter_dimension=0, tiled=True),
        lax.psum_scatter(g_out, "shard", scatter_dimension=0, tiled=True),
        lax.psum_scatter(g_up, "shard", scatter_dimension=0, tiled=True),
        lax.psum_scatter(g_down, "shard", scatter_dimension=0, tiled=True),
        lax.psum_scatter(gb_ada, "shard", scatter_dimension=0, tiled=True),
        lax.psum_scatter(gb_qkv, "shard", scatter_dimension=0, tiled=True),
        lax.psum_scatter(gb_out, "shard", scatter_dimension=0, tiled=True),
        lax.psum_scatter(gb_up, "shard", scatter_dimension=0, tiled=True),
        lax.psum_scatter(gb_down, "shard", scatter_dimension=0, tiled=True),
        lax.psum_scatter(g_table, "shard", scatter_dimension=1, tiled=True),
    )
    wide_sums = (
        lax.psum_scatter(group_sums[0], "grp", scatter_dimension=1, tiled=True),
        lax.psum_scatter(group_sums[1], "grp", scatter_dimension=1, tiled=True),
        lax.psum_scatter(group_sums[2], "grp", scatter_dimension=1, tiled=True),
        lax.psum_scatter(group_sums[3], "grp", scatter_dimension=1, tiled=True),
        lax.psum_scatter(group_sums[4], "grp", scatter_dimension=1, tiled=True),
    )
    small_sums = lax.psum(
        (group_sums[5], group_sums[6], group_sums[7], group_sums[8], group_sums[9], group_sums[10]),
        "grp",
    )
    finals = tuple(wide_sums) + tuple(small_sums)
    return (
        output,
        grad_frames,
        finals[10],
        finals[0],
        finals[5],
        finals[1],
        finals[6],
        finals[2],
        finals[7],
        finals[3],
        finals[8],
        finals[4],
        finals[9],
    )


LANES = 128
FREE = pl.CostEstimate(flops=2**20, bytes_accessed=2**16, transcendentals=0)
CHIPS = (2, 4, 6)
ORDER = (0, 2, 4, 6, 1, 3, 5, 7)
SEPARATE = -(2.0**100)
GELU_C = 0.7978845608028654
GELU_A = 0.044715
NT = (((1,), (1,)), ((), ()))
TN = (((0,), (0,)), ((), ()))
f32 = jnp.float32
bf16 = jnp.bfloat16


def dot(left, right, dims=(((1,), (0,)), ((), ()))):
    return lax.dot_general(left, right, dims, preferred_element_type=f32)


def params(limit_mib, steps=1):
    return pltpu.CompilerParams(
        dimension_semantics=("arbitrary",) * steps, vmem_limit_bytes=limit_mib * 2**20
    )


def moments(value):
    centred = value - jnp.mean(value, axis=1, keepdims=True)
    inv = lax.rsqrt(jnp.mean(centred * centred, axis=1, keepdims=True) + eps_norm)
    return centred * inv, inv


def norm_back(weighted, normal, inv):
    return (
        weighted
        - jnp.mean(weighted, axis=1, keepdims=True)
        - normal * jnp.mean(weighted * normal, axis=1, keepdims=True)
    ) * inv


def swap_halves(value):
    lane = lax.broadcasted_iota(jnp.int32, value.shape, 1)
    return jnp.where(lane % HD < HD // 2, pltpu.roll(value, 96, 1), pltpu.roll(value, 32, 1))


def rotary(cos_ref, sin_ref, here):
    cosine, sine = cos_ref[:, here].T, sin_ref[:, here].T
    return jnp.concatenate([cosine] * 4, axis=1), jnp.concatenate([-sine, sine] * 2, axis=1)


def members(seg_ref, block, rows):
    place = block * rows + lax.broadcasted_iota(jnp.int32, (rows, LANES), 0)
    out = []
    for slot in range(3):
        begin = seg_ref[block, slot]
        out.append((place >= begin) & (place < begin + seg_ref[block, 3 + slot]))
    return out


def mod_rows(table_ref, seg_ref, block, member, part):
    first, second, third = [table_ref[pl.ds(seg_ref[block, 6 + slot], 1), pl.ds(part * D, D)] for slot in range(3)]
    out = []
    for at in range(0, D, LANES):
        here = slice(at, at + LANES)
        out.append(jnp.where(member[0], first[:, here], jnp.where(member[1], second[:, here], third[:, here])))
    return jnp.concatenate(out, axis=1)


def slot_sums(member, value):
    out = []
    for column in member:
        sums = [
            jnp.sum(jnp.where(column, value[:, at : at + LANES], 0.0), axis=0, keepdims=True) for at in range(0, D, LANES)
        ]
        out.append(jnp.concatenate(sums, axis=1))
    return out


def qkv_kernel(order_ref, seg_ref, *refs):
    step = pl.program_id(0)
    last = pl.num_programs(0) - 1
    *pieces, table_ref, w_ref, b_ref, cos_ref, sin_ref, q_ref, k_ref, v_ref, h_ref, x_all, arrived = refs
    block = order_ref[step]
    rows = x_all.shape[1]
    copies, at = [], 0
    for piece in pieces:
        here = x_all.at[at : at + piece.shape[0]]
        copies.append((at, pltpu.make_async_copy(piece, here, arrived.at[len(copies)])))
        at += piece.shape[0]

    @pl.when(step == 0)
    def _():
        for _, copy in copies:
            copy.start()

    for at, copy in copies:

        @pl.when(step == at)
        def _(copy=copy):
            copy.wait()

    member = members(seg_ref, block, rows)
    normal, _ = moments(x_all[step].astype(f32))
    shift = mod_rows(table_ref, seg_ref, block, member, 0)
    scale = mod_rows(table_ref, seg_ref, block, member, 1)
    hidden = (normal * (1.0 + scale) + shift).astype(bf16)
    h_ref[...] = hidden
    projected = dot(hidden, w_ref[...]) + b_ref[...]
    cosine, sine = rotary(cos_ref, sin_ref, slice(None))
    turned = []
    for part in range(2):
        piece = projected[:, part * LANES : (part + 1) * LANES]
        turned.append(piece * cosine + swap_halves(piece) * sine)
    queries = turned[0].astype(bf16).astype(f32) * 0.125
    keys = turned[1]
    values = projected[:, 2 * LANES :]
    lane = lax.broadcasted_iota(jnp.int32, (rows, LANES), 1)
    lane_row = lane[:1]
    begins, ends = jnp.full((1, LANES), 2**30, jnp.int32), jnp.zeros((1, LANES), jnp.int32)
    for index in range(6):
        where, slot = (0, index) if index < 3 else (last, index - 3)
        begin = seg_ref[where, slot]
        begins = jnp.where(lane_row == HD + index, begin, begins)
        ends = jnp.where(lane_row == HD + index, begin + seg_ref[where, 3 + slot], ends)
    place = block * rows + lax.broadcasted_iota(jnp.int32, (rows, LANES), 0)
    inside = (place >= begins) & (place < ends)
    query_extra = jnp.where(inside | (lane >= HD + 6), 0.0, SEPARATE)
    key_extra = jnp.where(inside, 1.0, 0.0)
    value_extra = jnp.where((lane >= HD) & (lane < HD + 3), 1.0, 0.0)
    low = lane < HD
    for head in range(2):
        for ref, value, extra in (
            (q_ref, queries, query_extra),
            (k_ref, keys, key_extra),
            (v_ref, values, value_extra),
        ):
            own = value if head == 0 else pltpu.roll(value, HD, 1)
            ref[head] = jnp.where(low, own, extra).astype(bf16)


def attend_kernel(q_ref, k_ref, v_ref, o_ref, mixed_ref, l_ref):
    keys_in_all = k_ref.shape[1]
    tile = 256
    ratios, sums = [], []
    for head in range(2):
        query = q_ref[head]
        total = None
        for at in range(0, keys_in_all, tile):
            expo = jnp.exp(dot(query, k_ref[head, at : at + tile], NT))
            term = dot(expo.astype(bf16), v_ref[head, at : at + tile])
            total = term if total is None else total + term
        norm = total[:, HD : HD + 1]
        ratios.append(total / norm)
        sums.append(norm)
    lane = lax.broadcasted_iota(jnp.int32, ratios[0].shape, 1)
    mixed = jnp.where(lane < HD, ratios[0], pltpu.roll(ratios[1], HD, 1))
    mixed_ref[...] = mixed
    o_ref[...] = mixed.astype(bf16)
    l_ref[...] = jnp.where(lane < HD, sums[0], sums[1])


def block_kernel(
    order_ref, seg_ref, x_ref, cot_ref, o_ref, table_ref, w_ref, b_out_ref, b_up_ref, b_down_ref,
    out_ref, dx1_ref, do_ref, pair_ref, keep_ref, send_ref, slots_ref, gb_out_ref, gb_up_ref, gb_down_ref,
):
    rows = x_ref.shape[0]
    groups, shards = w_ref.shape[:2]
    block = order_ref[0]
    member = members(seg_ref, block, rows)
    modulation = partial(mod_rows, table_ref, seg_ref, block, member)
    wide = D // groups

    def weight(group, start):
        return w_ref[group, :, start : start + LANES, :].reshape(D, wide)

    def weight_down(group):
        return w_ref[group, :, 0 : 2 * LANES, :].reshape(2 * D, wide)

    def by_core(value, width, other):
        parts = [value[:, at : at + width] for at in range(0, value.shape[1], width)]
        even, odd = jnp.concatenate(parts[0::2], axis=1), jnp.concatenate(parts[1::2], axis=1)
        return jnp.where((block % 2 == 0) != other, even, odd)

    def share(start, value, width):
        half = value.shape[1] // 2
        keep_ref[:, start : start + half] = by_core(value, width, False)
        send_ref[:, start : start + half] = by_core(value, width, True)

    mixed = jnp.concatenate([o_ref[shard] for shard in range(shards)], axis=1)
    share(D, mixed, LANES)
    attn = jnp.concatenate([dot(mixed, weight(group, 256)) for group in range(groups)], axis=1)
    attn = attn + b_out_ref[...]
    gate1 = modulation(2)
    after = x_ref[...].astype(f32) + gate1 * attn
    normal, inv = moments(after)
    scale2 = 1.0 + modulation(4)
    hidden = (normal * scale2 + modulation(3)).astype(bf16)
    share(D + D // 2, hidden, LANES)
    up = [dot(hidden, weight(group, start)) for group in range(groups) for start in (384, 512)]
    up = jnp.concatenate(up, axis=1) + b_up_ref[...]
    inner = jnp.tanh(GELU_C * (up + GELU_A * (up * up * up)))
    act = (0.5 * up * (1.0 + inner)).astype(bf16)
    share(0, act, 2 * LANES)
    slope = 0.5 * (1.0 + inner) + (0.5 * GELU_C) * up * (1.0 - inner * inner) * (
        1.0 + (3.0 * GELU_A) * up * up
    )
    branch = jnp.concatenate([dot(act, weight_down(group)) for group in range(groups)], axis=1)
    branch = branch + b_down_ref[...]
    gate2 = modulation(5)
    out_ref[...] = (after + gate2 * branch).astype(bf16)

    cot = cot_ref[...].astype(f32)
    dff = (gate2 * cot).astype(bf16)
    pair_ref[:, 0:D] = dff
    gb_down_ref[...] = jnp.sum(dff.astype(f32), axis=0, keepdims=True)
    d_gate2 = slot_sums(member, cot * branch)
    d_act = sum(dot(dff[:, g * wide : (g + 1) * wide], weight_down(g), NT) for g in range(groups))
    du = (d_act * slope).astype(bf16)
    pair_ref[:, 2 * D :] = du
    gb_up_ref[...] = jnp.sum(du.astype(f32), axis=0, keepdims=True)
    d_hidden = None
    for index in range(2 * groups):
        piece = du[:, index * wide : (index + 1) * wide]
        term = dot(piece, weight(index // 2, 384 + LANES * (index % 2)), NT)
        d_hidden = term if d_hidden is None else d_hidden + term
    d_shift2 = slot_sums(member, d_hidden)
    d_scale2 = slot_sums(member, d_hidden * normal)
    d_after = cot + norm_back(d_hidden * scale2, normal, inv)
    dx1_ref[...] = d_after
    d_gate1 = slot_sums(member, d_after * attn)
    da = (gate1 * d_after).astype(bf16)
    pair_ref[:, D : 2 * D] = da
    gb_out_ref[...] = jnp.sum(da.astype(f32), axis=0, keepdims=True)
    d_mixed = sum(dot(da[:, g * wide : (g + 1) * wide], weight(g, 256), NT) for g in range(groups))
    d_mixed = d_mixed.astype(bf16)
    for shard in range(shards):
        do_ref[shard] = d_mixed[:, shard * LANES : (shard + 1) * LANES]
    slots_ref[...] = jnp.concatenate(d_gate1 + d_shift2 + d_scale2 + d_gate2, axis=0)


def weight_grad_kernel(
    order_ref, group_ref, keep_ref, send_ref, pair_ref, pair2_ref, first_x, first_y, own_x, own_y
):
    groups, half, wide = first_x.shape[1:]

    def product(at, width, start, stop):
        here = pl.ds(pl.multiple_of(at, LANES), width)
        return (
            dot(keep_ref[:, here], pair_ref[:, start:stop], TN) + dot(send_ref[:, here], pair2_ref[:, start:stop], TN)
        ).astype(bf16)

    places = (((own_x, 0), (own_y, 0)), ((first_x, 0), (own_y, 1)), ((own_x, 1), (first_y, 0)), ((first_x, 1), (first_y, 1)))
    for index in range(4):
        chip = order_ref[index] // 2
        down = product(chip * 2 * LANES, 2 * LANES, 0, D)
        out = product(D + chip * LANES, LANES, D, 2 * D)
        up = product(D + D // 2 + chip * LANES, LANES, 2 * D, 4 * D)
        (by_x, at_x), (by_y, at_y) = places[index]
        for group in range(groups):
            to = (group + groups - group_ref[0]) % groups
            columns = slice(group * wide, (group + 1) * wide)
            by_x[at_x, to, 0:256, :] = down[:, columns]
            by_x[at_x, to, 256:half, :] = out[: half - 256, columns]
            by_y[at_y, to, 0 : 384 - half, :] = out[half - 256 :, columns]
            for part in range(2):
                start = 384 - half + 128 * part
                at = (2 * group + part) * wide
                by_y[at_y, to, start : start + 128, :] = up[:, at : at + wide]


def attend_back_kernel(head, q_ref, k_ref, v_ref, do_ref, mixed_ref, l_ref, cos_ref, sin_ref, *refs):
    *refs, dn, dq_t, dk_all = refs
    if head == 0:
        qk_ref, dv_ref = refs
    else:
        qk_first, dv_first, second_ref, own_ref, gb_ref = refs
        qk_ref = second_ref.at[:, :LANES]
    step = pl.program_id(0)
    rows = k_ref.shape[1]
    frames = q_ref.shape[1]
    tile = 256
    lane = lax.broadcasted_iota(jnp.int32, (rows, LANES), 1)
    low = lane < HD

    @pl.when(step == 0)
    def _():
        dq_t[...] = jnp.zeros_like(dq_t)
        for at in range(0, frames, rows):
            here = slice(at, at + rows)
            d_out = do_ref[here].astype(f32)
            norm = l_ref[here]
            d_num = (d_out / norm).astype(bf16).astype(f32)
            mine = low if head == 0 else ~low
            total = jnp.sum(jnp.where(mine, d_out * mixed_ref[here], 0.0), axis=1, keepdims=True)
            delta = -total / norm[:, head * HD : head * HD + 1]
            first = delta.astype(bf16).astype(f32)
            second = (delta - first).astype(bf16).astype(f32)
            third = delta - first - second
            extra = jnp.where(lane == HD, first, jnp.where(lane == HD + 1, second, third))
            extra = jnp.where(lane < HD + 3, extra, 0.0)
            own = d_num if head == 0 else pltpu.roll(d_num, HD, 1)
            dn[here] = jnp.where(low, own, extra).astype(bf16)

    key, value = k_ref[0], v_ref[0]
    key_t = key.T
    dk_total, dv_total = None, None
    for at in range(0, frames, tile):
        here = slice(at, at + tile)
        query, d_num = q_ref[0, here], dn[here]
        expo = jnp.exp(dot(key, query, NT))
        d_score = (expo * dot(value, d_num, NT)).astype(bf16)
        dk_term = dot(d_score, query)
        dv_term = dot(expo.astype(bf16), d_num)
        dk_total = dk_term if dk_total is None else dk_total + dk_term
        dv_total = dv_term if dv_total is None else dv_total + dv_term
        dq_t[:, here] += dot(key_t, d_score)

    here = pl.ds(pl.multiple_of(step * rows, rows), rows)
    dk_all[here] = dk_total
    if head == 0:
        dv_ref[here] = dv_total.astype(bf16)
    else:
        both = jnp.where(low, dv_first[here].astype(f32), pltpu.roll(dv_total, HD, 1)).astype(bf16)
        own_ref[here, 2 * LANES :] = both
        second_ref[here, LANES:] = both

    @pl.when(step == pl.num_programs(0) - 1)
    def _():
        for at in range(0, frames, rows):
            part = slice(at, at + rows)
            cosine, sine = rotary(cos_ref, sin_ref, part)
            both = jnp.where(low, 0.125 * dq_t[:, part].T, pltpu.roll(dk_all[part], HD, 1))
            both = (both * cosine - swap_halves(both) * sine).astype(bf16)
            qk_ref[part] = both
            if head == 1:
                first, second = qk_first[part].astype(f32), both.astype(f32)
                own_ref[part, 0:LANES] = jnp.where(low, first, pltpu.roll(second, HD, 1)).astype(bf16)
                own_ref[part, LANES : 2 * LANES] = jnp.where(low, pltpu.roll(first, HD, 1), second).astype(bf16)
        if head == 1:
            ones = jnp.ones((8, frames), bf16)
            sums = dot(ones, own_ref[...])[0:1]
            for index in range(3):
                gb_ref[index : index + 1] = sums[:, index * LANES : (index + 1) * LANES]


def input_grad_kernel(
    base_ref, seg_ref, first_ref, second_ref, w_ref, x_ref, dx1_ref, table_ref, grad_ref, slots_ref, w_all, arrived
):
    shards, rows = first_ref.shape[:2]
    copies = [pltpu.make_async_copy(w_ref.at[shard], w_all.at[shard], arrived.at[shard]) for shard in range(shards)]
    for copy in copies:
        copy.start()
    block = base_ref[0]
    member = members(seg_ref, block, rows)
    scale = 1.0 + mod_rows(table_ref, seg_ref, block, member, 1)
    normal, inv = moments(x_ref[...].astype(f32))
    low = lax.broadcasted_iota(jnp.int32, (rows, LANES), 1) < HD
    d_hidden = None
    for shard in range(shards):
        first, second = first_ref[shard].astype(f32), second_ref[shard, :, :LANES].astype(f32)
        queries = jnp.where(low, first, pltpu.roll(second, HD, 1)).astype(bf16)
        keys = jnp.where(low, pltpu.roll(first, HD, 1), second).astype(bf16)
        whole_row = jnp.concatenate([queries, keys, second_ref[shard, :, LANES:]], axis=1)
        copies[shard].wait()
        term = dot(whole_row, w_all[shard], NT)
        d_hidden = term if d_hidden is None else d_hidden + term
    grad_ref[...] = dx1_ref[...] + norm_back(d_hidden * scale, normal, inv)
    sums = slot_sums(member, d_hidden) + slot_sums(member, d_hidden * normal)
    slots_ref[...] = jnp.concatenate(sums + [jnp.zeros((2, D), f32)], axis=0)


def add_kernel(own_x, came_x, own_y, came_y, by_y, by_x):
    by_y[...] = (own_x[0].astype(f32) + came_x[0].astype(f32)).astype(bf16)
    by_x[...] = (own_y[0].astype(f32) + came_y[0].astype(f32)).astype(bf16)


def total_kernel(own_x, came_x, by_y, own_y, came_y, by_x, *out_refs):
    half = by_y.shape[1]
    for group, ref in enumerate(out_refs):
        first = own_x[0, group].astype(f32) + came_x[0, group].astype(f32) + by_y[group].astype(f32)
        second = own_y[0, group].astype(f32) + came_y[0, group].astype(f32) + by_x[group].astype(f32)
        ref[:half] = first.astype(bf16)
        ref[half:] = second.astype(bf16)


def last_sum_kernel(*refs):
    *pieces, down_ref, out_ref, up_ref = refs
    total = sum(piece[...].astype(f32) for piece in pieces)
    wide = total.shape[1]
    down_ref[...] = total[: 2 * LANES]
    out_ref[...] = total[2 * LANES : 3 * LANES]
    up_ref[:, :wide] = total[3 * LANES : 4 * LANES]
    up_ref[:, wide:] = total[4 * LANES :]


def qkv_grad_kernel(h_ref, d_ref, out_ref):
    shards, depth = out_ref.shape[:2]
    for shard in range(shards):
        out_ref[shard] = dot(h_ref[:, shard * depth : (shard + 1) * depth], d_ref[...], TN).astype(bf16)


def qkv_piece_kernel(group_ref, came_ref, *out_refs):
    shards = came_ref.shape[0]
    units = 3 * shards // len(out_refs)
    for group, ref in enumerate(out_refs):
        start = lax.rem(group_ref[0] + group, len(out_refs)) * units
        for unit in range(units):
            part = pl.ds(pl.multiple_of((start + unit) // shards * LANES, LANES), LANES)
            ref[:, unit * LANES : (unit + 1) * LANES] = came_ref[lax.rem(start + unit, shards), :, part]


def qkv_sum_kernel(*refs):
    refs[-1][...] = sum(piece[...].astype(f32) for piece in refs[:-1])


def collect_kernel(shard_ref, seg_ref, tail_ref, out_ref, rows_ref, others_ref):
    shards = tail_ref.shape[0]
    groups = out_ref.shape[0]
    wide = out_ref.shape[2] - 2 * LANES
    shard = shard_ref[0]
    rows_ref[0:3] = tail_ref[0, 0:3]
    rows_ref[3:6] = tail_ref[shards - 1, 0:3]
    middle = sum(tail_ref[index, 0:3] for index in range(1, shards - 1))
    rows_ref[6:7] = jnp.sum(middle, axis=0, keepdims=True)
    rows_ref[7:8] = jnp.zeros((1, rows_ref.shape[1]), f32)
    others_ref[...] = sum(tail_ref[index, 3:4, 3 * LANES : 3 * LANES + 4 * D] for index in range(shards))

    def own(start, size):
        return pl.ds(pl.multiple_of(start + shard * size, LANES), size)

    sums = [jnp.sum(rows_ref[:, own(0, 6 * D // shards)], axis=0, keepdims=True)]
    for index in range(3 * D // shards // LANES):
        chunk = shard * (3 * D // shards // LANES) + index
        part = pl.ds(pl.multiple_of(chunk // shards * LANES, LANES), LANES)
        sums.append(tail_ref[lax.rem(chunk, shards), 3:4, part])
    sums += [others_ref[:, own(0, D // shards)], others_ref[:, own(D, 2 * D // shards)]]
    lane = lax.broadcasted_iota(jnp.int32, (1, LANES), 1)
    ids = jnp.zeros((1, LANES), jnp.int32)
    for index in range(6):
        where, slot = (0, index) if index < 3 else (shards - 1, index - 3)
        ids = jnp.where(lane == index, seg_ref[where, 6 + slot], ids)
    ids = jnp.where(lane == 6, seg_ref[1, 6] + seg_ref[1, 7] + seg_ref[1, 8], ids)
    rows_ref[7:8, 0:wide] = jnp.concatenate(sums, axis=1)
    for group in range(groups):
        out_ref[group, 0:7, 0:wide] = rows_ref[0:7, group * wide : (group + 1) * wide]
        out_ref[group, 7:8, 0:wide] = rows_ref[7:8, 0:wide]
        out_ref[group, :, wide:] = jnp.zeros((8, 2 * LANES), f32)
        out_ref[group, 0:1, wide : wide + LANES] = others_ref[:, own(3 * D, D // shards)]
        out_ref[group, 0:1, wide + LANES :] = ids.astype(f32)


def three(value):
    first = value.astype(bf16)
    second = (value - first.astype(f32)).astype(bf16)
    return [first, second, (value - first.astype(f32) - second.astype(f32)).astype(bf16)]


def table_kernel(*refs):
    all_parts, act_ref, w_ref, time_ref, ada_ref, time_grad_ref, b_ada, b_qkv, b_out, b_up, b_down = refs
    steps, wide = time_ref.shape[0], w_ref.shape[1]
    parts = [all_parts.at[index] for index in range(all_parts.shape[0])]
    step = lax.broadcasted_iota(jnp.int32, (steps, 1), 0)
    total = jnp.zeros((steps, wide), f32)
    for part in parts:
        for row in range(7):
            at = wide + LANES + row
            picked = part[0:1, at : at + 1].astype(jnp.int32) == step
            total = total + jnp.where(picked, part[row : row + 1, :wide], 0.0)
    pieces = three(total)
    act = act_ref[...]
    ada_ref[...] = dot(jnp.concatenate([act] * 3, axis=0), jnp.concatenate(pieces, axis=0), TN)
    d_act = dot(jnp.concatenate(pieces, axis=0), w_ref[...], NT)
    d_act = d_act[:steps] + d_act[steps : 2 * steps] + d_act[2 * steps :]
    value = time_ref[...]
    gate = 1.0 / (1.0 + jnp.exp(-value))
    for group in range(time_grad_ref.shape[0]):
        time_grad_ref[group] = d_act * gate * (1.0 + value * (1.0 - gate))
    first_row = sum(part[7:8, :wide] for part in parts)
    at = 0
    for ref in (b_ada, b_qkv, b_out, b_up):
        ref[...] = first_row[:, at : at + ref.shape[1]]
        at += ref.shape[1]
    b_down[...] = sum(part[0:1, wide : wide + b_down.shape[1]] for part in parts)


def spread(value, axis, size):
    return [value] + [
        lax.ppermute(value, axis, [(i, (i - step) % size) for i in range(size)]) for step in range(1, size)
    ]


def trade(pieces, axis, size):
    return [pieces[0]] + [
        lax.ppermute(pieces[size - step], axis, [(i, (i - step) % size) for i in range(size)])
        for step in range(1, size)
    ]


def in_order(pieces, axis, size):
    own = lax.axis_index(axis)
    out = []
    for place in range(size):
        pick = (place - own) % size
        value = pieces[0]
        for index in range(1, size):
            value = jnp.where(pick == index, pieces[index], value)
        out.append(value)
    return out


def hop(value, step):
    return lax.ppermute(value, "shard", [(i, i ^ step) for i in range(8)])


def after(value, *others):
    return pl.pallas_call(
        lambda *refs: None,
        in_specs=[anywhere] * (1 + len(others)),
        out_specs=anywhere,
        out_shape=jax.ShapeDtypeStruct(value.shape, value.dtype),
        input_output_aliases={0: 0},
        cost_estimate=FREE,
        name="after",
    )(value, *others)


anywhere = pl.BlockSpec(memory_space=pl.ANY)


def behind(kernel, count):
    return lambda *refs: kernel(*refs[count:])


def shape(*dims, kind=bf16):
    return jax.ShapeDtypeStruct(dims, kind)


def whole(*dims):
    return pl.BlockSpec(dims, lambda *_: (0,) * len(dims))


smem = pl.BlockSpec(memory_space=pltpu.SMEM)


def local_heads(
    groups, shards, frames, cotangent, seg_start, seg_length, seg_step, time_table,
    w_ada, b_ada, w_qkv, b_qkv, w_out, b_out, w_up, b_up, w_down, b_down,
):
    rows = frames.shape[0]
    packed = rows * shards
    steps = time_table.shape[0]
    shard = lax.axis_index("shard")
    depth = D // shards
    wide = D // groups

    group = lax.axis_index("grp")
    order = shard ^ jnp.array(ORDER, jnp.int32)

    inverse = 10000.0 ** (-jnp.arange(HD // 2, dtype=f32) / (HD // 2))
    phase = inverse[:, None] * jnp.arange(packed, dtype=f32)[None, :]
    cosine, sine = jnp.cos(phase), jnp.sin(phase)

    activated = jax.nn.silu(time_table).astype(bf16)
    act_own = lax.dynamic_slice_in_dim(activated, shard * depth, depth, 1)
    partial_mod = dot(act_own, w_ada)
    mod_wide = partial_mod.shape[1]
    biases = [b.astype(f32) for b in (b_ada, b_qkv, b_out, b_up, b_down)]
    sizes = [b.shape[0] for b in biases]
    segs = jnp.concatenate((seg_start, seg_length, seg_step), axis=1).astype(f32)
    extra = jnp.concatenate(biases + [jnp.floor(segs[0] / 128.0), segs[0] % 128.0])
    extra_rows = -(-extra.shape[0] // mod_wide)
    extra = jnp.pad(extra, (0, extra_rows * mod_wide - extra.shape[0])).reshape(extra_rows, mod_wide)
    units = 3 * shards // groups
    first = group * units
    by_unit = w_qkv.reshape(depth, units, LANES).transpose(1, 0, 2)
    which = jnp.minimum((jnp.arange(shards) - first) % shards, units - 1)
    by_shard = jnp.take(by_unit, which, axis=0, mode="clip")
    w_cols = jnp.broadcast_to(by_shard[None], (groups, shards, depth, LANES)).reshape(groups * shards, depth, LANES)
    w_cols = lax.all_to_all(w_cols, ("grp", "shard"), split_axis=0, concat_axis=0, tiled=True).reshape(groups, D, LANES)
    small = jnp.concatenate((partial_mod, extra), axis=0).astype(bf16)
    small = lax.all_gather(small, "shard", axis=0).astype(f32)
    held = after(frames, small)
    chips = [frames, hop(frames, 2), hop(frames, 4), hop(held, 6)]

    mod_own = jnp.sum(small[:, :steps], axis=0).astype(bf16)
    high = lax.all_gather(after(mod_own, w_cols), "grp", axis=1, tiled=True)

    w_heads = jnp.concatenate(
        [lax.dynamic_index_in_dim(w_cols, (part * shards + shard) // units, 0, keepdims=False) for part in range(3)], axis=1
    )

    chips = [held] + [after(piece, high) for piece in chips[1:]]
    others = [hop(piece, 1) for piece in chips]

    pack = jnp.concatenate((w_down, w_out, w_up[:, :wide], w_up[:, wide:]), axis=0)
    weights = lax.all_gather(pack, ("grp", "shard"), axis=0).reshape(groups, shards, 5 * LANES, wide)

    extra = small[:, steps:].reshape(shards, extra_rows * mod_wide)
    full, at = [], 0
    for size in sizes:
        full.append(extra[:, at : at + size].reshape(1, shards * size))
        at += size
    ada_bias, qkv_bias, out_bias, up_bias, down_bias = full
    seg_all = (extra[:, at : at + 9] * 128.0 + extra[:, at + 9 : at + 18]).astype(jnp.int32)
    qkv_bias = lax.dynamic_index_in_dim(qkv_bias.reshape(3, shards, LANES), shard, 1, keepdims=False)
    qkv_bias = qkv_bias.reshape(1, 3 * LANES)
    table = high.astype(f32) + ada_bias

    ordered = lambda width: pl.BlockSpec((rows, width), lambda i, order: (order[i], 0))
    ordered_heads = pl.BlockSpec((2, rows, LANES), lambda i, order: (0, order[i], 0))
    by_block = lambda width: pl.BlockSpec((rows, width), lambda i: (i, 0))
    two_heads = pl.BlockSpec((2, rows, LANES), lambda i: (0, i, 0))
    frame_pieces = [piece[None] for piece in chips + others]
    q, k, v, h1_all = pl.pallas_call(
        qkv_kernel,
        grid_spec=pltpu.PrefetchScalarGridSpec(
            num_scalar_prefetch=1,
            grid=(shards,),
            in_specs=[smem]
            + [pl.BlockSpec(memory_space=pl.ANY)] * len(frame_pieces)
            + [whole(steps, 2 * D), whole(D, 3 * LANES), whole(1, 3 * LANES)] + [pl.BlockSpec((HD // 2, rows), lambda i, order: (0, order[i]))] * 2,
            out_specs=[ordered_heads] * 3 + [ordered(D)],
            scratch_shapes=[pltpu.VMEM((shards, rows, D), bf16), pltpu.SemaphoreType.DMA((len(frame_pieces),))],
        ),
        out_shape=[shape(2, packed, LANES)] * 3 + [shape(packed, D)],
        compiler_params=params(60),
        cost_estimate=FREE,
        name="qkv",
    )(order, seg_all, *frame_pieces, table[:, : 2 * D], w_heads, qkv_bias, cosine, sine)

    attn_flops = 2 * 2 * packed * packed * 256
    some_rows = packed // 2
    some = pl.BlockSpec((some_rows, LANES), lambda i: (i, 0))
    o_heads, mixed, norm = pl.pallas_call(
        attend_kernel,
        grid=(packed // some_rows,),
        in_specs=[pl.BlockSpec((2, some_rows, LANES), lambda i: (0, i, 0))] + [whole(2, packed, LANES)] * 2,
        out_specs=[some] * 3,
        out_shape=[shape(packed, LANES), shape(packed, LANES, kind=f32), shape(packed, LANES, kind=f32)],
        compiler_params=params(60),
        cost_estimate=FREE,
        name="attend",
    )(q, k, v)

    o = lax.all_to_all(o_heads.reshape(shards, rows, LANES), "shard", split_axis=0, concat_axis=0, tiled=True)
    base = shard.astype(jnp.int32).reshape(1)
    block_flops = 2 * rows * D * D * 10
    out, dx1, d_mixed, pair, keep, send, slots_ff, gb_out, gb_up, gb_down = pl.pallas_call(
        block_kernel,
        grid=(1,),
        in_specs=[
            smem, smem, whole(rows, D), whole(rows, D), whole(shards, rows, LANES), whole(steps, 6 * D),
            whole(groups, shards, 5 * LANES, wide), whole(1, D), whole(1, 2 * D), whole(1, D),
        ],
        out_specs=[
            whole(rows, D), whole(rows, D), whole(shards, rows, LANES), whole(rows, 4 * D), whole(rows, 2 * D),
            whole(rows, 2 * D), whole(12, D), whole(1, D), whole(1, 2 * D), whole(1, D),
        ],
        out_shape=[
            shape(rows, D), shape(rows, D, kind=f32), shape(shards, rows, LANES), shape(rows, 4 * D), shape(rows, 2 * D),
            shape(rows, 2 * D), shape(12, D, kind=f32),
            shape(1, D, kind=f32), shape(1, 2 * D, kind=f32), shape(1, D, kind=f32),
        ],
        compiler_params=params(60),
        cost_estimate=FREE,
        name="block",
    )(order, seg_all, frames, cotangent, o, table, weights, out_bias, up_bias, down_bias)

    d_heads = lax.all_to_all(d_mixed, "shard", split_axis=0, concat_axis=0, tiled=True).reshape(packed, LANES)

    send, pair_send = hop(send, 1), hop(pair, 1)
    half = (2, groups, 5 * LANES // 2, wide)
    first_x, first_y, own_x, own_y = pl.pallas_call(
        weight_grad_kernel,
        grid=(1,),
        in_specs=[smem, smem, whole(rows, 2 * D), whole(rows, 2 * D), whole(rows, 4 * D), whole(rows, 4 * D)],
        out_specs=[whole(*half)] * 4,
        out_shape=[shape(*half)] * 4,
        compiler_params=params(60),
        cost_estimate=FREE,
        name="weight_grads",
    )(order, group.astype(jnp.int32).reshape(1), keep, send, pair, pair_send)
    first_x, first_y = after(first_x, d_heads), after(first_y, d_heads)

    back_specs = lambda head: [
        pl.BlockSpec((1, packed, LANES), lambda i: (head, 0, 0)),
        pl.BlockSpec((1, packed, LANES), lambda i: (head, i, 0)),
        pl.BlockSpec((1, packed, LANES), lambda i: (head, i, 0)),
    ] + [whole(packed, LANES)] * 3 + [whole(HD // 2, packed)] * 2
    back_scratch = [pltpu.VMEM((packed, LANES), bf16), pltpu.VMEM((LANES, packed), f32), pltpu.VMEM((packed, LANES), f32)]
    arguments = (q, k, v, d_heads, mixed, norm, cosine, sine)
    came_x, came_y = hop(first_x, 2), hop(first_y, 4)
    qk_first, dv_first = pl.pallas_call(
        behind(partial(attend_back_kernel, 0), 2),
        grid=(1,),
        in_specs=[anywhere] * 2 + back_specs(0),
        out_specs=[whole(packed, LANES), whole(packed, LANES)],
        out_shape=[shape(packed, LANES)] * 2,
        scratch_shapes=back_scratch,
        compiler_params=params(60),
        cost_estimate=FREE,
        name="attend_back_first",
    )(first_x, first_y, *arguments)
    d_first = lax.all_to_all(qk_first.reshape(shards, rows, LANES), "shard", split_axis=0, concat_axis=0, tiled=True)
    second, d_own, gb_qkv = pl.pallas_call(
        partial(attend_back_kernel, 1),
        grid=(1,),
        in_specs=back_specs(1) + [whole(packed, LANES)] * 2,
        out_specs=[whole(packed, 2 * LANES), whole(packed, 3 * LANES), whole(3, LANES)],
        out_shape=[shape(packed, 2 * LANES), shape(packed, 3 * LANES), shape(3, LANES, kind=f32)],
        scratch_shapes=back_scratch,
        compiler_params=params(60),
        cost_estimate=FREE,
        name="attend_back_second",
    )(*arguments, qk_first, dv_first)
    second = after(second, came_x, came_y)
    piece = (1, *half[2:])
    farther = pl.BlockSpec((1, *piece), lambda i: (1, i, 0, 0))
    next_y, next_x = pl.pallas_call(
        add_kernel,
        grid=(groups,),
        in_specs=[farther] * 4,
        out_specs=[pl.BlockSpec(piece, lambda i: (i, 0, 0))] * 2,
        out_shape=[shape(*half[1:])] * 2,
        compiler_params=params(60),
        cost_estimate=FREE,
        name="add",
    )(own_x, came_x, own_y, came_y)
    g_send = pl.pallas_call(
        behind(qkv_grad_kernel, 3),
        grid=(1,),
        in_specs=[anywhere] * 3 + [whole(packed, D), whole(packed, 3 * LANES)],
        out_specs=whole(shards, depth, 3 * LANES),
        out_shape=shape(shards, depth, 3 * LANES),
        compiler_params=params(60),
        cost_estimate=FREE,
        name="qkv_grad",
    )(next_y, next_x, d_first, h1_all, d_own)
    d_second = lax.all_to_all(second.reshape(shards, rows, 2 * LANES), "shard", split_axis=0, concat_axis=0, tiled=True)
    next_y, next_x = hop(next_y, 4), hop(next_x, 2)
    w_all = lax.all_gather(after(w_heads, q), "shard", axis=0)
    by_shard = lambda *dims: pl.BlockSpec((1, *dims), lambda i: (i, 0, 0))
    grad_frames, slots_qkv = pl.pallas_call(
        behind(input_grad_kernel, 1),
        grid=(1,),
        in_specs=[
            anywhere, smem, smem, whole(shards, rows, LANES), whole(shards, rows, 2 * LANES), pl.BlockSpec(memory_space=pl.ANY),
            whole(rows, D), whole(rows, D), whole(steps, 2 * D),
        ],
        out_specs=[whole(rows, D), whole(8, D)],
        out_shape=[shape(rows, D, kind=f32), shape(8, D, kind=f32)],
        scratch_shapes=[pltpu.VMEM((shards, D, 3 * LANES), bf16), pltpu.SemaphoreType.DMA((shards,))],
        compiler_params=params(60),
        cost_estimate=FREE,
        name="input_grad",
    )(g_send, base, seg_all, d_first, d_second, w_all, frames, dx1, table[:, : 2 * D])

    g_came = lax.all_to_all(after(g_send, slots_qkv), "shard", split_axis=0, concat_axis=0, tiled=True)

    d_slot = jnp.concatenate((slots_qkv[:6], slots_ff), axis=0).reshape(6, 3, D).transpose(1, 0, 2).reshape(3, 6 * D)
    row_sums = jnp.concatenate((gb_qkv.reshape(-1), gb_out[0], gb_up[0], gb_down[0]))
    sum_rows = -(-row_sums.shape[0] // (6 * D))
    row_sums = jnp.pad(row_sums, (0, sum_rows * 6 * D - row_sums.shape[0])).reshape(sum_rows, 6 * D)
    nearer = whole(1, *half[1:])
    totals = pl.pallas_call(
        behind(total_kernel, 1),
        grid=(1,),
        in_specs=[anywhere] + [nearer, nearer, whole(*half[1:])] * 2,
        out_specs=[whole(5 * LANES, wide)] * groups,
        out_shape=[shape(5 * LANES, wide)] * groups,
        compiler_params=params(60),
        cost_estimate=FREE,
        name="total",
    )(slots_qkv, own_x, came_x, next_y, own_y, came_y, next_x)
    tail = after(jnp.concatenate((d_slot, row_sums), axis=0), totals[0])
    tail = lax.all_gather(tail, "shard", axis=0)
    totals = trade(totals, "grp", groups)
    parts = pl.pallas_call(
        behind(collect_kernel, 1 + groups),
        grid=(1,),
        in_specs=[anywhere] * (1 + groups) + [smem, smem, whole(shards, 4, 6 * D)],
        out_specs=whole(groups, 8, mod_wide + 2 * LANES),
        out_shape=shape(groups, 8, mod_wide + 2 * LANES, kind=f32),
        scratch_shapes=[pltpu.VMEM((8, 6 * D), f32), pltpu.VMEM((1, 4 * D), f32)],
        compiler_params=params(20),
        cost_estimate=FREE,
        name="collect",
    )(g_came, *totals, base, seg_all, tail)
    g_down, g_out, g_up = pl.pallas_call(
        last_sum_kernel,
        grid=(1,),
        in_specs=[whole(5 * LANES, wide)] * groups,
        out_specs=[whole(2 * LANES, wide), whole(LANES, wide), whole(LANES, 2 * wide)],
        out_shape=[shape(2 * LANES, wide, kind=f32), shape(LANES, wide, kind=f32), shape(LANES, 2 * wide, kind=f32)],
        compiler_params=params(20),
        cost_estimate=FREE,
        name="last_sum",
    )(*totals)
    parts_own = parts
    parts = lax.all_to_all(parts, "grp", split_axis=0, concat_axis=0, tiled=True)
    pieces = pl.pallas_call(
        behind(qkv_piece_kernel, 1),
        grid=(1,),
        in_specs=[anywhere, smem, whole(shards, depth, 3 * LANES)],
        out_specs=[whole(depth, units * LANES)] * groups,
        out_shape=[shape(depth, units * LANES)] * groups,
        compiler_params=params(16),
        cost_estimate=FREE,
        name="qkv_pieces",
    )(parts_own, group.astype(jnp.int32).reshape(1), g_came)
    g_qkv = pl.pallas_call(
        qkv_sum_kernel,
        grid=(1,),
        in_specs=[whole(depth, units * LANES)] * groups,
        out_specs=whole(depth, units * LANES),
        out_shape=shape(depth, units * LANES, kind=f32),
        compiler_params=params(16),
        cost_estimate=FREE,
        name="qkv_sum",
    )(*trade(pieces, "grp", groups))
    table_own = lax.dynamic_slice_in_dim(time_table, shard * depth, depth, 1)
    g_ada, g_table, *sums = pl.pallas_call(
        table_kernel,
        grid=(1,),
        in_specs=[whole(groups, 8, mod_wide + 2 * LANES), whole(steps, depth), whole(depth, mod_wide), whole(steps, depth)],
        out_specs=[whole(depth, mod_wide), whole(groups, steps, depth)] + [whole(1, size) for size in sizes],
        out_shape=[shape(depth, mod_wide, kind=f32), shape(groups, steps, depth, kind=f32)]
        + [shape(1, size, kind=f32) for size in sizes],
        compiler_params=params(20),
        cost_estimate=FREE,
        name="table",
    )(parts, act_own, w_ada, table_own)
    gb_ada, gb_qkv, gb_out, gb_up, gb_down = [total.reshape(-1) for total in sums]
    g_table = jnp.sum(lax.all_to_all(g_table, "grp", split_axis=0, concat_axis=0, tiled=True), axis=0)
    return (
        out, grad_frames, g_table, g_ada, gb_ada, g_qkv, gb_qkv, g_out, gb_out, g_up, gb_up, g_down, gb_down,
    )


def solution(mesh):
    in_specs = (
        P(("grp", "shard"), None),
        P(("grp", "shard"), None),
        P(("grp", "shard"), None),
        P(("grp", "shard"), None),
        P(("grp", "shard"), None),
        P(),
        P("shard", "grp"),
        P("shard"),
        P("shard", "grp"),
        P("shard"),
        P("shard", "grp"),
        P("shard"),
        P("shard", "grp"),
        P("shard"),
        P("shard", "grp"),
        P("shard"),
    )
    out_specs = (
        P(("grp", "shard"), None),
        P(("grp", "shard"), None),
        P(None, "shard"),
        P("shard", "grp"),
        P("shard"),
        P("shard", "grp"),
        P("shard"),
        P("shard", "grp"),
        P("shard"),
        P("shard", "grp"),
        P("shard"),
        P("shard", "grp"),
        P("shard"),
    )
    by_heads = mesh.shape["shard"] * 2 * HD == D and mesh.shape["grp"] == 4
    local = partial(local_heads, mesh.shape["grp"], mesh.shape["shard"]) if by_heads else local_any
    return jax.shard_map(local, mesh=mesh, in_specs=in_specs, out_specs=out_specs, check_vma=False)
```

```python
from functools import partial

import jax
import jax.numpy as jnp
from jax import lax
from jax.experimental import pallas as pl
from jax.experimental.pallas import tpu as pltpu
from jax.sharding import PartitionSpec as P

D = 1024
H = 16
HD = 64


eps_norm = 1e-06
top_precision = lax.Precision.HIGHEST


def normalize(tensor):
    centred = tensor - jnp.mean(tensor, axis=-1, keepdims=True)
    return centred * lax.rsqrt(jnp.mean(centred * centred, axis=-1, keepdims=True) + eps_norm)


def modulate(tensor, scale_vec, shift_vec):
    return normalize(tensor) * (1.0 + scale_vec) + shift_vec


def angles(positions):
    half_width = HD // 2
    inverse = 10000.0 ** (-jnp.arange(half_width, dtype=jnp.float32) / half_width)
    phase_grid = positions[:, None] * inverse[None, :]
    return (jnp.cos(phase_grid), jnp.sin(phase_grid))


def rotate(tensor, cosine_vals, sine_vals):
    row_total = tensor.shape[0]
    halves = tensor.reshape(row_total, H, 2, HD // 2)
    former = halves[:, :, 0]
    latter = halves[:, :, 1]
    cosine_part = cosine_vals[:, None, :]
    sine_part = sine_vals[:, None, :]
    turned = jnp.stack(
        (former * cosine_part - latter * sine_part, latter * cosine_part + former * sine_part),
        axis=2,
    )
    return turned.reshape(row_total, D)


def tile_width(row_total):
    for candidate in (512, 256, 128):
        return candidate
    return row_total


def head_view(tensor):
    return tensor.reshape(tensor.shape[0], H, HD)


def local_any(
    frames,
    cotangent,
    seg_start,
    seg_length,
    seg_step,
    time_table,
    w_ada,
    b_ada,
    w_qkv,
    b_qkv,
    w_out,
    b_out,
    w_up,
    b_up,
    w_down,
    b_down,
):
    frame_rows = frames.shape[0]
    positions = lax.axis_index("shard") * frame_rows + jnp.arange(frame_rows, dtype=jnp.int32)
    slot_start = seg_start[0]
    slot_end = slot_start + seg_length[0]
    member_mask = (positions[:, None] >= slot_start[None, :]) & (
        positions[:, None] < slot_end[None, :]
    )
    member = member_mask.astype(jnp.float32)
    seg_low = jnp.sum(jnp.where(member_mask, slot_start[None, :], 0), axis=1)
    seg_high = jnp.sum(jnp.where(member_mask, slot_end[None, :], 0), axis=1)
    cosine_vals, sine_vals = angles((positions - seg_low).astype(jnp.float32))
    columns = (
        lax.all_gather(w_ada, "grp", axis=1, tiled=True),
        lax.all_gather(w_qkv, "grp", axis=1, tiled=True),
        lax.all_gather(w_out, "grp", axis=1, tiled=True),
        lax.all_gather(w_up, "grp", axis=1, tiled=True),
        lax.all_gather(w_down, "grp", axis=1, tiled=True),
    )
    gathered = (
        lax.all_gather(columns[0], "shard", axis=0, tiled=True),
        lax.all_gather(columns[1], "shard", axis=0, tiled=True),
        lax.all_gather(columns[2], "shard", axis=0, tiled=True),
        lax.all_gather(columns[3], "shard", axis=0, tiled=True),
        lax.all_gather(columns[4], "shard", axis=0, tiled=True),
        lax.all_gather(b_ada, "shard", axis=0, tiled=True),
        lax.all_gather(b_qkv, "shard", axis=0, tiled=True),
        lax.all_gather(b_out, "shard", axis=0, tiled=True),
        lax.all_gather(b_up, "shard", axis=0, tiled=True),
        lax.all_gather(b_down, "shard", axis=0, tiled=True),
    )
    ada_full, qkv_full, out_full, up_full, down_full = (
        gathered[0],
        gathered[1],
        gathered[2],
        gathered[3],
        gathered[4],
    )
    ada_bias, qkv_bias, out_bias, up_bias, down_bias = [
        bias_row.astype(jnp.float32) for bias_row in gathered[5:]
    ]
    step_onehot = (
        seg_step[0][:, None] == jnp.arange(time_table.shape[0], dtype=jnp.int32)[None, :]
    ).astype(jnp.float32)
    time_rows = jnp.dot(step_onehot, time_table, precision=top_precision)
    activated = jax.nn.silu(time_rows).astype(jnp.bfloat16)
    modulation = jnp.dot(activated, ada_full, preferred_element_type=jnp.float32) + ada_bias
    frame_mod = jnp.dot(member, modulation, precision=top_precision)
    shift_attn, scale_attn, gate_attn, shift_ff, scale_ff, gate_ff = jnp.split(frame_mod, 6, axis=1)
    inputs = frames.astype(jnp.float32)
    hidden_attn = modulate(inputs, scale_attn, shift_attn).astype(jnp.bfloat16)
    projected = jnp.dot(hidden_attn, qkv_full, preferred_element_type=jnp.float32) + qkv_bias
    queries = rotate(projected[:, :D], cosine_vals, sine_vals).astype(jnp.bfloat16)
    keys_rot = rotate(projected[:, D : 2 * D], cosine_vals, sine_vals).astype(jnp.bfloat16)
    values = projected[:, 2 * D :].astype(jnp.bfloat16)
    query_heads = head_view(queries)
    key_heads = head_view(keys_rot)
    value_heads = head_view(values)
    zero_heads = jnp.zeros((frame_rows, H, HD), jnp.float32)
    key_piece = lax.all_gather(keys_rot, "shard", axis=0, tiled=True)
    value_piece = lax.all_gather(values, "shard", axis=0, tiled=True)
    piece_rows = key_piece.shape[0]
    tile_rows = tile_width(piece_rows)
    tiles = piece_rows // tile_rows

    def tile_step(partial_sums, tile_item):
        key_tile, value_tile, offset = tile_item
        key_pos = offset + jnp.arange(tile_rows, dtype=jnp.int32)
        inside = (key_pos[None, :] >= seg_low[:, None]) & (key_pos[None, :] < seg_high[:, None])
        scores = 0.125 * jnp.einsum(
            "rhd,khd->hrk", query_heads, head_view(key_tile), preferred_element_type=jnp.float32
        )
        expo = jnp.where(inside[None], jnp.exp(scores), 0.0)
        numerator, denominator = partial_sums
        numerator = numerator + jnp.einsum(
            "hrk,khd->rhd",
            expo.astype(jnp.bfloat16),
            head_view(value_tile),
            preferred_element_type=jnp.float32,
        )
        denominator = denominator + jnp.sum(expo, axis=2).T
        return ((numerator, denominator), None)

    tile_items = (
        key_piece.reshape(tiles, tile_rows, D),
        value_piece.reshape(tiles, tile_rows, D),
        jnp.arange(tiles, dtype=jnp.int32) * tile_rows,
    )
    numerator, denominator = lax.scan(
        tile_step, (zero_heads, jnp.zeros((frame_rows, H), jnp.float32)), tile_items
    )[0]
    mixed = numerator / denominator[:, :, None]
    mixed_low = mixed.reshape(frame_rows, D).astype(jnp.bfloat16)
    attn_branch = jnp.dot(mixed_low, out_full, preferred_element_type=jnp.float32) + out_bias
    after_attn = inputs + gate_attn * attn_branch
    hidden_ff = modulate(after_attn, scale_ff, shift_ff).astype(jnp.bfloat16)
    upward = jnp.dot(hidden_ff, up_full, preferred_element_type=jnp.float32) + up_bias
    activation = jax.nn.gelu(upward, approximate=True).astype(jnp.bfloat16)
    ff_branch = jnp.dot(activation, down_full, preferred_element_type=jnp.float32) + down_bias
    output = (after_attn + gate_ff * ff_branch).astype(jnp.bfloat16)
    columns_back = (
        lax.all_gather(w_ada, "grp", axis=1, tiled=True),
        lax.all_gather(w_qkv, "grp", axis=1, tiled=True),
        lax.all_gather(w_out, "grp", axis=1, tiled=True),
        lax.all_gather(w_up, "grp", axis=1, tiled=True),
        lax.all_gather(w_down, "grp", axis=1, tiled=True),
    )
    gathered_back = (
        lax.all_gather(columns_back[0], "shard", axis=0, tiled=True),
        lax.all_gather(columns_back[1], "shard", axis=0, tiled=True),
        lax.all_gather(columns_back[2], "shard", axis=0, tiled=True),
        lax.all_gather(columns_back[3], "shard", axis=0, tiled=True),
        lax.all_gather(columns_back[4], "shard", axis=0, tiled=True),
    )
    ada_back, qkv_back, out_back, up_back, down_back = (
        gathered_back[0],
        gathered_back[1],
        gathered_back[2],
        gathered_back[3],
        gathered_back[4],
    )
    grad_out = cotangent.astype(jnp.float32)
    d_branch = (gate_ff * grad_out).astype(jnp.bfloat16)
    d_gate_ff = grad_out * ff_branch
    g_down = jnp.dot(activation.T, d_branch, preferred_element_type=jnp.float32)
    gb_down = jnp.sum(d_branch.astype(jnp.float32), axis=0)
    d_activation = jnp.dot(d_branch, down_back.T, preferred_element_type=jnp.float32)
    gelu_pull = jax.vjp(partial(jax.nn.gelu, approximate=True), upward)[1]
    d_upward = gelu_pull(d_activation)[0].astype(jnp.bfloat16)
    g_up = jnp.dot(hidden_ff.T, d_upward, preferred_element_type=jnp.float32)
    gb_up = jnp.sum(d_upward.astype(jnp.float32), axis=0)
    d_hidden_ff = jnp.dot(d_upward, up_back.T, preferred_element_type=jnp.float32)
    ff_pull = jax.vjp(modulate, after_attn, scale_ff, shift_ff)[1]
    dx_ff, d_scale_ff, d_shift_ff = ff_pull(d_hidden_ff)
    d_after = grad_out + dx_ff
    d_attn = (gate_attn * d_after).astype(jnp.bfloat16)
    d_gate_attn = d_after * attn_branch
    g_out = jnp.dot(mixed_low.T, d_attn, preferred_element_type=jnp.float32)
    gb_out = jnp.sum(d_attn.astype(jnp.float32), axis=0)
    d_mixed = jnp.dot(d_attn, out_back.T, preferred_element_type=jnp.float32).astype(jnp.bfloat16)
    d_mixed_heads = head_view(d_mixed).astype(jnp.float32)
    delta = jnp.sum(d_mixed_heads * mixed, axis=2) / denominator
    d_numer = (d_mixed_heads / denominator[:, :, None]).astype(jnp.bfloat16).reshape(frame_rows, D)
    dnum_heads = head_view(d_numer)
    delta_heads = delta.T
    key_piece = lax.all_gather(keys_rot, "shard", axis=0, tiled=True)
    value_piece = lax.all_gather(values, "shard", axis=0, tiled=True)
    piece_rows = key_piece.shape[0]
    fold_tile_rows = tile_width(piece_rows)
    tiles = piece_rows // fold_tile_rows

    def tile_step(grad_sum, tile_item):
        key_tile, value_tile, offset = tile_item
        key_pos = offset + jnp.arange(fold_tile_rows, dtype=jnp.int32)
        inside = (key_pos[None, :] >= seg_low[:, None]) & (key_pos[None, :] < seg_high[:, None])
        scores = 0.125 * jnp.einsum(
            "rhd,khd->hrk", query_heads, head_view(key_tile), preferred_element_type=jnp.float32
        )
        expo = jnp.where(inside[None], jnp.exp(scores), 0.0)
        slope = jnp.einsum(
            "rhd,khd->hrk", dnum_heads, head_view(value_tile), preferred_element_type=jnp.float32
        )
        d_scores = (expo * (slope - delta_heads[:, :, None])).astype(jnp.bfloat16)
        grad_sum = grad_sum + 0.125 * jnp.einsum(
            "hrk,khd->rhd", d_scores, head_view(key_tile), preferred_element_type=jnp.float32
        )
        return (grad_sum, None)

    tile_items = (
        key_piece.reshape(tiles, fold_tile_rows, D),
        value_piece.reshape(tiles, fold_tile_rows, D),
        jnp.arange(tiles, dtype=jnp.int32) * fold_tile_rows,
    )
    d_query = lax.scan(tile_step, zero_heads, tile_items)[0]
    delta_all = lax.all_gather(delta, "shard", axis=0, tiled=True)

    def fold_key_grad(running, piece):
        query_piece, dnum_piece = piece
        piece_rows = query_piece.shape[0]
        tile_rows = tile_width(piece_rows)
        tiles = piece_rows // tile_rows

        def tile_step(grad_pair, tile_item):
            query_tile, dnum_tile, delta_tile, offset = tile_item
            query_pos = offset + jnp.arange(tile_rows, dtype=jnp.int32)
            inside = (query_pos[:, None] >= seg_low[None, :]) & (
                query_pos[:, None] < seg_high[None, :]
            )
            query_tile_heads = head_view(query_tile)
            dnum_tile_heads = head_view(dnum_tile)
            scores = 0.125 * jnp.einsum(
                "qhd,rhd->hqr", query_tile_heads, key_heads, preferred_element_type=jnp.float32
            )
            expo = jnp.where(inside[None], jnp.exp(scores), 0.0)
            slope = jnp.einsum(
                "qhd,rhd->hqr", dnum_tile_heads, value_heads, preferred_element_type=jnp.float32
            )
            d_scores = (expo * (slope - delta_tile.T[:, :, None])).astype(jnp.bfloat16)
            d_keys, d_values = grad_pair
            d_keys = d_keys + 0.125 * jnp.einsum(
                "hqr,qhd->rhd", d_scores, query_tile_heads, preferred_element_type=jnp.float32
            )
            d_values = d_values + jnp.einsum(
                "hqr,qhd->rhd",
                expo.astype(jnp.bfloat16),
                dnum_tile_heads,
                preferred_element_type=jnp.float32,
            )
            return ((d_keys, d_values), None)

        tile_items = (
            query_piece.reshape(tiles, tile_rows, D),
            dnum_piece.reshape(tiles, tile_rows, D),
            delta_all.reshape(tiles, tile_rows, H),
            jnp.arange(tiles, dtype=jnp.int32) * tile_rows,
        )
        return lax.scan(tile_step, running, tile_items)[0]

    d_keys, d_values = fold_key_grad(
        (zero_heads, zero_heads),
        (
            lax.all_gather(queries, "shard", axis=0, tiled=True),
            lax.all_gather(d_numer, "shard", axis=0, tiled=True),
        ),
    )
    grad_query = rotate(d_query.reshape(frame_rows, D), cosine_vals, -sine_vals)
    grad_key = rotate(d_keys.reshape(frame_rows, D), cosine_vals, -sine_vals)
    d_projected = jnp.concatenate(
        (grad_query, grad_key, d_values.reshape(frame_rows, D)), axis=1
    ).astype(jnp.bfloat16)
    g_qkv = jnp.dot(hidden_attn.T, d_projected, preferred_element_type=jnp.float32)
    gb_qkv = jnp.sum(d_projected.astype(jnp.float32), axis=0)
    d_hidden_attn = jnp.dot(d_projected, qkv_back.T, preferred_element_type=jnp.float32)
    attn_pull = jax.vjp(modulate, inputs, scale_attn, shift_attn)[1]
    dx_attn, d_scale_attn, d_shift_attn = attn_pull(d_hidden_attn)
    grad_frames = d_after + dx_attn
    d_frame_mod = jnp.concatenate(
        (d_shift_attn, d_scale_attn, d_gate_attn, d_shift_ff, d_scale_ff, d_gate_ff), axis=1
    )
    d_slot = jnp.dot(member.T, d_frame_mod, precision=top_precision)
    g_ada = jnp.dot(activated.astype(jnp.float32).T, d_slot, precision=top_precision)
    gb_ada = jnp.sum(d_slot, axis=0)
    d_activated = jnp.dot(
        d_slot, ada_back.T, precision=top_precision, preferred_element_type=jnp.float32
    )
    silu_pull = jax.vjp(jax.nn.silu, time_rows)[1]
    d_time_rows = silu_pull(d_activated)[0]
    g_table = jnp.dot(step_onehot.T, d_time_rows, precision=top_precision)
    group_sums = (
        lax.psum_scatter(g_ada, "shard", scatter_dimension=0, tiled=True),
        lax.psum_scatter(g_qkv, "shard", scatter_dimension=0, tiled=True),
        lax.psum_scatter(g_out, "shard", scatter_dimension=0, tiled=True),
        lax.psum_scatter(g_up, "shard", scatter_dimension=0, tiled=True),
        lax.psum_scatter(g_down, "shard", scatter_dimension=0, tiled=True),
        lax.psum_scatter(gb_ada, "shard", scatter_dimension=0, tiled=True),
        lax.psum_scatter(gb_qkv, "shard", scatter_dimension=0, tiled=True),
        lax.psum_scatter(gb_out, "shard", scatter_dimension=0, tiled=True),
        lax.psum_scatter(gb_up, "shard", scatter_dimension=0, tiled=True),
        lax.psum_scatter(gb_down, "shard", scatter_dimension=0, tiled=True),
        lax.psum_scatter(g_table, "shard", scatter_dimension=1, tiled=True),
    )
    wide_sums = (
        lax.psum_scatter(group_sums[0], "grp", scatter_dimension=1, tiled=True),
        lax.psum_scatter(group_sums[1], "grp", scatter_dimension=1, tiled=True),
        lax.psum_scatter(group_sums[2], "grp", scatter_dimension=1, tiled=True),
        lax.psum_scatter(group_sums[3], "grp", scatter_dimension=1, tiled=True),
        lax.psum_scatter(group_sums[4], "grp", scatter_dimension=1, tiled=True),
    )
    small_sums = lax.psum(
        (group_sums[5], group_sums[6], group_sums[7], group_sums[8], group_sums[9], group_sums[10]),
        "grp",
    )
    finals = tuple(wide_sums) + tuple(small_sums)
    return (
        output,
        grad_frames,
        finals[10],
        finals[0],
        finals[5],
        finals[1],
        finals[6],
        finals[2],
        finals[7],
        finals[3],
        finals[8],
        finals[4],
        finals[9],
    )


LANES = 128
FREE = pl.CostEstimate(flops=2**20, bytes_accessed=2**16, transcendentals=0)
CHIPS = (2, 4, 6)
ORDER = (0, 2, 4, 6, 1, 3, 5, 7)
SEPARATE = -(2.0**100)
GELU_C = 0.7978845608028654
GELU_A = 0.044715
NT = (((1,), (1,)), ((), ()))
TN = (((0,), (0,)), ((), ()))
f32 = jnp.float32
bf16 = jnp.bfloat16


def dot(left, right, dims=(((1,), (0,)), ((), ()))):
    return lax.dot_general(left, right, dims, preferred_element_type=f32)


def params(limit_mib, steps=1):
    return pltpu.CompilerParams(
        dimension_semantics=("arbitrary",) * steps, vmem_limit_bytes=limit_mib * 2**20
    )


def moments(value):
    centred = value - jnp.mean(value, axis=1, keepdims=True)
    inv = lax.rsqrt(jnp.mean(centred * centred, axis=1, keepdims=True) + eps_norm)
    return centred * inv, inv


def norm_back(weighted, normal, inv):
    return (
        weighted
        - jnp.mean(weighted, axis=1, keepdims=True)
        - normal * jnp.mean(weighted * normal, axis=1, keepdims=True)
    ) * inv


def swap_halves(value):
    lane = lax.broadcasted_iota(jnp.int32, value.shape, 1)
    return jnp.where(lane % HD < HD // 2, pltpu.roll(value, 96, 1), pltpu.roll(value, 32, 1))


def rotary(cos_ref, sin_ref, here):
    cosine, sine = cos_ref[:, here].T, sin_ref[:, here].T
    return jnp.concatenate([cosine] * 4, axis=1), jnp.concatenate([-sine, sine] * 2, axis=1)


def members(seg_ref, block, rows):
    place = block * rows + lax.broadcasted_iota(jnp.int32, (rows, LANES), 0)
    out = []
    for slot in range(3):
        begin = seg_ref[block, slot]
        out.append((place >= begin) & (place < begin + seg_ref[block, 3 + slot]))
    return out


def mod_rows(table_ref, seg_ref, block, member, part):
    first, second, third = [table_ref[pl.ds(seg_ref[block, 6 + slot], 1), pl.ds(part * D, D)] for slot in range(3)]
    out = []
    for at in range(0, D, LANES):
        here = slice(at, at + LANES)
        out.append(jnp.where(member[0], first[:, here], jnp.where(member[1], second[:, here], third[:, here])))
    return jnp.concatenate(out, axis=1)


def slot_sums(member, value):
    out = []
    for column in member:
        sums = [
            jnp.sum(jnp.where(column, value[:, at : at + LANES], 0.0), axis=0, keepdims=True) for at in range(0, D, LANES)
        ]
        out.append(jnp.concatenate(sums, axis=1))
    return out


def qkv_kernel(order_ref, seg_ref, *refs):
    step = pl.program_id(0)
    last = pl.num_programs(0) - 1
    *pieces, table_ref, w_ref, b_ref, cos_ref, sin_ref, q_ref, k_ref, v_ref, h_ref, x_all, arrived = refs
    block = order_ref[step]
    rows = x_all.shape[1]
    copies, at = [], 0
    for piece in pieces:
        here = x_all.at[at : at + piece.shape[0]]
        copies.append((at, pltpu.make_async_copy(piece, here, arrived.at[len(copies)])))
        at += piece.shape[0]

    @pl.when(step == 0)
    def _():
        for _, copy in copies:
            copy.start()

    for at, copy in copies:

        @pl.when(step == at)
        def _(copy=copy):
            copy.wait()

    member = members(seg_ref, block, rows)
    normal, _ = moments(x_all[step].astype(f32))
    shift = mod_rows(table_ref, seg_ref, block, member, 0)
    scale = mod_rows(table_ref, seg_ref, block, member, 1)
    hidden = (normal * (1.0 + scale) + shift).astype(bf16)
    h_ref[...] = hidden
    projected = dot(hidden, w_ref[...]) + b_ref[...]
    cosine, sine = rotary(cos_ref, sin_ref, slice(None))
    turned = []
    for part in range(2):
        piece = projected[:, part * LANES : (part + 1) * LANES]
        turned.append(piece * cosine + swap_halves(piece) * sine)
    queries = turned[0].astype(bf16).astype(f32) * 0.125
    keys = turned[1]
    values = projected[:, 2 * LANES :]
    lane = lax.broadcasted_iota(jnp.int32, (rows, LANES), 1)
    lane_row = lane[:1]
    begins, ends = jnp.full((1, LANES), 2**30, jnp.int32), jnp.zeros((1, LANES), jnp.int32)
    for index in range(6):
        where, slot = (0, index) if index < 3 else (last, index - 3)
        begin = seg_ref[where, slot]
        begins = jnp.where(lane_row == HD + index, begin, begins)
        ends = jnp.where(lane_row == HD + index, begin + seg_ref[where, 3 + slot], ends)
    place = block * rows + lax.broadcasted_iota(jnp.int32, (rows, LANES), 0)
    inside = (place >= begins) & (place < ends)
    query_extra = jnp.where(inside | (lane >= HD + 6), 0.0, SEPARATE)
    key_extra = jnp.where(inside, 1.0, 0.0)
    value_extra = jnp.where((lane >= HD) & (lane < HD + 3), 1.0, 0.0)
    low = lane < HD
    for head in range(2):
        for ref, value, extra in (
            (q_ref, queries, query_extra),
            (k_ref, keys, key_extra),
            (v_ref, values, value_extra),
        ):
            own = value if head == 0 else pltpu.roll(value, HD, 1)
            ref[head] = jnp.where(low, own, extra).astype(bf16)


def attend_kernel(q_ref, k_ref, v_ref, o_ref, mixed_ref, l_ref):
    keys_in_all = k_ref.shape[1]
    tile = 256
    ratios, sums = [], []
    for head in range(2):
        query = q_ref[head]
        total = None
        for at in range(0, keys_in_all, tile):
            expo = jnp.exp(dot(query, k_ref[head, at : at + tile], NT))
            term = dot(expo.astype(bf16), v_ref[head, at : at + tile])
            total = term if total is None else total + term
        norm = total[:, HD : HD + 1]
        ratios.append(total / norm)
        sums.append(norm)
    lane = lax.broadcasted_iota(jnp.int32, ratios[0].shape, 1)
    mixed = jnp.where(lane < HD, ratios[0], pltpu.roll(ratios[1], HD, 1))
    mixed_ref[...] = mixed
    o_ref[...] = mixed.astype(bf16)
    l_ref[...] = jnp.where(lane < HD, sums[0], sums[1])


def block_kernel(
    order_ref, seg_ref, x_ref, cot_ref, o_ref, table_ref, w_ref, b_out_ref, b_up_ref, b_down_ref,
    out_ref, dx1_ref, do_ref, pair_ref, keep_ref, send_ref, slots_ref, gb_out_ref, gb_up_ref, gb_down_ref,
):
    rows = x_ref.shape[0]
    groups, shards = w_ref.shape[:2]
    block = order_ref[0]
    member = members(seg_ref, block, rows)
    modulation = partial(mod_rows, table_ref, seg_ref, block, member)
    wide = D // groups

    def weight(group, start):
        return w_ref[group, :, start : start + LANES, :].reshape(D, wide)

    def weight_down(group):
        return w_ref[group, :, 0 : 2 * LANES, :].reshape(2 * D, wide)

    def by_core(value, width, other):
        parts = [value[:, at : at + width] for at in range(0, value.shape[1], width)]
        even, odd = jnp.concatenate(parts[0::2], axis=1), jnp.concatenate(parts[1::2], axis=1)
        return jnp.where((block % 2 == 0) != other, even, odd)

    def share(start, value, width):
        half = value.shape[1] // 2
        keep_ref[:, start : start + half] = by_core(value, width, False)
        send_ref[:, start : start + half] = by_core(value, width, True)

    mixed = jnp.concatenate([o_ref[shard] for shard in range(shards)], axis=1)
    share(D, mixed, LANES)
    attn = jnp.concatenate([dot(mixed, weight(group, 256)) for group in range(groups)], axis=1)
    attn = attn + b_out_ref[...]
    gate1 = modulation(2)
    after = x_ref[...].astype(f32) + gate1 * attn
    normal, inv = moments(after)
    scale2 = 1.0 + modulation(4)
    hidden = (normal * scale2 + modulation(3)).astype(bf16)
    share(D + D // 2, hidden, LANES)
    up = [dot(hidden, weight(group, start)) for group in range(groups) for start in (384, 512)]
    up = jnp.concatenate(up, axis=1) + b_up_ref[...]
    inner = jnp.tanh(GELU_C * (up + GELU_A * (up * up * up)))
    act = (0.5 * up * (1.0 + inner)).astype(bf16)
    share(0, act, 2 * LANES)
    slope = 0.5 * (1.0 + inner) + (0.5 * GELU_C) * up * (1.0 - inner * inner) * (
        1.0 + (3.0 * GELU_A) * up * up
    )
    branch = jnp.concatenate([dot(act, weight_down(group)) for group in range(groups)], axis=1)
    branch = branch + b_down_ref[...]
    gate2 = modulation(5)
    out_ref[...] = (after + gate2 * branch).astype(bf16)

    cot = cot_ref[...].astype(f32)
    dff = (gate2 * cot).astype(bf16)
    pair_ref[:, 0:D] = dff
    gb_down_ref[...] = jnp.sum(dff.astype(f32), axis=0, keepdims=True)
    d_gate2 = slot_sums(member, cot * branch)
    d_act = sum(dot(dff[:, g * wide : (g + 1) * wide], weight_down(g), NT) for g in range(groups))
    du = (d_act * slope).astype(bf16)
    pair_ref[:, 2 * D :] = du
    gb_up_ref[...] = jnp.sum(du.astype(f32), axis=0, keepdims=True)
    d_hidden = None
    for index in range(2 * groups):
        piece = du[:, index * wide : (index + 1) * wide]
        term = dot(piece, weight(index // 2, 384 + LANES * (index % 2)), NT)
        d_hidden = term if d_hidden is None else d_hidden + term
    d_shift2 = slot_sums(member, d_hidden)
    d_scale2 = slot_sums(member, d_hidden * normal)
    d_after = cot + norm_back(d_hidden * scale2, normal, inv)
    dx1_ref[...] = d_after
    d_gate1 = slot_sums(member, d_after * attn)
    da = (gate1 * d_after).astype(bf16)
    pair_ref[:, D : 2 * D] = da
    gb_out_ref[...] = jnp.sum(da.astype(f32), axis=0, keepdims=True)
    d_mixed = sum(dot(da[:, g * wide : (g + 1) * wide], weight(g, 256), NT) for g in range(groups))
    d_mixed = d_mixed.astype(bf16)
    for shard in range(shards):
        do_ref[shard] = d_mixed[:, shard * LANES : (shard + 1) * LANES]
    slots_ref[...] = jnp.concatenate(d_gate1 + d_shift2 + d_scale2 + d_gate2, axis=0)


def weight_grad_kernel(
    order_ref, group_ref, keep_ref, send_ref, pair_ref, pair2_ref, first_x, first_y, own_x, own_y
):
    groups, half, wide = first_x.shape[1:]

    def product(at, width, start, stop):
        here = pl.ds(pl.multiple_of(at, LANES), width)
        return (
            dot(keep_ref[:, here], pair_ref[:, start:stop], TN) + dot(send_ref[:, here], pair2_ref[:, start:stop], TN)
        ).astype(bf16)

    places = (((own_x, 0), (own_y, 0)), ((first_x, 0), (own_y, 1)), ((own_x, 1), (first_y, 0)), ((first_x, 1), (first_y, 1)))
    for index in range(4):
        chip = order_ref[index] // 2
        down = product(chip * 2 * LANES, 2 * LANES, 0, D)
        out = product(D + chip * LANES, LANES, D, 2 * D)
        up = product(D + D // 2 + chip * LANES, LANES, 2 * D, 4 * D)
        (by_x, at_x), (by_y, at_y) = places[index]
        for group in range(groups):
            to = (group + groups - group_ref[0]) % groups
            columns = slice(group * wide, (group + 1) * wide)
            by_x[at_x, to, 0:256, :] = down[:, columns]
            by_x[at_x, to, 256:half, :] = out[: half - 256, columns]
            by_y[at_y, to, 0 : 384 - half, :] = out[half - 256 :, columns]
            for part in range(2):
                start = 384 - half + 128 * part
                at = (2 * group + part) * wide
                by_y[at_y, to, start : start + 128, :] = up[:, at : at + wide]


def attend_back_kernel(head, q_ref, k_ref, v_ref, do_ref, mixed_ref, l_ref, cos_ref, sin_ref, *refs):
    *refs, dn, dq_t, dk_all = refs
    if head == 0:
        qk_ref, dv_ref = refs
    else:
        qk_first, dv_first, second_ref, own_ref, gb_ref = refs
        qk_ref = second_ref.at[:, :LANES]
    step = pl.program_id(0)
    rows = k_ref.shape[1]
    frames = q_ref.shape[1]
    tile = 256
    lane = lax.broadcasted_iota(jnp.int32, (rows, LANES), 1)
    low = lane < HD

    @pl.when(step == 0)
    def _():
        dq_t[...] = jnp.zeros_like(dq_t)
        for at in range(0, frames, rows):
            here = slice(at, at + rows)
            d_out = do_ref[here].astype(f32)
            norm = l_ref[here]
            d_num = (d_out / norm).astype(bf16).astype(f32)
            mine = low if head == 0 else ~low
            total = jnp.sum(jnp.where(mine, d_out * mixed_ref[here], 0.0), axis=1, keepdims=True)
            delta = -total / norm[:, head * HD : head * HD + 1]
            first = delta.astype(bf16).astype(f32)
            second = (delta - first).astype(bf16).astype(f32)
            third = delta - first - second
            extra = jnp.where(lane == HD, first, jnp.where(lane == HD + 1, second, third))
            extra = jnp.where(lane < HD + 3, extra, 0.0)
            own = d_num if head == 0 else pltpu.roll(d_num, HD, 1)
            dn[here] = jnp.where(low, own, extra).astype(bf16)

    key, value = k_ref[0], v_ref[0]
    key_t = key.T
    dk_total, dv_total = None, None
    for at in range(0, frames, tile):
        here = slice(at, at + tile)
        query, d_num = q_ref[0, here], dn[here]
        expo = jnp.exp(dot(key, query, NT))
        d_score = (expo * dot(value, d_num, NT)).astype(bf16)
        dk_term = dot(d_score, query)
        dv_term = dot(expo.astype(bf16), d_num)
        dk_total = dk_term if dk_total is None else dk_total + dk_term
        dv_total = dv_term if dv_total is None else dv_total + dv_term
        dq_t[:, here] += dot(key_t, d_score)

    here = pl.ds(pl.multiple_of(step * rows, rows), rows)
    dk_all[here] = dk_total
    if head == 0:
        dv_ref[here] = dv_total.astype(bf16)
    else:
        both = jnp.where(low, dv_first[here].astype(f32), pltpu.roll(dv_total, HD, 1)).astype(bf16)
        own_ref[here, 2 * LANES :] = both
        second_ref[here, LANES:] = both

    @pl.when(step == pl.num_programs(0) - 1)
    def _():
        for at in range(0, frames, rows):
            part = slice(at, at + rows)
            cosine, sine = rotary(cos_ref, sin_ref, part)
            both = jnp.where(low, 0.125 * dq_t[:, part].T, pltpu.roll(dk_all[part], HD, 1))
            both = (both * cosine - swap_halves(both) * sine).astype(bf16)
            qk_ref[part] = both
            if head == 1:
                first, second = qk_first[part].astype(f32), both.astype(f32)
                own_ref[part, 0:LANES] = jnp.where(low, first, pltpu.roll(second, HD, 1)).astype(bf16)
                own_ref[part, LANES : 2 * LANES] = jnp.where(low, pltpu.roll(first, HD, 1), second).astype(bf16)
        if head == 1:
            ones = jnp.ones((8, frames), bf16)
            sums = dot(ones, own_ref[...])[0:1]
            for index in range(3):
                gb_ref[index : index + 1] = sums[:, index * LANES : (index + 1) * LANES]


def input_grad_kernel(
    base_ref, seg_ref, first_ref, second_ref, w_ref, x_ref, dx1_ref, table_ref, grad_ref, slots_ref, w_all, arrived
):
    shards, rows = first_ref.shape[:2]
    copies = [pltpu.make_async_copy(w_ref.at[shard], w_all.at[shard], arrived.at[shard]) for shard in range(shards)]
    for copy in copies:
        copy.start()
    block = base_ref[0]
    member = members(seg_ref, block, rows)
    scale = 1.0 + mod_rows(table_ref, seg_ref, block, member, 1)
    normal, inv = moments(x_ref[...].astype(f32))
    low = lax.broadcasted_iota(jnp.int32, (rows, LANES), 1) < HD
    d_hidden = None
    for shard in range(shards):
        first, second = first_ref[shard].astype(f32), second_ref[shard, :, :LANES].astype(f32)
        queries = jnp.where(low, first, pltpu.roll(second, HD, 1)).astype(bf16)
        keys = jnp.where(low, pltpu.roll(first, HD, 1), second).astype(bf16)
        whole_row = jnp.concatenate([queries, keys, second_ref[shard, :, LANES:]], axis=1)
        copies[shard].wait()
        term = dot(whole_row, w_all[shard], NT)
        d_hidden = term if d_hidden is None else d_hidden + term
    grad_ref[...] = dx1_ref[...] + norm_back(d_hidden * scale, normal, inv)
    sums = slot_sums(member, d_hidden) + slot_sums(member, d_hidden * normal)
    slots_ref[...] = jnp.concatenate(sums + [jnp.zeros((2, D), f32)], axis=0)


def add_kernel(own_x, came_x, own_y, came_y, by_y, by_x):
    by_y[...] = (own_x[0].astype(f32) + came_x[0].astype(f32)).astype(bf16)
    by_x[...] = (own_y[0].astype(f32) + came_y[0].astype(f32)).astype(bf16)


def total_kernel(own_x, came_x, by_y, own_y, came_y, by_x, *out_refs):
    half = by_y.shape[1]
    for group, ref in enumerate(out_refs):
        first = own_x[0, group].astype(f32) + came_x[0, group].astype(f32) + by_y[group].astype(f32)
        second = own_y[0, group].astype(f32) + came_y[0, group].astype(f32) + by_x[group].astype(f32)
        ref[:half] = first.astype(bf16)
        ref[half:] = second.astype(bf16)


def last_sum_kernel(*refs):
    *pieces, down_ref, out_ref, up_ref = refs
    total = sum(piece[...].astype(f32) for piece in pieces)
    wide = total.shape[1]
    down_ref[...] = total[: 2 * LANES]
    out_ref[...] = total[2 * LANES : 3 * LANES]
    up_ref[:, :wide] = total[3 * LANES : 4 * LANES]
    up_ref[:, wide:] = total[4 * LANES :]


def qkv_grad_kernel(h_ref, d_ref, out_ref):
    shards, depth = out_ref.shape[:2]
    for shard in range(shards):
        out_ref[shard] = dot(h_ref[:, shard * depth : (shard + 1) * depth], d_ref[...], TN).astype(bf16)


def qkv_piece_kernel(group_ref, came_ref, *out_refs):
    shards = came_ref.shape[0]
    units = 3 * shards // len(out_refs)
    for group, ref in enumerate(out_refs):
        start = lax.rem(group_ref[0] + group, len(out_refs)) * units
        for unit in range(units):
            part = pl.ds(pl.multiple_of((start + unit) // shards * LANES, LANES), LANES)
            ref[:, unit * LANES : (unit + 1) * LANES] = came_ref[lax.rem(start + unit, shards), :, part]


def qkv_sum_kernel(*refs):
    refs[-1][...] = sum(piece[...].astype(f32) for piece in refs[:-1])


def collect_kernel(shard_ref, seg_ref, tail_ref, out_ref, rows_ref, others_ref):
    shards = tail_ref.shape[0]
    groups = out_ref.shape[0]
    wide = out_ref.shape[2] - 2 * LANES
    shard = shard_ref[0]
    rows_ref[0:3] = tail_ref[0, 0:3]
    rows_ref[3:6] = tail_ref[shards - 1, 0:3]
    middle = sum(tail_ref[index, 0:3] for index in range(1, shards - 1))
    rows_ref[6:7] = jnp.sum(middle, axis=0, keepdims=True)
    rows_ref[7:8] = jnp.zeros((1, rows_ref.shape[1]), f32)
    others_ref[...] = sum(tail_ref[index, 3:4, 3 * LANES : 3 * LANES + 4 * D] for index in range(shards))

    def own(start, size):
        return pl.ds(pl.multiple_of(start + shard * size, LANES), size)

    sums = [jnp.sum(rows_ref[:, own(0, 6 * D // shards)], axis=0, keepdims=True)]
    for index in range(3 * D // shards // LANES):
        chunk = shard * (3 * D // shards // LANES) + index
        part = pl.ds(pl.multiple_of(chunk // shards * LANES, LANES), LANES)
        sums.append(tail_ref[lax.rem(chunk, shards), 3:4, part])
    sums += [others_ref[:, own(0, D // shards)], others_ref[:, own(D, 2 * D // shards)]]
    lane = lax.broadcasted_iota(jnp.int32, (1, LANES), 1)
    ids = jnp.zeros((1, LANES), jnp.int32)
    for index in range(6):
        where, slot = (0, index) if index < 3 else (shards - 1, index - 3)
        ids = jnp.where(lane == index, seg_ref[where, 6 + slot], ids)
    ids = jnp.where(lane == 6, seg_ref[1, 6] + seg_ref[1, 7] + seg_ref[1, 8], ids)
    rows_ref[7:8, 0:wide] = jnp.concatenate(sums, axis=1)
    for group in range(groups):
        out_ref[group, 0:7, 0:wide] = rows_ref[0:7, group * wide : (group + 1) * wide]
        out_ref[group, 7:8, 0:wide] = rows_ref[7:8, 0:wide]
        out_ref[group, :, wide:] = jnp.zeros((8, 2 * LANES), f32)
        out_ref[group, 0:1, wide : wide + LANES] = others_ref[:, own(3 * D, D // shards)]
        out_ref[group, 0:1, wide + LANES :] = ids.astype(f32)


def three(value):
    first = value.astype(bf16)
    second = (value - first.astype(f32)).astype(bf16)
    return [first, second, (value - first.astype(f32) - second.astype(f32)).astype(bf16)]


def table_kernel(*refs):
    all_parts, act_ref, w_ref, time_ref, ada_ref, time_grad_ref, b_ada, b_qkv, b_out, b_up, b_down = refs
    steps, wide = time_ref.shape[0], w_ref.shape[1]
    parts = [all_parts.at[index] for index in range(all_parts.shape[0])]
    step = lax.broadcasted_iota(jnp.int32, (steps, 1), 0)
    total = jnp.zeros((steps, wide), f32)
    for part in parts:
        for row in range(7):
            at = wide + LANES + row
            picked = part[0:1, at : at + 1].astype(jnp.int32) == step
            total = total + jnp.where(picked, part[row : row + 1, :wide], 0.0)
    pieces = three(total)
    act = act_ref[...]
    ada_ref[...] = dot(jnp.concatenate([act] * 3, axis=0), jnp.concatenate(pieces, axis=0), TN)
    d_act = dot(jnp.concatenate(pieces, axis=0), w_ref[...], NT)
    d_act = d_act[:steps] + d_act[steps : 2 * steps] + d_act[2 * steps :]
    value = time_ref[...]
    gate = 1.0 / (1.0 + jnp.exp(-value))
    for group in range(time_grad_ref.shape[0]):
        time_grad_ref[group] = d_act * gate * (1.0 + value * (1.0 - gate))
    first_row = sum(part[7:8, :wide] for part in parts)
    at = 0
    for ref in (b_ada, b_qkv, b_out, b_up):
        ref[...] = first_row[:, at : at + ref.shape[1]]
        at += ref.shape[1]
    b_down[...] = sum(part[0:1, wide : wide + b_down.shape[1]] for part in parts)


def spread(value, axis, size):
    return [value] + [
        lax.ppermute(value, axis, [(i, (i - step) % size) for i in range(size)]) for step in range(1, size)
    ]


def trade(pieces, axis, size):
    return [pieces[0]] + [
        lax.ppermute(pieces[size - step], axis, [(i, (i - step) % size) for i in range(size)])
        for step in range(1, size)
    ]


def in_order(pieces, axis, size):
    own = lax.axis_index(axis)
    out = []
    for place in range(size):
        pick = (place - own) % size
        value = pieces[0]
        for index in range(1, size):
            value = jnp.where(pick == index, pieces[index], value)
        out.append(value)
    return out


def hop(value, step):
    return lax.ppermute(value, "shard", [(i, i ^ step) for i in range(8)])


def after(value, *others):
    return pl.pallas_call(
        lambda *refs: None,
        in_specs=[anywhere] * (1 + len(others)),
        out_specs=anywhere,
        out_shape=jax.ShapeDtypeStruct(value.shape, value.dtype),
        input_output_aliases={0: 0},
        cost_estimate=FREE,
        name="after",
    )(value, *others)


anywhere = pl.BlockSpec(memory_space=pl.ANY)


def behind(kernel, count):
    return lambda *refs: kernel(*refs[count:])


def shape(*dims, kind=bf16):
    return jax.ShapeDtypeStruct(dims, kind)


def whole(*dims):
    return pl.BlockSpec(dims, lambda *_: (0,) * len(dims))


smem = pl.BlockSpec(memory_space=pltpu.SMEM)


def local_heads(
    groups, shards, frames, cotangent, seg_start, seg_length, seg_step, time_table,
    w_ada, b_ada, w_qkv, b_qkv, w_out, b_out, w_up, b_up, w_down, b_down,
):
    rows = frames.shape[0]
    packed = rows * shards
    steps = time_table.shape[0]
    shard = lax.axis_index("shard")
    depth = D // shards
    wide = D // groups

    group = lax.axis_index("grp")
    order = shard ^ jnp.array(ORDER, jnp.int32)

    inverse = 10000.0 ** (-jnp.arange(HD // 2, dtype=f32) / (HD // 2))
    phase = inverse[:, None] * jnp.arange(packed, dtype=f32)[None, :]
    cosine, sine = jnp.cos(phase), jnp.sin(phase)

    activated = jax.nn.silu(time_table).astype(bf16)
    act_own = lax.dynamic_slice_in_dim(activated, shard * depth, depth, 1)
    partial_mod = dot(act_own, w_ada)
    mod_wide = partial_mod.shape[1]
    biases = [b.astype(f32) for b in (b_ada, b_qkv, b_out, b_up, b_down)]
    sizes = [b.shape[0] for b in biases]
    segs = jnp.concatenate((seg_start, seg_length, seg_step), axis=1).astype(f32)
    extra = jnp.concatenate(biases + [jnp.floor(segs[0] / 128.0), segs[0] % 128.0])
    extra_rows = -(-extra.shape[0] // mod_wide)
    extra = jnp.pad(extra, (0, extra_rows * mod_wide - extra.shape[0])).reshape(extra_rows, mod_wide)
    units = 3 * shards // groups
    first = group * units
    by_unit = w_qkv.reshape(depth, units, LANES).transpose(1, 0, 2)
    which = jnp.minimum((jnp.arange(shards) - first) % shards, units - 1)
    by_shard = jnp.take(by_unit, which, axis=0, mode="clip")
    w_cols = jnp.broadcast_to(by_shard[None], (groups, shards, depth, LANES)).reshape(groups * shards, depth, LANES)
    w_cols = lax.all_to_all(w_cols, ("grp", "shard"), split_axis=0, concat_axis=0, tiled=True).reshape(groups, D, LANES)
    small = jnp.concatenate((partial_mod, extra), axis=0).astype(bf16)
    small = lax.all_gather(small, "shard", axis=0).astype(f32)
    held = after(frames, small)
    chips = [frames, hop(frames, 2), hop(frames, 4), hop(held, 6)]

    mod_own = jnp.sum(small[:, :steps], axis=0).astype(bf16)
    high = lax.all_gather(after(mod_own, w_cols), "grp", axis=1, tiled=True)

    w_heads = jnp.concatenate(
        [lax.dynamic_index_in_dim(w_cols, (part * shards + shard) // units, 0, keepdims=False) for part in range(3)], axis=1
    )

    chips = [held] + [after(piece, high) for piece in chips[1:]]
    others = [hop(piece, 1) for piece in chips]

    pack = jnp.concatenate((w_down, w_out, w_up[:, :wide], w_up[:, wide:]), axis=0)
    weights = lax.all_gather(pack, ("grp", "shard"), axis=0).reshape(groups, shards, 5 * LANES, wide)

    extra = small[:, steps:].reshape(shards, extra_rows * mod_wide)
    full, at = [], 0
    for size in sizes:
        full.append(extra[:, at : at + size].reshape(1, shards * size))
        at += size
    ada_bias, qkv_bias, out_bias, up_bias, down_bias = full
    seg_all = (extra[:, at : at + 9] * 128.0 + extra[:, at + 9 : at + 18]).astype(jnp.int32)
    qkv_bias = lax.dynamic_index_in_dim(qkv_bias.reshape(3, shards, LANES), shard, 1, keepdims=False)
    qkv_bias = qkv_bias.reshape(1, 3 * LANES)
    table = high.astype(f32) + ada_bias

    ordered = lambda width: pl.BlockSpec((rows, width), lambda i, order: (order[i], 0))
    ordered_heads = pl.BlockSpec((2, rows, LANES), lambda i, order: (0, order[i], 0))
    by_block = lambda width: pl.BlockSpec((rows, width), lambda i: (i, 0))
    two_heads = pl.BlockSpec((2, rows, LANES), lambda i: (0, i, 0))
    frame_pieces = [piece[None] for piece in chips + others]
    q, k, v, h1_all = pl.pallas_call(
        qkv_kernel,
        grid_spec=pltpu.PrefetchScalarGridSpec(
            num_scalar_prefetch=1,
            grid=(shards,),
            in_specs=[smem]
            + [pl.BlockSpec(memory_space=pl.ANY)] * len(frame_pieces)
            + [whole(steps, 2 * D), whole(D, 3 * LANES), whole(1, 3 * LANES)] + [pl.BlockSpec((HD // 2, rows), lambda i, order: (0, order[i]))] * 2,
            out_specs=[ordered_heads] * 3 + [ordered(D)],
            scratch_shapes=[pltpu.VMEM((shards, rows, D), bf16), pltpu.SemaphoreType.DMA((len(frame_pieces),))],
        ),
        out_shape=[shape(2, packed, LANES)] * 3 + [shape(packed, D)],
        compiler_params=params(60),
        cost_estimate=FREE,
        name="qkv",
    )(order, seg_all, *frame_pieces, table[:, : 2 * D], w_heads, qkv_bias, cosine, sine)

    attn_flops = 2 * 2 * packed * packed * 256
    some_rows = packed // 2
    some = pl.BlockSpec((some_rows, LANES), lambda i: (i, 0))
    o_heads, mixed, norm = pl.pallas_call(
        attend_kernel,
        grid=(packed // some_rows,),
        in_specs=[pl.BlockSpec((2, some_rows, LANES), lambda i: (0, i, 0))] + [whole(2, packed, LANES)] * 2,
        out_specs=[some] * 3,
        out_shape=[shape(packed, LANES), shape(packed, LANES, kind=f32), shape(packed, LANES, kind=f32)],
        compiler_params=params(60),
        cost_estimate=FREE,
        name="attend",
    )(q, k, v)

    o = lax.all_to_all(o_heads.reshape(shards, rows, LANES), "shard", split_axis=0, concat_axis=0, tiled=True)
    base = shard.astype(jnp.int32).reshape(1)
    block_flops = 2 * rows * D * D * 10
    out, dx1, d_mixed, pair, keep, send, slots_ff, gb_out, gb_up, gb_down = pl.pallas_call(
        block_kernel,
        grid=(1,),
        in_specs=[
            smem, smem, whole(rows, D), whole(rows, D), whole(shards, rows, LANES), whole(steps, 6 * D),
            whole(groups, shards, 5 * LANES, wide), whole(1, D), whole(1, 2 * D), whole(1, D),
        ],
        out_specs=[
            whole(rows, D), whole(rows, D), whole(shards, rows, LANES), whole(rows, 4 * D), whole(rows, 2 * D),
            whole(rows, 2 * D), whole(12, D), whole(1, D), whole(1, 2 * D), whole(1, D),
        ],
        out_shape=[
            shape(rows, D), shape(rows, D, kind=f32), shape(shards, rows, LANES), shape(rows, 4 * D), shape(rows, 2 * D),
            shape(rows, 2 * D), shape(12, D, kind=f32),
            shape(1, D, kind=f32), shape(1, 2 * D, kind=f32), shape(1, D, kind=f32),
        ],
        compiler_params=params(60),
        cost_estimate=FREE,
        name="block",
    )(order, seg_all, frames, cotangent, o, table, weights, out_bias, up_bias, down_bias)

    d_heads = lax.all_to_all(d_mixed, "shard", split_axis=0, concat_axis=0, tiled=True).reshape(packed, LANES)

    send, pair_send = hop(send, 1), hop(pair, 1)
    half = (2, groups, 5 * LANES // 2, wide)
    first_x, first_y, own_x, own_y = pl.pallas_call(
        weight_grad_kernel,
        grid=(1,),
        in_specs=[smem, smem, whole(rows, 2 * D), whole(rows, 2 * D), whole(rows, 4 * D), whole(rows, 4 * D)],
        out_specs=[whole(*half)] * 4,
        out_shape=[shape(*half)] * 4,
        compiler_params=params(60),
        cost_estimate=FREE,
        name="weight_grads",
    )(order, group.astype(jnp.int32).reshape(1), keep, send, pair, pair_send)
    first_x, first_y = after(first_x, d_heads), after(first_y, d_heads)

    back_specs = lambda head: [
        pl.BlockSpec((1, packed, LANES), lambda i: (head, 0, 0)),
        pl.BlockSpec((1, packed, LANES), lambda i: (head, i, 0)),
        pl.BlockSpec((1, packed, LANES), lambda i: (head, i, 0)),
    ] + [whole(packed, LANES)] * 3 + [whole(HD // 2, packed)] * 2
    back_scratch = [pltpu.VMEM((packed, LANES), bf16), pltpu.VMEM((LANES, packed), f32), pltpu.VMEM((packed, LANES), f32)]
    arguments = (q, k, v, d_heads, mixed, norm, cosine, sine)
    came_x, came_y = hop(first_x, 2), hop(first_y, 4)
    qk_first, dv_first = pl.pallas_call(
        behind(partial(attend_back_kernel, 0), 2),
        grid=(1,),
        in_specs=[anywhere] * 2 + back_specs(0),
        out_specs=[whole(packed, LANES), whole(packed, LANES)],
        out_shape=[shape(packed, LANES)] * 2,
        scratch_shapes=back_scratch,
        compiler_params=params(60),
        cost_estimate=FREE,
        name="attend_back_first",
    )(first_x, first_y, *arguments)
    d_first = lax.all_to_all(qk_first.reshape(shards, rows, LANES), "shard", split_axis=0, concat_axis=0, tiled=True)
    second, d_own, gb_qkv = pl.pallas_call(
        partial(attend_back_kernel, 1),
        grid=(1,),
        in_specs=back_specs(1) + [whole(packed, LANES)] * 2,
        out_specs=[whole(packed, 2 * LANES), whole(packed, 3 * LANES), whole(3, LANES)],
        out_shape=[shape(packed, 2 * LANES), shape(packed, 3 * LANES), shape(3, LANES, kind=f32)],
        scratch_shapes=back_scratch,
        compiler_params=params(60),
        cost_estimate=FREE,
        name="attend_back_second",
    )(*arguments, qk_first, dv_first)
    farther = pl.BlockSpec((1, *half[1:]), lambda i: (1, 0, 0, 0))
    next_y, next_x = pl.pallas_call(
        add_kernel,
        grid=(1,),
        in_specs=[farther] * 4,
        out_specs=[whole(*half[1:])] * 2,
        out_shape=[shape(*half[1:])] * 2,
        compiler_params=params(60),
        cost_estimate=FREE,
        name="add",
    )(own_x, came_x, own_y, came_y)
    g_send = pl.pallas_call(
        behind(qkv_grad_kernel, 3),
        grid=(1,),
        in_specs=[anywhere] * 3 + [whole(packed, D), whole(packed, 3 * LANES)],
        out_specs=whole(shards, depth, 3 * LANES),
        out_shape=shape(shards, depth, 3 * LANES),
        compiler_params=params(60),
        cost_estimate=FREE,
        name="qkv_grad",
    )(next_y, next_x, d_first, h1_all, d_own)
    second = after(second, next_y, next_x)
    d_second = lax.all_to_all(second.reshape(shards, rows, 2 * LANES), "shard", split_axis=0, concat_axis=0, tiled=True)
    next_y, next_x = hop(next_y, 4), hop(next_x, 2)
    w_all = lax.all_gather(after(w_heads, q), "shard", axis=0)
    by_shard = lambda *dims: pl.BlockSpec((1, *dims), lambda i: (i, 0, 0))
    grad_frames, slots_qkv = pl.pallas_call(
        behind(input_grad_kernel, 1),
        grid=(1,),
        in_specs=[
            anywhere, smem, smem, whole(shards, rows, LANES), whole(shards, rows, 2 * LANES), pl.BlockSpec(memory_space=pl.ANY),
            whole(rows, D), whole(rows, D), whole(steps, 2 * D),
        ],
        out_specs=[whole(rows, D), whole(8, D)],
        out_shape=[shape(rows, D, kind=f32), shape(8, D, kind=f32)],
        scratch_shapes=[pltpu.VMEM((shards, D, 3 * LANES), bf16), pltpu.SemaphoreType.DMA((shards,))],
        compiler_params=params(60),
        cost_estimate=FREE,
        name="input_grad",
    )(g_send, base, seg_all, d_first, d_second, w_all, frames, dx1, table[:, : 2 * D])

    g_came = lax.all_to_all(after(g_send, slots_qkv), "shard", split_axis=0, concat_axis=0, tiled=True)

    d_slot = jnp.concatenate((slots_qkv[:6], slots_ff), axis=0).reshape(6, 3, D).transpose(1, 0, 2).reshape(3, 6 * D)
    row_sums = jnp.concatenate((gb_qkv.reshape(-1), gb_out[0], gb_up[0], gb_down[0]))
    sum_rows = -(-row_sums.shape[0] // (6 * D))
    row_sums = jnp.pad(row_sums, (0, sum_rows * 6 * D - row_sums.shape[0])).reshape(sum_rows, 6 * D)
    nearer = whole(1, *half[1:])
    totals = pl.pallas_call(
        behind(total_kernel, 1),
        grid=(1,),
        in_specs=[anywhere] + [nearer, nearer, whole(*half[1:])] * 2,
        out_specs=[whole(5 * LANES, wide)] * groups,
        out_shape=[shape(5 * LANES, wide)] * groups,
        compiler_params=params(60),
        cost_estimate=FREE,
        name="total",
    )(slots_qkv, own_x, came_x, next_y, own_y, came_y, next_x)
    tail = after(jnp.concatenate((d_slot, row_sums), axis=0), totals[0])
    tail = lax.all_gather(tail, "shard", axis=0)
    totals = trade(totals, "grp", groups)
    parts = pl.pallas_call(
        behind(collect_kernel, 1 + groups),
        grid=(1,),
        in_specs=[anywhere] * (1 + groups) + [smem, smem, whole(shards, 4, 6 * D)],
        out_specs=whole(groups, 8, mod_wide + 2 * LANES),
        out_shape=shape(groups, 8, mod_wide + 2 * LANES, kind=f32),
        scratch_shapes=[pltpu.VMEM((8, 6 * D), f32), pltpu.VMEM((1, 4 * D), f32)],
        compiler_params=params(20),
        cost_estimate=FREE,
        name="collect",
    )(g_came, *totals, base, seg_all, tail)
    g_down, g_out, g_up = pl.pallas_call(
        last_sum_kernel,
        grid=(1,),
        in_specs=[whole(5 * LANES, wide)] * groups,
        out_specs=[whole(2 * LANES, wide), whole(LANES, wide), whole(LANES, 2 * wide)],
        out_shape=[shape(2 * LANES, wide, kind=f32), shape(LANES, wide, kind=f32), shape(LANES, 2 * wide, kind=f32)],
        compiler_params=params(20),
        cost_estimate=FREE,
        name="last_sum",
    )(*totals)
    parts_own = parts
    parts = lax.all_to_all(parts, "grp", split_axis=0, concat_axis=0, tiled=True)
    pieces = pl.pallas_call(
        behind(qkv_piece_kernel, 1),
        grid=(1,),
        in_specs=[anywhere, smem, whole(shards, depth, 3 * LANES)],
        out_specs=[whole(depth, units * LANES)] * groups,
        out_shape=[shape(depth, units * LANES)] * groups,
        compiler_params=params(16),
        cost_estimate=FREE,
        name="qkv_pieces",
    )(parts_own, group.astype(jnp.int32).reshape(1), g_came)
    g_qkv = pl.pallas_call(
        qkv_sum_kernel,
        grid=(1,),
        in_specs=[whole(depth, units * LANES)] * groups,
        out_specs=whole(depth, units * LANES),
        out_shape=shape(depth, units * LANES, kind=f32),
        compiler_params=params(16),
        cost_estimate=FREE,
        name="qkv_sum",
    )(*trade(pieces, "grp", groups))
    table_own = lax.dynamic_slice_in_dim(time_table, shard * depth, depth, 1)
    g_ada, g_table, *sums = pl.pallas_call(
        table_kernel,
        grid=(1,),
        in_specs=[whole(groups, 8, mod_wide + 2 * LANES), whole(steps, depth), whole(depth, mod_wide), whole(steps, depth)],
        out_specs=[whole(depth, mod_wide), whole(groups, steps, depth)] + [whole(1, size) for size in sizes],
        out_shape=[shape(depth, mod_wide, kind=f32), shape(groups, steps, depth, kind=f32)]
        + [shape(1, size, kind=f32) for size in sizes],
        compiler_params=params(20),
        cost_estimate=FREE,
        name="table",
    )(parts, act_own, w_ada, table_own)
    gb_ada, gb_qkv, gb_out, gb_up, gb_down = [total.reshape(-1) for total in sums]
    g_table = jnp.sum(lax.all_to_all(g_table, "grp", split_axis=0, concat_axis=0, tiled=True), axis=0)
    return (
        out, grad_frames, g_table, g_ada, gb_ada, g_qkv, gb_qkv, g_out, gb_out, g_up, gb_up, g_down, gb_down,
    )


def solution(mesh):
    in_specs = (
        P(("grp", "shard"), None),
        P(("grp", "shard"), None),
        P(("grp", "shard"), None),
        P(("grp", "shard"), None),
        P(("grp", "shard"), None),
        P(),
        P("shard", "grp"),
        P("shard"),
        P("shard", "grp"),
        P("shard"),
        P("shard", "grp"),
        P("shard"),
        P("shard", "grp"),
        P("shard"),
        P("shard", "grp"),
        P("shard"),
    )
    out_specs = (
        P(("grp", "shard"), None),
        P(("grp", "shard"), None),
        P(None, "shard"),
        P("shard", "grp"),
        P("shard"),
        P("shard", "grp"),
        P("shard"),
        P("shard", "grp"),
        P("shard"),
        P("shard", "grp"),
        P("shard"),
        P("shard", "grp"),
        P("shard"),
    )
    by_heads = mesh.shape["shard"] * 2 * HD == D and mesh.shape["grp"] == 4
    local = partial(local_heads, mesh.shape["grp"], mesh.shape["shard"]) if by_heads else local_any
    return jax.shard_map(local, mesh=mesh, in_specs=in_specs, out_specs=out_specs, check_vma=False)
```

```python
from functools import partial

import jax
import jax.numpy as jnp
from jax import lax
from jax.experimental import pallas as pl
from jax.experimental.pallas import tpu as pltpu
from jax.sharding import PartitionSpec as P

D = 1024
H = 16
HD = 64


eps_norm = 1e-06
top_precision = lax.Precision.HIGHEST


def normalize(tensor):
    centred = tensor - jnp.mean(tensor, axis=-1, keepdims=True)
    return centred * lax.rsqrt(jnp.mean(centred * centred, axis=-1, keepdims=True) + eps_norm)


def modulate(tensor, scale_vec, shift_vec):
    return normalize(tensor) * (1.0 + scale_vec) + shift_vec


def angles(positions):
    half_width = HD // 2
    inverse = 10000.0 ** (-jnp.arange(half_width, dtype=jnp.float32) / half_width)
    phase_grid = positions[:, None] * inverse[None, :]
    return (jnp.cos(phase_grid), jnp.sin(phase_grid))


def rotate(tensor, cosine_vals, sine_vals):
    row_total = tensor.shape[0]
    halves = tensor.reshape(row_total, H, 2, HD // 2)
    former = halves[:, :, 0]
    latter = halves[:, :, 1]
    cosine_part = cosine_vals[:, None, :]
    sine_part = sine_vals[:, None, :]
    turned = jnp.stack(
        (former * cosine_part - latter * sine_part, latter * cosine_part + former * sine_part),
        axis=2,
    )
    return turned.reshape(row_total, D)


def tile_width(row_total):
    for candidate in (512, 256, 128):
        return candidate
    return row_total


def head_view(tensor):
    return tensor.reshape(tensor.shape[0], H, HD)


def local_any(
    frames,
    cotangent,
    seg_start,
    seg_length,
    seg_step,
    time_table,
    w_ada,
    b_ada,
    w_qkv,
    b_qkv,
    w_out,
    b_out,
    w_up,
    b_up,
    w_down,
    b_down,
):
    frame_rows = frames.shape[0]
    positions = lax.axis_index("shard") * frame_rows + jnp.arange(frame_rows, dtype=jnp.int32)
    slot_start = seg_start[0]
    slot_end = slot_start + seg_length[0]
    member_mask = (positions[:, None] >= slot_start[None, :]) & (
        positions[:, None] < slot_end[None, :]
    )
    member = member_mask.astype(jnp.float32)
    seg_low = jnp.sum(jnp.where(member_mask, slot_start[None, :], 0), axis=1)
    seg_high = jnp.sum(jnp.where(member_mask, slot_end[None, :], 0), axis=1)
    cosine_vals, sine_vals = angles((positions - seg_low).astype(jnp.float32))
    columns = (
        lax.all_gather(w_ada, "grp", axis=1, tiled=True),
        lax.all_gather(w_qkv, "grp", axis=1, tiled=True),
        lax.all_gather(w_out, "grp", axis=1, tiled=True),
        lax.all_gather(w_up, "grp", axis=1, tiled=True),
        lax.all_gather(w_down, "grp", axis=1, tiled=True),
    )
    gathered = (
        lax.all_gather(columns[0], "shard", axis=0, tiled=True),
        lax.all_gather(columns[1], "shard", axis=0, tiled=True),
        lax.all_gather(columns[2], "shard", axis=0, tiled=True),
        lax.all_gather(columns[3], "shard", axis=0, tiled=True),
        lax.all_gather(columns[4], "shard", axis=0, tiled=True),
        lax.all_gather(b_ada, "shard", axis=0, tiled=True),
        lax.all_gather(b_qkv, "shard", axis=0, tiled=True),
        lax.all_gather(b_out, "shard", axis=0, tiled=True),
        lax.all_gather(b_up, "shard", axis=0, tiled=True),
        lax.all_gather(b_down, "shard", axis=0, tiled=True),
    )
    ada_full, qkv_full, out_full, up_full, down_full = (
        gathered[0],
        gathered[1],
        gathered[2],
        gathered[3],
        gathered[4],
    )
    ada_bias, qkv_bias, out_bias, up_bias, down_bias = [
        bias_row.astype(jnp.float32) for bias_row in gathered[5:]
    ]
    step_onehot = (
        seg_step[0][:, None] == jnp.arange(time_table.shape[0], dtype=jnp.int32)[None, :]
    ).astype(jnp.float32)
    time_rows = jnp.dot(step_onehot, time_table, precision=top_precision)
    activated = jax.nn.silu(time_rows).astype(jnp.bfloat16)
    modulation = jnp.dot(activated, ada_full, preferred_element_type=jnp.float32) + ada_bias
    frame_mod = jnp.dot(member, modulation, precision=top_precision)
    shift_attn, scale_attn, gate_attn, shift_ff, scale_ff, gate_ff = jnp.split(frame_mod, 6, axis=1)
    inputs = frames.astype(jnp.float32)
    hidden_attn = modulate(inputs, scale_attn, shift_attn).astype(jnp.bfloat16)
    projected = jnp.dot(hidden_attn, qkv_full, preferred_element_type=jnp.float32) + qkv_bias
    queries = rotate(projected[:, :D], cosine_vals, sine_vals).astype(jnp.bfloat16)
    keys_rot = rotate(projected[:, D : 2 * D], cosine_vals, sine_vals).astype(jnp.bfloat16)
    values = projected[:, 2 * D :].astype(jnp.bfloat16)
    query_heads = head_view(queries)
    key_heads = head_view(keys_rot)
    value_heads = head_view(values)
    zero_heads = jnp.zeros((frame_rows, H, HD), jnp.float32)
    key_piece = lax.all_gather(keys_rot, "shard", axis=0, tiled=True)
    value_piece = lax.all_gather(values, "shard", axis=0, tiled=True)
    piece_rows = key_piece.shape[0]
    tile_rows = tile_width(piece_rows)
    tiles = piece_rows // tile_rows

    def tile_step(partial_sums, tile_item):
        key_tile, value_tile, offset = tile_item
        key_pos = offset + jnp.arange(tile_rows, dtype=jnp.int32)
        inside = (key_pos[None, :] >= seg_low[:, None]) & (key_pos[None, :] < seg_high[:, None])
        scores = 0.125 * jnp.einsum(
            "rhd,khd->hrk", query_heads, head_view(key_tile), preferred_element_type=jnp.float32
        )
        expo = jnp.where(inside[None], jnp.exp(scores), 0.0)
        numerator, denominator = partial_sums
        numerator = numerator + jnp.einsum(
            "hrk,khd->rhd",
            expo.astype(jnp.bfloat16),
            head_view(value_tile),
            preferred_element_type=jnp.float32,
        )
        denominator = denominator + jnp.sum(expo, axis=2).T
        return ((numerator, denominator), None)

    tile_items = (
        key_piece.reshape(tiles, tile_rows, D),
        value_piece.reshape(tiles, tile_rows, D),
        jnp.arange(tiles, dtype=jnp.int32) * tile_rows,
    )
    numerator, denominator = lax.scan(
        tile_step, (zero_heads, jnp.zeros((frame_rows, H), jnp.float32)), tile_items
    )[0]
    mixed = numerator / denominator[:, :, None]
    mixed_low = mixed.reshape(frame_rows, D).astype(jnp.bfloat16)
    attn_branch = jnp.dot(mixed_low, out_full, preferred_element_type=jnp.float32) + out_bias
    after_attn = inputs + gate_attn * attn_branch
    hidden_ff = modulate(after_attn, scale_ff, shift_ff).astype(jnp.bfloat16)
    upward = jnp.dot(hidden_ff, up_full, preferred_element_type=jnp.float32) + up_bias
    activation = jax.nn.gelu(upward, approximate=True).astype(jnp.bfloat16)
    ff_branch = jnp.dot(activation, down_full, preferred_element_type=jnp.float32) + down_bias
    output = (after_attn + gate_ff * ff_branch).astype(jnp.bfloat16)
    columns_back = (
        lax.all_gather(w_ada, "grp", axis=1, tiled=True),
        lax.all_gather(w_qkv, "grp", axis=1, tiled=True),
        lax.all_gather(w_out, "grp", axis=1, tiled=True),
        lax.all_gather(w_up, "grp", axis=1, tiled=True),
        lax.all_gather(w_down, "grp", axis=1, tiled=True),
    )
    gathered_back = (
        lax.all_gather(columns_back[0], "shard", axis=0, tiled=True),
        lax.all_gather(columns_back[1], "shard", axis=0, tiled=True),
        lax.all_gather(columns_back[2], "shard", axis=0, tiled=True),
        lax.all_gather(columns_back[3], "shard", axis=0, tiled=True),
        lax.all_gather(columns_back[4], "shard", axis=0, tiled=True),
    )
    ada_back, qkv_back, out_back, up_back, down_back = (
        gathered_back[0],
        gathered_back[1],
        gathered_back[2],
        gathered_back[3],
        gathered_back[4],
    )
    grad_out = cotangent.astype(jnp.float32)
    d_branch = (gate_ff * grad_out).astype(jnp.bfloat16)
    d_gate_ff = grad_out * ff_branch
    g_down = jnp.dot(activation.T, d_branch, preferred_element_type=jnp.float32)
    gb_down = jnp.sum(d_branch.astype(jnp.float32), axis=0)
    d_activation = jnp.dot(d_branch, down_back.T, preferred_element_type=jnp.float32)
    gelu_pull = jax.vjp(partial(jax.nn.gelu, approximate=True), upward)[1]
    d_upward = gelu_pull(d_activation)[0].astype(jnp.bfloat16)
    g_up = jnp.dot(hidden_ff.T, d_upward, preferred_element_type=jnp.float32)
    gb_up = jnp.sum(d_upward.astype(jnp.float32), axis=0)
    d_hidden_ff = jnp.dot(d_upward, up_back.T, preferred_element_type=jnp.float32)
    ff_pull = jax.vjp(modulate, after_attn, scale_ff, shift_ff)[1]
    dx_ff, d_scale_ff, d_shift_ff = ff_pull(d_hidden_ff)
    d_after = grad_out + dx_ff
    d_attn = (gate_attn * d_after).astype(jnp.bfloat16)
    d_gate_attn = d_after * attn_branch
    g_out = jnp.dot(mixed_low.T, d_attn, preferred_element_type=jnp.float32)
    gb_out = jnp.sum(d_attn.astype(jnp.float32), axis=0)
    d_mixed = jnp.dot(d_attn, out_back.T, preferred_element_type=jnp.float32).astype(jnp.bfloat16)
    d_mixed_heads = head_view(d_mixed).astype(jnp.float32)
    delta = jnp.sum(d_mixed_heads * mixed, axis=2) / denominator
    d_numer = (d_mixed_heads / denominator[:, :, None]).astype(jnp.bfloat16).reshape(frame_rows, D)
    dnum_heads = head_view(d_numer)
    delta_heads = delta.T
    key_piece = lax.all_gather(keys_rot, "shard", axis=0, tiled=True)
    value_piece = lax.all_gather(values, "shard", axis=0, tiled=True)
    piece_rows = key_piece.shape[0]
    fold_tile_rows = tile_width(piece_rows)
    tiles = piece_rows // fold_tile_rows

    def tile_step(grad_sum, tile_item):
        key_tile, value_tile, offset = tile_item
        key_pos = offset + jnp.arange(fold_tile_rows, dtype=jnp.int32)
        inside = (key_pos[None, :] >= seg_low[:, None]) & (key_pos[None, :] < seg_high[:, None])
        scores = 0.125 * jnp.einsum(
            "rhd,khd->hrk", query_heads, head_view(key_tile), preferred_element_type=jnp.float32
        )
        expo = jnp.where(inside[None], jnp.exp(scores), 0.0)
        slope = jnp.einsum(
            "rhd,khd->hrk", dnum_heads, head_view(value_tile), preferred_element_type=jnp.float32
        )
        d_scores = (expo * (slope - delta_heads[:, :, None])).astype(jnp.bfloat16)
        grad_sum = grad_sum + 0.125 * jnp.einsum(
            "hrk,khd->rhd", d_scores, head_view(key_tile), preferred_element_type=jnp.float32
        )
        return (grad_sum, None)

    tile_items = (
        key_piece.reshape(tiles, fold_tile_rows, D),
        value_piece.reshape(tiles, fold_tile_rows, D),
        jnp.arange(tiles, dtype=jnp.int32) * fold_tile_rows,
    )
    d_query = lax.scan(tile_step, zero_heads, tile_items)[0]
    delta_all = lax.all_gather(delta, "shard", axis=0, tiled=True)

    def fold_key_grad(running, piece):
        query_piece, dnum_piece = piece
        piece_rows = query_piece.shape[0]
        tile_rows = tile_width(piece_rows)
        tiles = piece_rows // tile_rows

        def tile_step(grad_pair, tile_item):
            query_tile, dnum_tile, delta_tile, offset = tile_item
            query_pos = offset + jnp.arange(tile_rows, dtype=jnp.int32)
            inside = (query_pos[:, None] >= seg_low[None, :]) & (
                query_pos[:, None] < seg_high[None, :]
            )
            query_tile_heads = head_view(query_tile)
            dnum_tile_heads = head_view(dnum_tile)
            scores = 0.125 * jnp.einsum(
                "qhd,rhd->hqr", query_tile_heads, key_heads, preferred_element_type=jnp.float32
            )
            expo = jnp.where(inside[None], jnp.exp(scores), 0.0)
            slope = jnp.einsum(
                "qhd,rhd->hqr", dnum_tile_heads, value_heads, preferred_element_type=jnp.float32
            )
            d_scores = (expo * (slope - delta_tile.T[:, :, None])).astype(jnp.bfloat16)
            d_keys, d_values = grad_pair
            d_keys = d_keys + 0.125 * jnp.einsum(
                "hqr,qhd->rhd", d_scores, query_tile_heads, preferred_element_type=jnp.float32
            )
            d_values = d_values + jnp.einsum(
                "hqr,qhd->rhd",
                expo.astype(jnp.bfloat16),
                dnum_tile_heads,
                preferred_element_type=jnp.float32,
            )
            return ((d_keys, d_values), None)

        tile_items = (
            query_piece.reshape(tiles, tile_rows, D),
            dnum_piece.reshape(tiles, tile_rows, D),
            delta_all.reshape(tiles, tile_rows, H),
            jnp.arange(tiles, dtype=jnp.int32) * tile_rows,
        )
        return lax.scan(tile_step, running, tile_items)[0]

    d_keys, d_values = fold_key_grad(
        (zero_heads, zero_heads),
        (
            lax.all_gather(queries, "shard", axis=0, tiled=True),
            lax.all_gather(d_numer, "shard", axis=0, tiled=True),
        ),
    )
    grad_query = rotate(d_query.reshape(frame_rows, D), cosine_vals, -sine_vals)
    grad_key = rotate(d_keys.reshape(frame_rows, D), cosine_vals, -sine_vals)
    d_projected = jnp.concatenate(
        (grad_query, grad_key, d_values.reshape(frame_rows, D)), axis=1
    ).astype(jnp.bfloat16)
    g_qkv = jnp.dot(hidden_attn.T, d_projected, preferred_element_type=jnp.float32)
    gb_qkv = jnp.sum(d_projected.astype(jnp.float32), axis=0)
    d_hidden_attn = jnp.dot(d_projected, qkv_back.T, preferred_element_type=jnp.float32)
    attn_pull = jax.vjp(modulate, inputs, scale_attn, shift_attn)[1]
    dx_attn, d_scale_attn, d_shift_attn = attn_pull(d_hidden_attn)
    grad_frames = d_after + dx_attn
    d_frame_mod = jnp.concatenate(
        (d_shift_attn, d_scale_attn, d_gate_attn, d_shift_ff, d_scale_ff, d_gate_ff), axis=1
    )
    d_slot = jnp.dot(member.T, d_frame_mod, precision=top_precision)
    g_ada = jnp.dot(activated.astype(jnp.float32).T, d_slot, precision=top_precision)
    gb_ada = jnp.sum(d_slot, axis=0)
    d_activated = jnp.dot(
        d_slot, ada_back.T, precision=top_precision, preferred_element_type=jnp.float32
    )
    silu_pull = jax.vjp(jax.nn.silu, time_rows)[1]
    d_time_rows = silu_pull(d_activated)[0]
    g_table = jnp.dot(step_onehot.T, d_time_rows, precision=top_precision)
    group_sums = (
        lax.psum_scatter(g_ada, "shard", scatter_dimension=0, tiled=True),
        lax.psum_scatter(g_qkv, "shard", scatter_dimension=0, tiled=True),
        lax.psum_scatter(g_out, "shard", scatter_dimension=0, tiled=True),
        lax.psum_scatter(g_up, "shard", scatter_dimension=0, tiled=True),
        lax.psum_scatter(g_down, "shard", scatter_dimension=0, tiled=True),
        lax.psum_scatter(gb_ada, "shard", scatter_dimension=0, tiled=True),
        lax.psum_scatter(gb_qkv, "shard", scatter_dimension=0, tiled=True),
        lax.psum_scatter(gb_out, "shard", scatter_dimension=0, tiled=True),
        lax.psum_scatter(gb_up, "shard", scatter_dimension=0, tiled=True),
        lax.psum_scatter(gb_down, "shard", scatter_dimension=0, tiled=True),
        lax.psum_scatter(g_table, "shard", scatter_dimension=1, tiled=True),
    )
    wide_sums = (
        lax.psum_scatter(group_sums[0], "grp", scatter_dimension=1, tiled=True),
        lax.psum_scatter(group_sums[1], "grp", scatter_dimension=1, tiled=True),
        lax.psum_scatter(group_sums[2], "grp", scatter_dimension=1, tiled=True),
        lax.psum_scatter(group_sums[3], "grp", scatter_dimension=1, tiled=True),
        lax.psum_scatter(group_sums[4], "grp", scatter_dimension=1, tiled=True),
    )
    small_sums = lax.psum(
        (group_sums[5], group_sums[6], group_sums[7], group_sums[8], group_sums[9], group_sums[10]),
        "grp",
    )
    finals = tuple(wide_sums) + tuple(small_sums)
    return (
        output,
        grad_frames,
        finals[10],
        finals[0],
        finals[5],
        finals[1],
        finals[6],
        finals[2],
        finals[7],
        finals[3],
        finals[8],
        finals[4],
        finals[9],
    )


LANES = 128
FREE = pl.CostEstimate(flops=2**20, bytes_accessed=2**16, transcendentals=0)
CHIPS = (2, 4, 6)
ORDER = (0, 2, 4, 6, 1, 3, 5, 7)
SEPARATE = -(2.0**100)
GELU_C = 0.7978845608028654
GELU_A = 0.044715
NT = (((1,), (1,)), ((), ()))
TN = (((0,), (0,)), ((), ()))
f32 = jnp.float32
bf16 = jnp.bfloat16


def dot(left, right, dims=(((1,), (0,)), ((), ()))):
    return lax.dot_general(left, right, dims, preferred_element_type=f32)


def params(limit_mib, steps=1):
    return pltpu.CompilerParams(
        dimension_semantics=("arbitrary",) * steps, vmem_limit_bytes=limit_mib * 2**20
    )


def moments(value):
    centred = value - jnp.mean(value, axis=1, keepdims=True)
    inv = lax.rsqrt(jnp.mean(centred * centred, axis=1, keepdims=True) + eps_norm)
    return centred * inv, inv


def norm_back(weighted, normal, inv):
    return (
        weighted
        - jnp.mean(weighted, axis=1, keepdims=True)
        - normal * jnp.mean(weighted * normal, axis=1, keepdims=True)
    ) * inv


def swap_halves(value):
    lane = lax.broadcasted_iota(jnp.int32, value.shape, 1)
    return jnp.where(lane % HD < HD // 2, pltpu.roll(value, 96, 1), pltpu.roll(value, 32, 1))


def rotary(cos_ref, sin_ref, here):
    cosine, sine = cos_ref[:, here].T, sin_ref[:, here].T
    return jnp.concatenate([cosine] * 4, axis=1), jnp.concatenate([-sine, sine] * 2, axis=1)


def members(seg_ref, block, rows):
    place = block * rows + lax.broadcasted_iota(jnp.int32, (rows, LANES), 0)
    out = []
    for slot in range(3):
        begin = seg_ref[block, slot]
        out.append((place >= begin) & (place < begin + seg_ref[block, 3 + slot]))
    return out


def mod_rows(table_ref, seg_ref, block, member, part):
    first, second, third = [table_ref[pl.ds(seg_ref[block, 6 + slot], 1), pl.ds(part * D, D)] for slot in range(3)]
    out = []
    for at in range(0, D, LANES):
        here = slice(at, at + LANES)
        out.append(jnp.where(member[0], first[:, here], jnp.where(member[1], second[:, here], third[:, here])))
    return jnp.concatenate(out, axis=1)


def slot_sums(member, value):
    out = []
    for column in member:
        sums = [
            jnp.sum(jnp.where(column, value[:, at : at + LANES], 0.0), axis=0, keepdims=True) for at in range(0, D, LANES)
        ]
        out.append(jnp.concatenate(sums, axis=1))
    return out


def qkv_kernel(order_ref, seg_ref, *refs):
    step = pl.program_id(0)
    last = pl.num_programs(0) - 1
    *pieces, table_ref, w_ref, b_ref, cos_ref, sin_ref, q_ref, k_ref, v_ref, h_ref, x_all, arrived = refs
    block = order_ref[step]
    rows = x_all.shape[1]
    copies, at = [], 0
    for piece in pieces:
        here = x_all.at[at : at + piece.shape[0]]
        copies.append((at, pltpu.make_async_copy(piece, here, arrived.at[len(copies)])))
        at += piece.shape[0]

    @pl.when(step == 0)
    def _():
        for _, copy in copies:
            copy.start()

    for at, copy in copies:

        @pl.when(step == at)
        def _(copy=copy):
            copy.wait()

    member = members(seg_ref, block, rows)
    normal, _ = moments(x_all[step].astype(f32))
    shift = mod_rows(table_ref, seg_ref, block, member, 0)
    scale = mod_rows(table_ref, seg_ref, block, member, 1)
    hidden = (normal * (1.0 + scale) + shift).astype(bf16)
    h_ref[...] = hidden
    projected = dot(hidden, w_ref[...]) + b_ref[...]
    cosine, sine = rotary(cos_ref, sin_ref, slice(None))
    turned = []
    for part in range(2):
        piece = projected[:, part * LANES : (part + 1) * LANES]
        turned.append(piece * cosine + swap_halves(piece) * sine)
    queries = turned[0].astype(bf16).astype(f32) * 0.125
    keys = turned[1]
    values = projected[:, 2 * LANES :]
    lane = lax.broadcasted_iota(jnp.int32, (rows, LANES), 1)
    lane_row = lane[:1]
    begins, ends = jnp.full((1, LANES), 2**30, jnp.int32), jnp.zeros((1, LANES), jnp.int32)
    for index in range(6):
        where, slot = (0, index) if index < 3 else (last, index - 3)
        begin = seg_ref[where, slot]
        begins = jnp.where(lane_row == HD + index, begin, begins)
        ends = jnp.where(lane_row == HD + index, begin + seg_ref[where, 3 + slot], ends)
    place = block * rows + lax.broadcasted_iota(jnp.int32, (rows, LANES), 0)
    inside = (place >= begins) & (place < ends)
    query_extra = jnp.where(inside | (lane >= HD + 6), 0.0, SEPARATE)
    key_extra = jnp.where(inside, 1.0, 0.0)
    value_extra = jnp.where((lane >= HD) & (lane < HD + 3), 1.0, 0.0)
    low = lane < HD
    for head in range(2):
        for ref, value, extra in (
            (q_ref, queries, query_extra),
            (k_ref, keys, key_extra),
            (v_ref, values, value_extra),
        ):
            own = value if head == 0 else pltpu.roll(value, HD, 1)
            ref[head] = jnp.where(low, own, extra).astype(bf16)


def attend_kernel(q_ref, k_ref, v_ref, o_ref, mixed_ref, l_ref):
    keys_in_all = k_ref.shape[1]
    tile = 256
    ratios, sums = [], []
    for head in range(2):
        query = q_ref[head]
        total = None
        for at in range(0, keys_in_all, tile):
            expo = jnp.exp(dot(query, k_ref[head, at : at + tile], NT))
            term = dot(expo.astype(bf16), v_ref[head, at : at + tile])
            total = term if total is None else total + term
        norm = total[:, HD : HD + 1]
        ratios.append(total / norm)
        sums.append(norm)
    lane = lax.broadcasted_iota(jnp.int32, ratios[0].shape, 1)
    mixed = jnp.where(lane < HD, ratios[0], pltpu.roll(ratios[1], HD, 1))
    mixed_ref[...] = mixed
    o_ref[...] = mixed.astype(bf16)
    l_ref[...] = jnp.where(lane < HD, sums[0], sums[1])


def block_kernel(
    order_ref, seg_ref, x_ref, cot_ref, o_ref, table_ref, w_ref, b_out_ref, b_up_ref, b_down_ref,
    out_ref, dx1_ref, do_ref, pair_ref, keep_ref, send_ref, slots_ref, gb_out_ref, gb_up_ref, gb_down_ref,
):
    rows = x_ref.shape[0]
    groups, shards = w_ref.shape[:2]
    block = order_ref[0]
    member = members(seg_ref, block, rows)
    modulation = partial(mod_rows, table_ref, seg_ref, block, member)
    wide = D // groups

    def weight(group, start):
        return w_ref[group, :, start : start + LANES, :].reshape(D, wide)

    def weight_down(group):
        return w_ref[group, :, 0 : 2 * LANES, :].reshape(2 * D, wide)

    def by_core(value, width, other):
        parts = [value[:, at : at + width] for at in range(0, value.shape[1], width)]
        even, odd = jnp.concatenate(parts[0::2], axis=1), jnp.concatenate(parts[1::2], axis=1)
        return jnp.where((block % 2 == 0) != other, even, odd)

    def share(start, value, width):
        half = value.shape[1] // 2
        keep_ref[:, start : start + half] = by_core(value, width, False)
        send_ref[:, start : start + half] = by_core(value, width, True)

    mixed = jnp.concatenate([o_ref[shard] for shard in range(shards)], axis=1)
    share(D, mixed, LANES)
    attn = jnp.concatenate([dot(mixed, weight(group, 256)) for group in range(groups)], axis=1)
    attn = attn + b_out_ref[...]
    gate1 = modulation(2)
    after = x_ref[...].astype(f32) + gate1 * attn
    normal, inv = moments(after)
    scale2 = 1.0 + modulation(4)
    hidden = (normal * scale2 + modulation(3)).astype(bf16)
    share(D + D // 2, hidden, LANES)
    up = [dot(hidden, weight(group, start)) for group in range(groups) for start in (384, 512)]
    up = jnp.concatenate(up, axis=1) + b_up_ref[...]
    inner = jnp.tanh(GELU_C * (up + GELU_A * (up * up * up)))
    act = (0.5 * up * (1.0 + inner)).astype(bf16)
    share(0, act, 2 * LANES)
    slope = 0.5 * (1.0 + inner) + (0.5 * GELU_C) * up * (1.0 - inner * inner) * (
        1.0 + (3.0 * GELU_A) * up * up
    )
    branch = jnp.concatenate([dot(act, weight_down(group)) for group in range(groups)], axis=1)
    branch = branch + b_down_ref[...]
    gate2 = modulation(5)
    out_ref[...] = (after + gate2 * branch).astype(bf16)

    cot = cot_ref[...].astype(f32)
    dff = (gate2 * cot).astype(bf16)
    pair_ref[:, 0:D] = dff
    gb_down_ref[...] = jnp.sum(dff.astype(f32), axis=0, keepdims=True)
    d_gate2 = slot_sums(member, cot * branch)
    d_act = sum(dot(dff[:, g * wide : (g + 1) * wide], weight_down(g), NT) for g in range(groups))
    du = (d_act * slope).astype(bf16)
    pair_ref[:, 2 * D :] = du
    gb_up_ref[...] = jnp.sum(du.astype(f32), axis=0, keepdims=True)
    d_hidden = None
    for index in range(2 * groups):
        piece = du[:, index * wide : (index + 1) * wide]
        term = dot(piece, weight(index // 2, 384 + LANES * (index % 2)), NT)
        d_hidden = term if d_hidden is None else d_hidden + term
    d_shift2 = slot_sums(member, d_hidden)
    d_scale2 = slot_sums(member, d_hidden * normal)
    d_after = cot + norm_back(d_hidden * scale2, normal, inv)
    dx1_ref[...] = d_after
    d_gate1 = slot_sums(member, d_after * attn)
    da = (gate1 * d_after).astype(bf16)
    pair_ref[:, D : 2 * D] = da
    gb_out_ref[...] = jnp.sum(da.astype(f32), axis=0, keepdims=True)
    d_mixed = sum(dot(da[:, g * wide : (g + 1) * wide], weight(g, 256), NT) for g in range(groups))
    d_mixed = d_mixed.astype(bf16)
    for shard in range(shards):
        do_ref[shard] = d_mixed[:, shard * LANES : (shard + 1) * LANES]
    slots_ref[...] = jnp.concatenate(d_gate1 + d_shift2 + d_scale2 + d_gate2, axis=0)


def weight_grad_kernel(
    order_ref, group_ref, keep_ref, send_ref, pair_ref, pair2_ref, first_x, first_y, own_x, own_y
):
    groups, half, wide = first_x.shape[1:]

    def product(at, width, start, stop):
        here = pl.ds(pl.multiple_of(at, LANES), width)
        return (
            dot(keep_ref[:, here], pair_ref[:, start:stop], TN) + dot(send_ref[:, here], pair2_ref[:, start:stop], TN)
        ).astype(bf16)

    places = (((own_x, 0), (own_y, 0)), ((first_x, 0), (own_y, 1)), ((own_x, 1), (first_y, 0)), ((first_x, 1), (first_y, 1)))
    for index in range(4):
        chip = order_ref[index] // 2
        down = product(chip * 2 * LANES, 2 * LANES, 0, D)
        out = product(D + chip * LANES, LANES, D, 2 * D)
        up = product(D + D // 2 + chip * LANES, LANES, 2 * D, 4 * D)
        (by_x, at_x), (by_y, at_y) = places[index]
        for group in range(groups):
            to = (group + groups - group_ref[0]) % groups
            columns = slice(group * wide, (group + 1) * wide)
            by_x[at_x, to, 0:256, :] = down[:, columns]
            by_x[at_x, to, 256:half, :] = out[: half - 256, columns]
            by_y[at_y, to, 0 : 384 - half, :] = out[half - 256 :, columns]
            for part in range(2):
                start = 384 - half + 128 * part
                at = (2 * group + part) * wide
                by_y[at_y, to, start : start + 128, :] = up[:, at : at + wide]


def attend_back_kernel(head, q_ref, k_ref, v_ref, do_ref, mixed_ref, l_ref, cos_ref, sin_ref, *refs):
    *refs, dn, dq_t, dk_all = refs
    if head == 0:
        qk_ref, dv_ref = refs
    else:
        qk_first, dv_first, second_ref, own_ref, gb_ref = refs
        qk_ref = second_ref.at[:, :LANES]
    step = pl.program_id(0)
    rows = k_ref.shape[1]
    frames = q_ref.shape[1]
    tile = 256
    lane = lax.broadcasted_iota(jnp.int32, (rows, LANES), 1)
    low = lane < HD

    @pl.when(step == 0)
    def _():
        dq_t[...] = jnp.zeros_like(dq_t)
        for at in range(0, frames, rows):
            here = slice(at, at + rows)
            d_out = do_ref[here].astype(f32)
            norm = l_ref[here]
            d_num = (d_out / norm).astype(bf16).astype(f32)
            mine = low if head == 0 else ~low
            total = jnp.sum(jnp.where(mine, d_out * mixed_ref[here], 0.0), axis=1, keepdims=True)
            delta = -total / norm[:, head * HD : head * HD + 1]
            first = delta.astype(bf16).astype(f32)
            second = (delta - first).astype(bf16).astype(f32)
            third = delta - first - second
            extra = jnp.where(lane == HD, first, jnp.where(lane == HD + 1, second, third))
            extra = jnp.where(lane < HD + 3, extra, 0.0)
            own = d_num if head == 0 else pltpu.roll(d_num, HD, 1)
            dn[here] = jnp.where(low, own, extra).astype(bf16)

    key, value = k_ref[0], v_ref[0]
    key_t = key.T
    dk_total, dv_total = None, None
    for at in range(0, frames, tile):
        here = slice(at, at + tile)
        query, d_num = q_ref[0, here], dn[here]
        expo = jnp.exp(dot(key, query, NT))
        d_score = (expo * dot(value, d_num, NT)).astype(bf16)
        dk_term = dot(d_score, query)
        dv_term = dot(expo.astype(bf16), d_num)
        dk_total = dk_term if dk_total is None else dk_total + dk_term
        dv_total = dv_term if dv_total is None else dv_total + dv_term
        dq_t[:, here] += dot(key_t, d_score)

    here = pl.ds(pl.multiple_of(step * rows, rows), rows)
    dk_all[here] = dk_total
    if head == 0:
        dv_ref[here] = dv_total.astype(bf16)
    else:
        both = jnp.where(low, dv_first[here].astype(f32), pltpu.roll(dv_total, HD, 1)).astype(bf16)
        own_ref[here, 2 * LANES :] = both
        second_ref[here, LANES:] = both

    @pl.when(step == pl.num_programs(0) - 1)
    def _():
        for at in range(0, frames, rows):
            part = slice(at, at + rows)
            cosine, sine = rotary(cos_ref, sin_ref, part)
            both = jnp.where(low, 0.125 * dq_t[:, part].T, pltpu.roll(dk_all[part], HD, 1))
            both = (both * cosine - swap_halves(both) * sine).astype(bf16)
            qk_ref[part] = both
            if head == 1:
                first, second = qk_first[part].astype(f32), both.astype(f32)
                own_ref[part, 0:LANES] = jnp.where(low, first, pltpu.roll(second, HD, 1)).astype(bf16)
                own_ref[part, LANES : 2 * LANES] = jnp.where(low, pltpu.roll(first, HD, 1), second).astype(bf16)
        if head == 1:
            ones = jnp.ones((8, frames), bf16)
            sums = dot(ones, own_ref[...])[0:1]
            for index in range(3):
                gb_ref[index : index + 1] = sums[:, index * LANES : (index + 1) * LANES]


def input_grad_kernel(
    base_ref, seg_ref, first_ref, second_ref, w_ref, x_ref, dx1_ref, table_ref, grad_ref, slots_ref, w_all, arrived
):
    shards, rows = first_ref.shape[:2]
    copies = [pltpu.make_async_copy(w_ref.at[shard], w_all.at[shard], arrived.at[shard]) for shard in range(shards)]
    for copy in copies:
        copy.start()
    block = base_ref[0]
    member = members(seg_ref, block, rows)
    scale = 1.0 + mod_rows(table_ref, seg_ref, block, member, 1)
    normal, inv = moments(x_ref[...].astype(f32))
    low = lax.broadcasted_iota(jnp.int32, (rows, LANES), 1) < HD
    d_hidden = None
    for shard in range(shards):
        first, second = first_ref[shard].astype(f32), second_ref[shard, :, :LANES].astype(f32)
        queries = jnp.where(low, first, pltpu.roll(second, HD, 1)).astype(bf16)
        keys = jnp.where(low, pltpu.roll(first, HD, 1), second).astype(bf16)
        whole_row = jnp.concatenate([queries, keys, second_ref[shard, :, LANES:]], axis=1)
        copies[shard].wait()
        term = dot(whole_row, w_all[shard], NT)
        d_hidden = term if d_hidden is None else d_hidden + term
    grad_ref[...] = dx1_ref[...] + norm_back(d_hidden * scale, normal, inv)
    sums = slot_sums(member, d_hidden) + slot_sums(member, d_hidden * normal)
    slots_ref[...] = jnp.concatenate(sums + [jnp.zeros((2, D), f32)], axis=0)


def add_kernel(own_x, came_x, own_y, came_y, by_y, by_x):
    by_y[...] = (own_x[0].astype(f32) + came_x[0].astype(f32)).astype(bf16)
    by_x[...] = (own_y[0].astype(f32) + came_y[0].astype(f32)).astype(bf16)


def total_kernel(own_x, came_x, by_y, own_y, came_y, by_x, *out_refs):
    half = by_y.shape[1]
    for group, ref in enumerate(out_refs):
        first = own_x[0, group].astype(f32) + came_x[0, group].astype(f32) + by_y[group].astype(f32)
        second = own_y[0, group].astype(f32) + came_y[0, group].astype(f32) + by_x[group].astype(f32)
        ref[:half] = first.astype(bf16)
        ref[half:] = second.astype(bf16)


def last_sum_kernel(*refs):
    *pieces, down_ref, out_ref, up_ref = refs
    total = sum(piece[...].astype(f32) for piece in pieces)
    wide = total.shape[1]
    down_ref[...] = total[: 2 * LANES]
    out_ref[...] = total[2 * LANES : 3 * LANES]
    up_ref[:, :wide] = total[3 * LANES : 4 * LANES]
    up_ref[:, wide:] = total[4 * LANES :]


def qkv_grad_kernel(h_ref, d_ref, out_ref):
    shards, depth = out_ref.shape[:2]
    for shard in range(shards):
        out_ref[shard] = dot(h_ref[:, shard * depth : (shard + 1) * depth], d_ref[...], TN).astype(bf16)


def qkv_piece_kernel(group_ref, came_ref, *out_refs):
    shards = came_ref.shape[0]
    units = 3 * shards // len(out_refs)
    for group, ref in enumerate(out_refs):
        start = lax.rem(group_ref[0] + group, len(out_refs)) * units
        for unit in range(units):
            part = pl.ds(pl.multiple_of((start + unit) // shards * LANES, LANES), LANES)
            ref[:, unit * LANES : (unit + 1) * LANES] = came_ref[lax.rem(start + unit, shards), :, part]


def qkv_sum_kernel(*refs):
    refs[-1][...] = sum(piece[...].astype(f32) for piece in refs[:-1])


def collect_kernel(shard_ref, seg_ref, tail_ref, out_ref, rows_ref, others_ref):
    shards = tail_ref.shape[0]
    groups = out_ref.shape[0]
    wide = out_ref.shape[2] - 2 * LANES
    shard = shard_ref[0]
    rows_ref[0:3] = tail_ref[0, 0:3]
    rows_ref[3:6] = tail_ref[shards - 1, 0:3]
    middle = sum(tail_ref[index, 0:3] for index in range(1, shards - 1))
    rows_ref[6:7] = jnp.sum(middle, axis=0, keepdims=True)
    rows_ref[7:8] = jnp.zeros((1, rows_ref.shape[1]), f32)
    others_ref[...] = sum(tail_ref[index, 3:4, 3 * LANES : 3 * LANES + 4 * D] for index in range(shards))

    def own(start, size):
        return pl.ds(pl.multiple_of(start + shard * size, LANES), size)

    sums = [jnp.sum(rows_ref[:, own(0, 6 * D // shards)], axis=0, keepdims=True)]
    for index in range(3 * D // shards // LANES):
        chunk = shard * (3 * D // shards // LANES) + index
        part = pl.ds(pl.multiple_of(chunk // shards * LANES, LANES), LANES)
        sums.append(tail_ref[lax.rem(chunk, shards), 3:4, part])
    sums += [others_ref[:, own(0, D // shards)], others_ref[:, own(D, 2 * D // shards)]]
    lane = lax.broadcasted_iota(jnp.int32, (1, LANES), 1)
    ids = jnp.zeros((1, LANES), jnp.int32)
    for index in range(6):
        where, slot = (0, index) if index < 3 else (shards - 1, index - 3)
        ids = jnp.where(lane == index, seg_ref[where, 6 + slot], ids)
    ids = jnp.where(lane == 6, seg_ref[1, 6] + seg_ref[1, 7] + seg_ref[1, 8], ids)
    rows_ref[7:8, 0:wide] = jnp.concatenate(sums, axis=1)
    for group in range(groups):
        out_ref[group, 0:7, 0:wide] = rows_ref[0:7, group * wide : (group + 1) * wide]
        out_ref[group, 7:8, 0:wide] = rows_ref[7:8, 0:wide]
        out_ref[group, :, wide:] = jnp.zeros((8, 2 * LANES), f32)
        out_ref[group, 0:1, wide : wide + LANES] = others_ref[:, own(3 * D, D // shards)]
        out_ref[group, 0:1, wide + LANES :] = ids.astype(f32)


def three(value):
    first = value.astype(bf16)
    second = (value - first.astype(f32)).astype(bf16)
    return [first, second, (value - first.astype(f32) - second.astype(f32)).astype(bf16)]


def table_kernel(*refs):
    all_parts, act_ref, w_ref, time_ref, ada_ref, time_grad_ref, b_ada, b_qkv, b_out, b_up, b_down = refs
    steps, wide = time_ref.shape[0], w_ref.shape[1]
    parts = [all_parts.at[index] for index in range(all_parts.shape[0])]
    step = lax.broadcasted_iota(jnp.int32, (steps, 1), 0)
    total = jnp.zeros((steps, wide), f32)
    for part in parts:
        for row in range(7):
            at = wide + LANES + row
            picked = part[0:1, at : at + 1].astype(jnp.int32) == step
            total = total + jnp.where(picked, part[row : row + 1, :wide], 0.0)
    pieces = three(total)
    act = act_ref[...]
    ada_ref[...] = dot(jnp.concatenate([act] * 3, axis=0), jnp.concatenate(pieces, axis=0), TN)
    d_act = dot(jnp.concatenate(pieces, axis=0), w_ref[...], NT)
    d_act = d_act[:steps] + d_act[steps : 2 * steps] + d_act[2 * steps :]
    value = time_ref[...]
    gate = 1.0 / (1.0 + jnp.exp(-value))
    for group in range(time_grad_ref.shape[0]):
        time_grad_ref[group] = d_act * gate * (1.0 + value * (1.0 - gate))
    first_row = sum(part[7:8, :wide] for part in parts)
    at = 0
    for ref in (b_ada, b_qkv, b_out, b_up):
        ref[...] = first_row[:, at : at + ref.shape[1]]
        at += ref.shape[1]
    b_down[...] = sum(part[0:1, wide : wide + b_down.shape[1]] for part in parts)


def spread(value, axis, size):
    return [value] + [
        lax.ppermute(value, axis, [(i, (i - step) % size) for i in range(size)]) for step in range(1, size)
    ]


def trade(pieces, axis, size):
    return [pieces[0]] + [
        lax.ppermute(pieces[size - step], axis, [(i, (i - step) % size) for i in range(size)])
        for step in range(1, size)
    ]


def in_order(pieces, axis, size):
    own = lax.axis_index(axis)
    out = []
    for place in range(size):
        pick = (place - own) % size
        value = pieces[0]
        for index in range(1, size):
            value = jnp.where(pick == index, pieces[index], value)
        out.append(value)
    return out


def hop(value, step):
    return lax.ppermute(value, "shard", [(i, i ^ step) for i in range(8)])


def after(value, *others):
    return pl.pallas_call(
        lambda *refs: None,
        in_specs=[anywhere] * (1 + len(others)),
        out_specs=anywhere,
        out_shape=jax.ShapeDtypeStruct(value.shape, value.dtype),
        input_output_aliases={0: 0},
        cost_estimate=FREE,
        name="after",
    )(value, *others)


anywhere = pl.BlockSpec(memory_space=pl.ANY)


def behind(kernel, count):
    return lambda *refs: kernel(*refs[count:])


def shape(*dims, kind=bf16):
    return jax.ShapeDtypeStruct(dims, kind)


def whole(*dims):
    return pl.BlockSpec(dims, lambda *_: (0,) * len(dims))


smem = pl.BlockSpec(memory_space=pltpu.SMEM)


def local_heads(
    groups, shards, frames, cotangent, seg_start, seg_length, seg_step, time_table,
    w_ada, b_ada, w_qkv, b_qkv, w_out, b_out, w_up, b_up, w_down, b_down,
):
    rows = frames.shape[0]
    packed = rows * shards
    steps = time_table.shape[0]
    shard = lax.axis_index("shard")
    depth = D // shards
    wide = D // groups

    group = lax.axis_index("grp")
    order = shard ^ jnp.array(ORDER, jnp.int32)

    inverse = 10000.0 ** (-jnp.arange(HD // 2, dtype=f32) / (HD // 2))
    phase = inverse[:, None] * jnp.arange(packed, dtype=f32)[None, :]
    cosine, sine = jnp.cos(phase), jnp.sin(phase)

    activated = jax.nn.silu(time_table).astype(bf16)
    act_own = lax.dynamic_slice_in_dim(activated, shard * depth, depth, 1)
    partial_mod = dot(act_own, w_ada)
    mod_wide = partial_mod.shape[1]
    biases = [b.astype(f32) for b in (b_ada, b_qkv, b_out, b_up, b_down)]
    sizes = [b.shape[0] for b in biases]
    segs = jnp.concatenate((seg_start, seg_length, seg_step), axis=1).astype(f32)
    extra = jnp.concatenate(biases + [jnp.floor(segs[0] / 128.0), segs[0] % 128.0])
    extra_rows = -(-extra.shape[0] // mod_wide)
    extra = jnp.pad(extra, (0, extra_rows * mod_wide - extra.shape[0])).reshape(extra_rows, mod_wide)
    units = 3 * shards // groups
    first = group * units
    by_unit = w_qkv.reshape(depth, units, LANES).transpose(1, 0, 2)
    which = jnp.minimum((jnp.arange(shards) - first) % shards, units - 1)
    by_shard = jnp.take(by_unit, which, axis=0, mode="clip")
    w_cols = jnp.broadcast_to(by_shard[None], (groups, shards, depth, LANES)).reshape(groups * shards, depth, LANES)
    w_cols = lax.all_to_all(w_cols, ("grp", "shard"), split_axis=0, concat_axis=0, tiled=True).reshape(groups, D, LANES)
    small = jnp.concatenate((partial_mod, extra), axis=0).astype(bf16)
    small = lax.all_gather(small, "shard", axis=0).astype(f32)
    held = after(frames, small)
    chips = [frames, hop(frames, 2), hop(frames, 4), hop(held, 6)]

    mod_own = jnp.sum(small[:, :steps], axis=0).astype(bf16)
    high = lax.all_gather(after(mod_own, w_cols), "grp", axis=1, tiled=True)

    w_heads = jnp.concatenate(
        [lax.dynamic_index_in_dim(w_cols, (part * shards + shard) // units, 0, keepdims=False) for part in range(3)], axis=1
    )

    chips = [held] + [after(piece, high) for piece in chips[1:]]
    others = [hop(piece, 1) for piece in chips]

    pack = jnp.concatenate((w_down, w_out, w_up[:, :wide], w_up[:, wide:]), axis=0)
    weights = lax.all_gather(pack, ("grp", "shard"), axis=0).reshape(groups, shards, 5 * LANES, wide)

    extra = small[:, steps:].reshape(shards, extra_rows * mod_wide)
    full, at = [], 0
    for size in sizes:
        full.append(extra[:, at : at + size].reshape(1, shards * size))
        at += size
    ada_bias, qkv_bias, out_bias, up_bias, down_bias = full
    seg_all = (extra[:, at : at + 9] * 128.0 + extra[:, at + 9 : at + 18]).astype(jnp.int32)
    qkv_bias = lax.dynamic_index_in_dim(qkv_bias.reshape(3, shards, LANES), shard, 1, keepdims=False)
    qkv_bias = qkv_bias.reshape(1, 3 * LANES)
    table = high.astype(f32) + ada_bias

    ordered = lambda width: pl.BlockSpec((rows, width), lambda i, order: (order[i], 0))
    ordered_heads = pl.BlockSpec((2, rows, LANES), lambda i, order: (0, order[i], 0))
    by_block = lambda width: pl.BlockSpec((rows, width), lambda i: (i, 0))
    two_heads = pl.BlockSpec((2, rows, LANES), lambda i: (0, i, 0))
    frame_pieces = [piece[None] for piece in chips + others]
    q, k, v, h1_all = pl.pallas_call(
        qkv_kernel,
        grid_spec=pltpu.PrefetchScalarGridSpec(
            num_scalar_prefetch=1,
            grid=(shards,),
            in_specs=[smem]
            + [pl.BlockSpec(memory_space=pl.ANY)] * len(frame_pieces)
            + [whole(steps, 2 * D), whole(D, 3 * LANES), whole(1, 3 * LANES)] + [pl.BlockSpec((HD // 2, rows), lambda i, order: (0, order[i]))] * 2,
            out_specs=[ordered_heads] * 3 + [ordered(D)],
            scratch_shapes=[pltpu.VMEM((shards, rows, D), bf16), pltpu.SemaphoreType.DMA((len(frame_pieces),))],
        ),
        out_shape=[shape(2, packed, LANES)] * 3 + [shape(packed, D)],
        compiler_params=params(60),
        cost_estimate=FREE,
        name="qkv",
    )(order, seg_all, *frame_pieces, table[:, : 2 * D], w_heads, qkv_bias, cosine, sine)

    attn_flops = 2 * 2 * packed * packed * 256
    some_rows = packed // 2
    some = pl.BlockSpec((some_rows, LANES), lambda i: (i, 0))
    o_heads, mixed, norm = pl.pallas_call(
        attend_kernel,
        grid=(packed // some_rows,),
        in_specs=[pl.BlockSpec((2, some_rows, LANES), lambda i: (0, i, 0))] + [whole(2, packed, LANES)] * 2,
        out_specs=[some] * 3,
        out_shape=[shape(packed, LANES), shape(packed, LANES, kind=f32), shape(packed, LANES, kind=f32)],
        compiler_params=params(60),
        cost_estimate=FREE,
        name="attend",
    )(q, k, v)

    o = lax.all_to_all(o_heads.reshape(shards, rows, LANES), "shard", split_axis=0, concat_axis=0, tiled=True)
    base = shard.astype(jnp.int32).reshape(1)
    block_flops = 2 * rows * D * D * 10
    out, dx1, d_mixed, pair, keep, send, slots_ff, gb_out, gb_up, gb_down = pl.pallas_call(
        block_kernel,
        grid=(1,),
        in_specs=[
            smem, smem, whole(rows, D), whole(rows, D), whole(shards, rows, LANES), whole(steps, 6 * D),
            whole(groups, shards, 5 * LANES, wide), whole(1, D), whole(1, 2 * D), whole(1, D),
        ],
        out_specs=[
            whole(rows, D), whole(rows, D), whole(shards, rows, LANES), whole(rows, 4 * D), whole(rows, 2 * D),
            whole(rows, 2 * D), whole(12, D), whole(1, D), whole(1, 2 * D), whole(1, D),
        ],
        out_shape=[
            shape(rows, D), shape(rows, D, kind=f32), shape(shards, rows, LANES), shape(rows, 4 * D), shape(rows, 2 * D),
            shape(rows, 2 * D), shape(12, D, kind=f32),
            shape(1, D, kind=f32), shape(1, 2 * D, kind=f32), shape(1, D, kind=f32),
        ],
        compiler_params=params(60),
        cost_estimate=FREE,
        name="block",
    )(order, seg_all, frames, cotangent, o, table, weights, out_bias, up_bias, down_bias)

    d_heads = lax.all_to_all(d_mixed, "shard", split_axis=0, concat_axis=0, tiled=True).reshape(packed, LANES)

    send, pair_send = hop(send, 1), hop(pair, 1)
    half = (2, groups, 5 * LANES // 2, wide)
    first_x, first_y, own_x, own_y = pl.pallas_call(
        weight_grad_kernel,
        grid=(1,),
        in_specs=[smem, smem, whole(rows, 2 * D), whole(rows, 2 * D), whole(rows, 4 * D), whole(rows, 4 * D)],
        out_specs=[whole(*half)] * 4,
        out_shape=[shape(*half)] * 4,
        compiler_params=params(36),
        cost_estimate=FREE,
        name="weight_grads",
    )(order, group.astype(jnp.int32).reshape(1), keep, send, pair, pair_send)
    first_x, first_y = after(first_x, d_heads), after(first_y, d_heads)

    back_specs = lambda head: [
        pl.BlockSpec((1, packed, LANES), lambda i: (head, 0, 0)),
        pl.BlockSpec((1, packed, LANES), lambda i: (head, i, 0)),
        pl.BlockSpec((1, packed, LANES), lambda i: (head, i, 0)),
    ] + [whole(packed, LANES)] * 3 + [whole(HD // 2, packed)] * 2
    back_scratch = [pltpu.VMEM((packed, LANES), bf16), pltpu.VMEM((LANES, packed), f32), pltpu.VMEM((packed, LANES), f32)]
    arguments = (q, k, v, d_heads, mixed, norm, cosine, sine)
    came_x, came_y = hop(first_x, 2), hop(first_y, 4)
    qk_first, dv_first = pl.pallas_call(
        behind(partial(attend_back_kernel, 0), 2),
        grid=(1,),
        in_specs=[anywhere] * 2 + back_specs(0),
        out_specs=[whole(packed, LANES), whole(packed, LANES)],
        out_shape=[shape(packed, LANES)] * 2,
        scratch_shapes=back_scratch,
        compiler_params=params(60),
        cost_estimate=FREE,
        name="attend_back_first",
    )(first_x, first_y, *arguments)
    d_first = lax.all_to_all(qk_first.reshape(shards, rows, LANES), "shard", split_axis=0, concat_axis=0, tiled=True)
    second, d_own, gb_qkv = pl.pallas_call(
        partial(attend_back_kernel, 1),
        grid=(1,),
        in_specs=back_specs(1) + [whole(packed, LANES)] * 2,
        out_specs=[whole(packed, 2 * LANES), whole(packed, 3 * LANES), whole(3, LANES)],
        out_shape=[shape(packed, 2 * LANES), shape(packed, 3 * LANES), shape(3, LANES, kind=f32)],
        scratch_shapes=back_scratch,
        compiler_params=params(60),
        cost_estimate=FREE,
        name="attend_back_second",
    )(*arguments, qk_first, dv_first)
    farther = pl.BlockSpec((1, *half[1:]), lambda i: (1, 0, 0, 0))
    next_y, next_x = pl.pallas_call(
        add_kernel,
        grid=(1,),
        in_specs=[farther] * 4,
        out_specs=[whole(*half[1:])] * 2,
        out_shape=[shape(*half[1:])] * 2,
        compiler_params=params(60),
        cost_estimate=FREE,
        name="add",
    )(own_x, came_x, own_y, came_y)
    g_send = pl.pallas_call(
        behind(qkv_grad_kernel, 3),
        grid=(1,),
        in_specs=[anywhere] * 3 + [whole(packed, D), whole(packed, 3 * LANES)],
        out_specs=whole(shards, depth, 3 * LANES),
        out_shape=shape(shards, depth, 3 * LANES),
        compiler_params=params(60),
        cost_estimate=FREE,
        name="qkv_grad",
    )(next_y, next_x, d_first, h1_all, d_own)
    second = after(second, next_y, next_x)
    d_second = lax.all_to_all(second.reshape(shards, rows, 2 * LANES), "shard", split_axis=0, concat_axis=0, tiled=True)
    next_y, next_x = hop(next_y, 4), hop(next_x, 2)
    w_all = lax.all_gather(after(w_heads, q), "shard", axis=0)
    by_shard = lambda *dims: pl.BlockSpec((1, *dims), lambda i: (i, 0, 0))
    grad_frames, slots_qkv = pl.pallas_call(
        behind(input_grad_kernel, 1),
        grid=(1,),
        in_specs=[
            anywhere, smem, smem, whole(shards, rows, LANES), whole(shards, rows, 2 * LANES), pl.BlockSpec(memory_space=pl.ANY),
            whole(rows, D), whole(rows, D), whole(steps, 2 * D),
        ],
        out_specs=[whole(rows, D), whole(8, D)],
        out_shape=[shape(rows, D, kind=f32), shape(8, D, kind=f32)],
        scratch_shapes=[pltpu.VMEM((shards, D, 3 * LANES), bf16), pltpu.SemaphoreType.DMA((shards,))],
        compiler_params=params(60),
        cost_estimate=FREE,
        name="input_grad",
    )(g_send, base, seg_all, d_first, d_second, w_all, frames, dx1, table[:, : 2 * D])

    g_came = lax.all_to_all(after(g_send, slots_qkv), "shard", split_axis=0, concat_axis=0, tiled=True)

    d_slot = jnp.concatenate((slots_qkv[:6], slots_ff), axis=0).reshape(6, 3, D).transpose(1, 0, 2).reshape(3, 6 * D)
    row_sums = jnp.concatenate((gb_qkv.reshape(-1), gb_out[0], gb_up[0], gb_down[0]))
    sum_rows = -(-row_sums.shape[0] // (6 * D))
    row_sums = jnp.pad(row_sums, (0, sum_rows * 6 * D - row_sums.shape[0])).reshape(sum_rows, 6 * D)
    nearer = whole(1, *half[1:])
    totals = pl.pallas_call(
        behind(total_kernel, 1),
        grid=(1,),
        in_specs=[anywhere] + [nearer, nearer, whole(*half[1:])] * 2,
        out_specs=[whole(5 * LANES, wide)] * groups,
        out_shape=[shape(5 * LANES, wide)] * groups,
        compiler_params=params(60),
        cost_estimate=FREE,
        name="total",
    )(slots_qkv, own_x, came_x, next_y, own_y, came_y, next_x)
    tail = after(jnp.concatenate((d_slot, row_sums), axis=0), totals[0])
    tail = lax.all_gather(tail, "shard", axis=0)
    totals = trade(totals, "grp", groups)
    parts = pl.pallas_call(
        behind(collect_kernel, 1 + groups),
        grid=(1,),
        in_specs=[anywhere] * (1 + groups) + [smem, smem, whole(shards, 4, 6 * D)],
        out_specs=whole(groups, 8, mod_wide + 2 * LANES),
        out_shape=shape(groups, 8, mod_wide + 2 * LANES, kind=f32),
        scratch_shapes=[pltpu.VMEM((8, 6 * D), f32), pltpu.VMEM((1, 4 * D), f32)],
        compiler_params=params(20),
        cost_estimate=FREE,
        name="collect",
    )(g_came, *totals, base, seg_all, tail)
    g_down, g_out, g_up = pl.pallas_call(
        last_sum_kernel,
        grid=(1,),
        in_specs=[whole(5 * LANES, wide)] * groups,
        out_specs=[whole(2 * LANES, wide), whole(LANES, wide), whole(LANES, 2 * wide)],
        out_shape=[shape(2 * LANES, wide, kind=f32), shape(LANES, wide, kind=f32), shape(LANES, 2 * wide, kind=f32)],
        compiler_params=params(20),
        cost_estimate=FREE,
        name="last_sum",
    )(*totals)
    parts_own = parts
    parts = lax.all_to_all(parts, "grp", split_axis=0, concat_axis=0, tiled=True)
    pieces = pl.pallas_call(
        behind(qkv_piece_kernel, 1),
        grid=(1,),
        in_specs=[anywhere, smem, whole(shards, depth, 3 * LANES)],
        out_specs=[whole(depth, units * LANES)] * groups,
        out_shape=[shape(depth, units * LANES)] * groups,
        compiler_params=params(16),
        cost_estimate=FREE,
        name="qkv_pieces",
    )(parts_own, group.astype(jnp.int32).reshape(1), g_came)
    g_qkv = pl.pallas_call(
        qkv_sum_kernel,
        grid=(1,),
        in_specs=[whole(depth, units * LANES)] * groups,
        out_specs=whole(depth, units * LANES),
        out_shape=shape(depth, units * LANES, kind=f32),
        compiler_params=params(16),
        cost_estimate=FREE,
        name="qkv_sum",
    )(*trade(pieces, "grp", groups))
    table_own = lax.dynamic_slice_in_dim(time_table, shard * depth, depth, 1)
    g_ada, g_table, *sums = pl.pallas_call(
        table_kernel,
        grid=(1,),
        in_specs=[whole(groups, 8, mod_wide + 2 * LANES), whole(steps, depth), whole(depth, mod_wide), whole(steps, depth)],
        out_specs=[whole(depth, mod_wide), whole(groups, steps, depth)] + [whole(1, size) for size in sizes],
        out_shape=[shape(depth, mod_wide, kind=f32), shape(groups, steps, depth, kind=f32)]
        + [shape(1, size, kind=f32) for size in sizes],
        compiler_params=params(20),
        cost_estimate=FREE,
        name="table",
    )(parts, act_own, w_ada, table_own)
    gb_ada, gb_qkv, gb_out, gb_up, gb_down = [total.reshape(-1) for total in sums]
    g_table = jnp.sum(lax.all_to_all(g_table, "grp", split_axis=0, concat_axis=0, tiled=True), axis=0)
    return (
        out, grad_frames, g_table, g_ada, gb_ada, g_qkv, gb_qkv, g_out, gb_out, g_up, gb_up, g_down, gb_down,
    )


def solution(mesh):
    in_specs = (
        P(("grp", "shard"), None),
        P(("grp", "shard"), None),
        P(("grp", "shard"), None),
        P(("grp", "shard"), None),
        P(("grp", "shard"), None),
        P(),
        P("shard", "grp"),
        P("shard"),
        P("shard", "grp"),
        P("shard"),
        P("shard", "grp"),
        P("shard"),
        P("shard", "grp"),
        P("shard"),
        P("shard", "grp"),
        P("shard"),
    )
    out_specs = (
        P(("grp", "shard"), None),
        P(("grp", "shard"), None),
        P(None, "shard"),
        P("shard", "grp"),
        P("shard"),
        P("shard", "grp"),
        P("shard"),
        P("shard", "grp"),
        P("shard"),
        P("shard", "grp"),
        P("shard"),
        P("shard", "grp"),
        P("shard"),
    )
    by_heads = mesh.shape["shard"] * 2 * HD == D and mesh.shape["grp"] == 4
    local = partial(local_heads, mesh.shape["grp"], mesh.shape["shard"]) if by_heads else local_any
    return jax.shard_map(local, mesh=mesh, in_specs=in_specs, out_specs=out_specs, check_vma=False)
```
